128 devices in a mesh: mlp: 16 (over z, y_hi, core), seq: 8 (over x, y_lo).
Axes of the slice: x: 4, y: 4 (y_hi: 2, y_lo: 2; y = y_hi * 2 + y_lo), z: 4, core: 2. Of those that a mesh axis runs over, the one named last changes fastest.
Arguments:
- tokens: bfloat16 [65536, 1024], P(('mlp', 'seq')), may hold values from -6 to 6
- qkv_weight: bfloat16 [1024, 3072], P(('mlp', 'seq')), may hold values from -0.25 to 0.25
- out_weight: bfloat16 [1024, 1024], P(('mlp', 'seq')), may hold values from -0.75 to 0.75
- up_weight: bfloat16 [1024, 4096], P('seq', 'mlp'), may hold values from -0.1875 to 0.1875
- down_weight: bfloat16 [4096, 1024], P('mlp', 'seq'), may hold values from -0.09375 to 0.09375
- ln1_gain: float32 [1024], replicated, may hold values from 0.1 to 1.9
- ln1_bias: float32 [1024], replicated, may hold values from -1.75 to 1.75
- q_bias: float32 [1024], replicated, may hold values from -1.75 to 1.75
- v_bias: float32 [1024], replicated, may hold values from -1.75 to 1.75
- out_bias: float32 [1024], replicated, may hold values from -1.75 to 1.75
- ln2_gain: float32 [1024], replicated, may hold values from 0.1 to 1.9
- ln2_bias: float32 [1024], replicated, may hold values from -1.75 to 1.75
- up_bias: float32 [4096], replicated, may hold values from -1.75 to 1.75
- down_bias: float32 [1024], replicated, may hold values from -1.75 to 1.75
- segment_ids: int32 [65536], P(('mlp', 'seq')), may hold values from 0 to 127, never falling along the last dimension, each value on 1 to 2048 neighbouring positions
- cotangent: bfloat16 [65536, 1024], P(('mlp', 'seq')), may hold values from -6 to 6
Outputs:
- output: bfloat16 [65536, 1024], P(('mlp', 'seq'))
- input_grad: float32 [65536, 1024], P(('mlp', 'seq'))
- qkv_weight_grad: float32 [1024, 3072], P(('mlp', 'seq'))
- out_weight_grad: float32 [1024, 1024], P(('mlp', 'seq'))
- up_weight_grad: float32 [1024, 4096], P('seq', 'mlp')
- down_weight_grad: float32 [4096, 1024], P('mlp', 'seq')
- ln1_gain_grad: float32 [1024], replicated
- ln1_bias_grad: float32 [1024], replicated
- q_bias_grad: float32 [1024], replicated
- v_bias_grad: float32 [1024], replicated
- out_bias_grad: float32 [1024], replicated
- ln2_gain_grad: float32 [1024], replicated
- ln2_bias_grad: float32 [1024], replicated
- up_bias_grad: float32 [4096], replicated
- down_bias_grad: float32 [1024], replicated
The draws below stay inside these ranges and needn't reach their ends.
Inputs may be any that keep to these rules, and one draw needn't show every extreme that they name: `segment_ids`: clip numbers never fall along the tokens; each clip holds 1 to 2048 tokens.
All inputs are finite; a program needn't handle non-finite values.
Results may differ from the reference program's by a relative error of at most 0.018.
Values may be sent and summed in bfloat16 or wider, within the bound.
No kernel may reach another device: no remote copies, remote signals or barrier semaphores. Data moves between devices by JAX's collectives and lax.ppermute only.
A program may use at most 256 MiB of HBM per device.

```python
import math
import jax
import jax.numpy as jnp
import numpy as np
from jax import lax

D = 1024
HEADS = 16
HEAD_DIM = 64
FF = 4096
BLOCK = 128
TOKENS = 65536


def levels(rng, extent, split, smallest, high):
    gain, own = 1.0, jax.random.fold_in(rng, 6)
    for position, parts in split:
        draws = jnp.exp(jax.random.uniform(jax.random.fold_in(own, position), (parts,), jnp.float32, smallest / len(split), high / len(split)))
        gain = gain * jnp.repeat(draws, extent[position] // parts).reshape([-1 if axis == position else 1 for axis in range(len(extent))])
    return gain


def profile(amount, total, reach, slope):
    weights = [(1 << 20) // math.isqrt(standing ** slope) + 1 for standing in range(2, amount + 1)]
    rest, holding = total - reach - (amount - 1), [1] * (amount - 1)
    while rest > 0:
        free = [i for i in range(amount - 1) if holding[i] < reach]
        pool, budget = sum([weights[i] for i in free]), rest
        for i in free:
            addition = min(reach - holding[i], max(1, budget * weights[i] // pool), rest)
            holding[i] = holding[i] + addition
            rest = rest - addition
    return np.array([reach] + holding)


def ragged_sizes(key, count, total, bound, lean):
    if count == 2:
        one = jax.random.randint(key, (), max(1, total - bound), min(bound, total - 1) + 1)
        return jnp.stack([one, total - one])
    tallies = jnp.asarray(profile(count, total, bound, lean), jnp.int32)
    pairs = (count - 1) // 2
    source_of, receiver = tallies[1:1 + 2 * pairs:2], tallies[2:2 + 2 * pairs:2]
    margin = jnp.minimum(source_of - 1, bound - receiver)
    passed = jax.random.randint(jax.random.fold_in(key, 1), (pairs,), 0, 1 << 20) % (margin + 1)
    tallies = tallies.at[1:1 + 2 * pairs:2].set(source_of - passed).at[2:2 + 2 * pairs:2].set(receiver + passed)
    return tallies[jax.random.permutation(jax.random.fold_in(key, 2), count)]


def centred(stream_key, extent, width, limit, shards=(), dtype=jnp.bfloat16):
    gain = levels(stream_key, extent, shards, -0.22, 0.18) if shards else 1.0
    values = jax.random.normal(stream_key, extent, jnp.float32) * width * gain
    return jnp.minimum(jnp.maximum(values, -limit), limit).astype(dtype)


def setup_inputs(seed: int = 0) -> dict:
    key_of = jax.random.split(jax.random.key(seed), 17)
    return {
        "tokens": centred(key_of[0], (TOKENS, D), 1.0, 6.0, ((0, 128),)),
        "qkv_weight": centred(key_of[1], (D, 3 * D), (D // 2) ** -0.5, 0.25, ((0, 128),)),
        "out_weight": centred(key_of[2], (D, D), (D // 16) ** -0.5, 0.75, ((0, 128),)),
        "up_weight": centred(key_of[3], (D, FF), D ** -0.5, 0.1875, ((0, 8), (1, 16))),
        "down_weight": centred(key_of[4], (FF, D), FF ** -0.5, 0.09375, ((0, 16), (1, 8))),
        "ln1_gain": jnp.clip(1.0 + 0.18 * jax.random.normal(key_of[5], (D,), jnp.float32), 0.1, 1.9),
        "ln1_bias": centred(key_of[6], (D,), 0.3, 1.75, (), jnp.float32),
        "q_bias": centred(key_of[7], (D,), 0.3, 1.75, (), jnp.float32),
        "v_bias": centred(key_of[8], (D,), 0.3, 1.75, (), jnp.float32),
        "out_bias": centred(key_of[9], (D,), 0.3, 1.75, (), jnp.float32),
        "ln2_gain": jnp.clip(1.0 + 0.18 * jax.random.normal(key_of[10], (D,), jnp.float32), 0.1, 1.9),
        "ln2_bias": centred(key_of[11], (D,), 0.3, 1.75, (), jnp.float32),
        "up_bias": centred(key_of[12], (FF,), 0.3, 1.75, (), jnp.float32),
        "down_bias": centred(key_of[13], (D,), 0.3, 1.75, (), jnp.float32),
        "segment_ids": jnp.searchsorted(jnp.cumsum(ragged_sizes(key_of[14], TOKENS // (4 * BLOCK), TOKENS, 16 * BLOCK, 0)), jnp.arange(TOKENS), side="right").astype(jnp.int32),
        "cotangent": centred(key_of[15], (TOKENS, D), 1.0, 6.0, ((0, 128),)),
    }


@jax.custom_vjp
def low(v):
    return lax.optimization_barrier(v.astype(jnp.bfloat16)).astype(jnp.float32)

@jax.custom_vjp
def low_back(v):
    return v

def low_keep(v):
    return (low(v), None)

def low_pass(kept, grad):
    return (grad,)

def back_keep(v):
    return (v, None)

def back_low(kept, grad):
    return (low(grad),)
low.defvjp(low_keep, low_pass)
low_back.defvjp(back_keep, back_low)

def product(left, right):
    return jnp.dot(left, right, precision=lax.Precision.HIGHEST, preferred_element_type=jnp.float32)

def layer_norm(values, gain_vec, bias_vec):
    center = values - lax.optimization_barrier(jnp.mean(values, axis=-1, keepdims=True))
    spread = lax.optimization_barrier(jnp.mean(center * center, axis=-1, keepdims=True))
    return center * lax.rsqrt(spread + 1e-05) * gain_vec + bias_vec

def attend_group(pieces):
    query_blocks, key_blocks, value_blocks, clip_blocks = pieces
    raw_scores = jnp.einsum('gqhd,gkhd->ghqk', query_blocks, key_blocks, precision=lax.Precision.HIGHEST) * HEAD_DIM ** (-0.5)
    scores = low_back(raw_scores)
    row_index = lax.broadcasted_iota(jnp.int32, (BLOCK, BLOCK), 0)
    col_index = lax.broadcasted_iota(jnp.int32, (BLOCK, BLOCK), 1)
    same_clip = clip_blocks[:, :, None] == clip_blocks[:, None, :]
    allowed = (same_clip & (row_index >= col_index)[None])[:, None]
    scores = jnp.where(allowed, scores, -1e+30)
    row_peak = lax.optimization_barrier(jnp.max(scores, axis=-1, keepdims=True))
    powers = jnp.exp(scores - row_peak)
    weights = low(powers / lax.optimization_barrier(jnp.sum(powers, axis=-1, keepdims=True)))
    return jnp.einsum('ghqk,gkhd->gqhd', weights, value_blocks, precision=lax.Precision.HIGHEST)

def attention(queries, key_rows, value_rows, segment_ids):
    groups = TOKENS // BLOCK
    per_step = math.gcd(groups, max(1, 4096 // BLOCK))

    def to_groups(values):
        return values.reshape(groups // per_step, per_step, BLOCK, HEADS, HEAD_DIM)
    mixed = lax.map(jax.checkpoint(attend_group), (to_groups(queries), to_groups(key_rows), to_groups(value_rows), segment_ids.reshape(groups // per_step, per_step, BLOCK)))
    return mixed.reshape(TOKENS, D)

def forward(tokens, qkv_weight, out_weight, up_weight, down_weight, ln1_gain, ln1_bias, q_bias, v_bias, out_bias, ln2_gain, ln2_bias, up_bias, down_bias, segment_ids):
    normed_one = low(layer_norm(tokens, ln1_gain, ln1_bias))
    projected = product(normed_one, qkv_weight) + jnp.concatenate([q_bias, jnp.zeros_like(q_bias), v_bias])
    queries = low(low_back(projected[:, :D]))
    key_rows = low(low_back(projected[:, D:2 * D]))
    value_rows = low(low_back(projected[:, 2 * D:]))
    mixed = low(low_back(attention(queries, key_rows, value_rows, segment_ids)))
    branch = low_back(product(mixed, out_weight))
    hidden = tokens + branch + out_bias
    normed_two = low(layer_norm(hidden, ln2_gain, ln2_bias))
    pre_act = low_back(product(normed_two, up_weight) + up_bias)
    activation = low(jax.nn.gelu(pre_act))
    return hidden + product(activation, down_weight) + down_bias

def reference(tokens, qkv_weight, out_weight, up_weight, down_weight, ln1_gain, ln1_bias, q_bias, v_bias, out_bias, ln2_gain, ln2_bias, up_bias, down_bias, segment_ids, cotangent):
    floats = [value.astype(jnp.float32) for value in (tokens, qkv_weight, out_weight, up_weight, down_weight, ln1_gain, ln1_bias, q_bias, v_bias, out_bias, ln2_gain, ln2_bias, up_bias, down_bias)]

    def layer(*values):
        return forward(*values, segment_ids)
    result, pullback = jax.vjp(layer, *floats)
    gradients = pullback(cotangent.astype(jnp.float32))
    return (result.astype(jnp.bfloat16), gradients[0], gradients[1], gradients[2], gradients[3], gradients[4], gradients[5], gradients[6], gradients[7], gradients[8], gradients[9], gradients[10], gradients[11], gradients[12], gradients[13])
```

```python
import itertools

import jax
import jax.numpy as jnp
from jax import lax
from jax.sharding import Mesh, PartitionSpec as P

HEADS = 16
HEAD_DIM = 64
BLOCK = 128
AXES = ("z", "yh", "c", "x", "yl")


def device_number(place):
    return (
        ((place["z"] * 2 + place["y"] // 2) * 2 + place["c"]) * 4 + place["x"]
    ) * 2 + place["y"] % 2


def exchange_pairs(axis, second):
    pairs = []
    for z, y, c, x in itertools.product(range(4), range(4), range(2), range(4)):
        here = {"z": z, "y": y, "c": c, "x": x}
        mask = 1 if (c == 0) != second else 3
        there = dict(here)
        there[axis] = here[axis] ^ mask
        pairs.append((device_number(here), device_number(there)))
    return pairs


def swap_axis(values, axis, second):
    return lax.ppermute(values, AXES, exchange_pairs(axis, second))


def swap_core(values):
    return lax.ppermute(values, "c", [(0, 1), (1, 0)])


def position(axis):
    if axis == "y":
        return lax.axis_index("yh") * 2 + lax.axis_index("yl")
    return lax.axis_index(axis)


def masks():
    core = lax.axis_index("c")
    first = jnp.where(core == 0, 1, 3)
    return first, 4 - first


def place_pieces(pieces, slots):
    out = jnp.zeros((len(pieces),) + pieces[0].shape, pieces[0].dtype)
    for piece, slot in zip(pieces, slots):
        out = lax.dynamic_update_index_in_dim(out, piece, slot, 0)
    return out


def gather_all(values, order):
    first, second = masks()
    for axis in order:
        here = position(axis)
        near = swap_axis(values, axis, False)
        far = swap_axis(jnp.stack([values, near]), axis, True)
        values = place_pieces(
            [values, near, far[0], far[1]],
            [here, here ^ first, here ^ second, here ^ second ^ first],
        )
    core = lax.axis_index("c")
    other = swap_core(values)
    return place_pieces([values, other], [core, 1 - core])


def scatter_sum(values, order):
    first, second = masks()
    core = lax.axis_index("c")

    def at(array, slot):
        return lax.dynamic_index_in_dim(array, slot, 0, keepdims=False)

    def add(left, right):
        return (left.astype(jnp.float32) + right.astype(jnp.float32)).astype(jnp.bfloat16)

    values = add(at(values, core), swap_core(at(values, 1 - core)))
    for axis in reversed(order):
        here = position(axis)
        far = swap_axis(
            jnp.stack([at(values, here ^ second), at(values, here ^ second ^ first)]), axis, True
        )
        near = swap_axis(add(at(values, here ^ first), far[1]), axis, False)
        values = at(values, here).astype(jnp.float32) + far[0].astype(jnp.float32)
        values = values + near.astype(jnp.float32)
        if axis != order[0]:
            values = values.astype(jnp.bfloat16)
    return values


def sum_everywhere(values):
    for axis in ("x", "y", "z"):
        for second in (False, True):
            values = values + swap_axis(values, axis, second)
    return values + swap_core(values)


def names_of(order):
    return ["c"] + list(reversed(order))


def split_y(array, names):
    at = names.index("y")
    shape = array.shape
    array = array.reshape(shape[:at] + (2, 2) + shape[at + 1 :])
    return array, names[:at] + ["yh", "yl"] + names[at + 1 :]


ROW_LAYOUT = ["z", "yh", "c", "x", "yl", "r", "k"]
UP_LAYOUT = ["x", "yl", "r", "z", "yh", "c", "k"]
DOWN_LAYOUT = ["z", "yh", "c", "r", "x", "yl", "k"]


def whole(array, order, layout, shape):
    array, names = split_y(array, names_of(order))
    names = names + ["r", "k"]
    return array.transpose([names.index(n) for n in layout]).reshape(shape)


def pieces_of(array, order, layout, rows, cols):
    sizes = {"z": 4, "yh": 2, "c": 2, "x": 4, "yl": 2, "r": rows, "k": cols}
    array = array.reshape([sizes[n] for n in layout])
    names = []
    for n in names_of(order):
        names += ["yh", "yl"] if n == "y" else [n]
    names += ["r", "k"]
    array = array.transpose([layout.index(n) for n in names])
    return array.reshape((2, 4, 4, 4, rows, cols))


def layer_norm(values, gain_vec, bias_vec):
    center = values - jnp.mean(values, axis=-1, keepdims=True)
    spread = jnp.mean(center * center, axis=-1, keepdims=True)
    return center * lax.rsqrt(spread + 1e-05) * gain_vec + bias_vec


def blocked(values):
    return values.reshape(values.shape[0] // BLOCK, BLOCK, HEADS, HEAD_DIM)


def allowed_pairs(clip_ids):
    clip_blocks = clip_ids.reshape(-1, BLOCK)
    row_index = lax.broadcasted_iota(jnp.int32, (BLOCK, BLOCK), 0)
    col_index = lax.broadcasted_iota(jnp.int32, (BLOCK, BLOCK), 1)
    same_clip = clip_blocks[:, :, None] == clip_blocks[:, None, :]
    return (same_clip & (row_index >= col_index)[None])[:, None]


def masked_scores(query_blocks, key_blocks, allowed):
    raw_scores = jnp.einsum(
        "bqhd,bkhd->bhqk", query_blocks, key_blocks, preferred_element_type=jnp.float32
    ) * HEAD_DIM ** (-0.5)
    return jnp.where(allowed, raw_scores, -1e30)


def contract_rows(left, right):
    return lax.dot_general(
        left, right, (((0,), (0,)), ((), ())), preferred_element_type=jnp.float32
    )


def contract_cols(left, right):
    return lax.dot_general(
        left, right, (((1,), (1,)), ((), ())), preferred_element_type=jnp.float32
    )


Q_ORDER, K_ORDER, V_ORDER = ("x", "y", "z"), ("y", "z", "x"), ("z", "x", "y")
OUT_ORDER, UP_ORDER, DOWN_ORDER = ("x", "y", "z"), ("y", "z", "x"), ("z", "x", "y")


def on_device(
    tokens,
    qkv_weight,
    out_weight,
    up_weight,
    down_weight,
    ln1_gain,
    ln1_bias,
    q_bias,
    v_bias,
    out_bias,
    ln2_gain,
    ln2_bias,
    up_bias,
    down_bias,
    segment_ids,
    cotangent,
):
    tok_rows = tokens.shape[0]
    width = tokens.shape[1]
    rows = qkv_weight.shape[0]
    hidden_units = up_bias.shape[0]
    f32, bf16 = jnp.float32, jnp.bfloat16

    qkv_orders = (Q_ORDER, K_ORDER, V_ORDER)
    qkv_parts = [
        whole(
            gather_all(qkv_weight[:, i * width : (i + 1) * width], order),
            order,
            ROW_LAYOUT,
            (width, width),
        )
        for i, order in enumerate(qkv_orders)
    ]
    full_out = whole(gather_all(out_weight, OUT_ORDER), OUT_ORDER, ROW_LAYOUT, (width, width))
    full_up = whole(gather_all(up_weight, UP_ORDER), UP_ORDER, UP_LAYOUT, (width, hidden_units))
    full_down = whole(
        gather_all(down_weight, DOWN_ORDER), DOWN_ORDER, DOWN_LAYOUT, (hidden_units, width)
    )

    inputs = tokens.astype(f32)
    normed_one, norm_one_back = jax.vjp(layer_norm, inputs, ln1_gain, ln1_bias)
    normed_one_low = normed_one.astype(bf16)
    projected = [jnp.dot(normed_one_low, part, preferred_element_type=f32) for part in qkv_parts]
    query_blocks = blocked((projected[0] + q_bias).astype(bf16))
    key_blocks = blocked(projected[1].astype(bf16))
    value_blocks = blocked((projected[2] + v_bias).astype(bf16))
    allowed = allowed_pairs(segment_ids)
    scores = masked_scores(query_blocks, key_blocks, allowed)
    row_peak = jnp.max(scores, axis=-1, keepdims=True)
    powers = jnp.exp(scores - row_peak)
    row_total = jnp.sum(powers, axis=-1, keepdims=True)
    probs = powers / row_total
    weights_low = probs.astype(bf16)
    mixed_low = (
        jnp.einsum("bhqk,bkhd->bqhd", weights_low, value_blocks, preferred_element_type=f32)
        .reshape(tok_rows, width)
        .astype(bf16)
    )
    hidden = inputs + jnp.dot(mixed_low, full_out, preferred_element_type=f32) + out_bias
    normed_two, norm_two_back = jax.vjp(layer_norm, hidden, ln2_gain, ln2_bias)
    normed_two_low = normed_two.astype(bf16)
    pre_act = jnp.dot(normed_two_low, full_up, preferred_element_type=f32) + up_bias
    activation, gelu_back = jax.vjp(jax.nn.gelu, pre_act)
    activation_low = activation.astype(bf16)
    output = (
        hidden + jnp.dot(activation_low, full_down, preferred_element_type=f32) + down_bias
    ).astype(bf16)

    down_grad_part = contract_rows(activation_low, cotangent).astype(bf16)
    grad_pre = gelu_back(contract_cols(cotangent, full_down))[0].astype(bf16)
    up_grad_part = contract_rows(normed_two_low, grad_pre).astype(bf16)
    down_grad = scatter_sum(
        pieces_of(down_grad_part, DOWN_ORDER, DOWN_LAYOUT, *down_weight.shape), DOWN_ORDER
    )
    up_grad = scatter_sum(
        pieces_of(up_grad_part, UP_ORDER, UP_LAYOUT, *up_weight.shape), UP_ORDER
    )
    grad_normed_two = contract_cols(grad_pre, full_up)
    up_bias_grad = jnp.sum(grad_pre.astype(f32), axis=0)
    grad_hidden_norm, ln2_gain_grad, ln2_bias_grad = norm_two_back(grad_normed_two)
    grad_out = cotangent.astype(f32)
    grad_hidden = grad_out + grad_hidden_norm
    grad_hidden_low = grad_hidden.astype(bf16)
    out_grad_part = contract_rows(mixed_low, grad_hidden_low).astype(bf16)
    out_grad = scatter_sum(pieces_of(out_grad_part, OUT_ORDER, ROW_LAYOUT, rows, width), OUT_ORDER)
    grad_mixed_blocks = blocked(contract_cols(grad_hidden_low, full_out).astype(bf16))
    grad_probs = jnp.einsum(
        "bqhd,bkhd->bhqk", grad_mixed_blocks, value_blocks, preferred_element_type=f32
    )
    grad_scores = (
        probs * (grad_probs - jnp.sum(probs * grad_probs, axis=-1, keepdims=True))
    ).astype(bf16)
    score_scale = HEAD_DIM ** (-0.5)
    grad_query = (
        (
            jnp.einsum("bhqk,bkhd->bqhd", grad_scores, key_blocks, preferred_element_type=f32)
            * score_scale
        )
        .reshape(tok_rows, width)
        .astype(bf16)
    )
    grad_key = (
        (
            jnp.einsum("bhqk,bqhd->bkhd", grad_scores, query_blocks, preferred_element_type=f32)
            * score_scale
        )
        .reshape(tok_rows, width)
        .astype(bf16)
    )
    grad_value = (
        jnp.einsum("bhqk,bqhd->bkhd", weights_low, grad_mixed_blocks, preferred_element_type=f32)
        .reshape(tok_rows, width)
        .astype(bf16)
    )
    grad_parts = (grad_query, grad_key, grad_value)
    qkv_grad = jnp.concatenate(
        [
            scatter_sum(
                pieces_of(
                    contract_rows(normed_one_low, grad).astype(bf16), order, ROW_LAYOUT, rows, width
                ),
                order,
            )
            for grad, order in zip(grad_parts, qkv_orders)
        ],
        axis=1,
    )
    grad_normed_one = (
        contract_cols(grad_query, qkv_parts[0])
        + contract_cols(grad_key, qkv_parts[1])
        + contract_cols(grad_value, qkv_parts[2])
    )
    grad_input_norm, ln1_gain_grad, ln1_bias_grad = norm_one_back(grad_normed_one)
    grad_tokens = grad_hidden + grad_input_norm
    vectors = (
        ln1_gain_grad,
        ln1_bias_grad,
        jnp.sum(grad_query.astype(f32), axis=0),
        jnp.sum(grad_value.astype(f32), axis=0),
        jnp.sum(grad_hidden, axis=0),
        ln2_gain_grad,
        ln2_bias_grad,
        up_bias_grad,
        jnp.sum(grad_out, axis=0),
    )
    summed = sum_everywhere(jnp.concatenate(vectors).reshape(-1, 128)).reshape(-1)
    cuts, start = [], 0
    for vector in vectors:
        cuts.append(summed[start : start + vector.shape[0]])
        start += vector.shape[0]
    return (output, grad_tokens, qkv_grad, out_grad, up_grad, down_grad, *cuts)


def solution(mesh):
    fine = Mesh(mesh.devices.reshape(4, 2, 2, 4, 2), AXES)
    every, ff, model = AXES, ("z", "yh", "c"), ("x", "yl")
    weights = (P(every, None), P(every, None), P(model, ff), P(ff, model))
    return jax.shard_map(
        on_device,
        mesh=fine,
        in_specs=(P(every, None), *weights, *[P()] * 9, P(every), P(every, None)),
        out_specs=(P(every, None), P(every, None), *weights, *[P()] * 9),
        check_vma=False,
    )
```

```python
import functools
import itertools

import jax
import jax.numpy as jnp
from jax import lax
from jax.experimental import pallas as pl
from jax.experimental.pallas import tpu as pltpu
from jax.sharding import Mesh, PartitionSpec as P

F32, BF16 = jnp.float32, jnp.bfloat16
TOK, WIDTH, FF = 512, 1024, 4096
CHUNK = 1024
UNIT = 256
ROOT = 0.7978845608028654
CUBE = 0.044715


def dot(a, b):
    return lax.dot_general(a, b, (((1,), (0,)), ((), ())), preferred_element_type=F32)


def dot_t(a, b):
    return lax.dot_general(a, b, (((1,), (1,)), ((), ())), preferred_element_type=F32)


def strides(order):
    return {axis: 4**i for i, axis in enumerate(order)}


def tile_index(slots, side, order, x, y, z):
    step = strides(order)
    return (
        slots[side * 12 + x] * step["x"]
        + slots[side * 12 + 4 + y] * step["y"]
        + slots[side * 12 + 8 + z] * step["z"]
    )


def ffn_kernel(up_order, down_order, slots, low_ref, grad_ref, hidden_ref, gain_ref, down_bias_ref, bias_ref,
               up_own, up_other, down_own, down_other,
               out_ref, grad_hidden_ref, grad_low_ref, bias_grad_ref, vec_ref, dup_own, dup_other, ddown_own, ddown_other,
               up_buf, down_buf, dup_buf, ddown_buf, low_t, act_buf, gpre_buf, total, grad_total,
               up_sem, down_sem, dup_sem, ddown_sem):
    core = slots[24]

    def tiles(chunk):
        for side in (0, 1):
            for yh in (0, 1):
                for x in range(4):
                    for yl in (0, 1):
                        at_up = tile_index(slots, side, up_order, x, yh * 2 + yl, chunk)
                        at_down = tile_index(slots, side, down_order, x, yh * 2 + yl, chunk)
                        model = pl.ds((x * 2 + yl) * 128, 128)
                        unit = pl.ds((side * 2 + yh) * UNIT, UNIT)
                        yield side, at_up, at_down, model, unit

    def fetch(chunk, slot):
        for side, at_up, at_down, model, unit in tiles(chunk):
            pltpu.make_async_copy((up_own, up_other)[side].at[at_up], up_buf.at[slot, model, unit], up_sem.at[slot]).start()
            pltpu.make_async_copy((down_own, down_other)[side].at[at_down], down_buf.at[slot, unit, model], down_sem.at[slot]).start()

    def send(chunk, slot):
        for side, at_up, at_down, model, unit in tiles(chunk):
            pltpu.make_async_copy(dup_buf.at[slot, model, unit], (dup_own, dup_other)[side].at[at_up], dup_sem.at[slot]).start()
            pltpu.make_async_copy(ddown_buf.at[slot, unit, model], (ddown_own, ddown_other)[side].at[at_down], ddown_sem.at[slot]).start()

    def wait(buf, sem, slot):
        pltpu.make_async_copy(buf.at[slot], buf.at[slot], sem.at[slot]).wait()

    fetch(0, 0)
    low_t[...] = low_ref[...].T
    total[...] = jnp.zeros_like(total)
    grad_total[...] = jnp.zeros_like(grad_total)

    @pl.loop(0, 4)
    def _(chunk):
        slot = lax.rem(chunk, 2)

        @pl.when(chunk < 3)
        def _():
            fetch(chunk + 1, 1 - slot)

        wait(up_buf, up_sem, slot)
        wait(down_buf, down_sem, slot)

        @pl.when(chunk >= 2)
        def _():
            wait(dup_buf, dup_sem, slot)
            wait(ddown_buf, ddown_sem, slot)

        for n in range(CHUNK // UNIT):
            cols = slice(n * UNIT, (n + 1) * UNIT)
            side, yh = n // 2, n % 2
            block = (chunk * 2 + yh) * 2 + (core if side == 0 else 1 - core)
            pre = dot(low_ref[...], up_buf[slot, :, cols]) + bias_ref[block]
            gact = dot_t(grad_ref[...], down_buf[slot, cols, :])
            square = pre * pre
            bend = jnp.tanh(ROOT * (pre + CUBE * square * pre))
            half = 0.5 + 0.5 * bend
            act = (pre * half).astype(BF16)
            slope = half + 0.5 * pre * (1.0 - bend * bend) * (ROOT + 3.0 * ROOT * CUBE * square)
            gpre = (gact * slope).astype(BF16)
            act_buf[:, cols] = act
            gpre_buf[:, cols] = gpre
            bias_grad_ref[block] = jnp.sum(gpre.astype(F32), axis=0, keepdims=True)
            ddown_buf[slot, cols, :] = dot(act.T, grad_ref[...]).astype(BF16)
            dup_buf[slot, :, cols] = dot(low_t[...], gpre).astype(BF16)
        send(chunk, slot)
        total[...] += dot(act_buf[...], down_buf[slot])
        grad_total[...] += dot_t(gpre_buf[...], up_buf[slot])

    gain = gain_ref[...]
    vec_ref[...] = jnp.zeros_like(vec_ref)

    @pl.loop(0, TOK // 128)
    def _(part):
        rows = pl.ds(part * 128, 128)
        hidden = hidden_ref[rows, :]
        out_ref[rows, :] = (hidden + total[rows, :] + down_bias_ref[...]).astype(BF16)
        center = hidden - jnp.mean(hidden, axis=-1, keepdims=True)
        scale = lax.rsqrt(jnp.mean(center * center, axis=-1, keepdims=True) + 1e-05)
        norm = center * scale
        gc = grad_total[rows, :]
        edge = gc * gain
        back = (edge - jnp.mean(edge, axis=-1, keepdims=True) - norm * jnp.mean(edge * norm, axis=-1, keepdims=True)) * scale
        gout = grad_ref[rows, :].astype(F32)
        ghid = gout + back
        grad_hidden_ref[rows, :] = ghid
        grad_low_ref[rows, :] = ghid.astype(BF16)
        vec_ref[0:1, :] += jnp.sum(ghid, axis=0, keepdims=True)
        vec_ref[1:2, :] += jnp.sum(gc * norm, axis=0, keepdims=True)
        vec_ref[2:3, :] += jnp.sum(gc, axis=0, keepdims=True)
        vec_ref[3:4, :] += jnp.sum(gout, axis=0, keepdims=True)

    for slot in (0, 1):
        wait(dup_buf, dup_sem, slot)
        wait(ddown_buf, ddown_sem, slot)


def ffn(slots, low, grad, hidden, gain, down_bias, up_bias, up_own, up_other, down_own, down_other, up_order, down_order):
    vmem, anywhere = pl.BlockSpec(memory_space=pltpu.VMEM), pl.BlockSpec(memory_space=pl.ANY)
    tile_u, tile_d = jax.ShapeDtypeStruct((64, 128, 256), BF16), jax.ShapeDtypeStruct((64, 256, 128), BF16)
    big = pltpu.VMEM((2, 1024, 1024), BF16)
    sem = pltpu.SemaphoreType.DMA((2,))
    return pl.pallas_call(
        functools.partial(ffn_kernel, up_order, down_order),
        in_specs=[pl.BlockSpec(memory_space=pltpu.SMEM)] + [vmem] * 6 + [anywhere] * 4,
        out_specs=[vmem] * 5 + [anywhere] * 4,
        out_shape=[
            jax.ShapeDtypeStruct((TOK, WIDTH), BF16),
            jax.ShapeDtypeStruct((TOK, WIDTH), F32),
            jax.ShapeDtypeStruct((TOK, WIDTH), BF16),
            jax.ShapeDtypeStruct((16, 1, UNIT), F32),
            jax.ShapeDtypeStruct((8, WIDTH), F32),
            tile_u, tile_u, tile_d, tile_d,
        ],
        scratch_shapes=[
            big, big, big, big,
            pltpu.VMEM((WIDTH, TOK), BF16),
            pltpu.VMEM((TOK, CHUNK), BF16),
            pltpu.VMEM((TOK, CHUNK), BF16),
            pltpu.VMEM((TOK, WIDTH), F32),
            pltpu.VMEM((TOK, WIDTH), F32),
            sem, sem, sem, sem,
        ],
        compiler_params=pltpu.CompilerParams(vmem_limit_bytes=48 * 2**20),
        cost_estimate=pl.CostEstimate(flops=6 * 2 * TOK * WIDTH * FF, bytes_accessed=40 * 2**20, transcendentals=TOK * FF),
        name="ffn",
    )(slots, low, grad, hidden, gain.reshape(1, WIDTH), down_bias.reshape(1, WIDTH), up_bias.reshape(16, 1, UNIT),
      up_own, up_other, down_own, down_other)


BLOCK = 128
HALF = 512
PART = 3 * HALF
ORDERS = (("y", "x", "z"), ("y", "z", "x"))


def part_tiles(slots, part, rows_of):
    core = slots[24]
    for side in (0, 1):
        first = (core if side == 0 else 1 - core) * 64
        for x in range(4):
            for z in range(4):
                at_x, at_z = slots[side * 12 + x], slots[side * 12 + 8 + z]
                place = at_z * 4 + at_x if part == 0 else at_x * 4 + at_z
                for yh in (0, 1):
                    yield side, place, yh, pl.ds(pl.multiple_of(first + (z * 256 + yh * 128 + x * 16), 16), 16)


def fetch_part(slots, part, own, other, buf, sem):
    for side, place, yh, rows in part_tiles(slots, part, None):
        pltpu.make_async_copy((own, other)[side].at[place, yh], buf.at[part, rows], sem.at[part]).start()


def wait_part(buf, part, sem):
    pltpu.make_async_copy(buf.at[part], buf.at[part], sem.at[part]).wait()


def lane_marks():
    low = lax.broadcasted_iota(jnp.int32, (1, 128), 1) < 64
    return low, jnp.where(low, 1.0, 0.0).astype(BF16), jnp.where(low, 0.0, 1.0).astype(BF16)


def normed(values):
    center = values - jnp.mean(values, axis=-1, keepdims=True)
    scale = lax.rsqrt(jnp.mean(center * center, axis=-1, keepdims=True) + 1e-05)
    return center * scale, scale


def front_kernel(slots, tok_ref, pair_ref, ln1_ref, qkv_bias_ref, out_bias_ref, ln2_ref, own0, other0, own1, other1,
                 low_ref, qkv_ref, prob_ref, mixed_ref, hidden_ref, normed_ref, buf, sem):
    fetch_part(slots, 0, own0, other0, buf, sem)
    fetch_part(slots, 1, own1, other1, buf, sem)

    @pl.loop(0, TOK // 128)
    def _(i):
        rows = pl.ds(i * 128, 128)
        unit, _ = normed(tok_ref[rows, :].astype(F32))
        low_ref[rows, :] = (unit * ln1_ref[0:1, :] + ln1_ref[1:2, :]).astype(BF16)

    for part in (0, 1):
        wait_part(buf, part, sem)
        for n in range(3):
            cols = slice(n * HALF, (n + 1) * HALF)
            qkv_ref[part, :, cols] = (dot(low_ref[...], buf[part, :, cols]) + qkv_bias_ref[part, :, cols]).astype(BF16)
    low, near, far = lane_marks()
    near, far = near * 0.125, far * 0.125

    @pl.loop(0, 8)
    def _(pair):
        part = lax.div(pair, 4)
        start = pl.multiple_of(lax.rem(pair, 4) * 128, 128)
        lanes = pl.ds(pl.multiple_of(pair * 128, 128), 128)
        for block in range(TOK // BLOCK):
            rows = slice(block * BLOCK, (block + 1) * BLOCK)
            query = qkv_ref[part, rows, pl.ds(start, 128)]
            key = qkv_ref[part, rows, pl.ds(start + HALF, 128)]
            value = qkv_ref[part, rows, pl.ds(start + 2 * HALF, 128)]
            bias = pair_ref[block]
            score = dot_t(jnp.concatenate([query * near, query * far], axis=0), key) + jnp.concatenate([bias, bias], axis=0)
            power = jnp.exp(score - jnp.max(score, axis=-1, keepdims=True))
            prob = (power * (1.0 / jnp.sum(power, axis=-1, keepdims=True))).astype(BF16)
            prob_ref[pair, block] = prob
            both = dot(prob, value)
            mixed_ref[rows, lanes] = jnp.where(low, both[:BLOCK], both[BLOCK:]).astype(BF16)

    for part in (0, 1):
        cols = slice(part * HALF, (part + 1) * HALF)
        hidden_ref[:, cols] = tok_ref[:, cols].astype(F32) + dot(mixed_ref[...], buf[part, :, PART:]) + out_bias_ref[:, cols]

    @pl.loop(0, TOK // 128)
    def _(i):
        rows = pl.ds(i * 128, 128)
        unit, _ = normed(hidden_ref[rows, :])
        normed_ref[rows, :] = (unit * ln2_ref[0:1, :] + ln2_ref[1:2, :]).astype(BF16)


VMEM, ANY = pl.BlockSpec(memory_space=pltpu.VMEM), pl.BlockSpec(memory_space=pl.ANY)


def front(slots, tokens, pair_bias, ln1, qkv_bias, out_bias, ln2, parts):
    shape = jax.ShapeDtypeStruct
    return pl.pallas_call(
        front_kernel,
        in_specs=[pl.BlockSpec(memory_space=pltpu.SMEM)] + [VMEM] * 6 + [ANY] * 4,
        out_specs=[VMEM] * 6,
        out_shape=[
            shape((TOK, WIDTH), BF16),
            shape((2, TOK, PART), BF16),
            shape((8, 4, 2 * BLOCK, BLOCK), BF16),
            shape((TOK, WIDTH), BF16),
            shape((TOK, WIDTH), F32),
            shape((TOK, WIDTH), BF16),
        ],
        scratch_shapes=[pltpu.VMEM((2, WIDTH, 2048), BF16), pltpu.SemaphoreType.DMA((2,))],
        compiler_params=pltpu.CompilerParams(vmem_limit_bytes=40 * 2**20),
        cost_estimate=pl.CostEstimate(flops=2 * TOK * WIDTH * 4096 * 2, bytes_accessed=20 * 2**20, transcendentals=TOK * 2048),
        name="front",
    )(slots, tokens, pair_bias, ln1, qkv_bias, out_bias.reshape(1, WIDTH), ln2, *parts[0], *parts[1])


def back_kernel(slots, ghid_ref, glow_ref, tok_ref, ln1_ref, low_ref, qkv_ref, prob_ref, mixed_ref, own0, other0, own1, other1,
                gin_ref, vec_ref, down0, dother0, down1, dother1,
                buf, grad_buf, gmix_ref, gqkv_ref, low_t, total, sem, grad_sem):
    fetch_part(slots, 0, own0, other0, buf, sem)
    fetch_part(slots, 1, own1, other1, buf, sem)
    low_t[...] = mixed_ref[...].T
    vec_ref[...] = jnp.zeros_like(vec_ref)
    wait_part(buf, 0, sem)
    wait_part(buf, 1, sem)
    gmix_ref[...] = (dot_t(glow_ref[:, :HALF], buf[0, :, PART:]) + dot_t(glow_ref[:, HALF:], buf[1, :, PART:])).astype(BF16)
    for part in (0, 1):
        grad_buf[part, :, PART:] = dot(low_t[...], glow_ref[:, part * HALF:(part + 1) * HALF]).astype(BF16)
    low_t[...] = low_ref[...].T
    low, near, far = lane_marks()

    for part in (0, 1):
        @pl.loop(0, 4)
        def _(pair, part=part):
            start = pl.multiple_of(pair * 128, 128)
            lanes = pl.ds(pl.multiple_of(pair * 128 + part * HALF, 128), 128)
            for block in range(TOK // BLOCK):
                rows = slice(block * BLOCK, (block + 1) * BLOCK)
                query = qkv_ref[part, rows, pl.ds(start, 128)]
                key = qkv_ref[part, rows, pl.ds(start + HALF, 128)]
                value = qkv_ref[part, rows, pl.ds(start + 2 * HALF, 128)]
                gmix = gmix_ref[rows, lanes]
                gmix = jnp.concatenate([gmix * near, gmix * far], axis=0)
                query = jnp.concatenate([query * (near * 0.125), query * (far * 0.125)], axis=0)
                prob_low = prob_ref[pair + 4 * part, block]
                prob = prob_low.astype(F32)
                gprob = dot_t(gmix, value)
                gscore = (prob * (gprob - jnp.sum(prob * gprob, axis=-1, keepdims=True))).astype(BF16)
                both = dot(gscore, key) * 0.125
                gqkv_ref[part, rows, pl.ds(start, 128)] = jnp.where(low, both[:BLOCK], both[BLOCK:]).astype(BF16)
                gqkv_ref[part, rows, pl.ds(start + HALF, 128)] = dot(gscore.T, query).astype(BF16)
                gqkv_ref[part, rows, pl.ds(start + 2 * HALF, 128)] = dot(prob_low.T, gmix).astype(BF16)

        for n in range(3):
            cols = slice(n * HALF, (n + 1) * HALF)
            grad_buf[part, :, cols] = dot(low_t[...], gqkv_ref[part, :, cols]).astype(BF16)
        for side, place, yh, rows in part_tiles(slots, part, None):
            pltpu.make_async_copy(grad_buf.at[part, rows], ((down0, dother0), (down1, dother1))[part][side].at[place, yh], grad_sem.at[part]).start()
        more = dot_t(gqkv_ref[part], buf[part, :, :PART])
        if part == 0:
            total[...] = more
        else:
            total[...] += more
        vec_ref[2:3, part * HALF:(part + 1) * HALF] = jnp.sum(gqkv_ref[part, :, :HALF].astype(F32), axis=0, keepdims=True)
        vec_ref[3:4, part * HALF:(part + 1) * HALF] = jnp.sum(gqkv_ref[part, :, 2 * HALF:].astype(F32), axis=0, keepdims=True)

    @pl.loop(0, TOK // 128)
    def _(i):
        rows = pl.ds(i * 128, 128)
        unit, scale = normed(tok_ref[rows, :].astype(F32))
        grad = total[rows, :]
        edge = grad * ln1_ref[0:1, :]
        gin_ref[rows, :] = ghid_ref[rows, :] + (
            edge - jnp.mean(edge, axis=-1, keepdims=True) - unit * jnp.mean(edge * unit, axis=-1, keepdims=True)
        ) * scale
        vec_ref[0:1, :] += jnp.sum(grad * unit, axis=0, keepdims=True)
        vec_ref[1:2, :] += jnp.sum(grad, axis=0, keepdims=True)

    wait_part(grad_buf, 0, grad_sem)
    wait_part(grad_buf, 1, grad_sem)


def back(slots, ghid, glow, tokens, ln1, low, qkv, prob, mixed, parts):
    shape = jax.ShapeDtypeStruct
    tile = shape((16, 2, 16, 2048), BF16)
    return pl.pallas_call(
        back_kernel,
        in_specs=[pl.BlockSpec(memory_space=pltpu.SMEM)] + [VMEM] * 8 + [ANY] * 4,
        out_specs=[VMEM] * 2 + [ANY] * 4,
        out_shape=[shape((TOK, WIDTH), F32), shape((8, WIDTH), F32), tile, tile, tile, tile],
        scratch_shapes=[
            pltpu.VMEM((2, WIDTH, 2048), BF16),
            pltpu.VMEM((2, WIDTH, 2048), BF16),
            pltpu.VMEM((TOK, WIDTH), BF16),
            pltpu.VMEM((2, TOK, PART), BF16),
            pltpu.VMEM((WIDTH, TOK), BF16),
            pltpu.VMEM((TOK, WIDTH), F32),
            pltpu.SemaphoreType.DMA((2,)),
            pltpu.SemaphoreType.DMA((2,)),
        ],
        compiler_params=pltpu.CompilerParams(vmem_limit_bytes=48 * 2**20),
        cost_estimate=pl.CostEstimate(flops=2 * TOK * WIDTH * 4096 * 4, bytes_accessed=40 * 2**20, transcendentals=0),
        name="back",
    )(slots, ghid, glow, tokens, ln1, low, qkv, prob, mixed, *parts[0], *parts[1])


AXES = ("z", "yh", "c", "x", "yl")
UP_ORDER, DOWN_ORDER = ("z", "x", "y"), ("x", "y", "z")


def device_number(place):
    return (
        ((place["z"] * 2 + place["y"] // 2) * 2 + place["c"]) * 4 + place["x"]
    ) * 2 + place["y"] % 2


def exchange_pairs(axis, second):
    pairs = []
    for z, y, c, x in itertools.product(range(4), range(4), range(2), range(4)):
        here = {"z": z, "y": y, "c": c, "x": x}
        mask = 1 if (c == 0) != second else 3
        there = dict(here)
        there[axis] = here[axis] ^ mask
        pairs.append((device_number(here), device_number(there)))
    return pairs


def swap_axis(values, axis, second):
    return lax.ppermute(values, AXES, exchange_pairs(axis, second))


def swap_core(values):
    return lax.ppermute(values, "c", [(0, 1), (1, 0)])


def position(axis):
    if axis == "y":
        return lax.axis_index("yh") * 2 + lax.axis_index("yl")
    return lax.axis_index(axis)


def slot_of(core, distance):
    return jnp.where(
        core == 0, distance ^ (distance >> 1), ((distance << 1) & 3) ^ (3 * (distance >> 1))
    )


def slot_table():
    core, places = lax.axis_index("c"), jnp.arange(4, dtype=jnp.int32)
    rows = [
        slot_of(side, places ^ position(axis)) for side in (core, 1 - core) for axis in ("x", "y", "z")
    ]
    return jnp.concatenate(rows + [jnp.full((8,), core, jnp.int32)])


def steps_of(order):
    return [(axis, second) for axis in order for second in (False, True)]


def gather(values, order):
    for axis, second in steps_of(order):
        values = jnp.concatenate([values, swap_axis(values, axis, second)])
    return values


def add(left, right, dtype=BF16):
    return (left.astype(F32) + right.astype(F32)).astype(dtype)


def scatter(own, other, order):
    got = swap_core(other)
    count = own.shape[0]
    for axis, second in reversed(steps_of(order)):
        count //= 2
        moving = add(own[count:], got[count:])
        own = add(own[:count], got[:count])
        got = swap_axis(moving, axis, second)
    return own, got


def gather_rows(shard, order):
    pieces = gather(shard[None], ("y",))
    here, core = position("y"), lax.axis_index("c")
    pieces = [
        lax.dynamic_index_in_dim(pieces, slot_of(core, at ^ here), 0, keepdims=False)
        for at in range(4)
    ]
    return gather(jnp.stack(pieces).reshape(1, 2, 16, shard.shape[1]), order)


def scatter_rows(own, other, order):
    own, got = scatter(own, other, order)
    pieces = add(own, got).reshape(4, 8, -1)
    here, core = position("y"), lax.axis_index("c")
    first = jnp.where(core == 0, 1, 3)
    second = 4 - first

    def at(slot):
        return lax.dynamic_index_in_dim(pieces, slot, 0, keepdims=False)

    far = swap_axis(jnp.stack([at(here ^ second), at(here ^ second ^ first)]), "y", True)
    near = swap_axis(add(at(here ^ first), far[1]), "y", False)
    return at(here).astype(F32) + far[0].astype(F32) + near.astype(F32)


def sum_everywhere(values):
    for axis, second in steps_of(("x", "y", "z")):
        values = values + swap_axis(values, axis, second)
    return values + swap_core(values)


def pair_bias(clip_ids):
    clips = clip_ids.reshape(-1, BLOCK)
    row = lax.broadcasted_iota(jnp.int32, (BLOCK, BLOCK), 0)
    col = lax.broadcasted_iota(jnp.int32, (BLOCK, BLOCK), 1)
    allowed = (clips[:, :, None] == clips[:, None, :]) & (row >= col)[None]
    return jnp.where(allowed, 0.0, -1e30).astype(F32)


def on_device(
    tokens,
    qkv_weight,
    out_weight,
    up_weight,
    down_weight,
    ln1_gain,
    ln1_bias,
    q_bias,
    v_bias,
    out_bias,
    ln2_gain,
    ln2_bias,
    up_bias,
    down_bias,
    segment_ids,
    cotangent,
):
    slots = slot_table()
    heads = qkv_weight.reshape(8, 3, WIDTH)
    parts = []
    for part, order in enumerate(ORDERS):
        cols = slice(part * HALF, (part + 1) * HALF)
        shard = jnp.concatenate([heads[:, :, cols].reshape(8, PART), out_weight[:, cols]], axis=1)
        own = gather_rows(shard, order[1:])
        parts.append((own, swap_core(own)))
    up_own = gather(up_weight[None], UP_ORDER)
    up_other = swap_core(up_own)
    down_own = gather(down_weight[None], DOWN_ORDER)
    down_other = swap_core(down_own)

    ln1 = jnp.stack([ln1_gain, ln1_bias])
    nothing = jnp.zeros((HALF,), F32)
    qkv_bias = jnp.stack(
        [
            jnp.concatenate([q_bias[cols], nothing, v_bias[cols]])[None]
            for cols in (slice(0, HALF), slice(HALF, WIDTH))
        ]
    )
    low, qkv, prob, mixed, hidden, low2 = front(
        slots, tokens, pair_bias(segment_ids), ln1, qkv_bias, out_bias, jnp.stack([ln2_gain, ln2_bias]), parts
    )
    output, ghid, glow, up_bias_grad, vec2, dup_own, dup_other, ddown_own, ddown_other = ffn(
        slots, low2, cotangent, hidden, ln2_gain, down_bias, up_bias,
        up_own, up_other, down_own, down_other, UP_ORDER, DOWN_ORDER,
    )
    up_grad = add(*scatter(dup_own, dup_other, UP_ORDER), F32)[0]
    down_grad = add(*scatter(ddown_own, ddown_other, DOWN_ORDER), F32)[0]
    grad_tokens, vec1, *grads = back(slots, ghid, glow, tokens, ln1, low, qkv, prob, mixed, parts)
    sums = [
        scatter_rows(grads[2 * part], grads[2 * part + 1], order[1:]) for part, order in enumerate(ORDERS)
    ]
    qkv_grad = jnp.stack([s[:, :PART].reshape(8, 3, HALF) for s in sums], axis=2).reshape(8, 3 * WIDTH)
    out_grad = jnp.concatenate([s[:, PART:] for s in sums], axis=1)
    summed = sum_everywhere(
        jnp.concatenate([vec1[:4].reshape(-1, 128), vec2[:4].reshape(-1, 128), up_bias_grad.reshape(-1, 128)])
    ).reshape(-1)
    vectors = [summed[i * WIDTH : (i + 1) * WIDTH] for i in range(8)]
    return (
        output,
        grad_tokens,
        qkv_grad,
        out_grad,
        up_grad,
        down_grad,
        *vectors[:7],
        summed[8 * WIDTH :],
        vectors[7],
    )


def solution(mesh):
    fine = Mesh(mesh.devices.reshape(4, 2, 2, 4, 2), AXES)
    every, hidden, model = AXES, ("z", "yh", "c"), ("x", "yl")
    weights = (P(every, None), P(every, None), P(model, hidden), P(hidden, model))
    return jax.shard_map(
        on_device,
        mesh=fine,
        in_specs=(P(every, None), *weights, *[P()] * 9, P(every), P(every, None)),
        out_specs=(P(every, None), P(every, None), *weights, *[P()] * 9),
        check_vma=False,
    )
```

```python
import functools
import itertools

import jax
import jax.numpy as jnp
from jax import lax
from jax.experimental import pallas as pl
from jax.experimental.pallas import tpu as pltpu
from jax.sharding import Mesh, PartitionSpec as P

F32, BF16 = jnp.float32, jnp.bfloat16
TOK, WIDTH, FF = 512, 1024, 4096
BOTH = 2 * TOK
CHUNK = 1024
UNIT = 256
ROOT = 0.7978845608028654
CUBE = 0.044715


def dot(a, b):
    return lax.dot_general(a, b, (((1,), (0,)), ((), ())), preferred_element_type=F32)


def dot_t(a, b):
    return lax.dot_general(a, b, (((1,), (1,)), ((), ())), preferred_element_type=F32)


def normed(values):
    center = values - jnp.mean(values, axis=-1, keepdims=True)
    scale = lax.rsqrt(jnp.mean(center * center, axis=-1, keepdims=True) + 1e-05)
    return center * scale, scale


def norm_back(edge, unit, scale):
    return (edge - jnp.mean(edge, axis=-1, keepdims=True) - unit * jnp.mean(edge * unit, axis=-1, keepdims=True)) * scale


def tile_index(slots, order, x, y, z):
    step = {axis: 4**i for i, axis in enumerate(order)}
    return slots[x] * step["x"] + slots[4 + y] * step["y"] + slots[8 + z] * step["z"]


def ffn_kernel(up_order, down_orders, slots, bias_ref, low_own, low_other, grad_own, grad_other, up, down0, down1,
               bias_grad_ref, feed_ref, feed_low_ref, gc_ref, gc_low_ref,
               dup_keep, dup_move, ddown0_keep, ddown0_move, ddown1_keep, ddown1_move,
               up_buf, down_buf, dup_buf, ddown_buf, low, grad, low_t, act_buf, gpre_buf, total, grad_total,
               in_sem, up_sem, down_sem, dup_sem, ddown_sem):
    core = slots[24]
    downs = (down0, down1)
    ddowns = ((ddown0_keep, ddown0_move), (ddown1_keep, ddown1_move))

    def tiles(chunk):
        for part in (0, 1):
            for yh in (0, 1):
                for x in range(4):
                    for yl in (0, 1):
                        yield (x, yh * 2 + yl, chunk * 2 + part), pl.ds((x * 2 + yl) * 128, 128), (part * 2 + yh) * UNIT

    def fetch(chunk, slot):
        for place, model, unit in tiles(chunk):
            pltpu.make_async_copy(
                up.at[tile_index(slots, up_order, *place)], up_buf.at[slot, model, pl.ds(unit, UNIT)], up_sem.at[slot]
            ).start()
            for half in (0, 1):
                pltpu.make_async_copy(
                    downs[half].at[tile_index(slots, down_orders[half], *place)],
                    down_buf.at[slot, pl.ds(unit + half * 128, 128), model],
                    down_sem.at[slot],
                ).start()

    def put(source, keep, move, index, sem):
        @pl.when(index < 32)
        def _():
            pltpu.make_async_copy(source, keep.at[jnp.minimum(index, 31)], sem).start()

        @pl.when(index >= 32)
        def _():
            pltpu.make_async_copy(source, move.at[jnp.maximum(index - 32, 0)], sem).start()

    def send(chunk, slot):
        for place, model, unit in tiles(chunk):
            put(dup_buf.at[slot, model, pl.ds(unit, UNIT)], dup_keep, dup_move, tile_index(slots, up_order, *place), dup_sem.at[slot])
            for half in (0, 1):
                put(ddown_buf.at[slot, pl.ds(unit + half * 128, 128), model], *ddowns[half],
                    tile_index(slots, down_orders[half], *place), ddown_sem.at[slot])

    def wait(buf, sem, slot):
        pltpu.make_async_copy(buf.at[slot], buf.at[slot], sem.at[slot]).wait()

    for source, target, i in ((low_own, low, 0), (low_other, low, 1), (grad_own, grad, 0), (grad_other, grad, 1)):
        pltpu.make_async_copy(source, target.at[pl.ds(i * TOK, TOK)], in_sem).start()
    fetch(0, 0)
    fetch(1, 1)
    for target in (low, grad):
        pltpu.make_async_copy(target, target, in_sem).wait()
    low_t[...] = low[...].T
    bias_grad_ref[...] = jnp.zeros_like(bias_grad_ref)

    @pl.loop(0, 2)
    def _(chunk):
        wait(up_buf, up_sem, chunk)
        wait(down_buf, down_sem, chunk)
        for n in range(CHUNK // UNIT):
            cols = slice(n * UNIT, (n + 1) * UNIT)
            block = ((chunk * 2 + n // 2) * 2 + n % 2) * 2 + core
            pre = dot(low[...], up_buf[chunk, :, cols]) + bias_ref[block]
            gact = dot_t(grad[...], down_buf[chunk, cols, :])
            square = pre * pre
            bend = jnp.tanh(ROOT * (pre + CUBE * square * pre))
            half = 0.5 + 0.5 * bend
            act = (pre * half).astype(BF16)
            slope = half + 0.5 * pre * (1.0 - bend * bend) * (ROOT + 3.0 * ROOT * CUBE * square)
            gpre = (gact * slope).astype(BF16)
            act_buf[:, cols] = act
            gpre_buf[:, cols] = gpre
            bias_grad_ref[block] = jnp.sum(gpre.astype(F32), axis=0, keepdims=True)
            ddown_buf[chunk, cols, :] = dot(act.T, grad[...]).astype(BF16)
            dup_buf[chunk, :, cols] = dot(low_t[...], gpre).astype(BF16)
        send(chunk, chunk)
        more = dot_t(gpre_buf[...], up_buf[chunk])

        @pl.when(chunk == 0)
        def _():
            grad_total[...] = more

        @pl.when(chunk == 1)
        def _():
            more_total = grad_total[...] + more
            gc_ref[...] = more_total[:TOK]
            gc_low_ref[...] = more_total[TOK:].astype(BF16)

        feed = dot(act_buf[...], down_buf[chunk])

        @pl.when(chunk == 0)
        def _():
            total[...] = feed

        @pl.when(chunk == 1)
        def _():
            feed_total = total[...] + feed
            feed_ref[...] = feed_total[:TOK]
            feed_low_ref[...] = feed_total[TOK:].astype(BF16)

    for slot in (0, 1):
        wait(dup_buf, dup_sem, slot)
        wait(ddown_buf, ddown_sem, slot)


VMEM, ANY, SMEM = (pl.BlockSpec(memory_space=kind) for kind in (pltpu.VMEM, pl.ANY, pltpu.SMEM))


def ffn(slots, up_bias, low_own, low_other, grad_own, grad_other, weights, up_order, down_orders):
    shape = jax.ShapeDtypeStruct
    tile_u, tile_d = shape((32, 128, 256), BF16), shape((32, 128, 128), BF16)
    big = pltpu.VMEM((2, CHUNK, CHUNK), BF16)
    rows = pltpu.VMEM((BOTH, WIDTH), BF16)
    sem = pltpu.SemaphoreType.DMA((2,))
    return pl.pallas_call(
        functools.partial(ffn_kernel, up_order, down_orders),
        in_specs=[SMEM, VMEM] + [ANY] * 7,
        out_specs=[VMEM] * 5 + [ANY] * 6,
        out_shape=[
            shape((16, 1, UNIT), F32),
            shape((TOK, WIDTH), F32),
            shape((TOK, WIDTH), BF16),
            shape((TOK, WIDTH), F32),
            shape((TOK, WIDTH), BF16),
            tile_u, tile_u, tile_d, tile_d, tile_d, tile_d,
        ],
        scratch_shapes=[
            big, big, big, big,
            rows, rows, rows,
            pltpu.VMEM((BOTH, CHUNK), BF16),
            pltpu.VMEM((BOTH, CHUNK), BF16),
            pltpu.VMEM((BOTH, WIDTH), F32),
            pltpu.VMEM((BOTH, WIDTH), F32),
            pltpu.SemaphoreType.DMA, sem, sem, sem, sem,
        ],
        compiler_params=pltpu.CompilerParams(vmem_limit_bytes=56 * 2**20),
        cost_estimate=pl.CostEstimate(flops=6 * 2 * TOK * WIDTH * FF, bytes_accessed=40 * 2**20, transcendentals=TOK * FF),
        name="ffn",
    )(slots, up_bias.reshape(16, 1, UNIT), low_own, low_other, grad_own, grad_other, *weights)


def turn_kernel(hidden_ref, gain_ref, gc_ref, got_ref, grad_ref, ghid_ref, glow_ref, vec_ref):
    vec_ref[...] = jnp.zeros_like(vec_ref)

    @pl.loop(0, TOK // 128)
    def _(part):
        rows = pl.ds(part * 128, 128)
        unit, scale = normed(hidden_ref[rows, :])
        gc = gc_ref[rows, :] + got_ref[rows, :].astype(F32)
        gout = grad_ref[rows, :].astype(F32)
        ghid = gout + norm_back(gc * gain_ref[...], unit, scale)
        ghid_ref[rows, :] = ghid
        glow_ref[rows, :] = ghid.astype(BF16)
        vec_ref[0:1, :] += jnp.sum(ghid, axis=0, keepdims=True)
        vec_ref[1:2, :] += jnp.sum(gc * unit, axis=0, keepdims=True)
        vec_ref[2:3, :] += jnp.sum(gc, axis=0, keepdims=True)
        vec_ref[3:4, :] += jnp.sum(gout, axis=0, keepdims=True)


def turn(hidden, gain, gc, got, grad):
    shape = jax.ShapeDtypeStruct
    return pl.pallas_call(
        turn_kernel,
        in_specs=[VMEM] * 5,
        out_specs=[VMEM] * 3,
        out_shape=[shape((TOK, WIDTH), F32), shape((TOK, WIDTH), BF16), shape((8, WIDTH), F32)],
        compiler_params=pltpu.CompilerParams(vmem_limit_bytes=24 * 2**20),
        cost_estimate=pl.CostEstimate(flops=30 * TOK * WIDTH, bytes_accessed=10 * 2**20, transcendentals=0),
        name="turn",
    )(hidden, gain.reshape(1, WIDTH), gc, got, grad)


BLOCK = 128
HALF = 512
PART = 3 * HALF
ORDERS = (("y", "x", "z"), ("y", "z", "x"))


def part_tiles(slots, part):
    core = slots[24]
    for side in (0, 1):
        first = (core if side == 0 else 1 - core) * 64
        for x in range(4):
            for z in range(4):
                at_x, at_z = slots[side * 12 + x], slots[side * 12 + 8 + z]
                place = at_z * 4 + at_x if part == 0 else at_x * 4 + at_z
                for yh in (0, 1):
                    yield side, place, yh, pl.ds(pl.multiple_of(first + (z * 256 + yh * 128 + x * 16), 16), 16)


def fetch_part(slots, part, pair, buf, sem, cols=slice(None)):
    for side, place, yh, rows in part_tiles(slots, part):
        pltpu.make_async_copy(pair[side].at[place, yh, :, cols], buf.at[rows], sem).start()


def wait_for(buf, sem):
    pltpu.make_async_copy(buf, buf, sem).wait()


def lane_marks():
    low = lax.broadcasted_iota(jnp.int32, (1, 128), 1) < 64
    return low, jnp.where(low, 1.0, 0.0).astype(BF16), jnp.where(low, 0.0, 1.0).astype(BF16)


def front_kernel(slots, tok_ref, pair_ref, ln1_ref, qkv_bias_ref, own0, other0, own1, other1,
                 low_ref, qkv_ref, prob_ref, mixed_ref, buf, sem):
    fetch_part(slots, 0, (own0, other0), buf.at[0], sem.at[0], slice(0, PART))
    fetch_part(slots, 1, (own1, other1), buf.at[1], sem.at[1], slice(0, PART))

    @pl.loop(0, TOK // 128)
    def _(i):
        rows = pl.ds(i * 128, 128)
        unit, _ = normed(tok_ref[rows, :].astype(F32))
        low_ref[rows, :] = (unit * ln1_ref[0:1, :] + ln1_ref[1:2, :]).astype(BF16)

    for part in (0, 1):
        wait_for(buf.at[part], sem.at[part])
        for n in range(3):
            cols = slice(n * HALF, (n + 1) * HALF)
            qkv_ref[part, :, cols] = (dot(low_ref[...], buf[part, :, cols]) + qkv_bias_ref[part, :, cols]).astype(BF16)
    low, near, far = lane_marks()
    near, far = near * 0.125, far * 0.125

    @pl.loop(0, 8)
    def _(pair):
        part = lax.div(pair, 4)
        start = pl.multiple_of(lax.rem(pair, 4) * 128, 128)
        lanes = pl.ds(pl.multiple_of(pair * 128, 128), 128)
        for block in range(TOK // BLOCK):
            rows = slice(block * BLOCK, (block + 1) * BLOCK)
            query = qkv_ref[part, rows, pl.ds(start, 128)]
            key = qkv_ref[part, rows, pl.ds(start + HALF, 128)]
            value = qkv_ref[part, rows, pl.ds(start + 2 * HALF, 128)]
            bias = pair_ref[block]
            score = dot_t(jnp.concatenate([query * near, query * far], axis=0), key) + jnp.concatenate([bias, bias], axis=0)
            power = jnp.exp(score - jnp.max(score, axis=-1, keepdims=True))
            prob = (power * (1.0 / jnp.sum(power, axis=-1, keepdims=True))).astype(BF16)
            prob_ref[pair, block] = prob
            both = dot(prob, value)
            mixed_ref[rows, lanes] = jnp.where(low, both[:BLOCK], both[BLOCK:]).astype(BF16)


def front(slots, tokens, pair_bias, ln1, qkv_bias, parts):
    shape = jax.ShapeDtypeStruct
    return pl.pallas_call(
        front_kernel,
        in_specs=[SMEM] + [VMEM] * 4 + [ANY] * 4,
        out_specs=[VMEM] * 4,
        out_shape=[
            shape((TOK, WIDTH), BF16),
            shape((2, TOK, PART), BF16),
            shape((8, 4, 2 * BLOCK, BLOCK), BF16),
            shape((TOK, WIDTH), BF16),
        ],
        scratch_shapes=[pltpu.VMEM((2, WIDTH, PART), BF16), pltpu.SemaphoreType.DMA((2,))],
        compiler_params=pltpu.CompilerParams(vmem_limit_bytes=32 * 2**20),
        cost_estimate=pl.CostEstimate(flops=2 * TOK * WIDTH * 4096 * 2, bytes_accessed=20 * 2**20, transcendentals=TOK * 2048),
        name="front",
    )(slots, tokens, pair_bias, ln1, qkv_bias, *parts[0], *parts[1])


def join_kernel(slots, tok_ref, mixed_ref, out_bias_ref, ln2_ref, own0, other0, own1, other1, hidden_ref, normed_ref, buf, sem):
    fetch_part(slots, 0, (own0, other0), buf.at[0], sem.at[0], slice(PART, 2048))
    fetch_part(slots, 1, (own1, other1), buf.at[1], sem.at[1], slice(PART, 2048))
    for part in (0, 1):
        cols = slice(part * HALF, (part + 1) * HALF)
        wait_for(buf.at[part], sem.at[part])
        hidden_ref[:, cols] = tok_ref[:, cols].astype(F32) + dot(mixed_ref[...], buf[part]) + out_bias_ref[:, cols]

    @pl.loop(0, TOK // 128)
    def _(i):
        rows = pl.ds(i * 128, 128)
        unit, _ = normed(hidden_ref[rows, :])
        normed_ref[rows, :] = (unit * ln2_ref[0:1, :] + ln2_ref[1:2, :]).astype(BF16)


def join(slots, tokens, mixed, out_bias, ln2, parts):
    shape = jax.ShapeDtypeStruct
    return pl.pallas_call(
        join_kernel,
        in_specs=[SMEM] + [VMEM] * 4 + [ANY] * 4,
        out_specs=[VMEM] * 2,
        out_shape=[shape((TOK, WIDTH), F32), shape((TOK, WIDTH), BF16)],
        scratch_shapes=[pltpu.VMEM((2, WIDTH, HALF), BF16), pltpu.SemaphoreType.DMA((2,))],
        compiler_params=pltpu.CompilerParams(vmem_limit_bytes=16 * 2**20),
        cost_estimate=pl.CostEstimate(flops=2 * TOK * WIDTH * WIDTH, bytes_accessed=8 * 2**20, transcendentals=0),
        name="join",
    )(slots, tokens, mixed, out_bias.reshape(1, WIDTH), ln2, *parts[0], *parts[1])


def back_kernel(part, slots, glow_ref, low_ref, qkv_ref, prob_ref, mixed_ref, own0, other0, own1, other1,
                gqkv_ref, sum_ref, down, dother, buf, side_buf, grad_buf, gmix_ref, flip, sem, grad_sem):
    pairs = ((own0, other0), (own1, other1))
    tail = slice(PART, 2048)
    fetch_part(slots, part, pairs[part], buf, sem.at[0], tail)
    fetch_part(slots, 1 - part, pairs[1 - part], side_buf, sem.at[1], tail)
    flip[...] = mixed_ref[...].T
    heads = slice(part * HALF, (part + 1) * HALF)
    rest = slice((1 - part) * HALF, (2 - part) * HALF)
    grad_buf[:, PART:] = dot(flip[...], glow_ref[:, heads]).astype(BF16)
    wait_for(buf, sem.at[0])
    wait_for(side_buf, sem.at[1])
    gmix_ref[...] = (dot_t(glow_ref[:, heads], buf[heads, :]) + dot_t(glow_ref[:, rest], side_buf[heads, :])).astype(BF16)
    flip[...] = low_ref[...].T
    low, near, far = lane_marks()

    @pl.loop(0, 4)
    def _(pair):
        start = pl.multiple_of(pair * 128, 128)
        for block in range(TOK // BLOCK):
            rows = slice(block * BLOCK, (block + 1) * BLOCK)
            query = qkv_ref[part, rows, pl.ds(start, 128)]
            key = qkv_ref[part, rows, pl.ds(start + HALF, 128)]
            value = qkv_ref[part, rows, pl.ds(start + 2 * HALF, 128)]
            gmix = gmix_ref[rows, pl.ds(start, 128)]
            gmix = jnp.concatenate([gmix * near, gmix * far], axis=0)
            query = jnp.concatenate([query * (near * 0.125), query * (far * 0.125)], axis=0)
            prob_low = prob_ref[pair + 4 * part, block]
            prob = prob_low.astype(F32)
            gprob = dot_t(gmix, value)
            gscore = (prob * (gprob - jnp.sum(prob * gprob, axis=-1, keepdims=True))).astype(BF16)
            both = dot(gscore, key) * 0.125
            gqkv_ref[rows, pl.ds(start, 128)] = jnp.where(low, both[:BLOCK], both[BLOCK:]).astype(BF16)
            gqkv_ref[rows, pl.ds(start + HALF, 128)] = dot(gscore.T, query).astype(BF16)
            gqkv_ref[rows, pl.ds(start + 2 * HALF, 128)] = dot(prob_low.T, gmix).astype(BF16)

    for n in range(3):
        cols = slice(n * HALF, (n + 1) * HALF)
        grad_buf[:, cols] = dot(flip[...], gqkv_ref[:, cols]).astype(BF16)
    for side, place, yh, rows in part_tiles(slots, part):
        pltpu.make_async_copy(grad_buf.at[rows], (down, dother)[side].at[place, yh], grad_sem).start()
    sum_ref[...] = jnp.sum(gqkv_ref[...].astype(F32), axis=0, keepdims=True)
    wait_for(grad_buf, grad_sem)


def back(part, slots, glow, low, qkv, prob, mixed, parts):
    shape = jax.ShapeDtypeStruct
    tile = shape((16, 2, 16, 2048), BF16)
    return pl.pallas_call(
        functools.partial(back_kernel, part),
        in_specs=[SMEM] + [VMEM] * 5 + [ANY] * 4,
        out_specs=[VMEM] * 2 + [ANY] * 2,
        out_shape=[shape((TOK, PART), BF16), shape((1, PART), F32), tile, tile],
        scratch_shapes=[
            pltpu.VMEM((WIDTH, HALF), BF16),
            pltpu.VMEM((WIDTH, HALF), BF16),
            pltpu.VMEM((WIDTH, 2048), BF16),
            pltpu.VMEM((TOK, HALF), BF16),
            pltpu.VMEM((WIDTH, TOK), BF16),
            pltpu.SemaphoreType.DMA((2,)),
            pltpu.SemaphoreType.DMA,
        ],
        compiler_params=pltpu.CompilerParams(vmem_limit_bytes=40 * 2**20),
        cost_estimate=pl.CostEstimate(flops=2 * TOK * WIDTH * 4096, bytes_accessed=20 * 2**20, transcendentals=0),
        name="back" + str(part),
    )(slots, glow, low, qkv, prob, mixed, *parts[0], *parts[1])


def end_kernel(slots, gqkv0_ref, gqkv1_ref, ghid_ref, tok_ref, ln1_ref, hidden_ref, feed_ref, feed_got_ref, down_bias_ref,
               own0, other0, own1, other1, gin_ref, out_ref, vec_ref, buf, total, sem):
    fetch_part(slots, 0, (own0, other0), buf.at[0], sem.at[0], slice(0, PART))
    fetch_part(slots, 1, (own1, other1), buf.at[1], sem.at[1], slice(0, PART))
    out_ref[...] = (hidden_ref[...] + feed_ref[...] + feed_got_ref[...].astype(F32) + down_bias_ref[...]).astype(BF16)
    vec_ref[...] = jnp.zeros_like(vec_ref)
    wait_for(buf.at[0], sem.at[0])
    total[...] = dot_t(gqkv0_ref[...], buf[0])
    wait_for(buf.at[1], sem.at[1])
    total[...] += dot_t(gqkv1_ref[...], buf[1])

    @pl.loop(0, TOK // 128)
    def _(i):
        rows = pl.ds(i * 128, 128)
        unit, scale = normed(tok_ref[rows, :].astype(F32))
        grad = total[rows, :]
        gin_ref[rows, :] = ghid_ref[rows, :] + norm_back(grad * ln1_ref[0:1, :], unit, scale)
        vec_ref[0:1, :] += jnp.sum(grad * unit, axis=0, keepdims=True)
        vec_ref[1:2, :] += jnp.sum(grad, axis=0, keepdims=True)


def end(slots, gqkv0, gqkv1, ghid, tokens, ln1, hidden, feed, feed_got, down_bias, parts):
    shape = jax.ShapeDtypeStruct
    return pl.pallas_call(
        end_kernel,
        in_specs=[SMEM] + [VMEM] * 9 + [ANY] * 4,
        out_specs=[VMEM] * 3,
        out_shape=[shape((TOK, WIDTH), F32), shape((TOK, WIDTH), BF16), shape((8, WIDTH), F32)],
        scratch_shapes=[
            pltpu.VMEM((2, WIDTH, PART), BF16),
            pltpu.VMEM((TOK, WIDTH), F32),
            pltpu.SemaphoreType.DMA((2,)),
        ],
        compiler_params=pltpu.CompilerParams(vmem_limit_bytes=40 * 2**20),
        cost_estimate=pl.CostEstimate(flops=2 * TOK * WIDTH * 3072, bytes_accessed=20 * 2**20, transcendentals=0),
        name="end",
    )(slots, gqkv0, gqkv1, ghid, tokens, ln1, hidden, feed, feed_got, down_bias.reshape(1, WIDTH), *parts[0], *parts[1])


AXES = ("z", "yh", "c", "x", "yl")
UP_ORDER = ("z", "x", "y")


def device_number(place):
    return (
        ((place["z"] * 2 + place["y"] // 2) * 2 + place["c"]) * 4 + place["x"]
    ) * 2 + place["y"] % 2


def exchange_pairs(axis, second):
    pairs = []
    for z, y, c, x in itertools.product(range(4), range(4), range(2), range(4)):
        here = {"z": z, "y": y, "c": c, "x": x}
        mask = 1 if (c == 0) != second else 3
        there = dict(here)
        there[axis] = here[axis] ^ mask
        pairs.append((device_number(here), device_number(there)))
    return pairs


def swap_axis(values, axis, second):
    return lax.ppermute(values, AXES, exchange_pairs(axis, second))


def swap_core(values):
    return lax.ppermute(values, "c", [(0, 1), (1, 0)])


def position(axis):
    if axis == "y":
        return lax.axis_index("yh") * 2 + lax.axis_index("yl")
    return lax.axis_index(axis)


def slot_of(core, distance):
    return jnp.where(
        core == 0, distance ^ (distance >> 1), ((distance << 1) & 3) ^ (3 * (distance >> 1))
    )


def slot_table():
    core, places = lax.axis_index("c"), jnp.arange(4, dtype=jnp.int32)
    rows = [
        slot_of(side, places ^ position(axis)) for side in (core, 1 - core) for axis in ("x", "y", "z")
    ]
    return jnp.concatenate(rows + [jnp.full((8,), core, jnp.int32)])


def steps_of(order):
    return [(axis, second) for axis in order for second in (False, True)]


def gather(values, order):
    for axis, second in steps_of(order):
        values = jnp.concatenate([values, swap_axis(values, axis, second)])
    return values


def add(left, right, dtype=BF16):
    return (left.astype(F32) + right.astype(F32)).astype(dtype)


def halves(own, got):
    count = own.shape[0] // 2
    return add(own[count:], got[count:]), add(own[:count], got[:count])


def natural_y(pieces):
    here, core = position("y"), lax.axis_index("c")
    return jnp.stack(
        [
            lax.dynamic_index_in_dim(pieces, slot_of(core, at ^ here), 0, keepdims=False)
            for at in range(4)
        ]
    )


def together(*values):
    return lax.optimization_barrier(values)


def pair_bias(clip_ids):
    clips = clip_ids.reshape(-1, BLOCK)
    row = lax.broadcasted_iota(jnp.int32, (BLOCK, BLOCK), 0)
    col = lax.broadcasted_iota(jnp.int32, (BLOCK, BLOCK), 1)
    allowed = (clips[:, :, None] == clips[:, None, :]) & (row >= col)[None]
    return jnp.where(allowed, 0.0, -1e30).astype(F32)


def on_device(
    tokens,
    qkv_weight,
    out_weight,
    up_weight,
    down_weight,
    ln1_gain,
    ln1_bias,
    q_bias,
    v_bias,
    out_bias,
    ln2_gain,
    ln2_bias,
    up_bias,
    down_bias,
    segment_ids,
    cotangent,
):
    slots = slot_table()
    heads = qkv_weight.reshape(8, 3, WIDTH)
    pieces = []
    for cols in (slice(0, HALF), slice(HALF, WIDTH)):
        pieces += [heads[:, :, cols].reshape(8, PART), out_weight[:, cols]]
    rows = natural_y(gather(jnp.concatenate(pieces, axis=1)[None], ("y",)))
    down = gather(down_weight[None], ("y",))
    up = gather(up_weight[None], UP_ORDER[:2])
    starts = [rows[:, :, i * 2048 : (i + 1) * 2048].reshape(1, 2, 16, 2048) for i in (0, 1)]
    downs = [down[:, :128], down[:, 128:]]
    middle = [gather(start, order[1:2]) for start, order in zip(starts, ORDERS)]
    downs = [gather(d, order[1:2]) for d, order in zip(downs, ORDERS)]
    owns = [gather(m, order[2:]) for m, order in zip(middle, ORDERS)]
    up = gather(up, UP_ORDER[2:])
    *owns, down0, down1 = together(*owns, *downs)
    parts = [(own, swap_core(own)) for own in owns]
    weights = (up, gather(down0, ("z",)), gather(down1, ("x",)))
    grad_other = swap_core(cotangent)

    ln1 = jnp.stack([ln1_gain, ln1_bias])
    nothing = jnp.zeros((HALF,), F32)
    qkv_bias = jnp.stack(
        [
            jnp.concatenate([q_bias[cols], nothing, v_bias[cols]])[None]
            for cols in (slice(0, HALF), slice(HALF, WIDTH))
        ]
    )
    low, qkv, prob, mixed = front(slots, tokens, pair_bias(segment_ids), ln1, qkv_bias, parts)
    hidden, low2 = join(slots, tokens, mixed, out_bias, jnp.stack([ln2_gain, ln2_bias]), parts)
    up_bias_grad, feed, feed_low, gc, gc_low, *grads = ffn(
        slots, up_bias, low2, swap_core(low2), cotangent, grad_other, weights, UP_ORDER, ORDERS
    )
    feed_got, gc_got = swap_core(feed_low), swap_core(gc_low)
    orders = (UP_ORDER, *ORDERS)
    kept = grads[::2]
    got = [swap_axis(move, order[2], True) for move, order in zip(grads[1::2], orders)]
    ghid, glow, vec2 = turn(hidden, ln2_gain, gc, gc_got, cotangent)
    gqkv0, sum0, own_a, other_a = back(0, slots, glow, low, qkv, prob, mixed, parts)

    *got, gqkv0, glow = together(*got, gqkv0, glow)
    split = [halves(k, g) for k, g in zip(kept, got)]
    moves, kept = [m for m, _ in split], [k for _, k in split]
    *moves, glow = together(*moves, glow)
    got = [swap_axis(move, order[2], False) for move, order in zip(moves, orders)]
    got_a = swap_core(other_a)
    gqkv1, sum1, own_b, other_b = back(1, slots, glow, low, qkv, prob, mixed, parts)
    got_b = swap_core(other_b)
    *got, got_a, got_b = together(*got, got_a, got_b)
    grad_tokens, output, vec1 = end(
        slots, gqkv0, gqkv1, ghid, tokens, ln1, hidden, feed, feed_got, down_bias, parts
    )
    sums = jnp.concatenate([sum0.reshape(3, HALF), sum1.reshape(3, HALF)], axis=1)
    blocks = [vec1[0:2], sums[0:1], sums[2:3], vec2[0:4]]
    vector = jnp.concatenate(
        [block.reshape(-1, 128) for block in blocks] + [up_bias_grad.reshape(-1, 128)]
    )

    main, main_got = [own_a, own_b], [got_a, got_b]
    vector_steps = steps_of(("x", "y", "z"))
    plan = [
        ((2, 2), ((1, True), (1, True), (1, True))),
        ((2, 2), ((1, False), (1, False), (1, False))),
        ((1, 1), ((0, True), (0, True), (0, True))),
        ((1, 1), ((0, False), (0, False), (0, False))),
    ]
    down_done = None
    for round_number, (main_axes, side_steps) in enumerate(plan):
        second = round_number % 2 == 0
        split = [halves(k, g) for k, g in zip(main, main_got)]
        main = [k for _, k in split]
        main_got = [
            swap_axis(m, order[at], second) for (m, _), order, at in zip(split, ORDERS, main_axes)
        ]
        if round_number == 2:
            down = [add(k, g) for k, g in zip(kept[1:], got[1:])]
            kept, got = [kept[0], jnp.concatenate(down, axis=1)], [got[0], None]
        sides = []
        for i, (at, side_second) in enumerate(side_steps[: len(kept)]):
            if got[i] is None:
                count = kept[i].shape[0] // 2
                move, kept[i] = kept[i][count:], kept[i][:count]
            else:
                move, kept[i] = halves(kept[i], got[i])
            axis = orders[i][at] if len(kept) == 3 or i == 0 else "y"
            sides.append(swap_axis(move, axis, side_second))
        got = sides
        axis, vector_second = vector_steps[round_number]
        vector = vector + swap_axis(vector, axis, vector_second)
        *main_got, vector = together(*main_got, *got, vector)
        main_got, got = main_got[:2], main_got[2:]
    up_grad = add(kept[0], got[0], F32)[0]
    down_grad = add(kept[1], got[1], F32)[0]

    both = jnp.concatenate([add(k, g).reshape(4, 8, 2048) for k, g in zip(main, main_got)], axis=2)
    here, core = position("y"), lax.axis_index("c")
    first = jnp.where(core == 0, 1, 3)
    second = 4 - first

    def at(slot):
        return lax.dynamic_index_in_dim(both, slot, 0, keepdims=False)

    far = swap_axis(jnp.stack([at(here ^ second), at(here ^ second ^ first)]), "y", True)
    vector = vector + swap_axis(vector, *vector_steps[4])
    far, vector = together(far, vector)
    near = swap_axis(add(at(here ^ first), far[1]), "y", False)
    vector = vector + swap_axis(vector, *vector_steps[5])
    near, vector = together(near, vector)
    vector = vector + swap_core(vector)
    row = (at(here).astype(F32) + far[0].astype(F32) + near.astype(F32)).reshape(8, 2, 2048)
    qkv_grad = row[:, :, :PART].reshape(8, 2, 3, HALF).transpose(0, 2, 1, 3).reshape(8, 3 * WIDTH)
    out_grad = row[:, :, PART:].reshape(8, WIDTH)
    summed = vector.reshape(-1)
    vectors = [summed[i * WIDTH : (i + 1) * WIDTH] for i in range(8)]
    return (
        output,
        grad_tokens,
        qkv_grad,
        out_grad,
        up_grad,
        down_grad,
        *vectors[:7],
        summed[8 * WIDTH :],
        vectors[7],
    )


def solution(mesh):
    fine = Mesh(mesh.devices.reshape(4, 2, 2, 4, 2), AXES)
    every, hidden, model = AXES, ("z", "yh", "c"), ("x", "yl")
    weights = (P(every, None), P(every, None), P(model, hidden), P(hidden, model))
    return jax.shard_map(
        on_device,
        mesh=fine,
        in_specs=(P(every, None), *weights, *[P()] * 9, P(every), P(every, None)),
        out_specs=(P(every, None), P(every, None), *weights, *[P()] * 9),
        check_vma=False,
    )
```

```python
import functools
import itertools

import jax
import jax.numpy as jnp
from jax import lax
from jax.experimental import pallas as pl
from jax.experimental.pallas import tpu as pltpu
from jax.sharding import Mesh, PartitionSpec as P

F32, BF16 = jnp.float32, jnp.bfloat16
TOK, WIDTH, FF = 512, 1024, 4096
BOTH = 2 * TOK
CHUNK = 1024
UNIT = 256
ROOT = 0.7978845608028654
CUBE = 0.044715
VMEM, ANY, HBM, SMEM = (
    pl.BlockSpec(memory_space=kind) for kind in (pltpu.VMEM, pl.ANY, pltpu.HBM, pltpu.SMEM)
)
ONE = pltpu.SemaphoreType.DMA
TWO = pltpu.SemaphoreType.DMA((2,))
FEW = pltpu.SemaphoreType.DMA((8,))


def shape(*dims, dtype=BF16):
    return jax.ShapeDtypeStruct(dims, dtype)


def work(flops):
    return pl.CostEstimate(flops=int(flops), bytes_accessed=1 << 20, transcendentals=0)


def dot(a, b):
    return lax.dot_general(a, b, (((1,), (0,)), ((), ())), preferred_element_type=F32)


def dot_t(a, b):
    return lax.dot_general(a, b, (((1,), (1,)), ((), ())), preferred_element_type=F32)


def normed(values):
    center = values - jnp.mean(values, axis=-1, keepdims=True)
    scale = lax.rsqrt(jnp.mean(center * center, axis=-1, keepdims=True) + 1e-05)
    return center * scale, scale


def norm_back(edge, unit, scale):
    return (edge - jnp.mean(edge, axis=-1, keepdims=True) - unit * jnp.mean(edge * unit, axis=-1, keepdims=True)) * scale


def start(source, target, sem):
    pltpu.make_async_copy(source, target, sem).start()


def wait(ref, sem):
    pltpu.make_async_copy(ref, ref, sem).wait()


def place_of(places, side, axis, slot):
    return places[side * 12 + "xyz".index(axis) * 4 + slot]


def ffn_kernel(places, bias_ref, low_own, low_other, grad_own, grad_other, up, down_low, down_high,
               bias_grad_ref, feed_ref, feed_low_ref, gc_ref, gc_low_ref, dup, ddown_keep, ddown_move0, ddown_move1,
               up_buf, down_buf, dup_buf, ddown_buf, low, grad, low_t, act_buf, gpre_buf, total, grad_total,
               feed_low, gc_low, in_sem, up_sem, down_sem, out_sem):
    core = places[24]

    def tiles(chunk):
        for part in (0, 1):
            for sy in range(4):
                y = place_of(places, 0, "y", sy)
                yh, yl = lax.div(y, 2), lax.rem(y, 2)
                unit = pl.ds(pl.multiple_of((part * 2 + yh) * UNIT, UNIT), UNIT)
                for x in range(4):
                    yield sy, chunk * 2 + part, x, yl, unit

    def model(x, yl):
        return pl.ds(pl.multiple_of((x * 2 + yl) * 128, 128), 128)

    def fetch(chunk):
        for sy, sz, x, yl, unit in tiles(chunk):
            start(up.at[x * 16 + sy * 4 + sz], up_buf.at[chunk, model(x, yl), unit], up_sem.at[chunk])
        for sy, sz, sx, yl, unit in tiles(chunk):
            cols = model(place_of(places, 0, "x", sx), yl)
            start((down_low, down_high)[sy // 2].at[sy % 2 * 16 + sz * 4 + sx], down_buf.at[chunk, unit, cols], down_sem.at[chunk])

    def send_down(chunk):
        for sy, sz, sx, yl, unit in tiles(chunk):
            source = ddown_buf.at[chunk, unit, model(place_of(places, 0, "x", sx), yl)]
            if sy < 2:
                start(source, ddown_keep.at[sy * 16 + sz * 4 + sx], out_sem)
            else:
                start(source, (ddown_move0, ddown_move1)[sy - 2].at[sz * 4 + sx], out_sem)

    def send_up(chunk):
        for sy, sz, x, yl, unit in tiles(chunk):
            start(dup_buf.at[chunk, model(x, yl), unit], dup.at[x * 16 + sy * 4 + sz], out_sem)

    start(low_own, low.at[pl.ds(0, TOK)], in_sem.at[0])
    start(low_other, low.at[pl.ds(TOK, TOK)], in_sem.at[0])
    fetch(0)
    start(grad_own, grad.at[pl.ds(0, TOK)], in_sem.at[1])
    start(grad_other, grad.at[pl.ds(TOK, TOK)], in_sem.at[1])
    fetch(1)
    bias_grad_ref[...] = jnp.zeros_like(bias_grad_ref)
    wait(low, in_sem.at[0])
    low_t[...] = low[...].T
    wait(grad, in_sem.at[1])

    for chunk in (0, 1):
        wait(up_buf.at[chunk], up_sem.at[chunk])
        wait(down_buf.at[chunk], down_sem.at[chunk])
        for n in range(CHUNK // UNIT):
            cols = slice(n * UNIT, (n + 1) * UNIT)
            block = (place_of(places, 0, "z", chunk * 2 + n // 2) * 2 + n % 2) * 2 + core
            pre = dot(low[...], up_buf[chunk, :, cols]) + bias_ref[block]
            gact = dot_t(grad[...], down_buf[chunk, cols, :])
            square = pre * pre
            bend = jnp.tanh(ROOT * (pre + CUBE * square * pre))
            half = 0.5 + 0.5 * bend
            act = (pre * half).astype(BF16)
            slope = half + 0.5 * pre * (1.0 - bend * bend) * (ROOT + 3.0 * ROOT * CUBE * square)
            gpre = (gact * slope).astype(BF16)
            act_buf[:, cols] = act
            gpre_buf[:, cols] = gpre
            bias_grad_ref[block] = jnp.sum(gpre.astype(F32), axis=0, keepdims=True)
            ddown_buf[chunk, cols, :] = dot(act.T, grad[...]).astype(BF16)
            dup_buf[chunk, :, cols] = dot(low_t[...], gpre).astype(BF16)
        send_up(chunk)
        send_down(chunk)
        more = dot_t(gpre_buf[...], up_buf[chunk])
        feed = dot(act_buf[...], down_buf[chunk])
        if chunk == 0:
            grad_total[...] = more
            total[...] = feed
        else:
            grad_total[...] += more
            gc_low[...] = grad_total[TOK:, :].astype(BF16)
            start(gc_low, gc_low_ref, out_sem)
            start(grad_total.at[pl.ds(0, TOK)], gc_ref, out_sem)
            total[...] += feed
            feed_low[...] = total[TOK:, :].astype(BF16)
            start(feed_low, feed_low_ref, out_sem)
            start(total.at[pl.ds(0, TOK)], feed_ref, out_sem)
    for ref in (dup_buf, ddown_buf, gc_low, feed_low, grad_total.at[pl.ds(0, TOK)], total.at[pl.ds(0, TOK)]):
        wait(ref, out_sem)


def ffn(places, up_bias, low_own, low_other, grad_own, grad_other, weights):
    big = pltpu.VMEM((2, CHUNK, CHUNK), BF16)
    rows = pltpu.VMEM((BOTH, WIDTH), BF16)
    sums = pltpu.VMEM((BOTH, WIDTH), F32)
    half = pltpu.VMEM((TOK, WIDTH), BF16)
    return pl.pallas_call(
        ffn_kernel,
        in_specs=[SMEM, VMEM] + [ANY] * 4 + [HBM] * 3,
        out_specs=[VMEM] + [HBM] * 8,
        out_shape=[
            shape(16, 1, UNIT, dtype=F32),
            shape(TOK, WIDTH, dtype=F32),
            shape(TOK, WIDTH),
            shape(TOK, WIDTH, dtype=F32),
            shape(TOK, WIDTH),
            shape(64, 128, 256),
            shape(32, 256, 128),
            shape(16, 256, 128),
            shape(16, 256, 128),
        ],
        scratch_shapes=[
            big, big, big, big, rows, rows, rows,
            pltpu.VMEM((BOTH, CHUNK), BF16),
            pltpu.VMEM((BOTH, CHUNK), BF16),
            sums, sums, half, half, TWO, TWO, TWO, ONE,
        ],
        compiler_params=pltpu.CompilerParams(vmem_limit_bytes=56 * 2**20),
        cost_estimate=work(40e9),
        name="ffn",
    )(places, up_bias.reshape(16, 1, UNIT), low_own, low_other, grad_own, grad_other, *weights)


BLOCK = 128
HALF = 512
PART = 3 * HALF
ORDERS = (("y", "x", "z"), ("y", "z", "x"))


def row_tiles(places, order):
    core = places[24]
    for side in (0, 1):
        for sx in range(4):
            for sz in range(4):
                last, middle = (sz, sx) if order[2] == "z" else (sx, sz)
                x, z = place_of(places, side, "x", sx), place_of(places, side, "z", sz)
                yield side, last // 2, last % 2 * 4 + middle, z, core if side == 0 else 1 - core, x


def fetch_part(places, part, pieces, buf, sem, cols):
    cols = slice(part * 2048 + cols.start, part * 2048 + cols.stop)
    for side, high, within, z, c, x in row_tiles(places, ORDERS[0]):
        start(pieces[2 * side + high].at[within, :, :, cols], buf.at[z, :, c, x], sem)


def matrix(ref):
    return ref.reshape(WIDTH, ref.shape[-1])


def parts_buffer(cols):
    return pltpu.VMEM((4, 2, 2, 4, 16, cols), BF16)


def lane_marks():
    low = lax.broadcasted_iota(jnp.int32, (1, 128), 1) < 64
    return low, jnp.where(low, 1.0, 0.0).astype(BF16), jnp.where(low, 0.0, 1.0).astype(BF16)


def project_kernel(places, tok_ref, ln1_ref, qkv_bias_ref, *refs):
    pieces, (qkv_ref, low_out, qkv_out, buf0, buf1, low_ref, sem, out_sem) = refs[:4], refs[4:]
    for part, buf in ((0, buf0), (1, buf1)):
        fetch_part(places, part, pieces, buf, sem.at[part], slice(0, PART))

    @pl.loop(0, TOK // 128)
    def _(i):
        rows = pl.ds(i * 128, 128)
        unit, _ = normed(tok_ref[rows, :].astype(F32))
        low_ref[rows, :] = (unit * ln1_ref[0:1, :] + ln1_ref[1:2, :]).astype(BF16)

    start(low_ref, low_out, out_sem)
    for part, buf in ((0, buf0), (1, buf1)):
        wait(buf, sem.at[part])
        for n in range(3):
            cols = slice(n * HALF, (n + 1) * HALF)
            qkv_ref[part, :, cols] = (dot(low_ref[...], matrix(buf)[:, cols]) + qkv_bias_ref[part, :, cols]).astype(BF16)
        start(qkv_ref.at[part], qkv_out.at[part], out_sem)
    wait(low_ref, out_sem)
    wait(qkv_ref, out_sem)


def project(places, tokens, ln1, qkv_bias, pieces):
    return pl.pallas_call(
        project_kernel,
        in_specs=[SMEM] + [VMEM] * 3 + [HBM] * 4,
        out_specs=[VMEM] + [HBM] * 2,
        out_shape=[shape(2, TOK, PART), shape(TOK, WIDTH), shape(2, TOK, PART)],
        scratch_shapes=[parts_buffer(PART), parts_buffer(PART), pltpu.VMEM((TOK, WIDTH), BF16), TWO, ONE],
        compiler_params=pltpu.CompilerParams(vmem_limit_bytes=24 * 2**20),
        cost_estimate=work(8e9),
        name="project",
    )(places, tokens, ln1, qkv_bias, *pieces)


def attend_kernel(places, tok_ref, pair_ref, qkv_ref, out_bias_ref, ln2_ref, *refs):
    pieces, refs = refs[:4], refs[4:]
    prob_out, mixed_out, hidden_out, normed_out, buf0, buf1, prob_ref, mixed_ref, hidden_ref, normed_ref, sem, out_sem = refs
    for part, buf in ((0, buf0), (1, buf1)):
        fetch_part(places, part, pieces, buf, sem.at[part], slice(PART, 2048))
    low, near, far = lane_marks()
    near, far = near * 0.125, far * 0.125

    @pl.loop(0, 8)
    def _(pair):
        part = lax.div(pair, 4)
        begin = pl.multiple_of(lax.rem(pair, 4) * 128, 128)
        lanes = pl.ds(pl.multiple_of(pair * 128, 128), 128)
        for block in range(TOK // BLOCK):
            rows = slice(block * BLOCK, (block + 1) * BLOCK)
            query = qkv_ref[part, rows, pl.ds(begin, 128)]
            key = qkv_ref[part, rows, pl.ds(begin + HALF, 128)]
            value = qkv_ref[part, rows, pl.ds(begin + 2 * HALF, 128)]
            bias = pair_ref[block]
            score = dot_t(jnp.concatenate([query * near, query * far], axis=0), key) + jnp.concatenate([bias, bias], axis=0)
            power = jnp.exp(score - jnp.max(score, axis=-1, keepdims=True))
            prob = (power * (1.0 / jnp.sum(power, axis=-1, keepdims=True))).astype(BF16)
            prob_ref[pair, block] = prob
            both = dot(prob, value)
            mixed_ref[rows, lanes] = jnp.where(low, both[:BLOCK], both[BLOCK:]).astype(BF16)

    start(prob_ref, prob_out, out_sem)
    start(mixed_ref, mixed_out, out_sem)
    for part, buf in ((0, buf0), (1, buf1)):
        cols = slice(part * HALF, (part + 1) * HALF)
        wait(buf, sem.at[part])
        hidden_ref[:, cols] = tok_ref[:, cols].astype(F32) + dot(mixed_ref[...], matrix(buf)[...]) + out_bias_ref[:, cols]
    start(hidden_ref, hidden_out, out_sem)

    @pl.loop(0, TOK // 128)
    def _(i):
        rows = pl.ds(i * 128, 128)
        unit, _ = normed(hidden_ref[rows, :])
        normed_ref[rows, :] = (unit * ln2_ref[0:1, :] + ln2_ref[1:2, :]).astype(BF16)

    start(normed_ref, normed_out, out_sem)
    for ref in (prob_ref, mixed_ref, hidden_ref, normed_ref):
        wait(ref, out_sem)


def attend(places, tokens, pair_bias, qkv, out_bias, ln2, pieces):
    outs = [((8, 4, 2 * BLOCK, BLOCK), BF16), ((TOK, WIDTH), BF16), ((TOK, WIDTH), F32), ((TOK, WIDTH), BF16)]
    return pl.pallas_call(
        attend_kernel,
        in_specs=[SMEM] + [VMEM] * 5 + [HBM] * 4,
        out_specs=[HBM] * 4,
        out_shape=[jax.ShapeDtypeStruct(*out) for out in outs],
        scratch_shapes=[parts_buffer(HALF), parts_buffer(HALF)] + [pltpu.VMEM(*out) for out in outs] + [TWO, ONE],
        compiler_params=pltpu.CompilerParams(vmem_limit_bytes=32 * 2**20),
        cost_estimate=work(16e9),
        name="attend",
    )(places, tokens, pair_bias, qkv, out_bias.reshape(1, WIDTH), ln2, *pieces)


def turn(hidden_ref, gain_ref, gc_ref, got_ref, grad_ref, ghid_ref, glow_ref, vec_ref):
    vec_ref[...] = jnp.zeros_like(vec_ref)

    @pl.loop(0, TOK // 128)
    def _(part):
        rows = pl.ds(part * 128, 128)
        unit, scale = normed(hidden_ref[rows, :])
        gc = gc_ref[rows, :] + got_ref[rows, :].astype(F32)
        gout = grad_ref[rows, :].astype(F32)
        ghid = gout + norm_back(gc * gain_ref[...], unit, scale)
        ghid_ref[rows, :] = ghid
        glow_ref[rows, :] = ghid.astype(BF16)
        vec_ref[0:1, :] += jnp.sum(ghid, axis=0, keepdims=True)
        vec_ref[1:2, :] += jnp.sum(gc * unit, axis=0, keepdims=True)
        vec_ref[2:3, :] += jnp.sum(gc, axis=0, keepdims=True)
        vec_ref[3:4, :] += jnp.sum(gout, axis=0, keepdims=True)


TURN_SHAPES = [((TOK, WIDTH), F32), ((TOK, WIDTH), F32), ((TOK, WIDTH), BF16), ((TOK, WIDTH), BF16)]


def back_kernel(part, places, low_in, qkv_in, prob_in, mixed_in, *refs):
    pieces, refs = refs[:4], refs[4:]
    if part == 0:
        gain_ref, turn_in, refs = refs[0], refs[1:5], refs[5:]
        sum_ref, vec_ref, gqkv_out, *outs = refs[:7]
        ghid_out, glow_out = refs[7:9]
        turn_refs, refs = refs[9:13], refs[13:]
        ghid_ref, refs = refs[0], refs[1:]
    else:
        glow_in, refs = refs[0], refs[1:]
        sum_ref, gqkv_out, *outs = refs[:6]
        refs = refs[6:]
    low_ref, qkv_ref, prob_ref, mixed_ref, glow_ref, buf, side_buf, grad_buf, gmix_ref, gqkv_ref, flip, sem, out_sem = refs
    tail = slice(PART, 2048)
    if part == 0:
        for source, target in zip(turn_in, turn_refs):
            start(source, target, sem.at[0])
    else:
        start(glow_in, glow_ref, sem.at[0])
    start(mixed_in, mixed_ref, sem.at[1])
    fetch_part(places, part, pieces, buf, sem.at[2], tail)
    fetch_part(places, 1 - part, pieces, side_buf, sem.at[3], tail)
    start(qkv_in.at[part], qkv_ref, sem.at[4])
    start(prob_in.at[pl.ds(part * 4, 4)], prob_ref, sem.at[4])
    start(low_in, low_ref, sem.at[5])
    wait(mixed_ref, sem.at[1])
    flip[...] = mixed_ref[...].T
    if part == 0:
        for ref in turn_refs:
            wait(ref, sem.at[0])
        turn(turn_refs[0], gain_ref, turn_refs[1], turn_refs[2], turn_refs[3], ghid_ref, glow_ref, vec_ref)
        start(ghid_ref, ghid_out, out_sem)
        start(glow_ref, glow_out, out_sem)
    else:
        wait(glow_ref, sem.at[0])
    heads = slice(part * HALF, (part + 1) * HALF)
    rest = slice((1 - part) * HALF, (2 - part) * HALF)
    grad_matrix = matrix(grad_buf)
    grad_matrix[:, PART:] = dot(flip[...], glow_ref[:, heads]).astype(BF16)
    wait(buf, sem.at[2])
    wait(side_buf, sem.at[3])
    gmix_ref[...] = (
        dot_t(glow_ref[:, heads], matrix(buf)[heads, :]) + dot_t(glow_ref[:, rest], matrix(side_buf)[heads, :])
    ).astype(BF16)
    wait(low_ref, sem.at[5])
    flip[...] = low_ref[...].T
    wait(qkv_ref, sem.at[4])
    wait(prob_ref, sem.at[4])
    low, near, far = lane_marks()

    @pl.loop(0, 4)
    def _(pair):
        begin = pl.multiple_of(pair * 128, 128)
        for block in range(TOK // BLOCK):
            rows = slice(block * BLOCK, (block + 1) * BLOCK)
            query = qkv_ref[rows, pl.ds(begin, 128)]
            key = qkv_ref[rows, pl.ds(begin + HALF, 128)]
            value = qkv_ref[rows, pl.ds(begin + 2 * HALF, 128)]
            gmix = gmix_ref[rows, pl.ds(begin, 128)]
            gmix = jnp.concatenate([gmix * near, gmix * far], axis=0)
            query = jnp.concatenate([query * (near * 0.125), query * (far * 0.125)], axis=0)
            prob_low = prob_ref[pair, block]
            prob = prob_low.astype(F32)
            gprob = dot_t(gmix, value)
            gscore = (prob * (gprob - jnp.sum(prob * gprob, axis=-1, keepdims=True))).astype(BF16)
            both = dot(gscore, key) * 0.125
            gqkv_ref[rows, pl.ds(begin, 128)] = jnp.where(low, both[:BLOCK], both[BLOCK:]).astype(BF16)
            gqkv_ref[rows, pl.ds(begin + HALF, 128)] = dot(gscore.T, query).astype(BF16)
            gqkv_ref[rows, pl.ds(begin + 2 * HALF, 128)] = dot(prob_low.T, gmix).astype(BF16)

    start(gqkv_ref, gqkv_out, out_sem)
    for n in range(3):
        cols = slice(n * HALF, (n + 1) * HALF)
        grad_matrix[:, cols] = dot(flip[...], gqkv_ref[:, cols]).astype(BF16)
    for side, high, within, z, c, x in row_tiles(places, ORDERS[part]):
        start(grad_buf.at[z, :, c, x], outs[2 * side + high].at[within], out_sem)
    sum_ref[...] = jnp.sum(gqkv_ref[...].astype(F32), axis=0, keepdims=True)
    wait(grad_buf, out_sem)
    wait(gqkv_ref, out_sem)
    if part == 0:
        wait(ghid_ref, out_sem)
        wait(glow_ref, out_sem)


def back(part, places, low, qkv, prob, mixed, pieces, *more):
    tile = shape(8, 2, 16, 2048)
    first = part == 0
    wide = pltpu.VMEM((TOK, WIDTH), BF16)
    return pl.pallas_call(
        functools.partial(back_kernel, part),
        in_specs=[SMEM] + [HBM] * 8 + ([VMEM] + [ANY] * 4 if first else [HBM]),
        out_specs=[VMEM] * (2 if first else 1) + [HBM] * (7 if first else 5),
        out_shape=[shape(1, PART, dtype=F32)]
        + ([shape(8, WIDTH, dtype=F32)] if first else [])
        + [shape(TOK, PART), tile, tile, tile, tile]
        + ([shape(TOK, WIDTH, dtype=F32), shape(TOK, WIDTH)] if first else []),
        scratch_shapes=([pltpu.VMEM(*s) for s in TURN_SHAPES] + [pltpu.VMEM((TOK, WIDTH), F32)] if first else [])
        + [
            wide,
            pltpu.VMEM((TOK, PART), BF16),
            pltpu.VMEM((4, 4, 2 * BLOCK, BLOCK), BF16),
            wide,
            wide,
            parts_buffer(HALF),
            parts_buffer(HALF),
            parts_buffer(2048),
            pltpu.VMEM((TOK, HALF), BF16),
            pltpu.VMEM((TOK, PART), BF16),
            pltpu.VMEM((WIDTH, TOK), BF16),
            FEW,
            ONE,
        ],
        compiler_params=pltpu.CompilerParams(vmem_limit_bytes=44 * 2**20),
        cost_estimate=work(20e9),
        name="back" + str(part),
    )(places, low, qkv, prob, mixed, *pieces, *more)


def end_kernel(places, ln1_ref, down_bias_ref, gqkv0, gqkv1, ghid, tok, hidden, feed, feed_got, *refs):
    pieces, refs = refs[:4], refs[4:]
    gin_out, out_out, vec_ref, buf0, buf1, gqkv0_ref, gqkv1_ref, ghid_ref, tok_ref, hidden_ref, feed_ref, got_ref, out_ref, total, sem, out_sem = refs
    start(gqkv0, gqkv0_ref, sem.at[0])
    fetch_part(places, 0, pieces, buf0, sem.at[0], slice(0, PART))
    start(gqkv1, gqkv1_ref, sem.at[1])
    fetch_part(places, 1, pieces, buf1, sem.at[1], slice(0, PART))
    start(ghid, ghid_ref, sem.at[2])
    start(tok, tok_ref, sem.at[2])
    for source, target in ((hidden, hidden_ref), (feed, feed_ref), (feed_got, got_ref)):
        start(source, target, sem.at[3])
    vec_ref[...] = jnp.zeros_like(vec_ref)
    wait(gqkv0_ref, sem.at[0])
    wait(buf0, sem.at[0])
    total[...] = dot_t(gqkv0_ref[...], matrix(buf0)[...])
    wait(gqkv1_ref, sem.at[1])
    wait(buf1, sem.at[1])
    total[...] += dot_t(gqkv1_ref[...], matrix(buf1)[...])
    wait(ghid_ref, sem.at[2])
    wait(tok_ref, sem.at[2])

    @pl.loop(0, TOK // 128)
    def _(i):
        rows = pl.ds(i * 128, 128)
        unit, scale = normed(tok_ref[rows, :].astype(F32))
        grad = total[rows, :]
        ghid_ref[rows, :] += norm_back(grad * ln1_ref[0:1, :], unit, scale)
        vec_ref[0:1, :] += jnp.sum(grad * unit, axis=0, keepdims=True)
        vec_ref[1:2, :] += jnp.sum(grad, axis=0, keepdims=True)

    start(ghid_ref, gin_out, out_sem)
    for ref in (hidden_ref, feed_ref, got_ref):
        wait(ref, sem.at[3])
    out_ref[...] = (hidden_ref[...] + feed_ref[...] + got_ref[...].astype(F32) + down_bias_ref[...]).astype(BF16)
    start(out_ref, out_out, out_sem)
    wait(ghid_ref, out_sem)
    wait(out_ref, out_sem)


def end(places, ln1, down_bias, gqkv0, gqkv1, ghid, tokens, hidden, feed, feed_got, pieces):
    low, high = pltpu.VMEM((TOK, WIDTH), BF16), pltpu.VMEM((TOK, WIDTH), F32)
    heads = pltpu.VMEM((TOK, PART), BF16)
    return pl.pallas_call(
        end_kernel,
        in_specs=[SMEM] + [VMEM] * 2 + [ANY] * 7 + [HBM] * 4,
        out_specs=[HBM] * 2 + [VMEM],
        out_shape=[shape(TOK, WIDTH, dtype=F32), shape(TOK, WIDTH), shape(8, WIDTH, dtype=F32)],
        scratch_shapes=[parts_buffer(PART), parts_buffer(PART), heads, heads, high, low, high, high, low, low, high, FEW, ONE],
        compiler_params=pltpu.CompilerParams(vmem_limit_bytes=40 * 2**20),
        cost_estimate=work(10e9),
        name="end",
    )(places, ln1, down_bias.reshape(1, WIDTH), gqkv0, gqkv1, ghid, tokens, hidden, feed, feed_got, *pieces)


AXES = ("z", "yh", "c", "x", "yl")


def device_number(place):
    return (
        ((place["z"] * 2 + place["y"] // 2) * 2 + place["c"]) * 4 + place["x"]
    ) * 2 + place["y"] % 2


def exchange_pairs(axis, second, alike=False):
    pairs = []
    for z, y, c, x in itertools.product(range(4), range(4), range(2), range(4)):
        here = {"z": z, "y": y, "c": c, "x": x}
        mask = 1 if (c == 0 or alike) != second else 3
        there = dict(here)
        there[axis] = here[axis] ^ mask
        pairs.append((device_number(here), device_number(there)))
    return pairs


def swap_axis(values, axis, second, alike=False):
    return lax.ppermute(values, AXES, exchange_pairs(axis, second, alike))


def swap_core(values):
    return lax.ppermute(values, "c", [(0, 1), (1, 0)])


def position(axis):
    if axis == "y":
        return lax.axis_index("yh") * 2 + lax.axis_index("yl")
    return lax.axis_index(axis)


def distance_of(core, slot):
    return jnp.where(core == 0, slot ^ (slot >> 1), ((slot << 1) & 3) ^ ((slot ^ (slot >> 1)) & 1))


def place_table():
    core, slots = lax.axis_index("c"), jnp.arange(4, dtype=jnp.int32)
    rows = [
        distance_of(side, slots) ^ position(axis)
        for side in (core, 1 - core)
        for axis in ("x", "y", "z")
    ]
    return jnp.concatenate(rows + [jnp.full((8,), core, jnp.int32)])


def add(left, right, dtype=BF16):
    return (left.astype(F32) + right.astype(F32)).astype(dtype)


def halves(own, got):
    count = own.shape[0] // 2
    return add(own[count:], got[count:]), add(own[:count], got[:count])


def natural_y(pieces):
    here, core = position("y"), lax.axis_index("c")
    away = [jnp.int32(at) ^ here for at in range(4)]
    slots = [jnp.where(core == 0, d ^ (d >> 1), ((d << 1) & 3) ^ (3 * (d >> 1))) for d in away]
    return jnp.stack([lax.dynamic_index_in_dim(pieces, slot, 0, keepdims=False) for slot in slots])


def together(*values):
    return lax.optimization_barrier(values)


def pair_bias(clip_ids):
    clips = clip_ids.reshape(-1, BLOCK)
    row = lax.broadcasted_iota(jnp.int32, (BLOCK, BLOCK), 0)
    col = lax.broadcasted_iota(jnp.int32, (BLOCK, BLOCK), 1)
    allowed = (clips[:, :, None] == clips[:, None, :]) & (row >= col)[None]
    return jnp.where(allowed, 0.0, -1e30).astype(F32)


def on_device(
    tokens,
    qkv_weight,
    out_weight,
    up_weight,
    down_weight,
    ln1_gain,
    ln1_bias,
    q_bias,
    v_bias,
    out_bias,
    ln2_gain,
    ln2_bias,
    up_bias,
    down_bias,
    segment_ids,
    cotangent,
):
    places = place_table()
    heads = qkv_weight.reshape(8, 3, WIDTH)
    pieces = []
    for cols in (slice(0, HALF), slice(HALF, WIDTH)):
        pieces += [heads[:, :, cols].reshape(8, PART), out_weight[:, cols]]
    rows, down, up = jnp.concatenate(pieces, axis=1)[None], down_weight[None], up_weight[None]
    for stage, axes in enumerate((("y", "x", "z"), ("x", "z", "y"))):
        for second in (False, True):
            values = (rows, down, up)
            got = [swap_axis(v, axis, second) for v, axis in zip(values, axes)]
            if stage == 0 and not second:
                *got, grad_other = together(*got, swap_core(cotangent))
            else:
                got = together(*got)
            rows, down, up = [jnp.concatenate(pair) for pair in zip(values, got)]
        if stage == 0:
            rows = natural_y(rows).reshape(1, 2, 16, 4096)
    up = lax.all_gather(up, "x", axis=0).reshape(64, 128, 256)
    rows_got, down_got = together(swap_axis(rows, "z", False), swap_axis(down, "y", False))
    rows, down = jnp.concatenate([rows, rows_got]), jnp.concatenate([down, down_got])
    rows_got, down_got, other_rows = together(
        swap_axis(rows, "z", True), swap_axis(down, "y", True), swap_core(rows)
    )
    pieces = (rows, rows_got, other_rows, swap_core(rows_got))

    ln1 = jnp.stack([ln1_gain, ln1_bias])
    nothing = jnp.zeros((HALF,), F32)
    qkv_bias = jnp.stack(
        [
            jnp.concatenate([q_bias[cols], nothing, v_bias[cols]])[None]
            for cols in (slice(0, HALF), slice(HALF, WIDTH))
        ]
    )
    qkv, low, qkv_kept = project(places, tokens, ln1, qkv_bias, pieces)
    prob, mixed, hidden, low2 = attend(
        places, tokens, pair_bias(segment_ids), qkv, out_bias, jnp.stack([ln2_gain, ln2_bias]), pieces
    )
    up_bias_grad, feed, feed_low, gc, gc_low, dup, keep_down, *move_down = ffn(
        places, up_bias, low2, swap_core(low2), cotangent, grad_other, (up, down, down_got)
    )
    dup = lax.psum_scatter(dup.reshape(4, 16, 128, 256), "x", scatter_dimension=0, tiled=True)[0]

    down_got0 = swap_axis(move_down[0], "y", True)
    sum0, vec2, gqkv0, *main_a, ghid, glow = back(
        0, places, low, qkv_kept, prob, mixed, pieces,
        ln2_gain.reshape(1, WIDTH), hidden, gc, swap_core(gc_low), cotangent,
    )
    down_got0, glow, feed_got, *main_a = together(down_got0, glow, swap_core(feed_low), *main_a)
    move_a = add(main_a[1], swap_core(main_a[3]))
    move_a, move_down, glow = together(move_a, move_down[1], glow)
    got_a, down_got1 = swap_axis(move_a, "z", True), swap_axis(move_down, "y", True)
    got_keep = swap_core(main_a[2])
    sum1, gqkv1, *main_b = back(1, places, low, qkv_kept, prob, mixed, pieces, glow)
    got_a, down_got1, got_keep, gqkv1, *main_b = together(got_a, down_got1, got_keep, gqkv1, *main_b)

    swapped = swap_core(main_b[3])
    move_a, keep_a = halves(add(main_a[0], got_keep), got_a)
    move_down, keep_down = add(keep_down[16:], down_got1), add(keep_down[:16], down_got0)
    swapped, move_a, move_down, gqkv1 = together(swapped, move_a, move_down, gqkv1)
    move_b = add(main_b[1], swapped)
    move_b, gqkv1 = together(move_b, gqkv1)
    got_b, got_a = swap_axis(move_b, "x", True), swap_axis(move_a, "z", False)
    down_got = swap_axis(move_down, "y", False)
    got_keep = swap_core(main_b[2])
    grad_tokens, output, vec1 = end(
        places, ln1, down_bias, gqkv0, gqkv1, ghid, tokens, hidden, feed, feed_got, pieces
    )
    got_b, got_a, down_got, got_keep, dup, vec1 = together(got_b, got_a, down_got, got_keep, dup, vec1)
    sums = jnp.concatenate([sum0.reshape(3, HALF), sum1.reshape(3, HALF)], axis=1)
    blocks = [vec1[0:2], sums[0:1], sums[2:3], vec2[0:4]]
    vector = jnp.concatenate(
        [block.reshape(-1, 128) for block in blocks] + [up_bias_grad.reshape(-1, 128)]
    )
    vector = vector + swap_core(vector)

    def vector_step(axis, second):
        return vector + swap_axis(vector, axis, second, True)

    move_b, keep_b = halves(add(main_b[0], got_keep), got_b)
    move_a, keep_a = halves(keep_a, got_a)
    move_down, keep_down = halves(keep_down, down_got)
    got_b, got_a = swap_axis(move_b, "x", False), swap_axis(move_a, "x", True)
    down_got, up_got = swap_axis(move_down, "z", True), swap_axis(dup[8:], "y", True)
    vector = vector_step("x", False)
    vector = vector_step("x", True)
    got_b, got_a, down_got, up_got, vector = together(got_b, got_a, down_got, up_got, vector)

    move_b, keep_b = halves(keep_b, got_b)
    move_a, keep_a = halves(keep_a, got_a)
    move_down, keep_down = halves(keep_down, down_got)
    move_up, keep_up = halves(dup[:8], up_got)
    got_b, got_a = swap_axis(move_b, "z", True), swap_axis(move_a, "x", False)
    down_got, up_got = swap_axis(move_down, "z", False), swap_axis(move_up, "y", False)
    vector_got = swap_axis(vector, "y", False, True)
    got_b, got_a, down_got, up_got, vector_got = together(got_b, got_a, down_got, up_got, vector_got)

    move_b, keep_b = halves(keep_b, got_b)
    move_down, keep_down = halves(keep_down, down_got)
    move_up, keep_up = halves(keep_up, up_got)
    vector = vector + vector_got
    got_b = swap_axis(move_b, "z", False)
    down_got, up_got = swap_axis(move_down, "x", True), swap_axis(move_up, "z", True)
    vector_got = swap_axis(vector, "y", True, True)
    got_b, down_got, up_got, vector_got = together(got_b, down_got, up_got, vector_got)

    both = jnp.concatenate(
        [add(k, g).reshape(4, 8, 2048) for k, g in ((keep_a, got_a), (keep_b, got_b))], axis=2
    )
    here, core = position("y"), lax.axis_index("c")
    first = jnp.where(core == 0, 1, 3)
    second = 4 - first

    def at(slot):
        return lax.dynamic_index_in_dim(both, slot, 0, keepdims=False)

    move_down, keep_down = halves(keep_down, down_got)
    move_up, keep_up = halves(keep_up, up_got)
    vector = vector + vector_got
    far = swap_axis(jnp.stack([at(here ^ second), at(here ^ second ^ first)]), "y", True)
    down_got, up_got = swap_axis(move_down, "x", False), swap_axis(move_up, "z", False)
    vector_got = swap_axis(vector, "z", False, True)
    far, down_got, up_got, vector_got = together(far, down_got, up_got, vector_got)

    vector = vector + vector_got
    near = swap_axis(add(at(here ^ first), far[1]), "y", False)
    vector = vector_step("z", True)
    down_grad = add(keep_down, down_got, F32)[0]
    up_grad = add(keep_up, up_got, F32)[0]
    row = (at(here).astype(F32) + far[0].astype(F32) + near.astype(F32)).reshape(8, 2, 2048)
    qkv_grad = row[:, :, :PART].reshape(8, 2, 3, HALF).transpose(0, 2, 1, 3).reshape(8, 3 * WIDTH)
    out_grad = row[:, :, PART:].reshape(8, WIDTH)
    summed = vector.reshape(-1)
    vectors = [summed[i * WIDTH : (i + 1) * WIDTH] for i in range(8)]
    return (
        output,
        grad_tokens,
        qkv_grad,
        out_grad,
        up_grad,
        down_grad,
        *vectors[:7],
        summed[8 * WIDTH :],
        vectors[7],
    )


def solution(mesh):
    fine = Mesh(mesh.devices.reshape(4, 2, 2, 4, 2), AXES)
    every, hidden, model = AXES, ("z", "yh", "c"), ("x", "yl")
    weights = (P(every, None), P(every, None), P(model, hidden), P(hidden, model))
    return jax.shard_map(
        on_device,
        mesh=fine,
        in_specs=(P(every, None), *weights, *[P()] * 9, P(every), P(every, None)),
        out_specs=(P(every, None), P(every, None), *weights, *[P()] * 9),
        check_vma=False,
    )
```

```python
import functools
import itertools

import jax
import jax.numpy as jnp
from jax import lax
from jax.experimental import pallas as pl
from jax.experimental.pallas import tpu as pltpu
from jax.sharding import Mesh, PartitionSpec as P

F32, BF16 = jnp.float32, jnp.bfloat16
TOK, WIDTH, FF = 512, 1024, 4096
BOTH = 2 * TOK
CHUNK = 1024
UNIT = 256
ROOT = 0.7978845608028654
CUBE = 0.044715
VMEM, ANY, HBM, SMEM = (
    pl.BlockSpec(memory_space=kind) for kind in (pltpu.VMEM, pl.ANY, pltpu.HBM, pltpu.SMEM)
)
ROOM = 60 * 2**20
ONE = pltpu.SemaphoreType.DMA
TWO = pltpu.SemaphoreType.DMA((2,))
FEW = pltpu.SemaphoreType.DMA((8,))


def shape(*dims, dtype=BF16):
    return jax.ShapeDtypeStruct(dims, dtype)


def work(flops):
    return pl.CostEstimate(flops=int(flops), bytes_accessed=1 << 20, transcendentals=0)


def dot(a, b):
    return lax.dot_general(a, b, (((1,), (0,)), ((), ())), preferred_element_type=F32)


def dot_t(a, b):
    return lax.dot_general(a, b, (((1,), (1,)), ((), ())), preferred_element_type=F32)


def normed(values):
    center = values - jnp.mean(values, axis=-1, keepdims=True)
    scale = lax.rsqrt(jnp.mean(center * center, axis=-1, keepdims=True) + 1e-05)
    return center * scale, scale


def norm_back(edge, unit, scale):
    return (edge - jnp.mean(edge, axis=-1, keepdims=True) - unit * jnp.mean(edge * unit, axis=-1, keepdims=True)) * scale


def start(source, target, sem):
    pltpu.make_async_copy(source, target, sem).start()


def wait(ref, sem):
    pltpu.make_async_copy(ref, ref, sem).wait()


def place_of(places, side, axis, slot):
    return places[side * 12 + "xyz".index(axis) * 4 + slot]


def ffn_kernel(places, bias_ref, low_own, low_other, grad_own, grad_other, up, down_low, down_high,
               bias_grad_ref, feed_ref, feed_low_ref, gc_ref, gc_low_ref, dup, ddown_keep, ddown_move,
               up_buf, down_buf, dup_buf, ddown_buf, low, grad, low_t, act_buf, gpre_buf, total, grad_total,
               feed_low, gc_low, in_sem, up_sem, down_sem, out_sem):
    core = places[24]

    def tiles(chunk):
        for part in (0, 1):
            for sy in range(4):
                y = place_of(places, 0, "y", sy)
                yh, yl = lax.div(y, 2), lax.rem(y, 2)
                unit = pl.ds(pl.multiple_of((part * 2 + yh) * UNIT, UNIT), UNIT)
                for x in range(4):
                    yield sy, chunk * 2 + part, x, yl, unit

    def model(x, yl):
        return pl.ds(pl.multiple_of((x * 2 + yl) * 128, 128), 128)

    def fetch(chunk):
        for sy, sz, x, yl, unit in tiles(chunk):
            start(up.at[x * 16 + sy * 4 + sz], up_buf.at[chunk, model(x, yl), unit], up_sem.at[chunk])
        for sy, sz, sx, yl, unit in tiles(chunk):
            cols = model(place_of(places, 0, "x", sx), yl)
            start((down_low, down_high)[sy // 2].at[sy % 2 * 16 + sx * 4 + sz], down_buf.at[chunk, unit, cols], down_sem.at[chunk])

    def send_down(chunk):
        for sy, sz, sx, yl, unit in tiles(chunk):
            source = ddown_buf.at[chunk, unit, model(place_of(places, 0, "x", sx), yl)]
            start(source, (ddown_keep, ddown_move)[sy // 2].at[sy % 2 * 16 + sx * 4 + sz], out_sem)

    def send_up(chunk):
        for part in (0, 1):
            z = place_of(places, 0, "z", chunk * 2 + part)
            for y in range(4):
                for x in range(4):
                    unit = slice((part * 2 + y // 2) * UNIT, (part * 2 + y // 2 + 1) * UNIT)
                    start(dup_buf.at[chunk, model(x, y % 2), unit], dup.at[x, y, z], out_sem)

    start(low_own, low.at[pl.ds(0, TOK)], in_sem.at[0])
    start(low_other, low.at[pl.ds(TOK, TOK)], in_sem.at[0])
    fetch(0)
    start(grad_own, grad.at[pl.ds(0, TOK)], in_sem.at[1])
    start(grad_other, grad.at[pl.ds(TOK, TOK)], in_sem.at[1])
    fetch(1)
    bias_grad_ref[...] = jnp.zeros_like(bias_grad_ref)
    wait(low, in_sem.at[0])
    low_t[...] = low[...].T
    wait(grad, in_sem.at[1])

    for chunk in (0, 1):
        wait(up_buf.at[chunk], up_sem.at[chunk])
        wait(down_buf.at[chunk], down_sem.at[chunk])
        for n in range(CHUNK // UNIT):
            cols = slice(n * UNIT, (n + 1) * UNIT)
            block = (place_of(places, 0, "z", chunk * 2 + n // 2) * 2 + n % 2) * 2 + core
            pre = dot(low[...], up_buf[chunk, :, cols]) + bias_ref[block]
            gact = dot_t(grad[...], down_buf[chunk, cols, :])
            square = pre * pre
            bend = jnp.tanh(ROOT * (pre + CUBE * square * pre))
            half = 0.5 + 0.5 * bend
            act = (pre * half).astype(BF16)
            slope = half + 0.5 * pre * (1.0 - bend * bend) * (ROOT + 3.0 * ROOT * CUBE * square)
            gpre = (gact * slope).astype(BF16)
            act_buf[:, cols] = act
            gpre_buf[:, cols] = gpre
            bias_grad_ref[block] = jnp.sum(gpre.astype(F32), axis=0, keepdims=True)
            ddown_buf[chunk, cols, :] = dot(act.T, grad[...]).astype(BF16)
            dup_buf[chunk, :, cols] = dot(low_t[...], gpre).astype(BF16)
        send_up(chunk)
        send_down(chunk)
        more = dot_t(gpre_buf[...], up_buf[chunk])
        feed = dot(act_buf[...], down_buf[chunk])
        if chunk == 0:
            grad_total[...] = more
            total[...] = feed
        else:
            grad_total[...] += more
            gc_low[...] = grad_total[TOK:, :].astype(BF16)
            start(gc_low, gc_low_ref, out_sem)
            start(grad_total.at[pl.ds(0, TOK)], gc_ref, out_sem)
            total[...] += feed
            feed_low[...] = total[TOK:, :].astype(BF16)
            start(feed_low, feed_low_ref, out_sem)
            start(total.at[pl.ds(0, TOK)], feed_ref, out_sem)
    for ref in (dup_buf, ddown_buf, gc_low, feed_low, grad_total.at[pl.ds(0, TOK)], total.at[pl.ds(0, TOK)]):
        wait(ref, out_sem)


def ffn(places, up_bias, low_own, low_other, grad_own, grad_other, weights):
    big = pltpu.VMEM((2, CHUNK, CHUNK), BF16)
    rows = pltpu.VMEM((BOTH, WIDTH), BF16)
    sums = pltpu.VMEM((BOTH, WIDTH), F32)
    half = pltpu.VMEM((TOK, WIDTH), BF16)
    return pl.pallas_call(
        ffn_kernel,
        in_specs=[SMEM, VMEM] + [HBM] * 7,
        out_specs=[VMEM] + [HBM] * 7,
        out_shape=[
            shape(16, 1, UNIT, dtype=F32),
            shape(TOK, WIDTH, dtype=F32),
            shape(TOK, WIDTH),
            shape(TOK, WIDTH, dtype=F32),
            shape(TOK, WIDTH),
            shape(4, 4, 4, 128, 256),
            shape(32, 256, 128),
            shape(32, 256, 128),
        ],
        scratch_shapes=[
            big, big, big, big, rows, rows, rows,
            pltpu.VMEM((BOTH, CHUNK), BF16),
            pltpu.VMEM((BOTH, CHUNK), BF16),
            sums, sums, half, half, TWO, TWO, TWO, ONE,
        ],
        compiler_params=pltpu.CompilerParams(vmem_limit_bytes=ROOM),
        cost_estimate=work(40e9),
        name="ffn",
    )(places, up_bias.reshape(16, 1, UNIT), low_own, low_other, grad_own, grad_other, *weights)


BLOCK = 128
HALF = 512
PART = 3 * HALF


def row_tiles(places):
    core = places[24]
    for side in (0, 1):
        for slot in range(4):
            yield side, slot, place_of(places, side, "z", slot), core if side == 0 else 1 - core


def fetch_part(places, part, pieces, buf, sem, cols):
    cols = slice(part * 2048 + cols.start, part * 2048 + cols.stop)
    for side, slot, z, c in row_tiles(places):
        start(pieces[2 * side + slot // 2].at[slot % 2, :, :, cols], buf.at[z, :, c], sem)


def matrix(ref):
    return ref.reshape(WIDTH, ref.shape[-1])


def parts_buffer(cols):
    return pltpu.VMEM((4, 2, 2, 64, cols), BF16)


def lane_marks():
    low = lax.broadcasted_iota(jnp.int32, (1, 128), 1) < 64
    return low, jnp.where(low, 1.0, 0.0).astype(BF16), jnp.where(low, 0.0, 1.0).astype(BF16)


def project_kernel(places, ln1_ref, qkv_bias_ref, tok, *refs):
    pieces, (low_out, qkv_out, buf0, buf1, tok_ref, low_ref, qkv_ref, sem, out_sem) = refs[:4], refs[4:]
    start(tok, tok_ref, sem.at[2])
    for part, buf in ((0, buf0), (1, buf1)):
        fetch_part(places, part, pieces, buf, sem.at[part], slice(0, PART))
    wait(tok_ref, sem.at[2])

    @pl.loop(0, TOK // 128)
    def _(i):
        rows = pl.ds(i * 128, 128)
        unit, _ = normed(tok_ref[rows, :].astype(F32))
        low_ref[rows, :] = (unit * ln1_ref[0:1, :] + ln1_ref[1:2, :]).astype(BF16)

    start(low_ref, low_out, out_sem)
    for part, buf in ((0, buf0), (1, buf1)):
        wait(buf, sem.at[part])
        for n in range(3):
            cols = slice(n * HALF, (n + 1) * HALF)
            qkv_ref[part, :, cols] = (dot(low_ref[...], matrix(buf)[:, cols]) + qkv_bias_ref[part, :, cols]).astype(BF16)
        start(qkv_ref.at[part], qkv_out.at[part], out_sem)
    wait(low_ref, out_sem)
    wait(qkv_ref, out_sem)


def project(places, tokens, ln1, qkv_bias, pieces):
    wide, heads = pltpu.VMEM((TOK, WIDTH), BF16), pltpu.VMEM((2, TOK, PART), BF16)
    return pl.pallas_call(
        project_kernel,
        in_specs=[SMEM] + [VMEM] * 2 + [HBM] * 5,
        out_specs=[HBM] * 2,
        out_shape=[shape(TOK, WIDTH), shape(2, TOK, PART)],
        scratch_shapes=[parts_buffer(PART), parts_buffer(PART), wide, wide, heads, FEW, ONE],
        compiler_params=pltpu.CompilerParams(vmem_limit_bytes=ROOM),
        cost_estimate=work(8e9),
        name="project",
    )(places, ln1, qkv_bias, tokens, *pieces)


def attend_kernel(places, pair_ref, out_bias_ref, ln2_ref, tok, qkv, *refs):
    pieces, refs = refs[:4], refs[4:]
    prob_out, mixed_out, hidden_out, normed_out, buf0, buf1, tok_ref, qkv_ref = refs[:8]
    prob_ref, mixed_ref, hidden_ref, normed_ref, sem, out_sem = refs[8:]
    start(qkv, qkv_ref, sem.at[2])
    start(tok, tok_ref, sem.at[3])
    for part, buf in ((0, buf0), (1, buf1)):
        fetch_part(places, part, pieces, buf, sem.at[part], slice(PART, 2048))
    low, near, far = lane_marks()
    near, far = near * 0.125, far * 0.125
    wait(qkv_ref, sem.at[2])

    @pl.loop(0, 8)
    def _(pair):
        part = lax.div(pair, 4)
        begin = pl.multiple_of(lax.rem(pair, 4) * 128, 128)
        lanes = pl.ds(pl.multiple_of(pair * 128, 128), 128)
        for block in range(TOK // BLOCK):
            rows = slice(block * BLOCK, (block + 1) * BLOCK)
            query = qkv_ref[part, rows, pl.ds(begin, 128)]
            key = qkv_ref[part, rows, pl.ds(begin + HALF, 128)]
            value = qkv_ref[part, rows, pl.ds(begin + 2 * HALF, 128)]
            bias = pair_ref[block]
            score = dot_t(jnp.concatenate([query * near, query * far], axis=0), key) + jnp.concatenate([bias, bias], axis=0)
            power = jnp.exp(score - jnp.max(score, axis=-1, keepdims=True))
            prob = (power * (1.0 / jnp.sum(power, axis=-1, keepdims=True))).astype(BF16)
            prob_ref[pair, block] = prob
            both = dot(prob, value)
            mixed_ref[rows, lanes] = jnp.where(low, both[:BLOCK], both[BLOCK:]).astype(BF16)

    start(prob_ref, prob_out, out_sem)
    start(mixed_ref, mixed_out, out_sem)
    wait(tok_ref, sem.at[3])
    for part, buf in ((0, buf0), (1, buf1)):
        cols = slice(part * HALF, (part + 1) * HALF)
        wait(buf, sem.at[part])
        hidden_ref[:, cols] = tok_ref[:, cols].astype(F32) + dot(mixed_ref[...], matrix(buf)[...]) + out_bias_ref[:, cols]
    start(hidden_ref, hidden_out, out_sem)

    @pl.loop(0, TOK // 128)
    def _(i):
        rows = pl.ds(i * 128, 128)
        unit, _ = normed(hidden_ref[rows, :])
        normed_ref[rows, :] = (unit * ln2_ref[0:1, :] + ln2_ref[1:2, :]).astype(BF16)

    start(normed_ref, normed_out, out_sem)
    for ref in (prob_ref, mixed_ref, hidden_ref, normed_ref):
        wait(ref, out_sem)


def attend(places, tokens, pair_bias, qkv, out_bias, ln2, pieces):
    outs = [((8, 4, 2 * BLOCK, BLOCK), BF16), ((TOK, WIDTH), BF16), ((TOK, WIDTH), F32), ((TOK, WIDTH), BF16)]
    return pl.pallas_call(
        attend_kernel,
        in_specs=[SMEM] + [VMEM] * 3 + [HBM] * 6,
        out_specs=[HBM] * 4,
        out_shape=[jax.ShapeDtypeStruct(*out) for out in outs],
        scratch_shapes=[parts_buffer(HALF), parts_buffer(HALF), pltpu.VMEM((TOK, WIDTH), BF16), pltpu.VMEM((2, TOK, PART), BF16)]
        + [pltpu.VMEM(*out) for out in outs]
        + [FEW, ONE],
        compiler_params=pltpu.CompilerParams(vmem_limit_bytes=ROOM),
        cost_estimate=work(16e9),
        name="attend",
    )(places, pair_bias, out_bias.reshape(1, WIDTH), ln2, tokens, qkv, *pieces)


def turn(hidden_ref, gain_ref, gc_ref, got_ref, grad_ref, ghid_ref, glow_ref, vec_ref):
    vec_ref[...] = jnp.zeros_like(vec_ref)

    @pl.loop(0, TOK // 128)
    def _(part):
        rows = pl.ds(part * 128, 128)
        unit, scale = normed(hidden_ref[rows, :])
        gc = gc_ref[rows, :] + got_ref[rows, :].astype(F32)
        gout = grad_ref[rows, :].astype(F32)
        ghid = gout + norm_back(gc * gain_ref[...], unit, scale)
        ghid_ref[rows, :] = ghid
        glow_ref[rows, :] = ghid.astype(BF16)
        vec_ref[0:1, :] += jnp.sum(ghid, axis=0, keepdims=True)
        vec_ref[1:2, :] += jnp.sum(gc * unit, axis=0, keepdims=True)
        vec_ref[2:3, :] += jnp.sum(gc, axis=0, keepdims=True)
        vec_ref[3:4, :] += jnp.sum(gout, axis=0, keepdims=True)


TURN_SHAPES = [((TOK, WIDTH), F32), ((TOK, WIDTH), F32), ((TOK, WIDTH), BF16), ((TOK, WIDTH), BF16)]


def back_kernel(part, places, low_in, qkv_in, prob_in, mixed_in, *refs):
    pieces, refs = refs[:4], refs[4:]
    if part == 0:
        gain_ref, turn_in, refs = refs[0], refs[1:5], refs[5:]
        sum_ref, vec_ref, gqkv_out, *outs = refs[:7]
        ghid_out, glow_out = refs[7:9]
        turn_refs, refs = refs[9:13], refs[13:]
        ghid_ref, refs = refs[0], refs[1:]
    else:
        glow_in, refs = refs[0], refs[1:]
        sum_ref, gqkv_out, *outs = refs[:6]
        refs = refs[6:]
    low_ref, qkv_ref, prob_ref, mixed_ref, glow_ref, buf, side_buf, grad_buf, gmix_ref, gqkv_ref, flip, sem, out_sem = refs
    tail = slice(PART, 2048)
    if part == 0:
        for source, target in zip(turn_in, turn_refs):
            start(source, target, sem.at[0])
    else:
        start(glow_in, glow_ref, sem.at[0])
    start(mixed_in, mixed_ref, sem.at[1])
    fetch_part(places, part, pieces, buf, sem.at[2], tail)
    fetch_part(places, 1 - part, pieces, side_buf, sem.at[3], tail)
    start(qkv_in.at[part], qkv_ref, sem.at[4])
    start(prob_in.at[pl.ds(part * 4, 4)], prob_ref, sem.at[4])
    start(low_in, low_ref, sem.at[5])
    wait(mixed_ref, sem.at[1])
    flip[...] = mixed_ref[...].T
    if part == 0:
        for ref in turn_refs:
            wait(ref, sem.at[0])
        turn(turn_refs[0], gain_ref, turn_refs[1], turn_refs[2], turn_refs[3], ghid_ref, glow_ref, vec_ref)
        start(ghid_ref, ghid_out, out_sem)
        start(glow_ref, glow_out, out_sem)
    else:
        wait(glow_ref, sem.at[0])
    heads = slice(part * HALF, (part + 1) * HALF)
    rest = slice((1 - part) * HALF, (2 - part) * HALF)
    grad_matrix = matrix(grad_buf)
    grad_matrix[:, PART:] = dot(flip[...], glow_ref[:, heads]).astype(BF16)
    wait(buf, sem.at[2])
    wait(side_buf, sem.at[3])
    gmix_ref[...] = (
        dot_t(glow_ref[:, heads], matrix(buf)[heads, :]) + dot_t(glow_ref[:, rest], matrix(side_buf)[heads, :])
    ).astype(BF16)
    wait(low_ref, sem.at[5])
    flip[...] = low_ref[...].T
    wait(qkv_ref, sem.at[4])
    wait(prob_ref, sem.at[4])
    low, near, far = lane_marks()

    @pl.loop(0, 4)
    def _(pair):
        begin = pl.multiple_of(pair * 128, 128)
        for block in range(TOK // BLOCK):
            rows = slice(block * BLOCK, (block + 1) * BLOCK)
            query = qkv_ref[rows, pl.ds(begin, 128)]
            key = qkv_ref[rows, pl.ds(begin + HALF, 128)]
            value = qkv_ref[rows, pl.ds(begin + 2 * HALF, 128)]
            gmix = gmix_ref[rows, pl.ds(begin, 128)]
            gmix = jnp.concatenate([gmix * near, gmix * far], axis=0)
            query = jnp.concatenate([query * (near * 0.125), query * (far * 0.125)], axis=0)
            prob_low = prob_ref[pair, block]
            prob = prob_low.astype(F32)
            gprob = dot_t(gmix, value)
            gscore = (prob * (gprob - jnp.sum(prob * gprob, axis=-1, keepdims=True))).astype(BF16)
            both = dot(gscore, key) * 0.125
            gqkv_ref[rows, pl.ds(begin, 128)] = jnp.where(low, both[:BLOCK], both[BLOCK:]).astype(BF16)
            gqkv_ref[rows, pl.ds(begin + HALF, 128)] = dot(gscore.T, query).astype(BF16)
            gqkv_ref[rows, pl.ds(begin + 2 * HALF, 128)] = dot(prob_low.T, gmix).astype(BF16)

    start(gqkv_ref, gqkv_out, out_sem)
    for n in range(3):
        cols = slice(n * HALF, (n + 1) * HALF)
        grad_matrix[:, cols] = dot(flip[...], gqkv_ref[:, cols]).astype(BF16)
    for side, slot, z, c in row_tiles(places):
        start(grad_buf.at[z, :, c], outs[2 * side + slot // 2].at[slot % 2], out_sem)
    sum_ref[...] = jnp.sum(gqkv_ref[...].astype(F32), axis=0, keepdims=True)
    wait(grad_buf, out_sem)
    wait(gqkv_ref, out_sem)
    if part == 0:
        wait(ghid_ref, out_sem)
        wait(glow_ref, out_sem)


def back(part, places, low, qkv, prob, mixed, pieces, *more):
    tile = shape(2, 2, 64, 2048)
    first = part == 0
    wide = pltpu.VMEM((TOK, WIDTH), BF16)
    return pl.pallas_call(
        functools.partial(back_kernel, part),
        in_specs=[SMEM] + [HBM] * 8 + ([VMEM] + [HBM] * 4 if first else [HBM]),
        out_specs=[VMEM] * (2 if first else 1) + [HBM] * (7 if first else 5),
        out_shape=[shape(1, PART, dtype=F32)]
        + ([shape(8, WIDTH, dtype=F32)] if first else [])
        + [shape(TOK, PART), tile, tile, tile, tile]
        + ([shape(TOK, WIDTH, dtype=F32), shape(TOK, WIDTH)] if first else []),
        scratch_shapes=([pltpu.VMEM(*s) for s in TURN_SHAPES] + [pltpu.VMEM((TOK, WIDTH), F32)] if first else [])
        + [
            wide,
            pltpu.VMEM((TOK, PART), BF16),
            pltpu.VMEM((4, 4, 2 * BLOCK, BLOCK), BF16),
            wide,
            wide,
            parts_buffer(HALF),
            parts_buffer(HALF),
            parts_buffer(2048),
            pltpu.VMEM((TOK, HALF), BF16),
            pltpu.VMEM((TOK, PART), BF16),
            pltpu.VMEM((WIDTH, TOK), BF16),
            FEW,
            ONE,
        ],
        compiler_params=pltpu.CompilerParams(vmem_limit_bytes=ROOM),
        cost_estimate=work(20e9),
        name="back" + str(part),
    )(places, low, qkv, prob, mixed, *pieces, *more)


def end_kernel(places, ln1_ref, down_bias_ref, gqkv0, gqkv1, ghid, tok, hidden, feed, feed_got, *refs):
    pieces, refs = refs[:4], refs[4:]
    gin_out, out_out, vec_ref, buf0, buf1, gqkv0_ref, gqkv1_ref, ghid_ref, tok_ref, hidden_ref, feed_ref, got_ref, out_ref, total, sem, out_sem = refs
    start(gqkv0, gqkv0_ref, sem.at[0])
    fetch_part(places, 0, pieces, buf0, sem.at[0], slice(0, PART))
    start(gqkv1, gqkv1_ref, sem.at[1])
    fetch_part(places, 1, pieces, buf1, sem.at[1], slice(0, PART))
    start(ghid, ghid_ref, sem.at[2])
    start(tok, tok_ref, sem.at[2])
    for source, target in ((hidden, hidden_ref), (feed, feed_ref), (feed_got, got_ref)):
        start(source, target, sem.at[3])
    vec_ref[...] = jnp.zeros_like(vec_ref)
    wait(gqkv0_ref, sem.at[0])
    wait(buf0, sem.at[0])
    total[...] = dot_t(gqkv0_ref[...], matrix(buf0)[...])
    wait(gqkv1_ref, sem.at[1])
    wait(buf1, sem.at[1])
    total[...] += dot_t(gqkv1_ref[...], matrix(buf1)[...])
    wait(ghid_ref, sem.at[2])
    wait(tok_ref, sem.at[2])

    @pl.loop(0, TOK // 128)
    def _(i):
        rows = pl.ds(i * 128, 128)
        unit, scale = normed(tok_ref[rows, :].astype(F32))
        grad = total[rows, :]
        ghid_ref[rows, :] += norm_back(grad * ln1_ref[0:1, :], unit, scale)
        vec_ref[0:1, :] += jnp.sum(grad * unit, axis=0, keepdims=True)
        vec_ref[1:2, :] += jnp.sum(grad, axis=0, keepdims=True)

    start(ghid_ref, gin_out, out_sem)
    for ref in (hidden_ref, feed_ref, got_ref):
        wait(ref, sem.at[3])
    out_ref[...] = (hidden_ref[...] + feed_ref[...] + got_ref[...].astype(F32) + down_bias_ref[...]).astype(BF16)
    start(out_ref, out_out, out_sem)
    wait(ghid_ref, out_sem)
    wait(out_ref, out_sem)


def end(places, ln1, down_bias, gqkv0, gqkv1, ghid, tokens, hidden, feed, feed_got, pieces):
    low, high = pltpu.VMEM((TOK, WIDTH), BF16), pltpu.VMEM((TOK, WIDTH), F32)
    heads = pltpu.VMEM((TOK, PART), BF16)
    return pl.pallas_call(
        end_kernel,
        in_specs=[SMEM] + [VMEM] * 2 + [HBM] * 7 + [HBM] * 4,
        out_specs=[HBM] * 2 + [VMEM],
        out_shape=[shape(TOK, WIDTH, dtype=F32), shape(TOK, WIDTH), shape(8, WIDTH, dtype=F32)],
        scratch_shapes=[parts_buffer(PART), parts_buffer(PART), heads, heads, high, low, high, high, low, low, high, FEW, ONE],
        compiler_params=pltpu.CompilerParams(vmem_limit_bytes=ROOM),
        cost_estimate=work(10e9),
        name="end",
    )(places, ln1, down_bias.reshape(1, WIDTH), gqkv0, gqkv1, ghid, tokens, hidden, feed, feed_got, *pieces)


AXES = ("z", "yh", "c", "x", "yl")
ALONG_Y, PLANE = ("yh", "yl"), ("yh", "x", "yl")


def device_number(place):
    return (
        ((place["z"] * 2 + place["y"] // 2) * 2 + place["c"]) * 4 + place["x"]
    ) * 2 + place["y"] % 2


def exchange_pairs(axis, second, alike=False):
    pairs = []
    for z, y, c, x in itertools.product(range(4), range(4), range(2), range(4)):
        here = {"z": z, "y": y, "c": c, "x": x}
        mask = 1 if (c == 0 or alike) != second else 3
        there = dict(here)
        there[axis] = here[axis] ^ mask
        pairs.append((device_number(here), device_number(there)))
    return pairs


def swap_axis(values, axis, second, alike=False):
    return lax.ppermute(values, AXES, exchange_pairs(axis, second, alike))


def swap_core(values):
    return lax.ppermute(values, "c", [(0, 1), (1, 0)])


def position(axis):
    if axis == "y":
        return lax.axis_index("yh") * 2 + lax.axis_index("yl")
    return lax.axis_index(axis)


def distance_of(core, slot):
    return jnp.where(core == 0, slot ^ (slot >> 1), ((slot << 1) & 3) ^ ((slot ^ (slot >> 1)) & 1))


def place_table():
    core, slots = lax.axis_index("c"), jnp.arange(4, dtype=jnp.int32)
    rows = [
        distance_of(side, slots) ^ position(axis)
        for side in (core, 1 - core)
        for axis in ("x", "y", "z")
    ]
    return jnp.concatenate(rows + [jnp.full((8,), core, jnp.int32)])


def add(left, right, dtype=BF16):
    return (left.astype(F32) + right.astype(F32)).astype(dtype)


def halves(own, got):
    count = own.shape[0] // 2
    return add(own[count:], got[count:]), add(own[:count], got[:count])


def together(*values):
    return lax.optimization_barrier(values)


def pair_bias(clip_ids):
    clips = clip_ids.reshape(-1, BLOCK)
    row = lax.broadcasted_iota(jnp.int32, (BLOCK, BLOCK), 0)
    col = lax.broadcasted_iota(jnp.int32, (BLOCK, BLOCK), 1)
    allowed = (clips[:, :, None] == clips[:, None, :]) & (row >= col)[None]
    return jnp.where(allowed, 0.0, -1e30).astype(F32)


def on_device(
    tokens,
    qkv_weight,
    out_weight,
    up_weight,
    down_weight,
    ln1_gain,
    ln1_bias,
    q_bias,
    v_bias,
    out_bias,
    ln2_gain,
    ln2_bias,
    up_bias,
    down_bias,
    segment_ids,
    cotangent,
):
    places = place_table()
    heads = qkv_weight.reshape(8, 3, WIDTH)
    pieces = []
    for cols in (slice(0, HALF), slice(HALF, WIDTH)):
        pieces += [heads[:, :, cols].reshape(8, PART), out_weight[:, cols]]
    rows, down, up = jnp.concatenate(pieces, axis=1), down_weight[None], up_weight[None]

    def grow(values, axis, second):
        return jnp.concatenate([values, swap_axis(values, axis, second)])

    rows = lax.all_to_all(jnp.broadcast_to(rows, (16, 8, 4096)), PLANE, 0, 0).reshape(1, 2, 64, 4096)
    down, up = grow(down, "z", False), grow(up, "z", False)
    grad_other = swap_core(cotangent)
    rows_got = swap_axis(rows, "z", False)
    down, up = grow(down, "z", True), grow(up, "z", True)
    down, up = grow(down, "x", False), grow(up, "y", False)
    down, up, rows_got = together(down, up, rows_got)
    rows = jnp.concatenate([rows, rows_got])
    rows_got, other_rows = swap_axis(rows, "z", True), swap_core(rows)
    down, up = grow(down, "x", True), grow(up, "y", True)
    up = lax.all_gather(up, "x", axis=0).reshape(64, 128, 256)
    down = grow(down, "y", False)
    rows_got, down = together(rows_got, down)
    pieces = (rows, rows_got, other_rows, swap_core(rows_got))
    down_got = swap_axis(down, "y", True)

    ln1 = jnp.stack([ln1_gain, ln1_bias])
    nothing = jnp.zeros((HALF,), F32)
    qkv_bias = jnp.stack(
        [
            jnp.concatenate([q_bias[cols], nothing, v_bias[cols]])[None]
            for cols in (slice(0, HALF), slice(HALF, WIDTH))
        ]
    )
    low, qkv = project(places, tokens, ln1, qkv_bias, pieces)
    prob, mixed, hidden, low2 = attend(
        places, tokens, pair_bias(segment_ids), qkv, out_bias, jnp.stack([ln2_gain, ln2_bias]), pieces
    )
    up_bias_grad, feed, feed_low, gc, gc_low, dup, keep_down, move_down = ffn(
        places, up_bias, low2, swap_core(low2), cotangent, grad_other, (up, down, down_got)
    )
    dup = lax.psum_scatter(dup, "x", scatter_dimension=0, tiled=True)[0]
    dup = lax.psum_scatter(dup, ALONG_Y, scatter_dimension=0, tiled=True)[0]
    dup = lax.psum_scatter(dup, "z", scatter_dimension=0, tiled=True)[0]

    down_got = swap_axis(move_down, "y", True)
    sum0, vec2, gqkv0, *main_a, ghid, glow = back(
        0, places, low, qkv, prob, mixed, pieces,
        ln2_gain.reshape(1, WIDTH), hidden, gc, swap_core(gc_low), cotangent,
    )
    down_got, glow, feed_got, *main_a = together(down_got, glow, swap_core(feed_low), *main_a)
    swapped = swap_core(main_a[3])
    move_down, keep_down = halves(keep_down, down_got)
    move_a, move_down, glow = together(add(main_a[1], swapped), move_down, glow)
    got_a, down_got = swap_axis(move_a, "z", True), swap_axis(move_down, "y", False)
    got_keep = swap_core(main_a[2])
    sum1, gqkv1, *main_b = back(1, places, low, qkv, prob, mixed, pieces, glow)
    got_a, down_got, got_keep, gqkv1, *main_b = together(got_a, down_got, got_keep, gqkv1, *main_b)

    swapped = swap_core(main_b[3])
    move_a, keep_a = halves(add(main_a[0], got_keep), got_a)
    move_down, keep_down = halves(keep_down, down_got)
    swapped, move_a, move_down, gqkv1 = together(swapped, move_a, move_down, gqkv1)
    move_b = add(main_b[1], swapped)
    move_b, gqkv1 = together(move_b, gqkv1)
    got_b, got_a = swap_axis(move_b, "z", True), swap_axis(move_a, "z", False)
    down_got = swap_axis(move_down, "x", True)
    got_keep = swap_core(main_b[2])
    grad_tokens, output, vec1 = end(
        places, ln1, down_bias, gqkv0, gqkv1, ghid, tokens, hidden, feed, feed_got, pieces
    )
    got_b, got_a, down_got, got_keep, vec1 = together(got_b, got_a, down_got, got_keep, vec1)
    sums = jnp.concatenate([sum0.reshape(3, HALF), sum1.reshape(3, HALF)], axis=1)
    blocks = [vec1[0:2], sums[0:1], sums[2:3], vec2[0:4]]
    vector = jnp.concatenate(
        [block.reshape(-1, 128) for block in blocks] + [up_bias_grad.reshape(-1, 128)]
    )
    vector_got = swap_core(vector)
    move_b, keep_b = halves(add(main_b[0], got_keep), got_b)
    move_down, keep_down = halves(keep_down, down_got)
    got_b, down_got = swap_axis(move_b, "z", False), swap_axis(move_down, "x", False)
    vector = vector + vector_got
    for second in (False, True):
        vector = vector + swap_axis(vector, "z", second, True)
    got_b, down_got, vector = together(got_b, down_got, vector)

    move_down, keep_down = halves(keep_down, down_got)
    down_got = swap_axis(move_down, "z", True)
    high = lax.reduce_precision(vector, 8, 7)
    terms = jnp.concatenate([high, vector - high, jnp.zeros((64, 128), F32)]).astype(BF16).reshape(8, 4096)
    both = jnp.concatenate(
        [add(k, g).reshape(16, 8, 2048) for k, g in ((keep_a, got_a), (keep_b, got_b))], axis=2
    )
    both = jnp.concatenate([both, jnp.broadcast_to(terms, (16, 8, 4096))], axis=1)
    both = jnp.sum(lax.all_to_all(both, PLANE, 0, 0).astype(F32), axis=0)
    move_down, keep_down = halves(keep_down, down_got)
    down_grad = add(keep_down, swap_axis(move_down, "z", False), F32)[0]
    up_grad = dup.astype(F32)
    row = both[:8].reshape(8, 2, 2048)
    qkv_grad = row[:, :, :PART].reshape(8, 2, 3, HALF).transpose(0, 2, 1, 3).reshape(8, 3 * WIDTH)
    out_grad = row[:, :, PART:].reshape(8, WIDTH)
    vector = both[8:11] + both[11:14]
    summed = vector.reshape(-1)
    vectors = [summed[i * WIDTH : (i + 1) * WIDTH] for i in range(8)]
    return (
        output,
        grad_tokens,
        qkv_grad,
        out_grad,
        up_grad,
        down_grad,
        *vectors[:7],
        summed[8 * WIDTH :],
        vectors[7],
    )


def solution(mesh):
    fine = Mesh(mesh.devices.reshape(4, 2, 2, 4, 2), AXES)
    every, hidden, model = AXES, ("z", "yh", "c"), ("x", "yl")
    weights = (P(every, None), P(every, None), P(model, hidden), P(hidden, model))
    return jax.shard_map(
        on_device,
        mesh=fine,
        in_specs=(P(every, None), *weights, *[P()] * 9, P(every), P(every, None)),
        out_specs=(P(every, None), P(every, None), *weights, *[P()] * 9),
        check_vma=False,
    )
```

```python
import functools
import itertools

import jax
import jax.numpy as jnp
from jax import lax
from jax.experimental import pallas as pl
from jax.experimental.pallas import tpu as pltpu
from jax.sharding import Mesh, PartitionSpec as P

F32, BF16 = jnp.float32, jnp.bfloat16
TOK, WIDTH, FF = 512, 1024, 4096
BOTH = 2 * TOK
CHUNK = 1024
UNIT = 256
ROOT = 0.7978845608028654
CUBE = 0.044715
VMEM, ANY, HBM, SMEM = (
    pl.BlockSpec(memory_space=kind) for kind in (pltpu.VMEM, pl.ANY, pltpu.HBM, pltpu.SMEM)
)
ROOM = 60 * 2**20
ONE = pltpu.SemaphoreType.DMA
TWO = pltpu.SemaphoreType.DMA((2,))
FEW = pltpu.SemaphoreType.DMA((8,))


def shape(*dims, dtype=BF16):
    return jax.ShapeDtypeStruct(dims, dtype)


def work(flops):
    return pl.CostEstimate(flops=int(flops), bytes_accessed=1 << 20, transcendentals=0)


def dot(a, b):
    return lax.dot_general(a, b, (((1,), (0,)), ((), ())), preferred_element_type=F32)


def dot_t(a, b):
    return lax.dot_general(a, b, (((1,), (1,)), ((), ())), preferred_element_type=F32)


def normed(values):
    center = values - jnp.mean(values, axis=-1, keepdims=True)
    scale = lax.rsqrt(jnp.mean(center * center, axis=-1, keepdims=True) + 1e-05)
    return center * scale, scale


def norm_back(edge, unit, scale):
    return (edge - jnp.mean(edge, axis=-1, keepdims=True) - unit * jnp.mean(edge * unit, axis=-1, keepdims=True)) * scale


def start(source, target, sem):
    pltpu.make_async_copy(source, target, sem).start()


def wait(ref, sem):
    pltpu.make_async_copy(ref, ref, sem).wait()


def place_of(places, side, axis, slot):
    return places[side * 12 + "xyz".index(axis) * 4 + slot]


def ffn_kernel(places, bias_ref, low_own, low_other, grad_own, grad_other, up, down_low, down_high,
               bias_grad_ref, feed_ref, feed_low_ref, gc_ref, gc_low_ref, dup, ddown_keep, ddown_move,
               up_buf, down_buf, dup_buf, ddown_buf, low, grad, low_t, act_buf, gpre_buf, total, grad_total,
               feed_low, gc_low, in_sem, up_sem, down_sem, out_sem):
    core = places[24]

    def tiles(chunk):
        for part in (0, 1):
            for sy in range(4):
                y = place_of(places, 0, "y", sy)
                yh, yl = lax.div(y, 2), lax.rem(y, 2)
                unit = pl.ds(pl.multiple_of((part * 2 + yh) * UNIT, UNIT), UNIT)
                for x in range(4):
                    yield sy, chunk * 2 + part, x, yl, unit

    def model(x, yl):
        return pl.ds(pl.multiple_of((x * 2 + yl) * 128, 128), 128)

    def fetch(chunk):
        for sy, sz, x, yl, unit in tiles(chunk):
            start(up.at[x * 16 + sy * 4 + sz], up_buf.at[chunk, model(x, yl), unit], up_sem.at[chunk])
        for sy, sz, sx, yl, unit in tiles(chunk):
            cols = model(place_of(places, 0, "x", sx), yl)
            start((down_low, down_high)[sy // 2].at[sy % 2 * 16 + sx * 4 + sz], down_buf.at[chunk, unit, cols], down_sem.at[chunk])

    def send_down(chunk):
        for sy, sz, sx, yl, unit in tiles(chunk):
            source = ddown_buf.at[chunk, unit, model(place_of(places, 0, "x", sx), yl)]
            start(source, (ddown_keep, ddown_move)[sy // 2].at[sy % 2 * 16 + sx * 4 + sz], out_sem)

    def send_up(chunk):
        for part in (0, 1):
            z = place_of(places, 0, "z", chunk * 2 + part)
            for y in range(4):
                for x in range(4):
                    unit = slice((part * 2 + y // 2) * UNIT, (part * 2 + y // 2 + 1) * UNIT)
                    start(dup_buf.at[chunk, model(x, y % 2), unit], dup.at[x, y, z], out_sem)

    start(low_own, low.at[pl.ds(0, TOK)], in_sem.at[0])
    start(low_other, low.at[pl.ds(TOK, TOK)], in_sem.at[0])
    fetch(0)
    start(grad_own, grad.at[pl.ds(0, TOK)], in_sem.at[1])
    start(grad_other, grad.at[pl.ds(TOK, TOK)], in_sem.at[1])
    fetch(1)
    bias_grad_ref[...] = jnp.zeros_like(bias_grad_ref)
    wait(low, in_sem.at[0])
    low_t[...] = low[...].T
    wait(grad, in_sem.at[1])

    for chunk in (0, 1):
        wait(up_buf.at[chunk], up_sem.at[chunk])
        wait(down_buf.at[chunk], down_sem.at[chunk])
        for n in range(CHUNK // UNIT):
            cols = slice(n * UNIT, (n + 1) * UNIT)
            block = (place_of(places, 0, "z", chunk * 2 + n // 2) * 2 + n % 2) * 2 + core
            pre = dot(low[...], up_buf[chunk, :, cols]) + bias_ref[block]
            gact = dot_t(grad[...], down_buf[chunk, cols, :])
            square = pre * pre
            bend = jnp.tanh(ROOT * (pre + CUBE * square * pre))
            half = 0.5 + 0.5 * bend
            act = (pre * half).astype(BF16)
            slope = half + 0.5 * pre * (1.0 - bend * bend) * (ROOT + 3.0 * ROOT * CUBE * square)
            gpre = (gact * slope).astype(BF16)
            act_buf[:, cols] = act
            gpre_buf[:, cols] = gpre
            bias_grad_ref[block] = jnp.sum(gpre.astype(F32), axis=0, keepdims=True)
            ddown_buf[chunk, cols, :] = dot(act.T, grad[...]).astype(BF16)
            dup_buf[chunk, :, cols] = dot(low_t[...], gpre).astype(BF16)
        send_up(chunk)
        send_down(chunk)
        more = dot_t(gpre_buf[...], up_buf[chunk])
        feed = dot(act_buf[...], down_buf[chunk])
        if chunk == 0:
            grad_total[...] = more
            total[...] = feed
        else:
            grad_total[...] += more
            gc_low[...] = grad_total[TOK:, :].astype(BF16)
            start(gc_low, gc_low_ref, out_sem)
            start(grad_total.at[pl.ds(0, TOK)], gc_ref, out_sem)
            total[...] += feed
            feed_low[...] = total[TOK:, :].astype(BF16)
            start(feed_low, feed_low_ref, out_sem)
            start(total.at[pl.ds(0, TOK)], feed_ref, out_sem)
    for ref in (dup_buf, ddown_buf, gc_low, feed_low, grad_total.at[pl.ds(0, TOK)], total.at[pl.ds(0, TOK)]):
        wait(ref, out_sem)


def ffn(places, up_bias, low_own, low_other, grad_own, grad_other, weights):
    big = pltpu.VMEM((2, CHUNK, CHUNK), BF16)
    rows = pltpu.VMEM((BOTH, WIDTH), BF16)
    sums = pltpu.VMEM((BOTH, WIDTH), F32)
    half = pltpu.VMEM((TOK, WIDTH), BF16)
    return pl.pallas_call(
        ffn_kernel,
        in_specs=[SMEM, VMEM] + [HBM] * 7,
        out_specs=[VMEM] + [HBM] * 7,
        out_shape=[
            shape(16, 1, UNIT, dtype=F32),
            shape(TOK, WIDTH, dtype=F32),
            shape(TOK, WIDTH),
            shape(TOK, WIDTH, dtype=F32),
            shape(TOK, WIDTH),
            shape(4, 4, 4, 128, 256),
            shape(32, 256, 128),
            shape(32, 256, 128),
        ],
        scratch_shapes=[
            big, big, big, big, rows, rows, rows,
            pltpu.VMEM((BOTH, CHUNK), BF16),
            pltpu.VMEM((BOTH, CHUNK), BF16),
            sums, sums, half, half, TWO, TWO, TWO, ONE,
        ],
        compiler_params=pltpu.CompilerParams(vmem_limit_bytes=ROOM),
        cost_estimate=work(40e9),
        name="ffn",
    )(places, up_bias.reshape(16, 1, UNIT), low_own, low_other, grad_own, grad_other, *weights)


BLOCK = 128
HALF = 512
PART = 3 * HALF


def row_tiles(places, axis):
    core = places[24]
    for side in (0, 1):
        for slot in range(4):
            yield side, slot, place_of(places, side, axis, slot), core if side == 0 else 1 - core


def fetch_part(places, part, pieces, buf, sem, cols):
    cols = slice(part * 2048 + cols.start, part * 2048 + cols.stop)
    for side, slot, z, c in row_tiles(places, "z"):
        start(pieces[2 * side + slot // 2].at[slot % 2, :, :, cols], buf.at[z, :, c], sem)


def matrix(ref):
    return ref.reshape(WIDTH, ref.shape[-1])


def parts_buffer(cols):
    return pltpu.VMEM((4, 2, 2, 64, cols), BF16)


def lane_marks():
    low = lax.broadcasted_iota(jnp.int32, (1, 128), 1) < 64
    return low, jnp.where(low, 1.0, 0.0).astype(BF16), jnp.where(low, 0.0, 1.0).astype(BF16)


def project_kernel(places, ln1_ref, qkv_bias_ref, tok, *refs):
    pieces, (low_out, qkv_out, buf0, buf1, tok_ref, low_ref, qkv_ref, sem, out_sem) = refs[:4], refs[4:]
    start(tok, tok_ref, sem.at[2])
    for part, buf in ((0, buf0), (1, buf1)):
        fetch_part(places, part, pieces, buf, sem.at[part], slice(0, PART))
    wait(tok_ref, sem.at[2])

    @pl.loop(0, TOK // 128)
    def _(i):
        rows = pl.ds(i * 128, 128)
        unit, _ = normed(tok_ref[rows, :].astype(F32))
        low_ref[rows, :] = (unit * ln1_ref[0:1, :] + ln1_ref[1:2, :]).astype(BF16)

    start(low_ref, low_out, out_sem)
    for part, buf in ((0, buf0), (1, buf1)):
        wait(buf, sem.at[part])
        for n in range(3):
            cols = slice(n * HALF, (n + 1) * HALF)
            qkv_ref[part, :, cols] = (dot(low_ref[...], matrix(buf)[:, cols]) + qkv_bias_ref[part, :, cols]).astype(BF16)
        start(qkv_ref.at[part], qkv_out.at[part], out_sem)
    wait(low_ref, out_sem)
    wait(qkv_ref, out_sem)


def project(places, tokens, ln1, qkv_bias, pieces):
    wide, heads = pltpu.VMEM((TOK, WIDTH), BF16), pltpu.VMEM((2, TOK, PART), BF16)
    return pl.pallas_call(
        project_kernel,
        in_specs=[SMEM] + [VMEM] * 2 + [HBM] * 5,
        out_specs=[HBM] * 2,
        out_shape=[shape(TOK, WIDTH), shape(2, TOK, PART)],
        scratch_shapes=[parts_buffer(PART), parts_buffer(PART), wide, wide, heads, FEW, ONE],
        compiler_params=pltpu.CompilerParams(vmem_limit_bytes=ROOM),
        cost_estimate=work(8e9),
        name="project",
    )(places, ln1, qkv_bias, tokens, *pieces)


def attend_kernel(places, pair_ref, out_bias_ref, ln2_ref, tok, qkv, *refs):
    pieces, refs = refs[:4], refs[4:]
    prob_out, mixed_out, hidden_out, normed_out, buf0, buf1, tok_ref, qkv_ref = refs[:8]
    prob_ref, mixed_ref, hidden_ref, normed_ref, sem, out_sem = refs[8:]
    start(qkv, qkv_ref, sem.at[2])
    start(tok, tok_ref, sem.at[3])
    for part, buf in ((0, buf0), (1, buf1)):
        fetch_part(places, part, pieces, buf, sem.at[part], slice(PART, 2048))
    low, near, far = lane_marks()
    near, far = near * 0.125, far * 0.125
    wait(qkv_ref, sem.at[2])

    @pl.loop(0, 8)
    def _(pair):
        part = lax.div(pair, 4)
        begin = pl.multiple_of(lax.rem(pair, 4) * 128, 128)
        lanes = pl.ds(pl.multiple_of(pair * 128, 128), 128)
        for block in range(TOK // BLOCK):
            rows = slice(block * BLOCK, (block + 1) * BLOCK)
            query = qkv_ref[part, rows, pl.ds(begin, 128)]
            key = qkv_ref[part, rows, pl.ds(begin + HALF, 128)]
            value = qkv_ref[part, rows, pl.ds(begin + 2 * HALF, 128)]
            bias = pair_ref[block]
            score = dot_t(jnp.concatenate([query * near, query * far], axis=0), key) + jnp.concatenate([bias, bias], axis=0)
            power = jnp.exp(score - jnp.max(score, axis=-1, keepdims=True))
            prob = (power * (1.0 / jnp.sum(power, axis=-1, keepdims=True))).astype(BF16)
            prob_ref[pair, block] = prob
            both = dot(prob, value)
            mixed_ref[rows, lanes] = jnp.where(low, both[:BLOCK], both[BLOCK:]).astype(BF16)

    start(prob_ref, prob_out, out_sem)
    start(mixed_ref, mixed_out, out_sem)
    wait(tok_ref, sem.at[3])
    for part, buf in ((0, buf0), (1, buf1)):
        cols = slice(part * HALF, (part + 1) * HALF)
        wait(buf, sem.at[part])
        hidden_ref[:, cols] = tok_ref[:, cols].astype(F32) + dot(mixed_ref[...], matrix(buf)[...]) + out_bias_ref[:, cols]
    start(hidden_ref, hidden_out, out_sem)

    @pl.loop(0, TOK // 128)
    def _(i):
        rows = pl.ds(i * 128, 128)
        unit, _ = normed(hidden_ref[rows, :])
        normed_ref[rows, :] = (unit * ln2_ref[0:1, :] + ln2_ref[1:2, :]).astype(BF16)

    start(normed_ref, normed_out, out_sem)
    for ref in (prob_ref, mixed_ref, hidden_ref, normed_ref):
        wait(ref, out_sem)


def attend(places, tokens, pair_bias, qkv, out_bias, ln2, pieces):
    outs = [((8, 4, 2 * BLOCK, BLOCK), BF16), ((TOK, WIDTH), BF16), ((TOK, WIDTH), F32), ((TOK, WIDTH), BF16)]
    return pl.pallas_call(
        attend_kernel,
        in_specs=[SMEM] + [VMEM] * 3 + [HBM] * 6,
        out_specs=[HBM] * 4,
        out_shape=[jax.ShapeDtypeStruct(*out) for out in outs],
        scratch_shapes=[parts_buffer(HALF), parts_buffer(HALF), pltpu.VMEM((TOK, WIDTH), BF16), pltpu.VMEM((2, TOK, PART), BF16)]
        + [pltpu.VMEM(*out) for out in outs]
        + [FEW, ONE],
        compiler_params=pltpu.CompilerParams(vmem_limit_bytes=ROOM),
        cost_estimate=work(16e9),
        name="attend",
    )(places, pair_bias, out_bias.reshape(1, WIDTH), ln2, tokens, qkv, *pieces)


def turn(hidden_ref, gain_ref, gc_ref, got_ref, grad_ref, ghid_ref, glow_ref, vec_ref):
    vec_ref[...] = jnp.zeros_like(vec_ref)

    @pl.loop(0, TOK // 128)
    def _(part):
        rows = pl.ds(part * 128, 128)
        unit, scale = normed(hidden_ref[rows, :])
        gc = gc_ref[rows, :] + got_ref[rows, :].astype(F32)
        gout = grad_ref[rows, :].astype(F32)
        ghid = gout + norm_back(gc * gain_ref[...], unit, scale)
        ghid_ref[rows, :] = ghid
        glow_ref[rows, :] = ghid.astype(BF16)
        vec_ref[0:1, :] += jnp.sum(ghid, axis=0, keepdims=True)
        vec_ref[1:2, :] += jnp.sum(gc * unit, axis=0, keepdims=True)
        vec_ref[2:3, :] += jnp.sum(gc, axis=0, keepdims=True)
        vec_ref[3:4, :] += jnp.sum(gout, axis=0, keepdims=True)


TURN_SHAPES = [((TOK, WIDTH), F32), ((TOK, WIDTH), F32), ((TOK, WIDTH), BF16), ((TOK, WIDTH), BF16)]


def back_kernel(part, places, low_in, qkv_in, prob_in, mixed_in, *refs):
    pieces, refs = refs[:4], refs[4:]
    if part == 0:
        gain_ref, turn_in, refs = refs[0], refs[1:5], refs[5:]
        sum_ref, vec_ref, gqkv_out, *outs = refs[:7]
        ghid_out, glow_out = refs[7:9]
        turn_refs, refs = refs[9:13], refs[13:]
        ghid_ref, refs = refs[0], refs[1:]
    else:
        glow_in, refs = refs[0], refs[1:]
        sum_ref, gqkv_out, *outs = refs[:6]
        refs = refs[6:]
    low_ref, qkv_ref, prob_ref, mixed_ref, glow_ref, buf, side_buf, grad_buf, gmix_ref, gqkv_ref, flip, sem, out_sem = refs
    tail = slice(PART, 2048)
    if part == 0:
        for source, target in zip(turn_in, turn_refs):
            start(source, target, sem.at[0])
    else:
        start(glow_in, glow_ref, sem.at[0])
    start(mixed_in, mixed_ref, sem.at[1])
    fetch_part(places, part, pieces, buf, sem.at[2], tail)
    fetch_part(places, 1 - part, pieces, side_buf, sem.at[3], tail)
    start(qkv_in.at[part], qkv_ref, sem.at[4])
    start(prob_in.at[pl.ds(part * 4, 4)], prob_ref, sem.at[4])
    start(low_in, low_ref, sem.at[5])
    wait(mixed_ref, sem.at[1])
    flip[...] = mixed_ref[...].T
    if part == 0:
        for ref in turn_refs:
            wait(ref, sem.at[0])
        turn(turn_refs[0], gain_ref, turn_refs[1], turn_refs[2], turn_refs[3], ghid_ref, glow_ref, vec_ref)
        start(ghid_ref, ghid_out, out_sem)
        start(glow_ref, glow_out, out_sem)
    else:
        wait(glow_ref, sem.at[0])
    heads = slice(part * HALF, (part + 1) * HALF)
    rest = slice((1 - part) * HALF, (2 - part) * HALF)
    grad_matrix = matrix(grad_buf)
    grad_matrix[:, PART:] = dot(flip[...], glow_ref[:, heads]).astype(BF16)
    wait(buf, sem.at[2])
    wait(side_buf, sem.at[3])
    gmix_ref[...] = (
        dot_t(glow_ref[:, heads], matrix(buf)[heads, :]) + dot_t(glow_ref[:, rest], matrix(side_buf)[heads, :])
    ).astype(BF16)
    wait(low_ref, sem.at[5])
    flip[...] = low_ref[...].T
    wait(qkv_ref, sem.at[4])
    wait(prob_ref, sem.at[4])
    low, near, far = lane_marks()

    @pl.loop(0, 4)
    def _(pair):
        begin = pl.multiple_of(pair * 128, 128)
        for block in range(TOK // BLOCK):
            rows = slice(block * BLOCK, (block + 1) * BLOCK)
            query = qkv_ref[rows, pl.ds(begin, 128)]
            key = qkv_ref[rows, pl.ds(begin + HALF, 128)]
            value = qkv_ref[rows, pl.ds(begin + 2 * HALF, 128)]
            gmix = gmix_ref[rows, pl.ds(begin, 128)]
            gmix = jnp.concatenate([gmix * near, gmix * far], axis=0)
            query = jnp.concatenate([query * (near * 0.125), query * (far * 0.125)], axis=0)
            prob_low = prob_ref[pair, block]
            prob = prob_low.astype(F32)
            gprob = dot_t(gmix, value)
            gscore = (prob * (gprob - jnp.sum(prob * gprob, axis=-1, keepdims=True))).astype(BF16)
            both = dot(gscore, key) * 0.125
            gqkv_ref[rows, pl.ds(begin, 128)] = jnp.where(low, both[:BLOCK], both[BLOCK:]).astype(BF16)
            gqkv_ref[rows, pl.ds(begin + HALF, 128)] = dot(gscore.T, query).astype(BF16)
            gqkv_ref[rows, pl.ds(begin + 2 * HALF, 128)] = dot(prob_low.T, gmix).astype(BF16)

    start(gqkv_ref, gqkv_out, out_sem)
    for n in range(3):
        cols = slice(n * HALF, (n + 1) * HALF)
        grad_matrix[:, cols] = dot(flip[...], gqkv_ref[:, cols]).astype(BF16)
    for side, slot, at, c in row_tiles(places, "zx"[part]):
        source = grad_buf.at[at, :, c] if part == 0 else grad_buf.at[:, :, c, pl.ds(pl.multiple_of(at * 16, 16), 16)]
        start(source, outs[2 * side + slot // 2].at[slot % 2], out_sem)
    sum_ref[...] = jnp.sum(gqkv_ref[...].astype(F32), axis=0, keepdims=True)
    wait(grad_buf, out_sem)
    wait(gqkv_ref, out_sem)
    if part == 0:
        wait(ghid_ref, out_sem)
        wait(glow_ref, out_sem)


def back(part, places, low, qkv, prob, mixed, pieces, *more):
    first = part == 0
    tile = shape(2, 2, 64, 2048) if first else shape(2, 4, 2, 16, 2048)
    wide = pltpu.VMEM((TOK, WIDTH), BF16)
    return pl.pallas_call(
        functools.partial(back_kernel, part),
        in_specs=[SMEM] + [HBM] * 8 + ([VMEM] + [HBM] * 4 if first else [HBM]),
        out_specs=[VMEM] * (2 if first else 1) + [HBM] * (7 if first else 5),
        out_shape=[shape(1, PART, dtype=F32)]
        + ([shape(8, WIDTH, dtype=F32)] if first else [])
        + [shape(TOK, PART), tile, tile, tile, tile]
        + ([shape(TOK, WIDTH, dtype=F32), shape(TOK, WIDTH)] if first else []),
        scratch_shapes=([pltpu.VMEM(*s) for s in TURN_SHAPES] + [pltpu.VMEM((TOK, WIDTH), F32)] if first else [])
        + [
            wide,
            pltpu.VMEM((TOK, PART), BF16),
            pltpu.VMEM((4, 4, 2 * BLOCK, BLOCK), BF16),
            wide,
            wide,
            parts_buffer(HALF),
            parts_buffer(HALF),
            parts_buffer(2048),
            pltpu.VMEM((TOK, HALF), BF16),
            pltpu.VMEM((TOK, PART), BF16),
            pltpu.VMEM((WIDTH, TOK), BF16),
            FEW,
            ONE,
        ],
        compiler_params=pltpu.CompilerParams(vmem_limit_bytes=ROOM),
        cost_estimate=work(20e9),
        name="back" + str(part),
    )(places, low, qkv, prob, mixed, *pieces, *more)


def end_kernel(places, ln1_ref, down_bias_ref, gqkv0, gqkv1, ghid, tok, hidden, feed, feed_got, *refs):
    pieces, refs = refs[:4], refs[4:]
    gin_out, out_out, vec_ref, buf0, buf1, gqkv0_ref, gqkv1_ref, ghid_ref, tok_ref, hidden_ref, feed_ref, got_ref, out_ref, total, sem, out_sem = refs
    start(gqkv0, gqkv0_ref, sem.at[0])
    fetch_part(places, 0, pieces, buf0, sem.at[0], slice(0, PART))
    start(gqkv1, gqkv1_ref, sem.at[1])
    fetch_part(places, 1, pieces, buf1, sem.at[1], slice(0, PART))
    start(ghid, ghid_ref, sem.at[2])
    start(tok, tok_ref, sem.at[2])
    for source, target in ((hidden, hidden_ref), (feed, feed_ref), (feed_got, got_ref)):
        start(source, target, sem.at[3])
    vec_ref[...] = jnp.zeros_like(vec_ref)
    wait(gqkv0_ref, sem.at[0])
    wait(buf0, sem.at[0])
    total[...] = dot_t(gqkv0_ref[...], matrix(buf0)[...])
    wait(gqkv1_ref, sem.at[1])
    wait(buf1, sem.at[1])
    total[...] += dot_t(gqkv1_ref[...], matrix(buf1)[...])
    wait(ghid_ref, sem.at[2])
    wait(tok_ref, sem.at[2])

    @pl.loop(0, TOK // 128)
    def _(i):
        rows = pl.ds(i * 128, 128)
        unit, scale = normed(tok_ref[rows, :].astype(F32))
        grad = total[rows, :]
        ghid_ref[rows, :] += norm_back(grad * ln1_ref[0:1, :], unit, scale)
        vec_ref[0:1, :] += jnp.sum(grad * unit, axis=0, keepdims=True)
        vec_ref[1:2, :] += jnp.sum(grad, axis=0, keepdims=True)

    start(ghid_ref, gin_out, out_sem)
    for ref in (hidden_ref, feed_ref, got_ref):
        wait(ref, sem.at[3])
    out_ref[...] = (hidden_ref[...] + feed_ref[...] + got_ref[...].astype(F32) + down_bias_ref[...]).astype(BF16)
    start(out_ref, out_out, out_sem)
    wait(ghid_ref, out_sem)
    wait(out_ref, out_sem)


def end(places, ln1, down_bias, gqkv0, gqkv1, ghid, tokens, hidden, feed, feed_got, pieces):
    low, high = pltpu.VMEM((TOK, WIDTH), BF16), pltpu.VMEM((TOK, WIDTH), F32)
    heads = pltpu.VMEM((TOK, PART), BF16)
    return pl.pallas_call(
        end_kernel,
        in_specs=[SMEM] + [VMEM] * 2 + [HBM] * 7 + [HBM] * 4,
        out_specs=[HBM] * 2 + [VMEM],
        out_shape=[shape(TOK, WIDTH, dtype=F32), shape(TOK, WIDTH), shape(8, WIDTH, dtype=F32)],
        scratch_shapes=[parts_buffer(PART), parts_buffer(PART), heads, heads, high, low, high, high, low, low, high, FEW, ONE],
        compiler_params=pltpu.CompilerParams(vmem_limit_bytes=ROOM),
        cost_estimate=work(10e9),
        name="end",
    )(places, ln1, down_bias.reshape(1, WIDTH), gqkv0, gqkv1, ghid, tokens, hidden, feed, feed_got, *pieces)


AXES = ("z", "yh", "c", "x", "yl")
ALONG_Y, PLANE_XY, PLANE_ZY = ("yh", "yl"), ("yh", "x", "yl"), ("z", "yh", "yl")


def device_number(place):
    return (
        ((place["z"] * 2 + place["y"] // 2) * 2 + place["c"]) * 4 + place["x"]
    ) * 2 + place["y"] % 2


def exchange_pairs(axis, second, alike=False):
    pairs = []
    for z, y, c, x in itertools.product(range(4), range(4), range(2), range(4)):
        here = {"z": z, "y": y, "c": c, "x": x}
        mask = 1 if (c == 0 or alike) != second else 3
        there = dict(here)
        there[axis] = here[axis] ^ mask
        pairs.append((device_number(here), device_number(there)))
    return pairs


def swap_axis(values, axis, second, alike=False):
    return lax.ppermute(values, AXES, exchange_pairs(axis, second, alike))


def swap_core(values):
    return lax.ppermute(values, "c", [(0, 1), (1, 0)])


def position(axis):
    if axis == "y":
        return lax.axis_index("yh") * 2 + lax.axis_index("yl")
    return lax.axis_index(axis)


def distance_of(core, slot):
    return jnp.where(core == 0, slot ^ (slot >> 1), ((slot << 1) & 3) ^ ((slot ^ (slot >> 1)) & 1))


def place_table():
    core, slots = lax.axis_index("c"), jnp.arange(4, dtype=jnp.int32)
    rows = [
        distance_of(side, slots) ^ position(axis)
        for side in (core, 1 - core)
        for axis in ("x", "y", "z")
    ]
    return jnp.concatenate(rows + [jnp.full((8,), core, jnp.int32)])


def add(left, right, dtype=BF16):
    return (left.astype(F32) + right.astype(F32)).astype(dtype)


def halves(own, got):
    count = own.shape[0] // 2
    return add(own[count:], got[count:]), add(own[:count], got[:count])


def spread(values, axes):
    return lax.all_to_all(jnp.broadcast_to(values, (16,) + values.shape), axes, 0, 0)


def spread_back(values, axes):
    return lax.all_to_all(values, axes, 0, 0)


def together(*values):
    return lax.optimization_barrier(values)


def pair_bias(clip_ids):
    clips = clip_ids.reshape(-1, BLOCK)
    row = lax.broadcasted_iota(jnp.int32, (BLOCK, BLOCK), 0)
    col = lax.broadcasted_iota(jnp.int32, (BLOCK, BLOCK), 1)
    allowed = (clips[:, :, None] == clips[:, None, :]) & (row >= col)[None]
    return jnp.where(allowed, 0.0, -1e30).astype(F32)


def on_device(
    tokens,
    qkv_weight,
    out_weight,
    up_weight,
    down_weight,
    ln1_gain,
    ln1_bias,
    q_bias,
    v_bias,
    out_bias,
    ln2_gain,
    ln2_bias,
    up_bias,
    down_bias,
    segment_ids,
    cotangent,
):
    places = place_table()
    heads = qkv_weight.reshape(8, 3, WIDTH)
    pieces = []
    for cols in (slice(0, HALF), slice(HALF, WIDTH)):
        pieces += [heads[:, :, cols].reshape(8, PART), out_weight[:, cols]]
    def join(pairs):
        return together(*[jnp.concatenate(pair) for pair in pairs])

    rows = spread(jnp.concatenate(pieces, axis=1), PLANE_XY)
    down, up = down_weight[None], up_weight[None]
    down, up = join(((down, swap_axis(down, "z", False)), (up, swap_axis(up, "z", False))))
    rows, down_got, up_got = together(rows, swap_axis(down, "z", True), swap_axis(up, "z", True))
    rows = rows.reshape(1, 2, 64, 4096)
    rows_got = swap_axis(rows, "z", False)
    down, up = join(((down, down_got), (up, up_got)))
    down, up = join(((down, swap_axis(down, "x", False)), (up, swap_axis(up, "y", False))))
    rows_got, down_got, up_got, grad_other = together(
        rows_got, swap_axis(down, "x", True), swap_axis(up, "y", True), swap_core(cotangent)
    )
    rows, down, up = join(((rows, rows_got), (down, down_got), (up, up_got)))
    up = lax.all_gather(up, "x", axis=0).reshape(64, 128, 256)
    rows_got, down_got, other_rows = together(
        swap_axis(rows, "z", True), swap_axis(down, "y", False), swap_core(rows)
    )
    pieces = (rows, rows_got, other_rows, swap_core(rows_got))
    (down,) = join(((down, down_got),))
    down_got = swap_axis(down, "y", True)

    ln1 = jnp.stack([ln1_gain, ln1_bias])
    nothing = jnp.zeros((HALF,), F32)
    qkv_bias = jnp.stack(
        [
            jnp.concatenate([q_bias[cols], nothing, v_bias[cols]])[None]
            for cols in (slice(0, HALF), slice(HALF, WIDTH))
        ]
    )
    low, qkv = project(places, tokens, ln1, qkv_bias, pieces)
    prob, mixed, hidden, low2 = attend(
        places, tokens, pair_bias(segment_ids), qkv, out_bias, jnp.stack([ln2_gain, ln2_bias]), pieces
    )
    up_bias_grad, feed, feed_low, gc, gc_low, dup, keep_down, move_down = ffn(
        places, up_bias, low2, swap_core(low2), cotangent, grad_other, (up, down, down_got)
    )
    dup = lax.psum_scatter(dup, "x", scatter_dimension=0, tiled=True)[0]

    down_got = swap_axis(move_down, "y", True)
    sum0, vec2, gqkv0, *main_a, ghid, glow = back(
        0, places, low, qkv, prob, mixed, pieces,
        ln2_gain.reshape(1, WIDTH), hidden, gc, swap_core(gc_low), cotangent,
    )
    swapped_a, got_keep_a = swap_core(main_a[3]), swap_core(main_a[2])
    sum1, gqkv1, *main_b = back(1, places, low, qkv, prob, mixed, pieces, glow)
    swapped_a, got_keep_a, down_got, gqkv1, *main_b = together(swapped_a, got_keep_a, down_got, gqkv1, *main_b)

    swapped_b = swap_core(main_b[3])
    move_a = add(main_a[1], swapped_a)
    move_down, keep_down = halves(keep_down, down_got)
    swapped_b, move_a, move_down, gqkv1 = together(swapped_b, move_a, move_down, gqkv1)
    move_b = add(main_b[1], swapped_b)
    move_b, gqkv1 = together(move_b, gqkv1)
    got_b, got_a = swap_axis(move_b, "x", True), swap_axis(move_a, "z", True)
    down_got = swap_axis(move_down, "y", False)
    got_keep_b = swap_core(main_b[2])
    grad_tokens, output, vec1 = end(
        places, ln1, down_bias, gqkv0, gqkv1, ghid, tokens, hidden, feed, swap_core(feed_low), pieces
    )
    got_b, got_a, down_got, got_keep_b, dup, vec1 = together(got_b, got_a, down_got, got_keep_b, dup, vec1)
    sums = jnp.concatenate([sum0.reshape(3, HALF), sum1.reshape(3, HALF)], axis=1)
    blocks = [vec1[0:2], sums[0:1], sums[2:3], vec2[0:4]]
    vector = jnp.concatenate(
        [block.reshape(-1, 128) for block in blocks] + [up_bias_grad.reshape(-1, 128)]
    )
    vector_got = swap_core(vector)
    move_b, keep_b = halves(add(main_b[0], got_keep_b), got_b)
    move_a, keep_a = halves(add(main_a[0], got_keep_a), got_a)
    got_b, got_a = swap_axis(move_b, "x", False), swap_axis(move_a, "z", False)
    dup = lax.psum_scatter(dup, ALONG_Y, scatter_dimension=0, tiled=True)[0]
    vector = vector + vector_got
    for second in (False, True):
        vector = vector + swap_axis(vector, "z", second, True)
    got_b, got_a, vector = together(got_b, got_a, vector)

    row_a = spread_back(add(keep_a, got_a).reshape(16, 8, 2048), PLANE_XY)
    row_b = spread_back(add(keep_b, got_b).reshape(16, 8, 2048), PLANE_ZY)
    for axis in ("x", "z"):
        for second in (True, False):
            move_down, keep_down = halves(keep_down, down_got)
            down_got = swap_axis(move_down, axis, second)
    for axis in ("x", "y"):
        for second in (False, True):
            vector = vector + swap_axis(vector, axis, second, True)
    dup = lax.psum_scatter(dup, "z", scatter_dimension=0, tiled=True)[0]
    up_grad = dup.astype(F32)
    down_grad = add(keep_down, down_got, F32)[0]
    row = jnp.stack([jnp.sum(r.astype(F32), axis=0) for r in (row_a, row_b)], axis=1)
    qkv_grad = row[:, :, :PART].reshape(8, 2, 3, HALF).transpose(0, 2, 1, 3).reshape(8, 3 * WIDTH)
    out_grad = row[:, :, PART:].reshape(8, WIDTH)
    summed = vector.reshape(-1)
    vectors = [summed[i * WIDTH : (i + 1) * WIDTH] for i in range(8)]
    return (
        output,
        grad_tokens,
        qkv_grad,
        out_grad,
        up_grad,
        down_grad,
        *vectors[:7],
        summed[8 * WIDTH :],
        vectors[7],
    )


def solution(mesh):
    fine = Mesh(mesh.devices.reshape(4, 2, 2, 4, 2), AXES)
    every, hidden, model = AXES, ("z", "yh", "c"), ("x", "yl")
    weights = (P(every, None), P(every, None), P(model, hidden), P(hidden, model))
    return jax.shard_map(
        on_device,
        mesh=fine,
        in_specs=(P(every, None), *weights, *[P()] * 9, P(every), P(every, None)),
        out_specs=(P(every, None), P(every, None), *weights, *[P()] * 9),
        check_vma=False,
    )
```

```python
import functools
import itertools

import jax
import jax.numpy as jnp
from jax import lax
from jax.experimental import pallas as pl
from jax.experimental.pallas import tpu as pltpu
from jax.sharding import Mesh, PartitionSpec as P

F32, BF16 = jnp.float32, jnp.bfloat16
TOK, WIDTH, FF = 512, 1024, 4096
BOTH = 2 * TOK
CHUNK = 1024
UNIT = 256
ROOT = 0.7978845608028654
CUBE = 0.044715
VMEM, ANY, HBM, SMEM = (
    pl.BlockSpec(memory_space=kind) for kind in (pltpu.VMEM, pl.ANY, pltpu.HBM, pltpu.SMEM)
)
ROOM = 60 * 2**20
ONE = pltpu.SemaphoreType.DMA
TWO = pltpu.SemaphoreType.DMA((2,))
FEW = pltpu.SemaphoreType.DMA((8,))


def shape(*dims, dtype=BF16):
    return jax.ShapeDtypeStruct(dims, dtype)


def work(flops):
    return pl.CostEstimate(flops=int(flops), bytes_accessed=1 << 20, transcendentals=0)


def dot(a, b):
    return lax.dot_general(a, b, (((1,), (0,)), ((), ())), preferred_element_type=F32)


def dot_t(a, b):
    return lax.dot_general(a, b, (((1,), (1,)), ((), ())), preferred_element_type=F32)


def normed(values):
    center = values - jnp.mean(values, axis=-1, keepdims=True)
    scale = lax.rsqrt(jnp.mean(center * center, axis=-1, keepdims=True) + 1e-05)
    return center * scale, scale


def norm_back(edge, unit, scale):
    return (edge - jnp.mean(edge, axis=-1, keepdims=True) - unit * jnp.mean(edge * unit, axis=-1, keepdims=True)) * scale


def start(source, target, sem):
    pltpu.make_async_copy(source, target, sem).start()


def wait(ref, sem):
    pltpu.make_async_copy(ref, ref, sem).wait()


def place_of(places, side, axis, slot):
    return places[side * 12 + "xyz".index(axis) * 4 + slot]


def ffn_kernel(places, bias_ref, low_own, low_other, grad_own, grad_other, up, down_low, down_high,
               bias_grad_ref, feed_ref, feed_low_ref, gc_ref, gc_low_ref, dup, ddown_keep, ddown_move,
               up_buf, down_buf, dup_buf, ddown_buf, low, grad, low_t, act_buf, gpre_buf, total, grad_total,
               feed_low, gc_low, in_sem, up_sem, down_sem, out_sem):
    core = places[24]

    def tiles(chunk):
        for part in (0, 1):
            for sy in range(4):
                y = place_of(places, 0, "y", sy)
                yh, yl = lax.div(y, 2), lax.rem(y, 2)
                unit = pl.ds(pl.multiple_of((part * 2 + yh) * UNIT, UNIT), UNIT)
                for x in range(4):
                    yield sy, chunk * 2 + part, x, yl, unit

    def model(x, yl):
        return pl.ds(pl.multiple_of((x * 2 + yl) * 128, 128), 128)

    def fetch(chunk):
        for sy, sz, x, yl, unit in tiles(chunk):
            start(up.at[x * 16 + sy * 4 + sz], up_buf.at[chunk, model(x, yl), unit], up_sem.at[chunk])
        for sy, sz, sx, yl, unit in tiles(chunk):
            cols = model(place_of(places, 0, "x", sx), yl)
            start((down_low, down_high)[sy // 2].at[sy % 2 * 16 + sx * 4 + sz], down_buf.at[chunk, unit, cols], down_sem.at[chunk])

    def send_down(chunk):
        for sy, sz, sx, yl, unit in tiles(chunk):
            source = ddown_buf.at[chunk, unit, model(place_of(places, 0, "x", sx), yl)]
            start(source, (ddown_keep, ddown_move)[sy // 2].at[sy % 2 * 16 + sz * 4 + sx], out_sem)

    def send_up(chunk):
        for part in (0, 1):
            z = place_of(places, 0, "z", chunk * 2 + part)
            for y in range(4):
                for x in range(4):
                    unit = slice((part * 2 + y // 2) * UNIT, (part * 2 + y // 2 + 1) * UNIT)
                    start(dup_buf.at[chunk, model(x, y % 2), unit], dup.at[x, z, y], out_sem)

    start(low_own, low.at[pl.ds(0, TOK)], in_sem.at[0])
    start(low_other, low.at[pl.ds(TOK, TOK)], in_sem.at[0])
    fetch(0)
    start(grad_own, grad.at[pl.ds(0, TOK)], in_sem.at[1])
    start(grad_other, grad.at[pl.ds(TOK, TOK)], in_sem.at[1])
    fetch(1)
    bias_grad_ref[...] = jnp.zeros_like(bias_grad_ref)
    wait(low, in_sem.at[0])
    low_t[...] = low[...].T
    wait(grad, in_sem.at[1])

    for chunk in (0, 1):
        wait(up_buf.at[chunk], up_sem.at[chunk])
        wait(down_buf.at[chunk], down_sem.at[chunk])
        for n in range(CHUNK // UNIT):
            cols = slice(n * UNIT, (n + 1) * UNIT)
            block = (place_of(places, 0, "z", chunk * 2 + n // 2) * 2 + n % 2) * 2 + core
            pre = dot(low[...], up_buf[chunk, :, cols]) + bias_ref[block]
            gact = dot_t(grad[...], down_buf[chunk, cols, :])
            square = pre * pre
            bend = jnp.tanh(ROOT * (pre + CUBE * square * pre))
            half = 0.5 + 0.5 * bend
            act = (pre * half).astype(BF16)
            slope = half + 0.5 * pre * (1.0 - bend * bend) * (ROOT + 3.0 * ROOT * CUBE * square)
            gpre = (gact * slope).astype(BF16)
            act_buf[:, cols] = act
            gpre_buf[:, cols] = gpre
            bias_grad_ref[block] = jnp.sum(gpre.astype(F32), axis=0, keepdims=True)
            ddown_buf[chunk, cols, :] = dot(act.T, grad[...]).astype(BF16)
            dup_buf[chunk, :, cols] = dot(low_t[...], gpre).astype(BF16)
        send_up(chunk)
        send_down(chunk)
        more = dot_t(gpre_buf[...], up_buf[chunk])
        feed = dot(act_buf[...], down_buf[chunk])
        if chunk == 0:
            grad_total[...] = more
            total[...] = feed
        else:
            grad_total[...] += more
            gc_low[...] = grad_total[TOK:, :].astype(BF16)
            start(gc_low, gc_low_ref, out_sem)
            start(grad_total.at[pl.ds(0, TOK)], gc_ref, out_sem)
            total[...] += feed
            feed_low[...] = total[TOK:, :].astype(BF16)
            start(feed_low, feed_low_ref, out_sem)
            start(total.at[pl.ds(0, TOK)], feed_ref, out_sem)
    for ref in (dup_buf, ddown_buf, gc_low, feed_low, grad_total.at[pl.ds(0, TOK)], total.at[pl.ds(0, TOK)]):
        wait(ref, out_sem)


def ffn(places, up_bias, low_own, low_other, grad_own, grad_other, weights):
    big = pltpu.VMEM((2, CHUNK, CHUNK), BF16)
    rows = pltpu.VMEM((BOTH, WIDTH), BF16)
    sums = pltpu.VMEM((BOTH, WIDTH), F32)
    half = pltpu.VMEM((TOK, WIDTH), BF16)
    return pl.pallas_call(
        ffn_kernel,
        in_specs=[SMEM, VMEM] + [HBM] * 7,
        out_specs=[VMEM] + [HBM] * 7,
        out_shape=[
            shape(16, 1, UNIT, dtype=F32),
            shape(TOK, WIDTH, dtype=F32),
            shape(TOK, WIDTH),
            shape(TOK, WIDTH, dtype=F32),
            shape(TOK, WIDTH),
            shape(4, 4, 4, 128, 256),
            shape(32, 256, 128),
            shape(32, 256, 128),
        ],
        scratch_shapes=[
            big, big, big, big, rows, rows, rows,
            pltpu.VMEM((BOTH, CHUNK), BF16),
            pltpu.VMEM((BOTH, CHUNK), BF16),
            sums, sums, half, half, TWO, TWO, TWO, ONE,
        ],
        compiler_params=pltpu.CompilerParams(vmem_limit_bytes=ROOM),
        cost_estimate=work(40e9),
        name="ffn",
    )(places, up_bias.reshape(16, 1, UNIT), low_own, low_other, grad_own, grad_other, *weights)


BLOCK = 128
HALF = 512
PART = 3 * HALF


def row_tiles(places, axis):
    core = places[24]
    for side in (0, 1):
        for slot in range(4):
            yield side, slot, place_of(places, side, axis, slot), core if side == 0 else 1 - core


def fetch_part(places, part, pieces, buf, sem, cols):
    cols = slice(part * 2048 + cols.start, part * 2048 + cols.stop)
    for side, slot, z, c in row_tiles(places, "z"):
        start(pieces[2 * side + slot // 2].at[slot % 2, :, :, cols], buf.at[z, :, c], sem)


def matrix(ref):
    return ref.reshape(WIDTH, ref.shape[-1])


def parts_buffer(cols):
    return pltpu.VMEM((4, 2, 2, 64, cols), BF16)


def lane_marks():
    low = lax.broadcasted_iota(jnp.int32, (1, 128), 1) < 64
    return low, jnp.where(low, 1.0, 0.0).astype(BF16), jnp.where(low, 0.0, 1.0).astype(BF16)


def project_kernel(places, ln1_ref, qkv_bias_ref, tok, *refs):
    pieces, (low_out, qkv_out, buf0, buf1, tok_ref, low_ref, qkv_ref, sem, out_sem) = refs[:4], refs[4:]
    start(tok, tok_ref, sem.at[2])
    for part, buf in ((0, buf0), (1, buf1)):
        fetch_part(places, part, pieces, buf, sem.at[part], slice(0, PART))
    wait(tok_ref, sem.at[2])

    @pl.loop(0, TOK // 128)
    def _(i):
        rows = pl.ds(i * 128, 128)
        unit, _ = normed(tok_ref[rows, :].astype(F32))
        low_ref[rows, :] = (unit * ln1_ref[0:1, :] + ln1_ref[1:2, :]).astype(BF16)

    start(low_ref, low_out, out_sem)
    for part, buf in ((0, buf0), (1, buf1)):
        wait(buf, sem.at[part])
        for n in range(3):
            cols = slice(n * HALF, (n + 1) * HALF)
            qkv_ref[part, :, cols] = (dot(low_ref[...], matrix(buf)[:, cols]) + qkv_bias_ref[part, :, cols]).astype(BF16)
        start(qkv_ref.at[part], qkv_out.at[part], out_sem)
    wait(low_ref, out_sem)
    wait(qkv_ref, out_sem)


def project(places, tokens, ln1, qkv_bias, pieces):
    wide, heads = pltpu.VMEM((TOK, WIDTH), BF16), pltpu.VMEM((2, TOK, PART), BF16)
    return pl.pallas_call(
        project_kernel,
        in_specs=[SMEM] + [VMEM] * 2 + [HBM] * 5,
        out_specs=[HBM] * 2,
        out_shape=[shape(TOK, WIDTH), shape(2, TOK, PART)],
        scratch_shapes=[parts_buffer(PART), parts_buffer(PART), wide, wide, heads, FEW, ONE],
        compiler_params=pltpu.CompilerParams(vmem_limit_bytes=ROOM),
        cost_estimate=work(8e9),
        name="project",
    )(places, ln1, qkv_bias, tokens, *pieces)


def attend_kernel(places, pair_ref, out_bias_ref, ln2_ref, tok, qkv, *refs):
    pieces, refs = refs[:4], refs[4:]
    prob_out, mixed_out, hidden_out, normed_out, buf0, buf1, tok_ref, qkv_ref = refs[:8]
    prob_ref, mixed_ref, hidden_ref, normed_ref, sem, out_sem = refs[8:]
    start(qkv, qkv_ref, sem.at[2])
    start(tok, tok_ref, sem.at[3])
    for part, buf in ((0, buf0), (1, buf1)):
        fetch_part(places, part, pieces, buf, sem.at[part], slice(PART, 2048))
    low, near, far = lane_marks()
    near, far = near * 0.125, far * 0.125
    wait(qkv_ref, sem.at[2])

    @pl.loop(0, 8)
    def _(pair):
        part = lax.div(pair, 4)
        begin = pl.multiple_of(lax.rem(pair, 4) * 128, 128)
        lanes = pl.ds(pl.multiple_of(pair * 128, 128), 128)
        for block in range(TOK // BLOCK):
            rows = slice(block * BLOCK, (block + 1) * BLOCK)
            query = qkv_ref[part, rows, pl.ds(begin, 128)]
            key = qkv_ref[part, rows, pl.ds(begin + HALF, 128)]
            value = qkv_ref[part, rows, pl.ds(begin + 2 * HALF, 128)]
            bias = pair_ref[block]
            score = dot_t(jnp.concatenate([query * near, query * far], axis=0), key) + jnp.concatenate([bias, bias], axis=0)
            power = jnp.exp(score - jnp.max(score, axis=-1, keepdims=True))
            prob = (power * (1.0 / jnp.sum(power, axis=-1, keepdims=True))).astype(BF16)
            prob_ref[pair, block] = prob
            both = dot(prob, value)
            mixed_ref[rows, lanes] = jnp.where(low, both[:BLOCK], both[BLOCK:]).astype(BF16)

    start(prob_ref, prob_out, out_sem)
    start(mixed_ref, mixed_out, out_sem)
    wait(tok_ref, sem.at[3])
    for part, buf in ((0, buf0), (1, buf1)):
        cols = slice(part * HALF, (part + 1) * HALF)
        wait(buf, sem.at[part])
        hidden_ref[:, cols] = tok_ref[:, cols].astype(F32) + dot(mixed_ref[...], matrix(buf)[...]) + out_bias_ref[:, cols]
    start(hidden_ref, hidden_out, out_sem)

    @pl.loop(0, TOK // 128)
    def _(i):
        rows = pl.ds(i * 128, 128)
        unit, _ = normed(hidden_ref[rows, :])
        normed_ref[rows, :] = (unit * ln2_ref[0:1, :] + ln2_ref[1:2, :]).astype(BF16)

    start(normed_ref, normed_out, out_sem)
    for ref in (prob_ref, mixed_ref, hidden_ref, normed_ref):
        wait(ref, out_sem)


def attend(places, tokens, pair_bias, qkv, out_bias, ln2, pieces):
    outs = [((8, 4, 2 * BLOCK, BLOCK), BF16), ((TOK, WIDTH), BF16), ((TOK, WIDTH), F32), ((TOK, WIDTH), BF16)]
    return pl.pallas_call(
        attend_kernel,
        in_specs=[SMEM] + [VMEM] * 3 + [HBM] * 6,
        out_specs=[HBM] * 4,
        out_shape=[jax.ShapeDtypeStruct(*out) for out in outs],
        scratch_shapes=[parts_buffer(HALF), parts_buffer(HALF), pltpu.VMEM((TOK, WIDTH), BF16), pltpu.VMEM((2, TOK, PART), BF16)]
        + [pltpu.VMEM(*out) for out in outs]
        + [FEW, ONE],
        compiler_params=pltpu.CompilerParams(vmem_limit_bytes=ROOM),
        cost_estimate=work(16e9),
        name="attend",
    )(places, pair_bias, out_bias.reshape(1, WIDTH), ln2, tokens, qkv, *pieces)


def turn(hidden_ref, gain_ref, gc_ref, got_ref, grad_ref, ghid_ref, glow_ref, vec_ref):
    vec_ref[...] = jnp.zeros_like(vec_ref)

    @pl.loop(0, TOK // 128)
    def _(part):
        rows = pl.ds(part * 128, 128)
        unit, scale = normed(hidden_ref[rows, :])
        gc = gc_ref[rows, :] + got_ref[rows, :].astype(F32)
        gout = grad_ref[rows, :].astype(F32)
        ghid = gout + norm_back(gc * gain_ref[...], unit, scale)
        ghid_ref[rows, :] = ghid
        glow_ref[rows, :] = ghid.astype(BF16)
        vec_ref[0:1, :] += jnp.sum(ghid, axis=0, keepdims=True)
        vec_ref[1:2, :] += jnp.sum(gc * unit, axis=0, keepdims=True)
        vec_ref[2:3, :] += jnp.sum(gc, axis=0, keepdims=True)
        vec_ref[3:4, :] += jnp.sum(gout, axis=0, keepdims=True)


TURN_SHAPES = [((TOK, WIDTH), F32), ((TOK, WIDTH), F32), ((TOK, WIDTH), BF16), ((TOK, WIDTH), BF16)]


def back_kernel(part, places, low_in, qkv_in, prob_in, mixed_in, *refs):
    pieces, refs = refs[:4], refs[4:]
    if part == 0:
        gain_ref, turn_in, refs = refs[0], refs[1:5], refs[5:]
        sum_ref, vec_ref, gqkv_out, *outs = refs[:7]
        ghid_out, glow_out = refs[7:9]
        turn_refs, refs = refs[9:13], refs[13:]
        ghid_ref, refs = refs[0], refs[1:]
    else:
        glow_in, refs = refs[0], refs[1:]
        sum_ref, gqkv_out, *outs = refs[:6]
        refs = refs[6:]
    low_ref, qkv_ref, prob_ref, mixed_ref, glow_ref, buf, side_buf, grad_buf, gmix_ref, gqkv_ref, flip, sem, out_sem = refs
    tail = slice(PART, 2048)
    if part == 0:
        for source, target in zip(turn_in, turn_refs):
            start(source, target, sem.at[0])
    else:
        start(glow_in, glow_ref, sem.at[0])
    start(mixed_in, mixed_ref, sem.at[1])
    fetch_part(places, part, pieces, buf, sem.at[2], tail)
    fetch_part(places, 1 - part, pieces, side_buf, sem.at[3], tail)
    start(qkv_in.at[part], qkv_ref, sem.at[4])
    start(prob_in.at[pl.ds(part * 4, 4)], prob_ref, sem.at[4])
    start(low_in, low_ref, sem.at[5])
    wait(mixed_ref, sem.at[1])
    flip[...] = mixed_ref[...].T
    if part == 0:
        for ref in turn_refs:
            wait(ref, sem.at[0])
        turn(turn_refs[0], gain_ref, turn_refs[1], turn_refs[2], turn_refs[3], ghid_ref, glow_ref, vec_ref)
        start(ghid_ref, ghid_out, out_sem)
        start(glow_ref, glow_out, out_sem)
    else:
        wait(glow_ref, sem.at[0])
    heads = slice(part * HALF, (part + 1) * HALF)
    rest = slice((1 - part) * HALF, (2 - part) * HALF)
    grad_matrix = matrix(grad_buf)
    grad_matrix[:, PART:] = dot(flip[...], glow_ref[:, heads]).astype(BF16)
    wait(buf, sem.at[2])
    wait(side_buf, sem.at[3])
    gmix_ref[...] = (
        dot_t(glow_ref[:, heads], matrix(buf)[heads, :]) + dot_t(glow_ref[:, rest], matrix(side_buf)[heads, :])
    ).astype(BF16)
    wait(low_ref, sem.at[5])
    flip[...] = low_ref[...].T
    wait(qkv_ref, sem.at[4])
    wait(prob_ref, sem.at[4])
    low, near, far = lane_marks()

    @pl.loop(0, 4)
    def _(pair):
        begin = pl.multiple_of(pair * 128, 128)
        for block in range(TOK // BLOCK):
            rows = slice(block * BLOCK, (block + 1) * BLOCK)
            query = qkv_ref[rows, pl.ds(begin, 128)]
            key = qkv_ref[rows, pl.ds(begin + HALF, 128)]
            value = qkv_ref[rows, pl.ds(begin + 2 * HALF, 128)]
            gmix = gmix_ref[rows, pl.ds(begin, 128)]
            gmix = jnp.concatenate([gmix * near, gmix * far], axis=0)
            query = jnp.concatenate([query * (near * 0.125), query * (far * 0.125)], axis=0)
            prob_low = prob_ref[pair, block]
            prob = prob_low.astype(F32)
            gprob = dot_t(gmix, value)
            gscore = (prob * (gprob - jnp.sum(prob * gprob, axis=-1, keepdims=True))).astype(BF16)
            both = dot(gscore, key) * 0.125
            gqkv_ref[rows, pl.ds(begin, 128)] = jnp.where(low, both[:BLOCK], both[BLOCK:]).astype(BF16)
            gqkv_ref[rows, pl.ds(begin + HALF, 128)] = dot(gscore.T, query).astype(BF16)
            gqkv_ref[rows, pl.ds(begin + 2 * HALF, 128)] = dot(prob_low.T, gmix).astype(BF16)

    start(gqkv_ref, gqkv_out, out_sem)
    for n in range(3):
        cols = slice(n * HALF, (n + 1) * HALF)
        grad_matrix[:, cols] = dot(flip[...], gqkv_ref[:, cols]).astype(BF16)
    for side, slot, at, c in row_tiles(places, "zx"[part]):
        source = grad_buf.at[at, :, c] if part == 0 else grad_buf.at[:, :, c, pl.ds(pl.multiple_of(at * 16, 16), 16)]
        start(source, outs[2 * side + slot // 2].at[slot % 2], out_sem)
    sum_ref[...] = jnp.sum(gqkv_ref[...].astype(F32), axis=0, keepdims=True)
    wait(grad_buf, out_sem)
    wait(gqkv_ref, out_sem)
    if part == 0:
        wait(ghid_ref, out_sem)
        wait(glow_ref, out_sem)


def back(part, places, low, qkv, prob, mixed, pieces, *more):
    first = part == 0
    tile = shape(2, 2, 64, 2048) if first else shape(2, 4, 2, 16, 2048)
    wide = pltpu.VMEM((TOK, WIDTH), BF16)
    return pl.pallas_call(
        functools.partial(back_kernel, part),
        in_specs=[SMEM] + [HBM] * 8 + ([VMEM] + [HBM] * 4 if first else [HBM]),
        out_specs=[VMEM] * (2 if first else 1) + [HBM] * (7 if first else 5),
        out_shape=[shape(1, PART, dtype=F32)]
        + ([shape(8, WIDTH, dtype=F32)] if first else [])
        + [shape(TOK, PART), tile, tile, tile, tile]
        + ([shape(TOK, WIDTH, dtype=F32), shape(TOK, WIDTH)] if first else []),
        scratch_shapes=([pltpu.VMEM(*s) for s in TURN_SHAPES] + [pltpu.VMEM((TOK, WIDTH), F32)] if first else [])
        + [
            wide,
            pltpu.VMEM((TOK, PART), BF16),
            pltpu.VMEM((4, 4, 2 * BLOCK, BLOCK), BF16),
            wide,
            wide,
            parts_buffer(HALF),
            parts_buffer(HALF),
            parts_buffer(2048),
            pltpu.VMEM((TOK, HALF), BF16),
            pltpu.VMEM((TOK, PART), BF16),
            pltpu.VMEM((WIDTH, TOK), BF16),
            FEW,
            ONE,
        ],
        compiler_params=pltpu.CompilerParams(vmem_limit_bytes=ROOM),
        cost_estimate=work(20e9),
        name="back" + str(part),
    )(places, low, qkv, prob, mixed, *pieces, *more)


def end_kernel(places, ln1_ref, down_bias_ref, gqkv0, gqkv1, ghid, tok, hidden, feed, feed_got, *refs):
    pieces, refs = refs[:4], refs[4:]
    gin_out, out_out, vec_ref, buf0, buf1, gqkv0_ref, gqkv1_ref, ghid_ref, tok_ref, hidden_ref, feed_ref, got_ref, out_ref, total, sem, out_sem = refs
    start(gqkv0, gqkv0_ref, sem.at[0])
    fetch_part(places, 0, pieces, buf0, sem.at[0], slice(0, PART))
    start(gqkv1, gqkv1_ref, sem.at[1])
    fetch_part(places, 1, pieces, buf1, sem.at[1], slice(0, PART))
    start(ghid, ghid_ref, sem.at[2])
    start(tok, tok_ref, sem.at[2])
    for source, target in ((hidden, hidden_ref), (feed, feed_ref), (feed_got, got_ref)):
        start(source, target, sem.at[3])
    vec_ref[...] = jnp.zeros_like(vec_ref)
    wait(gqkv0_ref, sem.at[0])
    wait(buf0, sem.at[0])
    total[...] = dot_t(gqkv0_ref[...], matrix(buf0)[...])
    wait(gqkv1_ref, sem.at[1])
    wait(buf1, sem.at[1])
    total[...] += dot_t(gqkv1_ref[...], matrix(buf1)[...])
    wait(ghid_ref, sem.at[2])
    wait(tok_ref, sem.at[2])

    @pl.loop(0, TOK // 128)
    def _(i):
        rows = pl.ds(i * 128, 128)
        unit, scale = normed(tok_ref[rows, :].astype(F32))
        grad = total[rows, :]
        ghid_ref[rows, :] += norm_back(grad * ln1_ref[0:1, :], unit, scale)
        vec_ref[0:1, :] += jnp.sum(grad * unit, axis=0, keepdims=True)
        vec_ref[1:2, :] += jnp.sum(grad, axis=0, keepdims=True)

    start(ghid_ref, gin_out, out_sem)
    for ref in (hidden_ref, feed_ref, got_ref):
        wait(ref, sem.at[3])
    out_ref[...] = (hidden_ref[...] + feed_ref[...] + got_ref[...].astype(F32) + down_bias_ref[...]).astype(BF16)
    start(out_ref, out_out, out_sem)
    wait(ghid_ref, out_sem)
    wait(out_ref, out_sem)


def end(places, ln1, down_bias, gqkv0, gqkv1, ghid, tokens, hidden, feed, feed_got, pieces):
    low, high = pltpu.VMEM((TOK, WIDTH), BF16), pltpu.VMEM((TOK, WIDTH), F32)
    heads = pltpu.VMEM((TOK, PART), BF16)
    return pl.pallas_call(
        end_kernel,
        in_specs=[SMEM] + [VMEM] * 2 + [HBM] * 7 + [HBM] * 4,
        out_specs=[HBM] * 2 + [VMEM],
        out_shape=[shape(TOK, WIDTH, dtype=F32), shape(TOK, WIDTH), shape(8, WIDTH, dtype=F32)],
        scratch_shapes=[parts_buffer(PART), parts_buffer(PART), heads, heads, high, low, high, high, low, low, high, FEW, ONE],
        compiler_params=pltpu.CompilerParams(vmem_limit_bytes=ROOM),
        cost_estimate=work(10e9),
        name="end",
    )(places, ln1, down_bias.reshape(1, WIDTH), gqkv0, gqkv1, ghid, tokens, hidden, feed, feed_got, *pieces)


AXES = ("z", "yh", "c", "x", "yl")
PLANE_XY, PLANE_ZY = ("yh", "x", "yl"), ("z", "yh", "yl")


def device_number(place):
    return (
        ((place["z"] * 2 + place["y"] // 2) * 2 + place["c"]) * 4 + place["x"]
    ) * 2 + place["y"] % 2


def exchange_pairs(axis, second, alike=False):
    pairs = []
    for z, y, c, x in itertools.product(range(4), range(4), range(2), range(4)):
        here = {"z": z, "y": y, "c": c, "x": x}
        mask = 1 if (c == 0 or alike) != second else 3
        there = dict(here)
        there[axis] = here[axis] ^ mask
        pairs.append((device_number(here), device_number(there)))
    return pairs


def swap_axis(values, axis, second, alike=False):
    return lax.ppermute(values, AXES, exchange_pairs(axis, second, alike))


def swap_core(values):
    return lax.ppermute(values, "c", [(0, 1), (1, 0)])


def position(axis):
    if axis == "y":
        return lax.axis_index("yh") * 2 + lax.axis_index("yl")
    return lax.axis_index(axis)


def distance_of(core, slot):
    return jnp.where(core == 0, slot ^ (slot >> 1), ((slot << 1) & 3) ^ ((slot ^ (slot >> 1)) & 1))


def place_table():
    core, slots = lax.axis_index("c"), jnp.arange(4, dtype=jnp.int32)
    rows = [
        distance_of(side, slots) ^ position(axis)
        for side in (core, 1 - core)
        for axis in ("x", "y", "z")
    ]
    return jnp.concatenate(rows + [jnp.full((8,), core, jnp.int32)])


def add(left, right, dtype=BF16):
    return (left.astype(F32) + right.astype(F32)).astype(dtype)


def halves(own, got):
    count = own.shape[0] // 2
    return add(own[count:], got[count:]), add(own[:count], got[:count])


def spread(values, axes):
    return lax.all_to_all(jnp.broadcast_to(values, (16,) + values.shape), axes, 0, 0)


def spread_back(values, axes):
    return lax.all_to_all(values, axes, 0, 0)


def together(*values):
    return lax.optimization_barrier(values)


def pair_bias(clip_ids):
    clips = clip_ids.reshape(-1, BLOCK)
    row = lax.broadcasted_iota(jnp.int32, (BLOCK, BLOCK), 0)
    col = lax.broadcasted_iota(jnp.int32, (BLOCK, BLOCK), 1)
    allowed = (clips[:, :, None] == clips[:, None, :]) & (row >= col)[None]
    return jnp.where(allowed, 0.0, -1e30).astype(F32)


def on_device(
    tokens,
    qkv_weight,
    out_weight,
    up_weight,
    down_weight,
    ln1_gain,
    ln1_bias,
    q_bias,
    v_bias,
    out_bias,
    ln2_gain,
    ln2_bias,
    up_bias,
    down_bias,
    segment_ids,
    cotangent,
):
    places = place_table()
    heads = qkv_weight.reshape(8, 3, WIDTH)
    pieces = []
    for cols in (slice(0, HALF), slice(HALF, WIDTH)):
        pieces += [heads[:, :, cols].reshape(8, PART), out_weight[:, cols]]
    def join(pairs):
        return together(*[jnp.concatenate(pair) for pair in pairs])

    rows = spread(jnp.concatenate(pieces, axis=1), PLANE_XY)
    down, up = down_weight[None], up_weight[None]
    down, up = join(((down, swap_axis(down, "z", False)), (up, swap_axis(up, "z", False))))
    rows, down_got, up_got = together(rows, swap_axis(down, "z", True), swap_axis(up, "z", True))
    rows = rows.reshape(1, 2, 64, 4096)
    rows_got = swap_axis(rows, "z", False)
    down, up = join(((down, down_got), (up, up_got)))
    down, up = join(((down, swap_axis(down, "x", False)), (up, swap_axis(up, "y", False))))
    rows_got, down_got, up_got, grad_other = together(
        rows_got, swap_axis(down, "x", True), swap_axis(up, "y", True), swap_core(cotangent)
    )
    rows, down, up = join(((rows, rows_got), (down, down_got), (up, up_got)))
    up = lax.all_gather(up, "x", axis=0).reshape(64, 128, 256)
    rows_got, down_got, other_rows = together(
        swap_axis(rows, "z", True), swap_axis(down, "y", False), swap_core(rows)
    )
    pieces = (rows, rows_got, other_rows, swap_core(rows_got))
    (down,) = join(((down, down_got),))
    down_got = swap_axis(down, "y", True)

    ln1 = jnp.stack([ln1_gain, ln1_bias])
    nothing = jnp.zeros((HALF,), F32)
    qkv_bias = jnp.stack(
        [
            jnp.concatenate([q_bias[cols], nothing, v_bias[cols]])[None]
            for cols in (slice(0, HALF), slice(HALF, WIDTH))
        ]
    )
    low, qkv = project(places, tokens, ln1, qkv_bias, pieces)
    prob, mixed, hidden, low2 = attend(
        places, tokens, pair_bias(segment_ids), qkv, out_bias, jnp.stack([ln2_gain, ln2_bias]), pieces
    )
    up_bias_grad, feed, feed_low, gc, gc_low, dup, keep_down, move_down = ffn(
        places, up_bias, low2, swap_core(low2), cotangent, grad_other, (up, down, down_got)
    )
    dup = lax.psum_scatter(dup, "x", scatter_dimension=0, tiled=True).reshape(16, 128, 256)

    down_got = swap_axis(move_down, "y", True)
    sum0, vec2, gqkv0, *main_a, ghid, glow = back(
        0, places, low, qkv, prob, mixed, pieces,
        ln2_gain.reshape(1, WIDTH), hidden, gc, swap_core(gc_low), cotangent,
    )
    glow, *main_a = together(glow, *main_a)
    move_a = add(main_a[1], swap_core(main_a[3]))
    move_a, glow = together(move_a, glow)
    got_a, got_keep_a = swap_axis(move_a, "z", True), swap_core(main_a[2])
    sum1, gqkv1, *main_b = back(1, places, low, qkv, prob, mixed, pieces, glow)
    got_a, got_keep_a, down_got, dup, gqkv1, *main_b = together(
        got_a, got_keep_a, down_got, dup, gqkv1, *main_b
    )

    swapped_b, got_keep_b = swap_core(main_b[3]), swap_core(main_b[2])
    up_pieces = spread_back(dup, PLANE_ZY)
    move_a, keep_a = halves(add(main_a[0], got_keep_a), got_a)
    got_a = swap_axis(move_a, "z", False)
    move_b = add(main_b[1], swapped_b)
    move_b, gqkv1 = together(move_b, gqkv1)
    got_b = swap_axis(move_b, "x", True)
    move_down, keep_down = halves(keep_down, down_got)
    down_got = swap_axis(move_down, "y", False)
    grad_tokens, output, vec1 = end(
        places, ln1, down_bias, gqkv0, gqkv1, ghid, tokens, hidden, feed, swap_core(feed_low), pieces
    )
    sums = jnp.concatenate([sum0.reshape(3, HALF), sum1.reshape(3, HALF)], axis=1)
    blocks = [vec1[0:2], sums[0:1], sums[2:3], vec2[0:4]]
    vector = jnp.concatenate(
        [block.reshape(-1, 128) for block in blocks] + [up_bias_grad.reshape(-1, 128)]
    )
    vector_got = swap_core(vector)
    got_b, got_a, down_got, got_keep_b, up_pieces, vector_got = together(
        got_b, got_a, down_got, got_keep_b, up_pieces, vector_got
    )
    move_b, keep_b = halves(add(main_b[0], got_keep_b), got_b)
    got_b = swap_axis(move_b, "x", False)
    row_a = spread_back(add(keep_a, got_a).reshape(16, 8, 2048), PLANE_XY)
    move_down, keep_down = halves(keep_down, down_got)
    down_got = swap_axis(move_down, "z", True)
    vector = vector + vector_got
    for axis, second in (("z", False), ("z", True), ("x", False)):
        vector = vector + swap_axis(vector, axis, second, True)
    vector_got = swap_axis(vector, "x", True, True)
    got_b, row_a, down_got, vector_got = together(got_b, row_a, down_got, vector_got)

    row_b = spread_back(add(keep_b, got_b).reshape(16, 8, 2048), PLANE_ZY)
    vector = vector + vector_got
    for axis, second in (("z", False), ("x", True), ("x", False)):
        move_down, keep_down = halves(keep_down, down_got)
        down_got = swap_axis(move_down, axis, second)
    for second in (False, True):
        vector = vector + swap_axis(vector, "y", second, True)
    up_grad = jnp.sum(up_pieces.astype(F32), axis=0)
    down_grad = add(keep_down, down_got, F32)[0]
    row = jnp.stack([jnp.sum(r.astype(F32), axis=0) for r in (row_a, row_b)], axis=1)
    qkv_grad = row[:, :, :PART].reshape(8, 2, 3, HALF).transpose(0, 2, 1, 3).reshape(8, 3 * WIDTH)
    out_grad = row[:, :, PART:].reshape(8, WIDTH)
    summed = vector.reshape(-1)
    vectors = [summed[i * WIDTH : (i + 1) * WIDTH] for i in range(8)]
    return (
        output,
        grad_tokens,
        qkv_grad,
        out_grad,
        up_grad,
        down_grad,
        *vectors[:7],
        summed[8 * WIDTH :],
        vectors[7],
    )


def solution(mesh):
    fine = Mesh(mesh.devices.reshape(4, 2, 2, 4, 2), AXES)
    every, hidden, model = AXES, ("z", "yh", "c"), ("x", "yl")
    weights = (P(every, None), P(every, None), P(model, hidden), P(hidden, model))
    return jax.shard_map(
        on_device,
        mesh=fine,
        in_specs=(P(every, None), *weights, *[P()] * 9, P(every), P(every, None)),
        out_specs=(P(every, None), P(every, None), *weights, *[P()] * 9),
        check_vma=False,
    )
```

```python
import functools
import itertools

import jax
import jax.numpy as jnp
from jax import lax
from jax.experimental import pallas as pl
from jax.experimental.pallas import tpu as pltpu
from jax.sharding import Mesh, PartitionSpec as P

F32, BF16 = jnp.float32, jnp.bfloat16
TOK, WIDTH, FF = 512, 1024, 4096
BOTH = 2 * TOK
CHUNK = 1024
UNIT = 256
ROOT = 0.7978845608028654
CUBE = 0.044715
VMEM, ANY, HBM, SMEM = (
    pl.BlockSpec(memory_space=kind) for kind in (pltpu.VMEM, pl.ANY, pltpu.HBM, pltpu.SMEM)
)
ROOM = 60 * 2**20
ONE = pltpu.SemaphoreType.DMA
TWO = pltpu.SemaphoreType.DMA((2,))
FEW = pltpu.SemaphoreType.DMA((8,))


def shape(*dims, dtype=BF16):
    return jax.ShapeDtypeStruct(dims, dtype)


def work(flops):
    return pl.CostEstimate(flops=int(flops * 0.4), bytes_accessed=1 << 20, transcendentals=0)


def dot(a, b):
    return lax.dot_general(a, b, (((1,), (0,)), ((), ())), preferred_element_type=F32)


def dot_t(a, b):
    return lax.dot_general(a, b, (((1,), (1,)), ((), ())), preferred_element_type=F32)


def normed(values):
    center = values - jnp.mean(values, axis=-1, keepdims=True)
    scale = lax.rsqrt(jnp.mean(center * center, axis=-1, keepdims=True) + 1e-05)
    return center * scale, scale


def norm_back(edge, unit, scale):
    return (edge - jnp.mean(edge, axis=-1, keepdims=True) - unit * jnp.mean(edge * unit, axis=-1, keepdims=True)) * scale


def start(source, target, sem):
    pltpu.make_async_copy(source, target, sem).start()


def wait(ref, sem):
    pltpu.make_async_copy(ref, ref, sem).wait()


def place_of(places, side, axis, slot):
    return places[side * 12 + "xyz".index(axis) * 4 + slot]


def ffn_kernel(places, bias_ref, low_own, low_other, grad_own, grad_other, up, down_low, down_high,
               bias_grad_ref, feed_ref, feed_low_ref, gc_ref, gc_low_ref, dup, ddown_keep, ddown_move,
               up_buf, down_buf, dup_buf, ddown_buf, low, grad, low_t, act_buf, gpre_buf, total, grad_total,
               feed_low, gc_low, in_sem, up_sem, down_sem, out_sem):
    core = places[24]

    def tiles(chunk):
        for part in (0, 1):
            for sy in range(4):
                y = place_of(places, 0, "y", sy)
                yh, yl = lax.div(y, 2), lax.rem(y, 2)
                unit = pl.ds(pl.multiple_of((part * 2 + yh) * UNIT, UNIT), UNIT)
                for x in range(4):
                    yield sy, chunk * 2 + part, x, yl, unit

    def model(x, yl):
        return pl.ds(pl.multiple_of((x * 2 + yl) * 128, 128), 128)

    def fetch(chunk):
        for sy, sz, x, yl, unit in tiles(chunk):
            start(up.at[x * 16 + sy * 4 + sz], up_buf.at[chunk, model(x, yl), unit], up_sem.at[chunk])
        for sy, sz, sx, yl, unit in tiles(chunk):
            cols = model(place_of(places, 0, "x", sx), yl)
            start((down_low, down_high)[sy // 2].at[sy % 2 * 16 + sx * 4 + sz], down_buf.at[chunk, unit, cols], down_sem.at[chunk])

    def send_down(chunk):
        for sy, sz, sx, yl, unit in tiles(chunk):
            source = ddown_buf.at[chunk, unit, model(place_of(places, 0, "x", sx), yl)]
            start(source, (ddown_keep, ddown_move)[sy // 2].at[sy % 2 * 16 + sz * 4 + sx], out_sem)

    def send_up(chunk):
        for part in (0, 1):
            z = place_of(places, 0, "z", chunk * 2 + part)
            for y in range(4):
                for x in range(4):
                    unit = slice((part * 2 + y // 2) * UNIT, (part * 2 + y // 2 + 1) * UNIT)
                    start(dup_buf.at[chunk, model(x, y % 2), unit], dup.at[x, y, z], out_sem)

    start(low_own, low.at[pl.ds(0, TOK)], in_sem.at[0])
    start(low_other, low.at[pl.ds(TOK, TOK)], in_sem.at[0])
    fetch(0)
    start(grad_own, grad.at[pl.ds(0, TOK)], in_sem.at[1])
    start(grad_other, grad.at[pl.ds(TOK, TOK)], in_sem.at[1])
    fetch(1)
    bias_grad_ref[...] = jnp.zeros_like(bias_grad_ref)
    wait(low, in_sem.at[0])
    low_t[...] = low[...].T
    wait(grad, in_sem.at[1])

    for chunk in (0, 1):
        wait(up_buf.at[chunk], up_sem.at[chunk])
        wait(down_buf.at[chunk], down_sem.at[chunk])
        for n in range(CHUNK // UNIT):
            cols = slice(n * UNIT, (n + 1) * UNIT)
            block = (place_of(places, 0, "z", chunk * 2 + n // 2) * 2 + n % 2) * 2 + core
            pre = dot(low[...], up_buf[chunk, :, cols]) + bias_ref[block]
            gact = dot_t(grad[...], down_buf[chunk, cols, :])
            square = pre * pre
            bend = jnp.tanh(ROOT * (pre + CUBE * square * pre))
            half = 0.5 + 0.5 * bend
            act = (pre * half).astype(BF16)
            slope = half + 0.5 * pre * (1.0 - bend * bend) * (ROOT + 3.0 * ROOT * CUBE * square)
            gpre = (gact * slope).astype(BF16)
            act_buf[:, cols] = act
            gpre_buf[:, cols] = gpre
            bias_grad_ref[block] = jnp.sum(gpre.astype(F32), axis=0, keepdims=True)
            ddown_buf[chunk, cols, :] = dot(act.T, grad[...]).astype(BF16)
            dup_buf[chunk, :, cols] = dot(low_t[...], gpre).astype(BF16)
        send_up(chunk)
        send_down(chunk)
        more = dot_t(gpre_buf[...], up_buf[chunk])
        feed = dot(act_buf[...], down_buf[chunk])
        if chunk == 0:
            grad_total[...] = more
            total[...] = feed
        else:
            grad_total[...] += more
            gc_low[...] = grad_total[TOK:, :].astype(BF16)
            start(gc_low, gc_low_ref, out_sem)
            start(grad_total.at[pl.ds(0, TOK)], gc_ref, out_sem)
            total[...] += feed
            feed_low[...] = total[TOK:, :].astype(BF16)
            start(feed_low, feed_low_ref, out_sem)
            start(total.at[pl.ds(0, TOK)], feed_ref, out_sem)
    for ref in (dup_buf, ddown_buf, gc_low, feed_low, grad_total.at[pl.ds(0, TOK)], total.at[pl.ds(0, TOK)]):
        wait(ref, out_sem)


def ffn(places, up_bias, low_own, low_other, grad_own, grad_other, weights):
    big = pltpu.VMEM((2, CHUNK, CHUNK), BF16)
    rows = pltpu.VMEM((BOTH, WIDTH), BF16)
    sums = pltpu.VMEM((BOTH, WIDTH), F32)
    half = pltpu.VMEM((TOK, WIDTH), BF16)
    return pl.pallas_call(
        ffn_kernel,
        in_specs=[SMEM, VMEM] + [HBM] * 7,
        out_specs=[VMEM] + [HBM] * 7,
        out_shape=[
            shape(16, 1, UNIT, dtype=F32),
            shape(TOK, WIDTH, dtype=F32),
            shape(TOK, WIDTH),
            shape(TOK, WIDTH, dtype=F32),
            shape(TOK, WIDTH),
            shape(4, 4, 4, 128, 256),
            shape(32, 256, 128),
            shape(32, 256, 128),
        ],
        scratch_shapes=[
            big, big, big, big, rows, rows, rows,
            pltpu.VMEM((BOTH, CHUNK), BF16),
            pltpu.VMEM((BOTH, CHUNK), BF16),
            sums, sums, half, half, TWO, TWO, TWO, ONE,
        ],
        compiler_params=pltpu.CompilerParams(vmem_limit_bytes=ROOM),
        cost_estimate=work(40e9),
        name="ffn",
    )(places, up_bias.reshape(16, 1, UNIT), low_own, low_other, grad_own, grad_other, *weights)


BLOCK = 128
HALF = 512
PART = 3 * HALF


def core_of(places, side):
    return places[24] if side == 0 else 1 - places[24]


def fetch_part(places, part, pieces, buf, sem, cols):
    cols = slice(part * 2048 + cols.start, part * 2048 + cols.stop)
    for side in (0, 1):
        start(pieces[side].at[:, :, :, cols], buf.at[:, :, core_of(places, side)], sem)


def matrix(ref):
    return ref.reshape(WIDTH, ref.shape[-1])


def parts_buffer(cols):
    return pltpu.VMEM((4, 2, 2, 64, cols), BF16)


def lane_marks():
    low = lax.broadcasted_iota(jnp.int32, (1, 128), 1) < 64
    return low, jnp.where(low, 1.0, 0.0).astype(BF16), jnp.where(low, 0.0, 1.0).astype(BF16)


def project_kernel(places, ln1_ref, qkv_bias_ref, tok, *refs):
    pieces, (low_out, qkv_out, buf0, buf1, tok_ref, low_ref, qkv_ref, sem, out_sem) = refs[:2], refs[2:]
    start(tok, tok_ref, sem.at[2])
    for part, buf in ((0, buf0), (1, buf1)):
        fetch_part(places, part, pieces, buf, sem.at[part], slice(0, PART))
    wait(tok_ref, sem.at[2])

    @pl.loop(0, TOK // 128)
    def _(i):
        rows = pl.ds(i * 128, 128)
        unit, _ = normed(tok_ref[rows, :].astype(F32))
        low_ref[rows, :] = (unit * ln1_ref[0:1, :] + ln1_ref[1:2, :]).astype(BF16)

    start(low_ref, low_out, out_sem)
    for part, buf in ((0, buf0), (1, buf1)):
        wait(buf, sem.at[part])
        for n in range(3):
            cols = slice(n * HALF, (n + 1) * HALF)
            qkv_ref[part, :, cols] = (dot(low_ref[...], matrix(buf)[:, cols]) + qkv_bias_ref[part, :, cols]).astype(BF16)
        start(qkv_ref.at[part], qkv_out.at[part], out_sem)
    wait(low_ref, out_sem)
    wait(qkv_ref, out_sem)


def project(places, tokens, ln1, qkv_bias, pieces):
    wide, heads = pltpu.VMEM((TOK, WIDTH), BF16), pltpu.VMEM((2, TOK, PART), BF16)
    return pl.pallas_call(
        project_kernel,
        in_specs=[SMEM] + [VMEM] * 2 + [HBM] * 3,
        out_specs=[HBM] * 2,
        out_shape=[shape(TOK, WIDTH), shape(2, TOK, PART)],
        scratch_shapes=[parts_buffer(PART), parts_buffer(PART), wide, wide, heads, FEW, ONE],
        compiler_params=pltpu.CompilerParams(vmem_limit_bytes=ROOM),
        cost_estimate=work(8e9),
        name="project",
    )(places, ln1, qkv_bias, tokens, *pieces)


def attend_kernel(places, pair_ref, out_bias_ref, ln2_ref, tok, qkv, *refs):
    pieces, refs = refs[:2], refs[2:]
    prob_out, mixed_out, hidden_out, normed_out, buf0, buf1, tok_ref, qkv_ref = refs[:8]
    prob_ref, mixed_ref, hidden_ref, normed_ref, sem, out_sem = refs[8:]
    start(qkv, qkv_ref, sem.at[2])
    start(tok, tok_ref, sem.at[3])
    for part, buf in ((0, buf0), (1, buf1)):
        fetch_part(places, part, pieces, buf, sem.at[part], slice(PART, 2048))
    low, near, far = lane_marks()
    near, far = near * 0.125, far * 0.125
    wait(qkv_ref, sem.at[2])

    @pl.loop(0, 8)
    def _(pair):
        part = lax.div(pair, 4)
        begin = pl.multiple_of(lax.rem(pair, 4) * 128, 128)
        lanes = pl.ds(pl.multiple_of(pair * 128, 128), 128)
        for block in range(TOK // BLOCK):
            rows = slice(block * BLOCK, (block + 1) * BLOCK)
            query = qkv_ref[part, rows, pl.ds(begin, 128)]
            key = qkv_ref[part, rows, pl.ds(begin + HALF, 128)]
            value = qkv_ref[part, rows, pl.ds(begin + 2 * HALF, 128)]
            bias = pair_ref[block]
            score = dot_t(jnp.concatenate([query * near, query * far], axis=0), key) + jnp.concatenate([bias, bias], axis=0)
            power = jnp.exp(score - jnp.max(score, axis=-1, keepdims=True))
            prob = (power * (1.0 / jnp.sum(power, axis=-1, keepdims=True))).astype(BF16)
            prob_ref[pair, block] = prob
            both = dot(prob, value)
            mixed_ref[rows, lanes] = jnp.where(low, both[:BLOCK], both[BLOCK:]).astype(BF16)

    start(prob_ref, prob_out, out_sem)
    start(mixed_ref, mixed_out, out_sem)
    wait(tok_ref, sem.at[3])
    for part, buf in ((0, buf0), (1, buf1)):
        cols = slice(part * HALF, (part + 1) * HALF)
        wait(buf, sem.at[part])
        hidden_ref[:, cols] = tok_ref[:, cols].astype(F32) + dot(mixed_ref[...], matrix(buf)[...]) + out_bias_ref[:, cols]
    start(hidden_ref, hidden_out, out_sem)

    @pl.loop(0, TOK // 128)
    def _(i):
        rows = pl.ds(i * 128, 128)
        unit, _ = normed(hidden_ref[rows, :])
        normed_ref[rows, :] = (unit * ln2_ref[0:1, :] + ln2_ref[1:2, :]).astype(BF16)

    start(normed_ref, normed_out, out_sem)
    for ref in (prob_ref, mixed_ref, hidden_ref, normed_ref):
        wait(ref, out_sem)


def attend(places, tokens, pair_bias, qkv, out_bias, ln2, pieces):
    outs = [((8, 4, 2 * BLOCK, BLOCK), BF16), ((TOK, WIDTH), BF16), ((TOK, WIDTH), F32), ((TOK, WIDTH), BF16)]
    return pl.pallas_call(
        attend_kernel,
        in_specs=[SMEM] + [VMEM] * 3 + [HBM] * 4,
        out_specs=[HBM] * 4,
        out_shape=[jax.ShapeDtypeStruct(*out) for out in outs],
        scratch_shapes=[parts_buffer(HALF), parts_buffer(HALF), pltpu.VMEM((TOK, WIDTH), BF16), pltpu.VMEM((2, TOK, PART), BF16)]
        + [pltpu.VMEM(*out) for out in outs]
        + [FEW, ONE],
        compiler_params=pltpu.CompilerParams(vmem_limit_bytes=ROOM),
        cost_estimate=work(16e9),
        name="attend",
    )(places, pair_bias, out_bias.reshape(1, WIDTH), ln2, tokens, qkv, *pieces)


def turn(hidden_ref, gain_ref, gc_ref, got_ref, grad_ref, ghid_ref, glow_ref, vec_ref):
    vec_ref[...] = jnp.zeros_like(vec_ref)

    @pl.loop(0, TOK // 128)
    def _(part):
        rows = pl.ds(part * 128, 128)
        unit, scale = normed(hidden_ref[rows, :])
        gc = gc_ref[rows, :] + got_ref[rows, :].astype(F32)
        gout = grad_ref[rows, :].astype(F32)
        ghid = gout + norm_back(gc * gain_ref[...], unit, scale)
        ghid_ref[rows, :] = ghid
        glow_ref[rows, :] = ghid.astype(BF16)
        vec_ref[0:1, :] += jnp.sum(ghid, axis=0, keepdims=True)
        vec_ref[1:2, :] += jnp.sum(gc * unit, axis=0, keepdims=True)
        vec_ref[2:3, :] += jnp.sum(gc, axis=0, keepdims=True)
        vec_ref[3:4, :] += jnp.sum(gout, axis=0, keepdims=True)


TURN_SHAPES = [((TOK, WIDTH), F32), ((TOK, WIDTH), F32), ((TOK, WIDTH), BF16), ((TOK, WIDTH), BF16)]


def back_kernel(part, places, low_in, qkv_in, prob_in, mixed_in, *refs):
    pieces, refs = refs[:2], refs[2:]
    if part == 0:
        gain_ref, turn_in, refs = refs[0], refs[1:5], refs[5:]
        sum_ref, vec_ref, gqkv_out, *outs = refs[:5]
        ghid_out, glow_out = refs[5:7]
        turn_refs, refs = refs[7:11], refs[11:]
        ghid_ref, refs = refs[0], refs[1:]
    else:
        glow_in, refs = refs[0], refs[1:]
        sum_ref, gqkv_out, *outs = refs[:4]
        refs = refs[4:]
    low_ref, qkv_ref, prob_ref, mixed_ref, glow_ref, buf, side_buf, grad_buf, gmix_ref, gqkv_ref, flip, sem, out_sem = refs
    tail = slice(PART, 2048)
    if part == 0:
        for source, target in zip(turn_in, turn_refs):
            start(source, target, sem.at[0])
    else:
        start(glow_in, glow_ref, sem.at[0])
    start(mixed_in, mixed_ref, sem.at[1])
    fetch_part(places, part, pieces, buf, sem.at[2], tail)
    fetch_part(places, 1 - part, pieces, side_buf, sem.at[3], tail)
    start(qkv_in.at[part], qkv_ref, sem.at[4])
    start(prob_in.at[pl.ds(part * 4, 4)], prob_ref, sem.at[4])
    start(low_in, low_ref, sem.at[5])
    wait(mixed_ref, sem.at[1])
    flip[...] = mixed_ref[...].T
    if part == 0:
        for ref in turn_refs:
            wait(ref, sem.at[0])
        turn(turn_refs[0], gain_ref, turn_refs[1], turn_refs[2], turn_refs[3], ghid_ref, glow_ref, vec_ref)
        start(ghid_ref, ghid_out, out_sem)
        start(glow_ref, glow_out, out_sem)
    else:
        wait(glow_ref, sem.at[0])
    heads = slice(part * HALF, (part + 1) * HALF)
    rest = slice((1 - part) * HALF, (2 - part) * HALF)
    grad_matrix = matrix(grad_buf)
    grad_matrix[:, PART:] = dot(flip[...], glow_ref[:, heads]).astype(BF16)
    wait(buf, sem.at[2])
    wait(side_buf, sem.at[3])
    gmix_ref[...] = (
        dot_t(glow_ref[:, heads], matrix(buf)[heads, :]) + dot_t(glow_ref[:, rest], matrix(side_buf)[heads, :])
    ).astype(BF16)
    wait(low_ref, sem.at[5])
    flip[...] = low_ref[...].T
    wait(qkv_ref, sem.at[4])
    wait(prob_ref, sem.at[4])
    low, near, far = lane_marks()

    @pl.loop(0, 4)
    def _(pair):
        begin = pl.multiple_of(pair * 128, 128)
        for block in range(TOK // BLOCK):
            rows = slice(block * BLOCK, (block + 1) * BLOCK)
            query = qkv_ref[rows, pl.ds(begin, 128)]
            key = qkv_ref[rows, pl.ds(begin + HALF, 128)]
            value = qkv_ref[rows, pl.ds(begin + 2 * HALF, 128)]
            gmix = gmix_ref[rows, pl.ds(begin, 128)]
            gmix = jnp.concatenate([gmix * near, gmix * far], axis=0)
            query = jnp.concatenate([query * (near * 0.125), query * (far * 0.125)], axis=0)
            prob_low = prob_ref[pair, block]
            prob = prob_low.astype(F32)
            gprob = dot_t(gmix, value)
            gscore = (prob * (gprob - jnp.sum(prob * gprob, axis=-1, keepdims=True))).astype(BF16)
            both = dot(gscore, key) * 0.125
            gqkv_ref[rows, pl.ds(begin, 128)] = jnp.where(low, both[:BLOCK], both[BLOCK:]).astype(BF16)
            gqkv_ref[rows, pl.ds(begin + HALF, 128)] = dot(gscore.T, query).astype(BF16)
            gqkv_ref[rows, pl.ds(begin + 2 * HALF, 128)] = dot(prob_low.T, gmix).astype(BF16)

    start(gqkv_ref, gqkv_out, out_sem)
    for n in range(3):
        cols = slice(n * HALF, (n + 1) * HALF)
        grad_matrix[:, cols] = dot(flip[...], gqkv_ref[:, cols]).astype(BF16)
    for side in (0, 1):
        start(grad_buf.at[:, :, core_of(places, side)], outs[side], out_sem)
    sum_ref[...] = jnp.sum(gqkv_ref[...].astype(F32), axis=0, keepdims=True)
    wait(grad_buf, out_sem)
    wait(gqkv_ref, out_sem)
    if part == 0:
        wait(ghid_ref, out_sem)
        wait(glow_ref, out_sem)


def back(part, places, low, qkv, prob, mixed, pieces, *more):
    first = part == 0
    rows = shape(4, 2, 64, 2048)
    wide = pltpu.VMEM((TOK, WIDTH), BF16)
    return pl.pallas_call(
        functools.partial(back_kernel, part),
        in_specs=[SMEM] + [HBM] * 6 + ([VMEM] + [HBM] * 4 if first else [HBM]),
        out_specs=[VMEM] * (2 if first else 1) + [HBM] * (5 if first else 3),
        out_shape=[shape(1, PART, dtype=F32)]
        + ([shape(8, WIDTH, dtype=F32)] if first else [])
        + [shape(TOK, PART), rows, rows]
        + ([shape(TOK, WIDTH, dtype=F32), shape(TOK, WIDTH)] if first else []),
        scratch_shapes=([pltpu.VMEM(*s) for s in TURN_SHAPES] + [pltpu.VMEM((TOK, WIDTH), F32)] if first else [])
        + [
            wide,
            pltpu.VMEM((TOK, PART), BF16),
            pltpu.VMEM((4, 4, 2 * BLOCK, BLOCK), BF16),
            wide,
            wide,
            parts_buffer(HALF),
            parts_buffer(HALF),
            parts_buffer(2048),
            pltpu.VMEM((TOK, HALF), BF16),
            pltpu.VMEM((TOK, PART), BF16),
            pltpu.VMEM((WIDTH, TOK), BF16),
            FEW,
            ONE,
        ],
        compiler_params=pltpu.CompilerParams(vmem_limit_bytes=ROOM),
        cost_estimate=work(20e9),
        name="back" + str(part),
    )(places, low, qkv, prob, mixed, *pieces, *more)


def end_kernel(places, ln1_ref, down_bias_ref, gqkv0, gqkv1, ghid, tok, hidden, feed, feed_got, *refs):
    pieces, refs = refs[:2], refs[2:]
    gin_out, out_out, vec_ref, buf0, buf1, gqkv0_ref, gqkv1_ref, ghid_ref, tok_ref, hidden_ref, feed_ref, got_ref, out_ref, total, sem, out_sem = refs
    start(gqkv0, gqkv0_ref, sem.at[0])
    fetch_part(places, 0, pieces, buf0, sem.at[0], slice(0, PART))
    start(gqkv1, gqkv1_ref, sem.at[1])
    fetch_part(places, 1, pieces, buf1, sem.at[1], slice(0, PART))
    start(ghid, ghid_ref, sem.at[2])
    start(tok, tok_ref, sem.at[2])
    for source, target in ((hidden, hidden_ref), (feed, feed_ref), (feed_got, got_ref)):
        start(source, target, sem.at[3])
    vec_ref[...] = jnp.zeros_like(vec_ref)
    wait(gqkv0_ref, sem.at[0])
    wait(buf0, sem.at[0])
    total[...] = dot_t(gqkv0_ref[...], matrix(buf0)[...])
    wait(gqkv1_ref, sem.at[1])
    wait(buf1, sem.at[1])
    total[...] += dot_t(gqkv1_ref[...], matrix(buf1)[...])
    wait(ghid_ref, sem.at[2])
    wait(tok_ref, sem.at[2])

    @pl.loop(0, TOK // 128)
    def _(i):
        rows = pl.ds(i * 128, 128)
        unit, scale = normed(tok_ref[rows, :].astype(F32))
        grad = total[rows, :]
        ghid_ref[rows, :] += norm_back(grad * ln1_ref[0:1, :], unit, scale)
        vec_ref[0:1, :] += jnp.sum(grad * unit, axis=0, keepdims=True)
        vec_ref[1:2, :] += jnp.sum(grad, axis=0, keepdims=True)

    start(ghid_ref, gin_out, out_sem)
    for ref in (hidden_ref, feed_ref, got_ref):
        wait(ref, sem.at[3])
    out_ref[...] = (hidden_ref[...] + feed_ref[...] + got_ref[...].astype(F32) + down_bias_ref[...]).astype(BF16)
    start(out_ref, out_out, out_sem)
    wait(ghid_ref, out_sem)
    wait(out_ref, out_sem)


def end(places, ln1, down_bias, gqkv0, gqkv1, ghid, tokens, hidden, feed, feed_got, pieces):
    low, high = pltpu.VMEM((TOK, WIDTH), BF16), pltpu.VMEM((TOK, WIDTH), F32)
    heads = pltpu.VMEM((TOK, PART), BF16)
    return pl.pallas_call(
        end_kernel,
        in_specs=[SMEM] + [VMEM] * 2 + [HBM] * 7 + [HBM] * 2,
        out_specs=[HBM] * 2 + [VMEM],
        out_shape=[shape(TOK, WIDTH, dtype=F32), shape(TOK, WIDTH), shape(8, WIDTH, dtype=F32)],
        scratch_shapes=[parts_buffer(PART), parts_buffer(PART), heads, heads, high, low, high, high, low, low, high, FEW, ONE],
        compiler_params=pltpu.CompilerParams(vmem_limit_bytes=ROOM),
        cost_estimate=work(10e9),
        name="end",
    )(places, ln1, down_bias.reshape(1, WIDTH), gqkv0, gqkv1, ghid, tokens, hidden, feed, feed_got, *pieces)


AXES = ("z", "yh", "c", "x", "yl")
ALONG_Y, CHIPS = ("yh", "yl"), ("z", "yh", "x", "yl")


def device_number(place):
    return (
        ((place["z"] * 2 + place["y"] // 2) * 2 + place["c"]) * 4 + place["x"]
    ) * 2 + place["y"] % 2


def exchange_pairs(axis, second, alike=False):
    pairs = []
    for z, y, c, x in itertools.product(range(4), range(4), range(2), range(4)):
        here = {"z": z, "y": y, "c": c, "x": x}
        mask = 1 if (c == 0 or alike) != second else 3
        there = dict(here)
        there[axis] = here[axis] ^ mask
        pairs.append((device_number(here), device_number(there)))
    return pairs


def swap_axis(values, axis, second, alike=False):
    return lax.ppermute(values, AXES, exchange_pairs(axis, second, alike))


def swap_core(values):
    return lax.ppermute(values, "c", [(0, 1), (1, 0)])


def position(axis):
    if axis == "y":
        return lax.axis_index("yh") * 2 + lax.axis_index("yl")
    return lax.axis_index(axis)


def distance_of(core, slot):
    return jnp.where(core == 0, slot ^ (slot >> 1), ((slot << 1) & 3) ^ ((slot ^ (slot >> 1)) & 1))


def place_table():
    core, slots = lax.axis_index("c"), jnp.arange(4, dtype=jnp.int32)
    rows = [
        distance_of(side, slots) ^ position(axis)
        for side in (core, 1 - core)
        for axis in ("x", "y", "z")
    ]
    return jnp.concatenate(rows + [jnp.full((8,), core, jnp.int32)])


def add(left, right, dtype=BF16):
    return (left.astype(F32) + right.astype(F32)).astype(dtype)


def halves(own, got):
    count = own.shape[0] // 2
    return add(own[count:], got[count:]), add(own[:count], got[:count])


def spread(values, axes):
    return lax.all_to_all(jnp.broadcast_to(values, (64,) + values.shape), axes, 0, 0)


def together(*values):
    return lax.optimization_barrier(values)


def pair_bias(clip_ids):
    clips = clip_ids.reshape(-1, BLOCK)
    row = lax.broadcasted_iota(jnp.int32, (BLOCK, BLOCK), 0)
    col = lax.broadcasted_iota(jnp.int32, (BLOCK, BLOCK), 1)
    allowed = (clips[:, :, None] == clips[:, None, :]) & (row >= col)[None]
    return jnp.where(allowed, 0.0, -1e30).astype(F32)


def on_device(
    tokens,
    qkv_weight,
    out_weight,
    up_weight,
    down_weight,
    ln1_gain,
    ln1_bias,
    q_bias,
    v_bias,
    out_bias,
    ln2_gain,
    ln2_bias,
    up_bias,
    down_bias,
    segment_ids,
    cotangent,
):
    places = place_table()
    heads = qkv_weight.reshape(8, 3, WIDTH)
    pieces = []
    for cols in (slice(0, HALF), slice(HALF, WIDTH)):
        pieces += [heads[:, :, cols].reshape(8, PART), out_weight[:, cols]]
    def join(pairs):
        return together(*[jnp.concatenate(pair) for pair in pairs])

    rows = spread(jnp.concatenate(pieces, axis=1), CHIPS)
    down, up = down_weight[None], up_weight[None]
    for axes in (("z", "z"), ("x", "y")):
        for second in (False, True):
            got = [swap_axis(v, axis, second) for v, axis in zip((down, up), axes)]
            down, up = join(((down, got[0]), (up, got[1])))
    up = lax.all_gather(up, "x", axis=0).reshape(64, 128, 256)
    down_got, rows, grad_other = together(swap_axis(down, "y", False), rows, swap_core(cotangent))
    rows = rows.reshape(4, 2, 64, 4096)
    pieces = (rows, swap_core(rows))
    (down,) = join(((down, down_got),))
    down_got = swap_axis(down, "y", True)

    ln1 = jnp.stack([ln1_gain, ln1_bias])
    nothing = jnp.zeros((HALF,), F32)
    qkv_bias = jnp.stack(
        [
            jnp.concatenate([q_bias[cols], nothing, v_bias[cols]])[None]
            for cols in (slice(0, HALF), slice(HALF, WIDTH))
        ]
    )
    low, qkv = project(places, tokens, ln1, qkv_bias, pieces)
    prob, mixed, hidden, low2 = attend(
        places, tokens, pair_bias(segment_ids), qkv, out_bias, jnp.stack([ln2_gain, ln2_bias]), pieces
    )
    up_bias_grad, feed, feed_low, gc, gc_low, dup, keep_down, move_down = ffn(
        places, up_bias, low2, swap_core(low2), cotangent, grad_other, (up, down, down_got)
    )
    dup = lax.psum_scatter(dup, "x", scatter_dimension=0, tiled=True)[0]

    down_got = swap_axis(move_down, "y", True)
    sum0, vec2, gqkv0, *main_a, ghid, glow = back(
        0, places, low, qkv, prob, mixed, pieces,
        ln2_gain.reshape(1, WIDTH), hidden, gc, swap_core(gc_low), cotangent,
    )
    sent_a = swap_core(main_a[1])
    sum1, gqkv1, *main_b = back(1, places, low, qkv, prob, mixed, pieces, glow)
    sent_a, down_got, dup, gqkv1, *main_b = together(sent_a, down_got, dup, gqkv1, *main_b)

    sent_b = swap_core(main_b[1])
    row_sums = jnp.concatenate([add(main_a[0], sent_a), add(main_b[0], sent_b)], axis=3).reshape(64, 8, 4096)
    row_sums, gqkv1 = together(row_sums, gqkv1)
    row_parts = lax.all_to_all(row_sums, CHIPS, 0, 0)
    move_down, keep_down = halves(keep_down, down_got)
    down_got = swap_axis(move_down, "y", False)
    dup = lax.psum_scatter(dup, ALONG_Y, scatter_dimension=0, tiled=True)[0]
    grad_tokens, output, vec1 = end(
        places, ln1, down_bias, gqkv0, gqkv1, ghid, tokens, hidden, feed, swap_core(feed_low), pieces
    )
    down_got, vec1 = together(down_got, vec1)
    sums = jnp.concatenate([sum0.reshape(3, HALF), sum1.reshape(3, HALF)], axis=1)
    blocks = [vec1[0:2], sums[0:1], sums[2:3], vec2[0:4]]
    vector = jnp.concatenate(
        [block.reshape(-1, 128) for block in blocks] + [up_bias_grad.reshape(-1, 128)]
    )
    vector = vector + swap_core(vector)
    dup = lax.psum_scatter(dup, "z", scatter_dimension=0, tiled=True)[0]
    for axis, second in (("z", True), ("z", False), ("x", True), ("x", False)):
        move_down, keep_down = halves(keep_down, down_got)
        down_got = swap_axis(move_down, axis, second)
    for axis in ("z", "x", "y"):
        for second in (False, True):
            vector = vector + swap_axis(vector, axis, second, True)
    up_grad = dup.astype(F32)
    down_grad = add(keep_down, down_got, F32)[0]
    row = jnp.sum(row_parts.astype(F32), axis=0).reshape(8, 2, 2048)
    qkv_grad = row[:, :, :PART].reshape(8, 2, 3, HALF).transpose(0, 2, 1, 3).reshape(8, 3 * WIDTH)
    out_grad = row[:, :, PART:].reshape(8, WIDTH)
    summed = vector.reshape(-1)
    vectors = [summed[i * WIDTH : (i + 1) * WIDTH] for i in range(8)]
    return (
        output,
        grad_tokens,
        qkv_grad,
        out_grad,
        up_grad,
        down_grad,
        *vectors[:7],
        summed[8 * WIDTH :],
        vectors[7],
    )


def solution(mesh):
    fine = Mesh(mesh.devices.reshape(4, 2, 2, 4, 2), AXES)
    every, hidden, model = AXES, ("z", "yh", "c"), ("x", "yl")
    weights = (P(every, None), P(every, None), P(model, hidden), P(hidden, model))
    return jax.shard_map(
        on_device,
        mesh=fine,
        in_specs=(P(every, None), *weights, *[P()] * 9, P(every), P(every, None)),
        out_specs=(P(every, None), P(every, None), *weights, *[P()] * 9),
        check_vma=False,
    )
```

```python
import functools
import itertools

import jax
import jax.numpy as jnp
from jax import lax
from jax.experimental import pallas as pl
from jax.experimental.pallas import tpu as pltpu
from jax.sharding import Mesh, PartitionSpec as P

F32, BF16 = jnp.float32, jnp.bfloat16
TOK, WIDTH, FF = 512, 1024, 4096
BOTH = 2 * TOK
CHUNK = 1024
UNIT = 256
ROOT = 0.7978845608028654
CUBE = 0.044715
VMEM, ANY, HBM, SMEM = (
    pl.BlockSpec(memory_space=kind) for kind in (pltpu.VMEM, pl.ANY, pltpu.HBM, pltpu.SMEM)
)
ROOM = 60 * 2**20
ONE = pltpu.SemaphoreType.DMA
TWO = pltpu.SemaphoreType.DMA((2,))
FEW = pltpu.SemaphoreType.DMA((8,))


def shape(*dims, dtype=BF16):
    return jax.ShapeDtypeStruct(dims, dtype)


def work(flops):
    return pl.CostEstimate(flops=int(flops * 0.4), bytes_accessed=1 << 20, transcendentals=0)


def dot(a, b):
    return lax.dot_general(a, b, (((1,), (0,)), ((), ())), preferred_element_type=F32)


def dot_t(a, b):
    return lax.dot_general(a, b, (((1,), (1,)), ((), ())), preferred_element_type=F32)


def normed(values):
    center = values - jnp.mean(values, axis=-1, keepdims=True)
    scale = lax.rsqrt(jnp.mean(center * center, axis=-1, keepdims=True) + 1e-05)
    return center * scale, scale


def norm_back(edge, unit, scale):
    return (edge - jnp.mean(edge, axis=-1, keepdims=True) - unit * jnp.mean(edge * unit, axis=-1, keepdims=True)) * scale


def start(source, target, sem):
    pltpu.make_async_copy(source, target, sem).start()


def wait(ref, sem):
    pltpu.make_async_copy(ref, ref, sem).wait()


def place_of(places, side, axis, slot):
    return places[side * 12 + "xyz".index(axis) * 4 + slot]


def ffn_kernel(places, bias_ref, low_own, low_other, grad_own, grad_other, up, down_low, down_high,
               bias_grad_ref, feed_ref, feed_low_ref, gc_ref, gc_low_ref, dup, ddown_keep, ddown_move,
               up_buf, down_buf, dup_buf, ddown_buf, low, grad, low_t, act_buf, gpre_buf, total, grad_total,
               feed_low, gc_low, in_sem, up_sem, down_sem, out_sem):
    core = places[24]

    def tiles(chunk):
        for part in (0, 1):
            for sy in range(4):
                y = place_of(places, 0, "y", sy)
                yh, yl = lax.div(y, 2), lax.rem(y, 2)
                unit = pl.ds(pl.multiple_of((part * 2 + yh) * UNIT, UNIT), UNIT)
                for x in range(4):
                    yield sy, chunk * 2 + part, x, yl, unit

    def model(x, yl):
        return pl.ds(pl.multiple_of((x * 2 + yl) * 128, 128), 128)

    def fetch(chunk):
        for sy, sz, x, yl, unit in tiles(chunk):
            start(up.at[x * 16 + sy * 4 + sz], up_buf.at[chunk, model(x, yl), unit], up_sem.at[chunk])
        for sy, sz, sx, yl, unit in tiles(chunk):
            cols = model(place_of(places, 0, "x", sx), yl)
            start((down_low, down_high)[sy // 2].at[sy % 2 * 16 + sx * 4 + sz], down_buf.at[chunk, unit, cols], down_sem.at[chunk])

    def send_down(chunk):
        for sy, sz, sx, yl, unit in tiles(chunk):
            source = ddown_buf.at[chunk, unit, model(place_of(places, 0, "x", sx), yl)]
            start(source, (ddown_keep, ddown_move)[sy // 2].at[sy % 2 * 16 + sz * 4 + sx], out_sem)

    def send_up(chunk):
        for part in (0, 1):
            z = place_of(places, 0, "z", chunk * 2 + part)
            for y in range(4):
                for x in range(4):
                    unit = slice((part * 2 + y // 2) * UNIT, (part * 2 + y // 2 + 1) * UNIT)
                    start(dup_buf.at[chunk, model(x, y % 2), unit], dup.at[x, y, z], out_sem)

    start(low_own, low.at[pl.ds(0, TOK)], in_sem.at[0])
    start(low_other, low.at[pl.ds(TOK, TOK)], in_sem.at[0])
    fetch(0)
    start(grad_own, grad.at[pl.ds(0, TOK)], in_sem.at[1])
    start(grad_other, grad.at[pl.ds(TOK, TOK)], in_sem.at[1])
    fetch(1)
    bias_grad_ref[...] = jnp.zeros_like(bias_grad_ref)
    wait(low, in_sem.at[0])
    low_t[...] = low[...].T
    wait(grad, in_sem.at[1])

    for chunk in (0, 1):
        wait(up_buf.at[chunk], up_sem.at[chunk])
        wait(down_buf.at[chunk], down_sem.at[chunk])
        for n in range(CHUNK // UNIT):
            cols = slice(n * UNIT, (n + 1) * UNIT)
            block = (place_of(places, 0, "z", chunk * 2 + n // 2) * 2 + n % 2) * 2 + core
            pre = dot(low[...], up_buf[chunk, :, cols]) + bias_ref[block]
            gact = dot_t(grad[...], down_buf[chunk, cols, :])
            square = pre * pre
            bend = jnp.tanh(ROOT * (pre + CUBE * square * pre))
            half = 0.5 + 0.5 * bend
            act = (pre * half).astype(BF16)
            slope = half + 0.5 * pre * (1.0 - bend * bend) * (ROOT + 3.0 * ROOT * CUBE * square)
            gpre = (gact * slope).astype(BF16)
            act_buf[:, cols] = act
            gpre_buf[:, cols] = gpre
            bias_grad_ref[block] = jnp.sum(gpre.astype(F32), axis=0, keepdims=True)
            ddown_buf[chunk, cols, :] = dot(act.T, grad[...]).astype(BF16)
            dup_buf[chunk, :, cols] = dot(low_t[...], gpre).astype(BF16)
        send_up(chunk)
        send_down(chunk)
        more = dot_t(gpre_buf[...], up_buf[chunk])
        feed = dot(act_buf[...], down_buf[chunk])
        if chunk == 0:
            grad_total[...] = more
            total[...] = feed
        else:
            grad_total[...] += more
            gc_low[...] = grad_total[TOK:, :].astype(BF16)
            start(gc_low, gc_low_ref, out_sem)
            start(grad_total.at[pl.ds(0, TOK)], gc_ref, out_sem)
            total[...] += feed
            feed_low[...] = total[TOK:, :].astype(BF16)
            start(feed_low, feed_low_ref, out_sem)
            start(total.at[pl.ds(0, TOK)], feed_ref, out_sem)
    for ref in (dup_buf, ddown_buf, gc_low, feed_low, grad_total.at[pl.ds(0, TOK)], total.at[pl.ds(0, TOK)]):
        wait(ref, out_sem)


def ffn(places, up_bias, low_own, low_other, grad_own, grad_other, weights):
    big = pltpu.VMEM((2, CHUNK, CHUNK), BF16)
    rows = pltpu.VMEM((BOTH, WIDTH), BF16)
    sums = pltpu.VMEM((BOTH, WIDTH), F32)
    half = pltpu.VMEM((TOK, WIDTH), BF16)
    return pl.pallas_call(
        ffn_kernel,
        in_specs=[SMEM, VMEM] + [HBM] * 7,
        out_specs=[VMEM] + [HBM] * 7,
        out_shape=[
            shape(16, 1, UNIT, dtype=F32),
            shape(TOK, WIDTH, dtype=F32),
            shape(TOK, WIDTH),
            shape(TOK, WIDTH, dtype=F32),
            shape(TOK, WIDTH),
            shape(4, 4, 4, 128, 256),
            shape(32, 256, 128),
            shape(32, 256, 128),
        ],
        scratch_shapes=[
            big, big, big, big, rows, rows, rows,
            pltpu.VMEM((BOTH, CHUNK), BF16),
            pltpu.VMEM((BOTH, CHUNK), BF16),
            sums, sums, half, half, TWO, TWO, TWO, ONE,
        ],
        compiler_params=pltpu.CompilerParams(vmem_limit_bytes=ROOM),
        cost_estimate=work(40e9),
        name="ffn",
    )(places, up_bias.reshape(16, 1, UNIT), low_own, low_other, grad_own, grad_other, *weights)


BLOCK = 128
HALF = 512
PART = 3 * HALF


def row_tiles(places, axis):
    core = places[24]
    for side in (0, 1):
        for slot in range(4):
            yield side, slot, place_of(places, side, axis, slot), core if side == 0 else 1 - core


def fetch_part(places, part, pieces, buf, sem, cols):
    cols = slice(part * 2048 + cols.start, part * 2048 + cols.stop)
    for side, slot, z, c in row_tiles(places, "z"):
        start(pieces[2 * side + slot // 2].at[slot % 2, :, :, cols], buf.at[z, :, c], sem)


def matrix(ref):
    return ref.reshape(WIDTH, ref.shape[-1])


def parts_buffer(cols):
    return pltpu.VMEM((4, 2, 2, 64, cols), BF16)


def lane_marks():
    low = lax.broadcasted_iota(jnp.int32, (1, 128), 1) < 64
    return low, jnp.where(low, 1.0, 0.0).astype(BF16), jnp.where(low, 0.0, 1.0).astype(BF16)


def project_kernel(places, ln1_ref, qkv_bias_ref, tok, *refs):
    pieces, (low_out, qkv_out, buf0, buf1, tok_ref, low_ref, qkv_ref, sem, out_sem) = refs[:4], refs[4:]
    start(tok, tok_ref, sem.at[2])
    for part, buf in ((0, buf0), (1, buf1)):
        fetch_part(places, part, pieces, buf, sem.at[part], slice(0, PART))
    wait(tok_ref, sem.at[2])

    @pl.loop(0, TOK // 128)
    def _(i):
        rows = pl.ds(i * 128, 128)
        unit, _ = normed(tok_ref[rows, :].astype(F32))
        low_ref[rows, :] = (unit * ln1_ref[0:1, :] + ln1_ref[1:2, :]).astype(BF16)

    start(low_ref, low_out, out_sem)
    for part, buf in ((0, buf0), (1, buf1)):
        wait(buf, sem.at[part])
        for n in range(3):
            cols = slice(n * HALF, (n + 1) * HALF)
            qkv_ref[part, :, cols] = (dot(low_ref[...], matrix(buf)[:, cols]) + qkv_bias_ref[part, :, cols]).astype(BF16)
        start(qkv_ref.at[part], qkv_out.at[part], out_sem)
    wait(low_ref, out_sem)
    wait(qkv_ref, out_sem)


def project(places, tokens, ln1, qkv_bias, pieces):
    wide, heads = pltpu.VMEM((TOK, WIDTH), BF16), pltpu.VMEM((2, TOK, PART), BF16)
    return pl.pallas_call(
        project_kernel,
        in_specs=[SMEM] + [VMEM] * 2 + [HBM] * 5,
        out_specs=[HBM] * 2,
        out_shape=[shape(TOK, WIDTH), shape(2, TOK, PART)],
        scratch_shapes=[parts_buffer(PART), parts_buffer(PART), wide, wide, heads, FEW, ONE],
        compiler_params=pltpu.CompilerParams(vmem_limit_bytes=ROOM),
        cost_estimate=work(8e9),
        name="project",
    )(places, ln1, qkv_bias, tokens, *pieces)


def attend_kernel(places, pair_ref, out_bias_ref, ln2_ref, tok, qkv, *refs):
    pieces, refs = refs[:4], refs[4:]
    prob_out, mixed_out, hidden_out, normed_out, buf0, buf1, tok_ref, qkv_ref = refs[:8]
    prob_ref, mixed_ref, hidden_ref, normed_ref, sem, out_sem = refs[8:]
    start(qkv, qkv_ref, sem.at[2])
    start(tok, tok_ref, sem.at[3])
    for part, buf in ((0, buf0), (1, buf1)):
        fetch_part(places, part, pieces, buf, sem.at[part], slice(PART, 2048))
    low, near, far = lane_marks()
    near, far = near * 0.125, far * 0.125
    wait(qkv_ref, sem.at[2])

    @pl.loop(0, 8)
    def _(pair):
        part = lax.div(pair, 4)
        begin = pl.multiple_of(lax.rem(pair, 4) * 128, 128)
        lanes = pl.ds(pl.multiple_of(pair * 128, 128), 128)
        for block in range(TOK // BLOCK):
            rows = slice(block * BLOCK, (block + 1) * BLOCK)
            query = qkv_ref[part, rows, pl.ds(begin, 128)]
            key = qkv_ref[part, rows, pl.ds(begin + HALF, 128)]
            value = qkv_ref[part, rows, pl.ds(begin + 2 * HALF, 128)]
            bias = pair_ref[block]
            score = dot_t(jnp.concatenate([query * near, query * far], axis=0), key) + jnp.concatenate([bias, bias], axis=0)
            power = jnp.exp(score - jnp.max(score, axis=-1, keepdims=True))
            prob = (power * (1.0 / jnp.sum(power, axis=-1, keepdims=True))).astype(BF16)
            prob_ref[pair, block] = prob
            both = dot(prob, value)
            mixed_ref[rows, lanes] = jnp.where(low, both[:BLOCK], both[BLOCK:]).astype(BF16)

    start(prob_ref, prob_out, out_sem)
    start(mixed_ref, mixed_out, out_sem)
    wait(tok_ref, sem.at[3])
    for part, buf in ((0, buf0), (1, buf1)):
        cols = slice(part * HALF, (part + 1) * HALF)
        wait(buf, sem.at[part])
        hidden_ref[:, cols] = tok_ref[:, cols].astype(F32) + dot(mixed_ref[...], matrix(buf)[...]) + out_bias_ref[:, cols]
    start(hidden_ref, hidden_out, out_sem)

    @pl.loop(0, TOK // 128)
    def _(i):
        rows = pl.ds(i * 128, 128)
        unit, _ = normed(hidden_ref[rows, :])
        normed_ref[rows, :] = (unit * ln2_ref[0:1, :] + ln2_ref[1:2, :]).astype(BF16)

    start(normed_ref, normed_out, out_sem)
    for ref in (prob_ref, mixed_ref, hidden_ref, normed_ref):
        wait(ref, out_sem)


def attend(places, tokens, pair_bias, qkv, out_bias, ln2, pieces):
    outs = [((8, 4, 2 * BLOCK, BLOCK), BF16), ((TOK, WIDTH), BF16), ((TOK, WIDTH), F32), ((TOK, WIDTH), BF16)]
    return pl.pallas_call(
        attend_kernel,
        in_specs=[SMEM] + [VMEM] * 3 + [HBM] * 6,
        out_specs=[HBM] * 4,
        out_shape=[jax.ShapeDtypeStruct(*out) for out in outs],
        scratch_shapes=[parts_buffer(HALF), parts_buffer(HALF), pltpu.VMEM((TOK, WIDTH), BF16), pltpu.VMEM((2, TOK, PART), BF16)]
        + [pltpu.VMEM(*out) for out in outs]
        + [FEW, ONE],
        compiler_params=pltpu.CompilerParams(vmem_limit_bytes=ROOM),
        cost_estimate=work(16e9),
        name="attend",
    )(places, pair_bias, out_bias.reshape(1, WIDTH), ln2, tokens, qkv, *pieces)


def turn(hidden_ref, gain_ref, gc_ref, got_ref, grad_ref, ghid_ref, glow_ref, vec_ref):
    vec_ref[...] = jnp.zeros_like(vec_ref)

    @pl.loop(0, TOK // 128)
    def _(part):
        rows = pl.ds(part * 128, 128)
        unit, scale = normed(hidden_ref[rows, :])
        gc = gc_ref[rows, :] + got_ref[rows, :].astype(F32)
        gout = grad_ref[rows, :].astype(F32)
        ghid = gout + norm_back(gc * gain_ref[...], unit, scale)
        ghid_ref[rows, :] = ghid
        glow_ref[rows, :] = ghid.astype(BF16)
        vec_ref[0:1, :] += jnp.sum(ghid, axis=0, keepdims=True)
        vec_ref[1:2, :] += jnp.sum(gc * unit, axis=0, keepdims=True)
        vec_ref[2:3, :] += jnp.sum(gc, axis=0, keepdims=True)
        vec_ref[3:4, :] += jnp.sum(gout, axis=0, keepdims=True)


TURN_SHAPES = [((TOK, WIDTH), F32), ((TOK, WIDTH), F32), ((TOK, WIDTH), BF16), ((TOK, WIDTH), BF16)]


def back_kernel(part, places, low_in, qkv_in, prob_in, mixed_in, *refs):
    pieces, refs = refs[:4], refs[4:]
    if part == 0:
        gain_ref, turn_in, refs = refs[0], refs[1:5], refs[5:]
        sum_ref, vec_ref, gqkv_out, *outs = refs[:7]
        ghid_out, glow_out = refs[7:9]
        turn_refs, refs = refs[9:13], refs[13:]
        ghid_ref, refs = refs[0], refs[1:]
    else:
        glow_in, refs = refs[0], refs[1:]
        sum_ref, gqkv_out, *outs = refs[:6]
        refs = refs[6:]
    low_ref, qkv_ref, prob_ref, mixed_ref, glow_ref, buf, side_buf, grad_buf, gmix_ref, gqkv_ref, flip, sem, out_sem = refs
    tail = slice(PART, 2048)
    if part == 0:
        for source, target in zip(turn_in, turn_refs):
            start(source, target, sem.at[0])
    else:
        start(glow_in, glow_ref, sem.at[0])
    start(mixed_in, mixed_ref, sem.at[1])
    fetch_part(places, part, pieces, buf, sem.at[2], tail)
    fetch_part(places, 1 - part, pieces, side_buf, sem.at[3], tail)
    start(qkv_in.at[part], qkv_ref, sem.at[4])
    start(prob_in.at[pl.ds(part * 4, 4)], prob_ref, sem.at[4])
    start(low_in, low_ref, sem.at[5])
    wait(mixed_ref, sem.at[1])
    flip[...] = mixed_ref[...].T
    if part == 0:
        for ref in turn_refs:
            wait(ref, sem.at[0])
        turn(turn_refs[0], gain_ref, turn_refs[1], turn_refs[2], turn_refs[3], ghid_ref, glow_ref, vec_ref)
        start(ghid_ref, ghid_out, out_sem)
        start(glow_ref, glow_out, out_sem)
    else:
        wait(glow_ref, sem.at[0])
    heads = slice(part * HALF, (part + 1) * HALF)
    rest = slice((1 - part) * HALF, (2 - part) * HALF)
    grad_matrix = matrix(grad_buf)
    grad_matrix[:, PART:] = dot(flip[...], glow_ref[:, heads]).astype(BF16)
    wait(buf, sem.at[2])
    wait(side_buf, sem.at[3])
    gmix_ref[...] = (
        dot_t(glow_ref[:, heads], matrix(buf)[heads, :]) + dot_t(glow_ref[:, rest], matrix(side_buf)[heads, :])
    ).astype(BF16)
    wait(low_ref, sem.at[5])
    flip[...] = low_ref[...].T
    wait(qkv_ref, sem.at[4])
    wait(prob_ref, sem.at[4])
    low, near, far = lane_marks()

    @pl.loop(0, 4)
    def _(pair):
        begin = pl.multiple_of(pair * 128, 128)
        for block in range(TOK // BLOCK):
            rows = slice(block * BLOCK, (block + 1) * BLOCK)
            query = qkv_ref[rows, pl.ds(begin, 128)]
            key = qkv_ref[rows, pl.ds(begin + HALF, 128)]
            value = qkv_ref[rows, pl.ds(begin + 2 * HALF, 128)]
            gmix = gmix_ref[rows, pl.ds(begin, 128)]
            gmix = jnp.concatenate([gmix * near, gmix * far], axis=0)
            query = jnp.concatenate([query * (near * 0.125), query * (far * 0.125)], axis=0)
            prob_low = prob_ref[pair, block]
            prob = prob_low.astype(F32)
            gprob = dot_t(gmix, value)
            gscore = (prob * (gprob - jnp.sum(prob * gprob, axis=-1, keepdims=True))).astype(BF16)
            both = dot(gscore, key) * 0.125
            gqkv_ref[rows, pl.ds(begin, 128)] = jnp.where(low, both[:BLOCK], both[BLOCK:]).astype(BF16)
            gqkv_ref[rows, pl.ds(begin + HALF, 128)] = dot(gscore.T, query).astype(BF16)
            gqkv_ref[rows, pl.ds(begin + 2 * HALF, 128)] = dot(prob_low.T, gmix).astype(BF16)

    start(gqkv_ref, gqkv_out, out_sem)
    for n in range(3):
        cols = slice(n * HALF, (n + 1) * HALF)
        grad_matrix[:, cols] = dot(flip[...], gqkv_ref[:, cols]).astype(BF16)
    for side, slot, at, c in row_tiles(places, "zx"[part]):
        source = grad_buf.at[at, :, c] if part == 0 else grad_buf.at[:, :, c, pl.ds(pl.multiple_of(at * 16, 16), 16)]
        start(source, outs[2 * side + slot // 2].at[slot % 2], out_sem)
    sum_ref[...] = jnp.sum(gqkv_ref[...].astype(F32), axis=0, keepdims=True)
    wait(grad_buf, out_sem)
    wait(gqkv_ref, out_sem)
    if part == 0:
        wait(ghid_ref, out_sem)
        wait(glow_ref, out_sem)


def back(part, places, low, qkv, prob, mixed, pieces, *more):
    first = part == 0
    tile = shape(2, 2, 64, 2048) if first else shape(2, 4, 2, 16, 2048)
    wide = pltpu.VMEM((TOK, WIDTH), BF16)
    return pl.pallas_call(
        functools.partial(back_kernel, part),
        in_specs=[SMEM] + [HBM] * 8 + ([VMEM] + [HBM] * 4 if first else [HBM]),
        out_specs=[VMEM] * (2 if first else 1) + [HBM] * (7 if first else 5),
        out_shape=[shape(1, PART, dtype=F32)]
        + ([shape(8, WIDTH, dtype=F32)] if first else [])
        + [shape(TOK, PART), tile, tile, tile, tile]
        + ([shape(TOK, WIDTH, dtype=F32), shape(TOK, WIDTH)] if first else []),
        scratch_shapes=([pltpu.VMEM(*s) for s in TURN_SHAPES] + [pltpu.VMEM((TOK, WIDTH), F32)] if first else [])
        + [
            wide,
            pltpu.VMEM((TOK, PART), BF16),
            pltpu.VMEM((4, 4, 2 * BLOCK, BLOCK), BF16),
            wide,
            wide,
            parts_buffer(HALF),
            parts_buffer(HALF),
            parts_buffer(2048),
            pltpu.VMEM((TOK, HALF), BF16),
            pltpu.VMEM((TOK, PART), BF16),
            pltpu.VMEM((WIDTH, TOK), BF16),
            FEW,
            ONE,
        ],
        compiler_params=pltpu.CompilerParams(vmem_limit_bytes=ROOM),
        cost_estimate=work(20e9),
        name="back" + str(part),
    )(places, low, qkv, prob, mixed, *pieces, *more)


def end_kernel(places, ln1_ref, down_bias_ref, sum0_ref, sum1_ref, vec2_ref, up_bias_grad_ref,
               gqkv0, gqkv1, ghid, tok, hidden, feed, feed_got, *refs):
    pieces, refs = refs[:4], refs[4:]
    gin_out, out_out, vec_ref, buf0, buf1, gqkv0_ref, gqkv1_ref, ghid_ref, tok_ref, hidden_ref, feed_ref, got_ref, out_ref, total, sem, out_sem = refs
    start(gqkv0, gqkv0_ref, sem.at[0])
    fetch_part(places, 0, pieces, buf0, sem.at[0], slice(0, PART))
    start(gqkv1, gqkv1_ref, sem.at[1])
    fetch_part(places, 1, pieces, buf1, sem.at[1], slice(0, PART))
    start(ghid, ghid_ref, sem.at[2])
    start(tok, tok_ref, sem.at[2])
    for source, target in ((hidden, hidden_ref), (feed, feed_ref), (feed_got, got_ref)):
        start(source, target, sem.at[3])
    vec_ref[...] = jnp.zeros_like(vec_ref)
    for part, ref in ((0, sum0_ref), (1, sum1_ref)):
        for row, n in ((2, 0), (3, 2)):
            vec_ref[row : row + 1, part * HALF : (part + 1) * HALF] = ref[:, n * HALF : (n + 1) * HALF]
    vec_ref[4:8, :] = vec2_ref[0:4, :]
    for block in range(16):
        row, col = 8 + block // 4, block % 4 * UNIT
        vec_ref[row : row + 1, col : col + UNIT] = up_bias_grad_ref[block]
    wait(gqkv0_ref, sem.at[0])
    wait(buf0, sem.at[0])
    total[...] = dot_t(gqkv0_ref[...], matrix(buf0)[...])
    wait(gqkv1_ref, sem.at[1])
    wait(buf1, sem.at[1])
    total[...] += dot_t(gqkv1_ref[...], matrix(buf1)[...])
    wait(ghid_ref, sem.at[2])
    wait(tok_ref, sem.at[2])

    @pl.loop(0, TOK // 128)
    def _(i):
        rows = pl.ds(i * 128, 128)
        unit, scale = normed(tok_ref[rows, :].astype(F32))
        grad = total[rows, :]
        ghid_ref[rows, :] += norm_back(grad * ln1_ref[0:1, :], unit, scale)
        vec_ref[0:1, :] += jnp.sum(grad * unit, axis=0, keepdims=True)
        vec_ref[1:2, :] += jnp.sum(grad, axis=0, keepdims=True)

    start(ghid_ref, gin_out, out_sem)
    for ref in (hidden_ref, feed_ref, got_ref):
        wait(ref, sem.at[3])
    out_ref[...] = (hidden_ref[...] + feed_ref[...] + got_ref[...].astype(F32) + down_bias_ref[...]).astype(BF16)
    start(out_ref, out_out, out_sem)
    wait(ghid_ref, out_sem)
    wait(out_ref, out_sem)


def end(places, ln1, down_bias, vectors, gqkv0, gqkv1, ghid, tokens, hidden, feed, feed_got, pieces):
    low, high = pltpu.VMEM((TOK, WIDTH), BF16), pltpu.VMEM((TOK, WIDTH), F32)
    heads = pltpu.VMEM((TOK, PART), BF16)
    return pl.pallas_call(
        end_kernel,
        in_specs=[SMEM] + [VMEM] * 6 + [HBM] * 7 + [HBM] * 4,
        out_specs=[HBM] * 2 + [VMEM],
        out_shape=[shape(TOK, WIDTH, dtype=F32), shape(TOK, WIDTH), shape(16, WIDTH, dtype=F32)],
        scratch_shapes=[parts_buffer(PART), parts_buffer(PART), heads, heads, high, low, high, high, low, low, high, FEW, ONE],
        compiler_params=pltpu.CompilerParams(vmem_limit_bytes=ROOM),
        cost_estimate=work(10e9),
        name="end",
    )(places, ln1, down_bias.reshape(1, WIDTH), *vectors, gqkv0, gqkv1, ghid, tokens, hidden, feed, feed_got, *pieces)


AXES = ("z", "yh", "c", "x", "yl")
ALONG_Y, PLANE_XY, PLANE_ZY = ("yh", "yl"), ("yh", "x", "yl"), ("z", "yh", "yl")


def device_number(place):
    return (
        ((place["z"] * 2 + place["y"] // 2) * 2 + place["c"]) * 4 + place["x"]
    ) * 2 + place["y"] % 2


def exchange_pairs(axis, second, alike=False):
    pairs = []
    for z, y, c, x in itertools.product(range(4), range(4), range(2), range(4)):
        here = {"z": z, "y": y, "c": c, "x": x}
        mask = 1 if (c == 0 or alike) != second else 3
        there = dict(here)
        there[axis] = here[axis] ^ mask
        pairs.append((device_number(here), device_number(there)))
    return pairs


def swap_axis(values, axis, second, alike=False):
    return lax.ppermute(values, AXES, exchange_pairs(axis, second, alike))


def swap_core(values):
    return lax.ppermute(values, "c", [(0, 1), (1, 0)])


def position(axis):
    if axis == "y":
        return lax.axis_index("yh") * 2 + lax.axis_index("yl")
    return lax.axis_index(axis)


def distance_of(core, slot):
    return jnp.where(core == 0, slot ^ (slot >> 1), ((slot << 1) & 3) ^ ((slot ^ (slot >> 1)) & 1))


def place_table():
    core, slots = lax.axis_index("c"), jnp.arange(4, dtype=jnp.int32)
    rows = [
        distance_of(side, slots) ^ position(axis)
        for side in (core, 1 - core)
        for axis in ("x", "y", "z")
    ]
    return jnp.concatenate(rows + [jnp.full((8,), core, jnp.int32)])


def add(left, right, dtype=BF16):
    return (left.astype(F32) + right.astype(F32)).astype(dtype)


def halves(own, got):
    count = own.shape[0] // 2
    return add(own[count:], got[count:]), add(own[:count], got[:count])


def spread(values, axes):
    return lax.all_to_all(jnp.broadcast_to(values, (16,) + values.shape), axes, 0, 0)


def spread_back(values, axes):
    return lax.all_to_all(values, axes, 0, 0)


def together(*values):
    return lax.optimization_barrier(values)


def pair_bias(clip_ids):
    clips = clip_ids.reshape(-1, BLOCK)
    row = lax.broadcasted_iota(jnp.int32, (BLOCK, BLOCK), 0)
    col = lax.broadcasted_iota(jnp.int32, (BLOCK, BLOCK), 1)
    allowed = (clips[:, :, None] == clips[:, None, :]) & (row >= col)[None]
    return jnp.where(allowed, 0.0, -1e30).astype(F32)


def on_device(
    tokens,
    qkv_weight,
    out_weight,
    up_weight,
    down_weight,
    ln1_gain,
    ln1_bias,
    q_bias,
    v_bias,
    out_bias,
    ln2_gain,
    ln2_bias,
    up_bias,
    down_bias,
    segment_ids,
    cotangent,
):
    places = place_table()
    ln1 = jnp.stack([ln1_gain, ln1_bias])
    nothing = jnp.zeros((HALF,), F32)
    qkv_bias = jnp.stack(
        [
            jnp.concatenate([q_bias[cols], nothing, v_bias[cols]])[None]
            for cols in (slice(0, HALF), slice(HALF, WIDTH))
        ]
    )
    ln2 = jnp.stack([ln2_gain, ln2_bias])
    allowed = pair_bias(segment_ids)

    heads = qkv_weight.reshape(8, 3, WIDTH)
    pieces = []
    for cols in (slice(0, HALF), slice(HALF, WIDTH)):
        pieces += [heads[:, :, cols].reshape(8, PART), out_weight[:, cols]]
    def join(pairs):
        return together(*[jnp.concatenate(pair) for pair in pairs])

    rows = spread(jnp.concatenate(pieces, axis=1), PLANE_XY)
    down, up = down_weight[None], up_weight[None]
    down, up = join(((down, swap_axis(down, "z", False)), (up, swap_axis(up, "z", False))))
    rows, down_got, up_got, places, ln1, ln2, qkv_bias, allowed = together(
        rows, swap_axis(down, "z", True), swap_axis(up, "z", True), places, ln1, ln2, qkv_bias, allowed
    )
    rows = rows.reshape(1, 2, 64, 4096)
    rows_got = swap_axis(rows, "z", False)
    down, up = join(((down, down_got), (up, up_got)))
    down, up = join(((down, swap_axis(down, "x", False)), (up, swap_axis(up, "y", False))))
    rows_got, down_got, up_got, grad_other = together(
        rows_got, swap_axis(down, "x", True), swap_axis(up, "y", True), swap_core(cotangent)
    )
    rows, down, up = join(((rows, rows_got), (down, down_got), (up, up_got)))
    up = lax.all_gather(up, "x", axis=0).reshape(64, 128, 256)
    rows_got, down_got, other_rows = together(
        swap_axis(rows, "z", True), swap_axis(down, "y", False), swap_core(rows)
    )
    pieces = (rows, rows_got, other_rows, swap_core(rows_got))
    (down,) = join(((down, down_got),))
    down_got = swap_axis(down, "y", True)

    low, qkv = project(places, tokens, ln1, qkv_bias, pieces)
    prob, mixed, hidden, low2 = attend(
        places, tokens, allowed, qkv, out_bias, ln2, pieces
    )
    up_bias_grad, feed, feed_low, gc, gc_low, dup, keep_down, move_down = ffn(
        places, up_bias, low2, swap_core(low2), cotangent, grad_other, (up, down, down_got)
    )
    dup = lax.psum_scatter(dup, "x", scatter_dimension=0, tiled=True)[0]

    down_got = swap_axis(move_down, "y", True)
    sum0, vec2, gqkv0, *main_a, ghid, glow = back(
        0, places, low, qkv, prob, mixed, pieces,
        ln2_gain.reshape(1, WIDTH), hidden, gc, swap_core(gc_low), cotangent,
    )
    swapped_a, down_got, glow = together(swap_core(main_a[3]), down_got, glow)
    move_a = add(main_a[1], swapped_a)
    move_a, glow = together(move_a, glow)
    got_a, got_keep_a = swap_axis(move_a, "z", True), swap_core(main_a[2])
    sum1, gqkv1, *main_b = back(1, places, low, qkv, prob, mixed, pieces, glow)
    got_a, got_keep_a, dup, gqkv1, *main_b = together(got_a, got_keep_a, dup, gqkv1, *main_b)

    swapped_b, got_keep_b = swap_core(main_b[3]), swap_core(main_b[2])
    dup = lax.psum_scatter(dup, ALONG_Y, scatter_dimension=0, tiled=True)[0]
    move_a, keep_a = halves(add(main_a[0], got_keep_a), got_a)
    got_a = swap_axis(move_a, "z", False)
    move_b = add(main_b[1], swapped_b)
    move_b, down_got, keep_down = together(move_b, down_got, keep_down)
    got_b = swap_axis(move_b, "x", True)
    move_down, keep_down = halves(keep_down, down_got)
    down_got = swap_axis(move_down, "y", False)
    grad_tokens, output, vector = end(
        places, ln1, down_bias, (sum0, sum1, vec2, up_bias_grad),
        gqkv0, gqkv1, ghid, tokens, hidden, feed, swap_core(feed_low), pieces,
    )
    got_b, got_a, down_got, got_keep_b, dup, vector = together(got_b, got_a, down_got, got_keep_b, dup, vector)

    dup = lax.psum_scatter(dup, "z", scatter_dimension=0, tiled=True)[0]
    move_b, keep_b = halves(add(main_b[0], got_keep_b), got_b)
    got_b = swap_axis(move_b, "x", False)
    row_a = spread_back(add(keep_a, got_a).reshape(16, 8, 2048), PLANE_XY)
    move_down, keep_down = halves(keep_down, down_got)
    down_got = swap_axis(move_down, "z", True)
    vector = vector + swap_core(vector)
    vector = vector + swap_axis(vector, "x", False, True)
    got_b, row_a, down_got, vector_got = together(got_b, row_a, down_got, swap_axis(vector, "x", True, True))

    vector = (vector + vector_got)[:12].reshape(6, 2048)
    high = lax.reduce_precision(vector, 8, 7)
    terms = jnp.concatenate([high, vector - high, jnp.zeros((4, 2048), F32)]).astype(BF16)
    row_b = jnp.concatenate(
        [add(keep_b, got_b).reshape(16, 8, 2048), jnp.broadcast_to(terms, (16, 16, 2048))], axis=1
    )
    move_down, keep_down = halves(keep_down, down_got)
    row_b, move_down = together(row_b, move_down)
    row_b = spread_back(row_b, PLANE_ZY)
    down_got = swap_axis(move_down, "z", False)
    for second in (True, False):
        move_down, keep_down = halves(keep_down, down_got)
        down_got = swap_axis(move_down, "x", second)
    up_grad = dup.astype(F32)
    down_grad = add(keep_down, down_got, F32)[0]
    row_a, row_b = [jnp.sum(r.astype(F32), axis=0) for r in (row_a, row_b)]
    vector = row_b[8:14] + row_b[14:20]
    row = jnp.stack([row_a, row_b[:8]], axis=1)
    qkv_grad = row[:, :, :PART].reshape(8, 2, 3, HALF).transpose(0, 2, 1, 3).reshape(8, 3 * WIDTH)
    out_grad = row[:, :, PART:].reshape(8, WIDTH)
    summed = vector.reshape(-1)
    vectors = [summed[i * WIDTH : (i + 1) * WIDTH] for i in range(8)]
    return (
        output,
        grad_tokens,
        qkv_grad,
        out_grad,
        up_grad,
        down_grad,
        *vectors[:7],
        summed[8 * WIDTH :],
        vectors[7],
    )


def solution(mesh):
    fine = Mesh(mesh.devices.reshape(4, 2, 2, 4, 2), AXES)
    every, hidden, model = AXES, ("z", "yh", "c"), ("x", "yl")
    weights = (P(every, None), P(every, None), P(model, hidden), P(hidden, model))
    return jax.shard_map(
        on_device,
        mesh=fine,
        in_specs=(P(every, None), *weights, *[P()] * 9, P(every), P(every, None)),
        out_specs=(P(every, None), P(every, None), *weights, *[P()] * 9),
        check_vma=False,
    )
```

```python
import functools
import itertools

import jax
import jax.numpy as jnp
from jax import lax
from jax.experimental import pallas as pl
from jax.experimental.pallas import tpu as pltpu
from jax.sharding import Mesh, PartitionSpec as P

F32, BF16 = jnp.float32, jnp.bfloat16
TOK, WIDTH, FF = 512, 1024, 4096
BOTH = 2 * TOK
CHUNK = 1024
UNIT = 256
ROOT = 0.7978845608028654
CUBE = 0.044715
VMEM, ANY, HBM, SMEM = (
    pl.BlockSpec(memory_space=kind) for kind in (pltpu.VMEM, pl.ANY, pltpu.HBM, pltpu.SMEM)
)
ROOM = 60 * 2**20
ONE = pltpu.SemaphoreType.DMA
TWO = pltpu.SemaphoreType.DMA((2,))
FEW = pltpu.SemaphoreType.DMA((8,))


def shape(*dims, dtype=BF16):
    return jax.ShapeDtypeStruct(dims, dtype)


def work(flops):
    return pl.CostEstimate(flops=int(flops * 0.4), bytes_accessed=1 << 20, transcendentals=0)


def dot(a, b):
    return lax.dot_general(a, b, (((1,), (0,)), ((), ())), preferred_element_type=F32)


def dot_t(a, b):
    return lax.dot_general(a, b, (((1,), (1,)), ((), ())), preferred_element_type=F32)


def normed(values):
    center = values - jnp.mean(values, axis=-1, keepdims=True)
    scale = lax.rsqrt(jnp.mean(center * center, axis=-1, keepdims=True) + 1e-05)
    return center * scale, scale


def norm_back(edge, unit, scale):
    return (edge - jnp.mean(edge, axis=-1, keepdims=True) - unit * jnp.mean(edge * unit, axis=-1, keepdims=True)) * scale


def start(source, target, sem):
    pltpu.make_async_copy(source, target, sem).start()


def wait(ref, sem):
    pltpu.make_async_copy(ref, ref, sem).wait()


def place_of(places, side, axis, slot):
    return places[side * 12 + "xyz".index(axis) * 4 + slot]


def ffn_kernel(places, bias_ref, low_own, low_other, grad_own, grad_other, up, down_low, down_high,
               bias_grad_ref, feed_ref, feed_low_ref, gc_ref, gc_low_ref, dup, ddown_keep, ddown_move,
               up_buf, down_buf, dup_buf, ddown_buf, low, grad, low_t, act_buf, gpre_buf, total, grad_total,
               feed_low, gc_low, in_sem, up_sem, down_sem, out_sem):
    core = places[24]

    def tiles(chunk, *parts):
        for part in parts or (0, 1):
            for sy in range(4):
                y = place_of(places, 0, "y", sy)
                yh, yl = lax.div(y, 2), lax.rem(y, 2)
                unit = pl.ds(pl.multiple_of((part * 2 + yh) * UNIT, UNIT), UNIT)
                for x in range(4):
                    yield sy, chunk * 2 + part, x, yl, unit

    def model(x, yl):
        return pl.ds(pl.multiple_of((x * 2 + yl) * 128, 128), 128)

    def fetch(chunk):
        for sy, sz, x, yl, unit in tiles(chunk):
            start(up.at[x * 16 + sy * 4 + sz], up_buf.at[chunk, model(x, yl), unit], up_sem.at[chunk])
        for sy, sz, sx, yl, unit in tiles(chunk):
            cols = model(place_of(places, 0, "x", sx), yl)
            start((down_low, down_high)[sy // 2].at[sy % 2 * 16 + sx * 4 + sz], down_buf.at[chunk, unit, cols], down_sem.at[chunk])

    def send(chunk, part):
        for y in range(4):
            for x in range(4):
                unit = slice((part * 2 + y // 2) * UNIT, (part * 2 + y // 2 + 1) * UNIT)
                start(dup_buf.at[chunk, model(x, y % 2), unit], dup.at[x, y, chunk * 2 + part], out_sem)
        for sy, sz, sx, yl, unit in tiles(chunk, part):
            source = ddown_buf.at[chunk, unit, model(place_of(places, 0, "x", sx), yl)]
            start(source, (ddown_keep, ddown_move)[sy // 2].at[sy % 2 * 16 + sz * 4 + sx], out_sem)

    start(low_own, low.at[pl.ds(0, TOK)], in_sem.at[0])
    start(low_other, low.at[pl.ds(TOK, TOK)], in_sem.at[0])
    fetch(0)
    start(grad_own, grad.at[pl.ds(0, TOK)], in_sem.at[1])
    start(grad_other, grad.at[pl.ds(TOK, TOK)], in_sem.at[1])
    fetch(1)
    bias_grad_ref[...] = jnp.zeros_like(bias_grad_ref)
    wait(low, in_sem.at[0])
    low_t[...] = low[...].T
    wait(grad, in_sem.at[1])

    for chunk in (0, 1):
        wait(up_buf.at[chunk], up_sem.at[chunk])
        wait(down_buf.at[chunk], down_sem.at[chunk])
        for n in range(CHUNK // UNIT):
            cols = slice(n * UNIT, (n + 1) * UNIT)
            block = (place_of(places, 0, "z", chunk * 2 + n // 2) * 2 + n % 2) * 2 + core
            pre = dot(low[...], up_buf[chunk, :, cols]) + bias_ref[block]
            gact = dot_t(grad[...], down_buf[chunk, cols, :])
            square = pre * pre
            bend = jnp.tanh(ROOT * (pre + CUBE * square * pre))
            half = 0.5 + 0.5 * bend
            act = (pre * half).astype(BF16)
            slope = half + 0.5 * pre * (1.0 - bend * bend) * (ROOT + 3.0 * ROOT * CUBE * square)
            gpre = (gact * slope).astype(BF16)
            act_buf[:, cols] = act
            gpre_buf[:, cols] = gpre
            bias_grad_ref[block] = jnp.sum(gpre.astype(F32), axis=0, keepdims=True)
            ddown_buf[chunk, cols, :] = dot(act.T, grad[...]).astype(BF16)
            dup_buf[chunk, :, cols] = dot(low_t[...], gpre).astype(BF16)
            if n % 2 == 1:
                send(chunk, n // 2)
        more = dot_t(gpre_buf[...], up_buf[chunk])
        feed = dot(act_buf[...], down_buf[chunk])
        if chunk == 0:
            grad_total[...] = more
            total[...] = feed
        else:
            grad_total[...] += more
            gc_low[...] = grad_total[TOK:, :].astype(BF16)
            start(gc_low, gc_low_ref, out_sem)
            start(grad_total.at[pl.ds(0, TOK)], gc_ref, out_sem)
            total[...] += feed
            feed_low[...] = total[TOK:, :].astype(BF16)
            start(feed_low, feed_low_ref, out_sem)
            start(total.at[pl.ds(0, TOK)], feed_ref, out_sem)
    for ref in (dup_buf, ddown_buf, gc_low, feed_low, grad_total.at[pl.ds(0, TOK)], total.at[pl.ds(0, TOK)]):
        wait(ref, out_sem)


def ffn(places, up_bias, low_own, low_other, grad_own, grad_other, weights):
    big = pltpu.VMEM((2, CHUNK, CHUNK), BF16)
    rows = pltpu.VMEM((BOTH, WIDTH), BF16)
    sums = pltpu.VMEM((BOTH, WIDTH), F32)
    half = pltpu.VMEM((TOK, WIDTH), BF16)
    return pl.pallas_call(
        ffn_kernel,
        in_specs=[SMEM, VMEM] + [HBM] * 7,
        out_specs=[VMEM] + [HBM] * 7,
        out_shape=[
            shape(16, 1, UNIT, dtype=F32),
            shape(TOK, WIDTH, dtype=F32),
            shape(TOK, WIDTH),
            shape(TOK, WIDTH, dtype=F32),
            shape(TOK, WIDTH),
            shape(4, 4, 4, 128, 256),
            shape(32, 256, 128),
            shape(32, 256, 128),
        ],
        scratch_shapes=[
            big, big, big, big, rows, rows, rows,
            pltpu.VMEM((BOTH, CHUNK), BF16),
            pltpu.VMEM((BOTH, CHUNK), BF16),
            sums, sums, half, half, TWO, TWO, TWO, ONE,
        ],
        compiler_params=pltpu.CompilerParams(vmem_limit_bytes=ROOM),
        cost_estimate=work(40e9),
        name="ffn",
    )(places, up_bias.reshape(16, 1, UNIT), low_own, low_other, grad_own, grad_other, *weights)


BLOCK = 128
HALF = 512
PART = 3 * HALF


def row_tiles(places):
    core = places[24]
    for side in (0, 1):
        for slot in range(4):
            yield side, slot, place_of(places, side, "z", slot), core if side == 0 else 1 - core


def part_cols(part, cols):
    return slice(part * 2048 + cols.start, part * 2048 + cols.stop)


def fetch_part(places, part, pieces, buf, sem, cols):
    for side, slot, z, c in row_tiles(places):
        start(pieces[2 * side + slot // 2].at[slot % 2, :, :, part_cols(part, cols)], buf.at[z, :, c], sem)


def matrix(ref):
    return ref.reshape(WIDTH, ref.shape[-1])


def parts_buffer(cols):
    return pltpu.VMEM((4, 2, 2, 64, cols), BF16)


def lane_marks():
    low = lax.broadcasted_iota(jnp.int32, (1, 128), 1) < 64
    return low, jnp.where(low, 1.0, 0.0).astype(BF16), jnp.where(low, 0.0, 1.0).astype(BF16)


def front_kernel(places, ln1_ref, qkv_bias_ref, pair_ref, out_bias_ref, ln2_ref, tok, *refs):
    pieces, refs = refs[:4], refs[4:]
    low_out, qkv_out, prob_out, mixed_out, hidden_out, normed_out, qkv_buf0, qkv_buf1, out_buf0, out_buf1 = refs[:10]
    tok_ref, low_ref, qkv_ref, prob_ref, mixed_ref, hidden_ref, normed_ref, sem, out_sem = refs[10:]
    start(tok, tok_ref, sem.at[4])
    for part, buf in ((0, qkv_buf0), (1, qkv_buf1)):
        fetch_part(places, part, pieces, buf, sem.at[part], slice(0, PART))
    for part, buf in ((0, out_buf0), (1, out_buf1)):
        fetch_part(places, part, pieces, buf, sem.at[2 + part], slice(PART, 2048))
    wait(tok_ref, sem.at[4])

    @pl.loop(0, TOK // 128)
    def _(i):
        rows = pl.ds(i * 128, 128)
        unit, _ = normed(tok_ref[rows, :].astype(F32))
        low_ref[rows, :] = (unit * ln1_ref[0:1, :] + ln1_ref[1:2, :]).astype(BF16)

    start(low_ref, low_out, out_sem)
    for part, buf in ((0, qkv_buf0), (1, qkv_buf1)):
        wait(buf, sem.at[part])
        for n in range(3):
            cols = slice(n * HALF, (n + 1) * HALF)
            qkv_ref[part, :, cols] = (dot(low_ref[...], matrix(buf)[:, cols]) + qkv_bias_ref[part, :, cols]).astype(BF16)
        start(qkv_ref.at[part], qkv_out.at[part], out_sem)
    low, near, far = lane_marks()
    near, far = near * 0.125, far * 0.125

    @pl.loop(0, 8)
    def _(pair):
        part = lax.div(pair, 4)
        begin = pl.multiple_of(lax.rem(pair, 4) * 128, 128)
        lanes = pl.ds(pl.multiple_of(pair * 128, 128), 128)
        for block in range(TOK // BLOCK):
            rows = slice(block * BLOCK, (block + 1) * BLOCK)
            query = qkv_ref[part, rows, pl.ds(begin, 128)]
            key = qkv_ref[part, rows, pl.ds(begin + HALF, 128)]
            value = qkv_ref[part, rows, pl.ds(begin + 2 * HALF, 128)]
            bias = pair_ref[block]
            score = dot_t(jnp.concatenate([query * near, query * far], axis=0), key) + jnp.concatenate([bias, bias], axis=0)
            power = jnp.exp(score - jnp.max(score, axis=-1, keepdims=True))
            prob = (power * (1.0 / jnp.sum(power, axis=-1, keepdims=True))).astype(BF16)
            prob_ref[pair, block] = prob
            both = dot(prob, value)
            mixed_ref[rows, lanes] = jnp.where(low, both[:BLOCK], both[BLOCK:]).astype(BF16)

    start(prob_ref, prob_out, out_sem)
    start(mixed_ref, mixed_out, out_sem)
    for part, buf in ((0, out_buf0), (1, out_buf1)):
        cols = slice(part * HALF, (part + 1) * HALF)
        wait(buf, sem.at[2 + part])
        hidden_ref[:, cols] = tok_ref[:, cols].astype(F32) + dot(mixed_ref[...], matrix(buf)[...]) + out_bias_ref[:, cols]
    start(hidden_ref, hidden_out, out_sem)

    @pl.loop(0, TOK // 128)
    def _(i):
        rows = pl.ds(i * 128, 128)
        unit, _ = normed(hidden_ref[rows, :])
        normed_ref[rows, :] = (unit * ln2_ref[0:1, :] + ln2_ref[1:2, :]).astype(BF16)

    start(normed_ref, normed_out, out_sem)
    for ref in (low_ref, qkv_ref, prob_ref, mixed_ref, hidden_ref, normed_ref):
        wait(ref, out_sem)


def front(places, tokens, ln1, qkv_bias, allowed, out_bias, ln2, pieces):
    wide = ((TOK, WIDTH), BF16)
    outs = [wide, ((2, TOK, PART), BF16), ((8, 4, 2 * BLOCK, BLOCK), BF16), wide, ((TOK, WIDTH), F32), wide]
    return pl.pallas_call(
        front_kernel,
        in_specs=[SMEM] + [VMEM] * 5 + [HBM] * 5,
        out_specs=[HBM] * 6,
        out_shape=[jax.ShapeDtypeStruct(*out) for out in outs],
        scratch_shapes=[parts_buffer(PART)] * 2 + [parts_buffer(HALF)] * 2 + [pltpu.VMEM(*s) for s in [wide] + outs] + [FEW, ONE],
        compiler_params=pltpu.CompilerParams(vmem_limit_bytes=ROOM),
        cost_estimate=work(24e9),
        name="front",
    )(places, ln1, qkv_bias, allowed, out_bias.reshape(1, WIDTH), ln2, tokens, *pieces)


def turn(hidden_ref, gain_ref, gc_ref, got_ref, grad_ref, ghid_ref, glow_ref, vec_ref):
    @pl.loop(0, TOK // 128)
    def _(part):
        rows = pl.ds(part * 128, 128)
        unit, scale = normed(hidden_ref[rows, :])
        gc = gc_ref[rows, :] + got_ref[rows, :].astype(F32)
        gout = grad_ref[rows, :].astype(F32)
        ghid = gout + norm_back(gc * gain_ref[...], unit, scale)
        ghid_ref[rows, :] = ghid
        glow_ref[rows, :] = ghid.astype(BF16)
        vec_ref[4:5, :] += jnp.sum(ghid, axis=0, keepdims=True)
        vec_ref[5:6, :] += jnp.sum(gc * unit, axis=0, keepdims=True)
        vec_ref[6:7, :] += jnp.sum(gc, axis=0, keepdims=True)
        vec_ref[7:8, :] += jnp.sum(gout, axis=0, keepdims=True)


def back_kernel(places, ln1_ref, ln2_gain_ref, down_bias_ref, up_bias_grad_ref,
                hidden, gc, gc_got, cot, mixed, low_in, qkv, prob, tok, feed, feed_got, *refs):
    pieces, refs = refs[:4], refs[4:]
    gin_out, out_out, vec_ref, *outs = refs[:7]
    qkv_buf0, qkv_buf1, out_buf0, out_buf1, grad_buf0, grad_buf1 = refs[7:13]
    hidden_ref, gc_ref, gc_got_ref, cot_ref, mixed_ref, low_ref, qkv_ref, prob_ref, tok_ref, feed_ref, feed_got_ref = refs[13:24]
    ghid_ref, glow_ref, gmix_ref, gqkv_ref, flip, out_ref, sem, out_sem = refs[24:]
    for source, target in ((hidden, hidden_ref), (gc, gc_ref), (gc_got, gc_got_ref), (cot, cot_ref)):
        start(source, target, sem.at[0])
    start(mixed, mixed_ref, sem.at[1])
    for part, buf in ((0, out_buf0), (1, out_buf1)):
        fetch_part(places, part, pieces, buf, sem.at[2], slice(PART, 2048))
    start(qkv, qkv_ref, sem.at[3])
    start(prob, prob_ref, sem.at[3])
    start(low_in, low_ref, sem.at[4])
    for part, buf in ((0, qkv_buf0), (1, qkv_buf1)):
        fetch_part(places, part, pieces, buf, sem.at[5], slice(0, PART))
    for source, target in ((tok, tok_ref), (feed, feed_ref), (feed_got, feed_got_ref)):
        start(source, target, sem.at[6])
    vec_ref[...] = jnp.zeros_like(vec_ref)
    for block in range(16):
        row, col = 8 + block // 4, block % 4 * UNIT
        vec_ref[row : row + 1, col : col + UNIT] = up_bias_grad_ref[block]
    wait(mixed_ref, sem.at[1])
    flip[...] = mixed_ref[...].T
    for ref in (hidden_ref, gc_ref, gc_got_ref, cot_ref):
        wait(ref, sem.at[0])
    turn(hidden_ref, ln2_gain_ref, gc_ref, gc_got_ref, cot_ref, ghid_ref, glow_ref, vec_ref)
    grads = [matrix(grad_buf0), matrix(grad_buf1)]
    for part in (0, 1):
        heads = slice(part * HALF, (part + 1) * HALF)
        grads[part][:, PART:] = dot(flip[...], glow_ref[:, heads]).astype(BF16)
    for buf in (out_buf0, out_buf1):
        wait(buf, sem.at[2])
    gmix_ref[...] = (
        dot_t(glow_ref[:, :HALF], matrix(out_buf0)[...]) + dot_t(glow_ref[:, HALF:], matrix(out_buf1)[...])
    ).astype(BF16)
    wait(low_ref, sem.at[4])
    flip[...] = low_ref[...].T
    wait(qkv_ref, sem.at[3])
    wait(prob_ref, sem.at[3])
    low, near, far = lane_marks()

    for part, grad_buf in ((0, grad_buf0), (1, grad_buf1)):
        @pl.loop(0, 4)
        def _(pair, part=part):
            begin = pl.multiple_of(pair * 128, 128)
            for block in range(TOK // BLOCK):
                rows = slice(block * BLOCK, (block + 1) * BLOCK)
                query = qkv_ref[part, rows, pl.ds(begin, 128)]
                key = qkv_ref[part, rows, pl.ds(begin + HALF, 128)]
                value = qkv_ref[part, rows, pl.ds(begin + 2 * HALF, 128)]
                gmix = gmix_ref[rows, pl.ds(pl.multiple_of(begin + part * HALF, 128), 128)]
                gmix = jnp.concatenate([gmix * near, gmix * far], axis=0)
                query = jnp.concatenate([query * (near * 0.125), query * (far * 0.125)], axis=0)
                prob_low = prob_ref[pair + 4 * part, block]
                prob = prob_low.astype(F32)
                gprob = dot_t(gmix, value)
                gscore = (prob * (gprob - jnp.sum(prob * gprob, axis=-1, keepdims=True))).astype(BF16)
                both = dot(gscore, key) * 0.125
                gqkv_ref[part, rows, pl.ds(begin, 128)] = jnp.where(low, both[:BLOCK], both[BLOCK:]).astype(BF16)
                gqkv_ref[part, rows, pl.ds(begin + HALF, 128)] = dot(gscore.T, query).astype(BF16)
                gqkv_ref[part, rows, pl.ds(begin + 2 * HALF, 128)] = dot(prob_low.T, gmix).astype(BF16)

        for n in range(3):
            cols = slice(n * HALF, (n + 1) * HALF)
            grads[part][:, cols] = dot(flip[...], gqkv_ref[part, :, cols]).astype(BF16)
        for side, slot, z, c in row_tiles(places):
            start(grad_buf.at[z, :, c], outs[2 * side + slot // 2].at[slot % 2, :, :, part * 2048 : (part + 1) * 2048], out_sem)
        heads = slice(part * HALF, (part + 1) * HALF)
        for row, n in ((2, 0), (3, 2)):
            vec_ref[row : row + 1, heads] = jnp.sum(gqkv_ref[part, :, n * HALF : (n + 1) * HALF].astype(F32), axis=0, keepdims=True)

    for ref in (tok_ref, feed_ref, feed_got_ref):
        wait(ref, sem.at[6])
    out_ref[...] = (hidden_ref[...] + feed_ref[...] + feed_got_ref[...].astype(F32) + down_bias_ref[...]).astype(BF16)
    start(out_ref, out_out, out_sem)
    for buf in (qkv_buf0, qkv_buf1):
        wait(buf, sem.at[5])
    gc_ref[...] = dot_t(gqkv_ref[0], matrix(qkv_buf0)[...]) + dot_t(gqkv_ref[1], matrix(qkv_buf1)[...])

    @pl.loop(0, TOK // 128)
    def _(i):
        rows = pl.ds(i * 128, 128)
        unit, scale = normed(tok_ref[rows, :].astype(F32))
        grad = gc_ref[rows, :]
        ghid_ref[rows, :] += norm_back(grad * ln1_ref[0:1, :], unit, scale)
        vec_ref[0:1, :] += jnp.sum(grad * unit, axis=0, keepdims=True)
        vec_ref[1:2, :] += jnp.sum(grad, axis=0, keepdims=True)

    start(ghid_ref, gin_out, out_sem)
    for ref in (grad_buf0, grad_buf1, out_ref, ghid_ref):
        wait(ref, out_sem)


def back(places, ln1, ln2_gain, down_bias, up_bias_grad, streams, pieces):
    wide, high = ((TOK, WIDTH), BF16), ((TOK, WIDTH), F32)
    heads = ((2, TOK, PART), BF16)
    scratch = [high, high, wide, wide, wide, wide, heads, ((8, 4, 2 * BLOCK, BLOCK), BF16), wide, high, wide]
    scratch += [high, wide, wide, heads, ((WIDTH, TOK), BF16), wide]
    rows = shape(2, 2, 64, 4096)
    return pl.pallas_call(
        back_kernel,
        in_specs=[SMEM] + [VMEM] * 4 + [HBM] * 15,
        out_specs=[HBM] * 2 + [VMEM] + [HBM] * 4,
        out_shape=[shape(TOK, WIDTH, dtype=F32), shape(TOK, WIDTH), shape(16, WIDTH, dtype=F32), rows, rows, rows, rows],
        scratch_shapes=[parts_buffer(PART)] * 2 + [parts_buffer(HALF)] * 2 + [parts_buffer(2048)] * 2
        + [pltpu.VMEM(*s) for s in scratch]
        + [FEW, ONE],
        compiler_params=pltpu.CompilerParams(vmem_limit_bytes=ROOM),
        cost_estimate=work(40e9),
        name="back",
    )(places, ln1, ln2_gain.reshape(1, WIDTH), down_bias.reshape(1, WIDTH), up_bias_grad, *streams, *pieces)


AXES = ("z", "yh", "c", "x", "yl")
ALONG_Y, PLANE_XY = ("yh", "yl"), ("yh", "x", "yl")


def device_number(place):
    return (
        ((place["z"] * 2 + place["y"] // 2) * 2 + place["c"]) * 4 + place["x"]
    ) * 2 + place["y"] % 2


def exchange_pairs(axis, second, alike=False):
    pairs = []
    for z, y, c, x in itertools.product(range(4), range(4), range(2), range(4)):
        here = {"z": z, "y": y, "c": c, "x": x}
        mask = 1 if (c == 0 or alike) != second else 3
        there = dict(here)
        there[axis] = here[axis] ^ mask
        pairs.append((device_number(here), device_number(there)))
    return pairs


def swap_axis(values, axis, second, alike=False):
    return lax.ppermute(values, AXES, exchange_pairs(axis, second, alike))


def swap_core(values):
    return lax.ppermute(values, "c", [(0, 1), (1, 0)])


def position(axis):
    if axis == "y":
        return lax.axis_index("yh") * 2 + lax.axis_index("yl")
    return lax.axis_index(axis)


def distance_of(core, slot):
    return jnp.where(core == 0, slot ^ (slot >> 1), ((slot << 1) & 3) ^ ((slot ^ (slot >> 1)) & 1))


def place_table():
    core, slots = lax.axis_index("c"), jnp.arange(4, dtype=jnp.int32)
    rows = [
        distance_of(side, slots) ^ position(axis)
        for side in (core, 1 - core)
        for axis in ("x", "y", "z")
    ]
    return jnp.concatenate(rows + [jnp.full((8,), core, jnp.int32)])


def add(left, right, dtype=BF16):
    return (left.astype(F32) + right.astype(F32)).astype(dtype)


def halves(own, got):
    count = own.shape[0] // 2
    return add(own[count:], got[count:]), add(own[:count], got[:count])


def spread(values, axes):
    return lax.all_to_all(jnp.broadcast_to(values, (16,) + values.shape), axes, 0, 0)


def together(*values):
    return lax.optimization_barrier(values)


def pair_bias(clip_ids):
    clips = clip_ids.reshape(-1, BLOCK)
    row = lax.broadcasted_iota(jnp.int32, (BLOCK, BLOCK), 0)
    col = lax.broadcasted_iota(jnp.int32, (BLOCK, BLOCK), 1)
    allowed = (clips[:, :, None] == clips[:, None, :]) & (row >= col)[None]
    return jnp.where(allowed, 0.0, -1e30).astype(F32)


def on_device(
    tokens,
    qkv_weight,
    out_weight,
    up_weight,
    down_weight,
    ln1_gain,
    ln1_bias,
    q_bias,
    v_bias,
    out_bias,
    ln2_gain,
    ln2_bias,
    up_bias,
    down_bias,
    segment_ids,
    cotangent,
):
    places = place_table()
    ln1 = jnp.stack([ln1_gain, ln1_bias])
    nothing = jnp.zeros((HALF,), F32)
    qkv_bias = jnp.stack(
        [
            jnp.concatenate([q_bias[cols], nothing, v_bias[cols]])[None]
            for cols in (slice(0, HALF), slice(HALF, WIDTH))
        ]
    )
    ln2 = jnp.stack([ln2_gain, ln2_bias])
    allowed = pair_bias(segment_ids)

    heads = qkv_weight.reshape(8, 3, WIDTH)
    pieces = []
    for cols in (slice(0, HALF), slice(HALF, WIDTH)):
        pieces += [heads[:, :, cols].reshape(8, PART), out_weight[:, cols]]
    def join(pairs):
        return together(*[jnp.concatenate(pair) for pair in pairs])

    rows = spread(jnp.concatenate(pieces, axis=1), PLANE_XY)
    down, up = down_weight[None], up_weight[None]
    down, up = join(((down, swap_axis(down, "z", False)), (up, swap_axis(up, "z", False))))
    rows, down_got, up_got, places, ln1, ln2, qkv_bias, allowed = together(
        rows, swap_axis(down, "z", True), swap_axis(up, "z", True), places, ln1, ln2, qkv_bias, allowed
    )
    rows = rows.reshape(1, 2, 64, 4096)
    rows_got = swap_axis(rows, "z", False)
    down, up = join(((down, down_got), (up, up_got)))
    down, up = join(((down, swap_axis(down, "x", False)), (up, swap_axis(up, "y", False))))
    rows_got, down_got, up_got, grad_other = together(
        rows_got, swap_axis(down, "x", True), swap_axis(up, "y", True), swap_core(cotangent)
    )
    rows, down, up = join(((rows, rows_got), (down, down_got), (up, up_got)))
    up = lax.all_gather(up, "x", axis=0).reshape(64, 128, 256)
    rows_got, down_got, other_rows = together(
        swap_axis(rows, "z", True), swap_axis(down, "y", False), swap_core(rows)
    )
    pieces = (rows, rows_got, other_rows, swap_core(rows_got))
    (down,) = join(((down, down_got),))
    down_got = swap_axis(down, "y", True)

    low, qkv, prob, mixed, hidden, low2 = front(
        places, tokens, ln1, qkv_bias, allowed, out_bias, ln2, pieces
    )
    up_bias_grad, feed, feed_low, gc, gc_low, dup, keep_down, move_down = ffn(
        places, up_bias, low2, swap_core(low2), cotangent, grad_other, (up, down, down_got)
    )
    dup = lax.psum_scatter(dup, "x", scatter_dimension=0, tiled=True)[0]

    down_got = swap_axis(move_down, "y", True)
    grad_tokens, output, vector, own_keep, own_move, other_keep, other_move = back(
        places, ln1, ln2_gain, down_bias, up_bias_grad,
        (hidden, gc, swap_core(gc_low), cotangent, mixed, low, qkv, prob, tokens, feed, swap_core(feed_low)),
        pieces,
    )
    down_got, vector, own_keep, own_move, other_keep, other_move = together(
        down_got, vector, own_keep, own_move, other_keep, other_move
    )
    got_move, got_keep, vector_got = swap_core(other_move), swap_core(other_keep), swap_core(vector)
    move = add(own_move, got_move)
    move, down_got, vector, vector_got = together(move, down_got, vector, vector_got)
    got = swap_axis(move, "z", True)
    move_down, keep_down = halves(keep_down, down_got)
    down_got = swap_axis(move_down, "y", False)
    vector = vector + vector_got
    for axis, second in (("z", False), ("z", True)):
        vector = vector + swap_axis(vector, axis, second, True)
    vector_got = swap_axis(vector, "x", False, True)
    got, got_keep, down_got, vector_got, dup = together(got, got_keep, down_got, vector_got, dup)

    move, keep = halves(add(own_keep, got_keep), got)
    move, down_got, vector_got = together(move, down_got, vector_got)
    got = swap_axis(move, "z", False)
    move_down, keep_down = halves(keep_down, down_got)
    down_got = swap_axis(move_down, "z", True)
    dup = lax.psum_scatter(dup, ALONG_Y, scatter_dimension=0, tiled=True)[0]
    vector = vector + vector_got
    vector = vector + swap_axis(vector, "x", True, True)
    vector_got = swap_axis(vector, "y", False, True)
    got, down_got, vector_got = together(got, down_got, vector_got)

    rows_sum = add(keep, got).reshape(16, 8, 4096)
    rows_sum, down_got, vector_got = together(rows_sum, down_got, vector_got)
    rows_parts = lax.all_to_all(rows_sum, PLANE_XY, 0, 0)
    vector = vector + vector_got
    vector = vector + swap_axis(vector, "y", True, True)
    for axis, second in (("z", False), ("x", True), ("x", False)):
        move_down, keep_down = halves(keep_down, down_got)
        down_got = swap_axis(move_down, axis, second)
    up_got = swap_axis(dup[2:], "z", True)
    move_up, keep_up = halves(dup[:2], up_got)
    up_grad = add(keep_up, swap_axis(move_up, "z", False), F32)[0]
    down_grad = add(keep_down, down_got, F32)[0]
    row = jnp.sum(rows_parts.astype(F32), axis=0).reshape(8, 2, 2048)
    qkv_grad = row[:, :, :PART].reshape(8, 2, 3, HALF).transpose(0, 2, 1, 3).reshape(8, 3 * WIDTH)
    out_grad = row[:, :, PART:].reshape(8, WIDTH)
    summed = vector.reshape(-1)
    vectors = [summed[i * WIDTH : (i + 1) * WIDTH] for i in range(8)]
    return (
        output,
        grad_tokens,
        qkv_grad,
        out_grad,
        up_grad,
        down_grad,
        *vectors[:7],
        summed[8 * WIDTH : 12 * WIDTH],
        vectors[7],
    )


def solution(mesh):
    fine = Mesh(mesh.devices.reshape(4, 2, 2, 4, 2), AXES)
    every, hidden, model = AXES, ("z", "yh", "c"), ("x", "yl")
    weights = (P(every, None), P(every, None), P(model, hidden), P(hidden, model))
    return jax.shard_map(
        on_device,
        mesh=fine,
        in_specs=(P(every, None), *weights, *[P()] * 9, P(every), P(every, None)),
        out_specs=(P(every, None), P(every, None), *weights, *[P()] * 9),
        check_vma=False,
    )
```

```python
import functools
import itertools

import jax
import jax.numpy as jnp
from jax import lax
from jax.experimental import pallas as pl
from jax.experimental.pallas import tpu as pltpu
from jax.sharding import Mesh, PartitionSpec as P

F32, BF16 = jnp.float32, jnp.bfloat16
TOK, WIDTH, FF = 512, 1024, 4096
BOTH = 2 * TOK
CHUNK = 1024
UNIT = 256
ROOT = 0.7978845608028654
CUBE = 0.044715
VMEM, ANY, HBM, SMEM = (
    pl.BlockSpec(memory_space=kind) for kind in (pltpu.VMEM, pl.ANY, pltpu.HBM, pltpu.SMEM)
)
ROOM = 60 * 2**20
ONE = pltpu.SemaphoreType.DMA
TWO = pltpu.SemaphoreType.DMA((2,))
FEW = pltpu.SemaphoreType.DMA((8,))


def shape(*dims, dtype=BF16):
    return jax.ShapeDtypeStruct(dims, dtype)


def work(flops):
    return pl.CostEstimate(flops=int(flops * 0.4), bytes_accessed=1 << 20, transcendentals=0)


def dot(a, b):
    return lax.dot_general(a, b, (((1,), (0,)), ((), ())), preferred_element_type=F32)


def dot_t(a, b):
    return lax.dot_general(a, b, (((1,), (1,)), ((), ())), preferred_element_type=F32)


def normed(values):
    center = values - jnp.mean(values, axis=-1, keepdims=True)
    scale = lax.rsqrt(jnp.mean(center * center, axis=-1, keepdims=True) + 1e-05)
    return center * scale, scale


def norm_back(edge, unit, scale):
    return (edge - jnp.mean(edge, axis=-1, keepdims=True) - unit * jnp.mean(edge * unit, axis=-1, keepdims=True)) * scale


def start(source, target, sem):
    pltpu.make_async_copy(source, target, sem).start()


def wait(ref, sem):
    pltpu.make_async_copy(ref, ref, sem).wait()


def place_of(places, side, axis, slot):
    return places[side * 12 + "xyz".index(axis) * 4 + slot]


def ffn_kernel(places, bias_ref, low_own, low_other, grad_own, grad_other, up, down_low, down_high,
               bias_grad_ref, feed_ref, feed_low_ref, gc_ref, gc_low_ref, dup, ddown_keep, ddown_move,
               up_buf, down_buf, dup_buf, ddown_buf, low, grad, low_t, act_buf, gpre_buf, total, grad_total,
               feed_low, gc_low, in_sem, up_sem, down_sem, out_sem):
    core = places[24]

    def tiles(chunk, *parts):
        for part in parts or (0, 1):
            for sy in range(4):
                y = place_of(places, 0, "y", sy)
                yh, yl = lax.div(y, 2), lax.rem(y, 2)
                unit = pl.ds(pl.multiple_of((part * 2 + yh) * UNIT, UNIT), UNIT)
                for x in range(4):
                    yield sy, chunk * 2 + part, x, yl, unit

    def model(x, yl):
        return pl.ds(pl.multiple_of((x * 2 + yl) * 128, 128), 128)

    def fetch(chunk):
        for sy, sz, x, yl, unit in tiles(chunk):
            start(up.at[x * 16 + sy * 4 + sz], up_buf.at[chunk, model(x, yl), unit], up_sem.at[chunk])
        for sy, sz, sx, yl, unit in tiles(chunk):
            cols = model(place_of(places, 0, "x", sx), yl)
            start((down_low, down_high)[sy // 2].at[sy % 2 * 16 + sx * 4 + sz], down_buf.at[chunk, unit, cols], down_sem.at[chunk])

    def send(chunk, part):
        for y in range(4):
            for x in range(4):
                unit = slice((part * 2 + y // 2) * UNIT, (part * 2 + y // 2 + 1) * UNIT)
                start(dup_buf.at[chunk, model(x, y % 2), unit], dup.at[x, y, chunk * 2 + part], out_sem)
        for sy, sz, sx, yl, unit in tiles(chunk, part):
            source = ddown_buf.at[chunk, unit, model(place_of(places, 0, "x", sx), yl)]
            start(source, (ddown_keep, ddown_move)[sy // 2].at[sy % 2 * 16 + sx * 4 + sz], out_sem)

    start(low_own, low.at[pl.ds(0, TOK)], in_sem.at[0])
    start(low_other, low.at[pl.ds(TOK, TOK)], in_sem.at[0])
    fetch(0)
    start(grad_own, grad.at[pl.ds(0, TOK)], in_sem.at[1])
    start(grad_other, grad.at[pl.ds(TOK, TOK)], in_sem.at[1])
    fetch(1)
    bias_grad_ref[...] = jnp.zeros_like(bias_grad_ref)
    wait(low, in_sem.at[0])
    low_t[...] = low[...].T
    wait(grad, in_sem.at[1])

    for chunk in (0, 1):
        wait(up_buf.at[chunk], up_sem.at[chunk])
        wait(down_buf.at[chunk], down_sem.at[chunk])
        for n in range(CHUNK // UNIT):
            cols = slice(n * UNIT, (n + 1) * UNIT)
            block = (place_of(places, 0, "z", chunk * 2 + n // 2) * 2 + n % 2) * 2 + core
            pre = dot(low[...], up_buf[chunk, :, cols]) + bias_ref[block]
            gact = dot_t(grad[...], down_buf[chunk, cols, :])
            square = pre * pre
            bend = jnp.tanh(ROOT * (pre + CUBE * square * pre))
            half = 0.5 + 0.5 * bend
            act = (pre * half).astype(BF16)
            slope = half + 0.5 * pre * (1.0 - bend * bend) * (ROOT + 3.0 * ROOT * CUBE * square)
            gpre = (gact * slope).astype(BF16)
            act_buf[:, cols] = act
            gpre_buf[:, cols] = gpre
            bias_grad_ref[block] = jnp.sum(gpre.astype(F32), axis=0, keepdims=True)
            ddown_buf[chunk, cols, :] = dot(act.T, grad[...]).astype(BF16)
            dup_buf[chunk, :, cols] = dot(low_t[...], gpre).astype(BF16)
            if n % 2 == 1:
                send(chunk, n // 2)
        more = dot_t(gpre_buf[...], up_buf[chunk])
        feed = dot(act_buf[...], down_buf[chunk])
        if chunk == 0:
            grad_total[...] = more
            total[...] = feed
        else:
            grad_total[...] += more
            gc_low[...] = grad_total[TOK:, :].astype(BF16)
            start(gc_low, gc_low_ref, out_sem)
            start(grad_total.at[pl.ds(0, TOK)], gc_ref, out_sem)
            total[...] += feed
            feed_low[...] = total[TOK:, :].astype(BF16)
            start(feed_low, feed_low_ref, out_sem)
            start(total.at[pl.ds(0, TOK)], feed_ref, out_sem)
    for ref in (dup_buf, ddown_buf, gc_low, feed_low, grad_total.at[pl.ds(0, TOK)], total.at[pl.ds(0, TOK)]):
        wait(ref, out_sem)


def ffn(places, up_bias, low_own, low_other, grad_own, grad_other, weights):
    big = pltpu.VMEM((2, CHUNK, CHUNK), BF16)
    rows = pltpu.VMEM((BOTH, WIDTH), BF16)
    sums = pltpu.VMEM((BOTH, WIDTH), F32)
    half = pltpu.VMEM((TOK, WIDTH), BF16)
    return pl.pallas_call(
        ffn_kernel,
        in_specs=[SMEM, VMEM] + [HBM] * 7,
        out_specs=[VMEM] + [HBM] * 7,
        out_shape=[
            shape(16, 1, UNIT, dtype=F32),
            shape(TOK, WIDTH, dtype=F32),
            shape(TOK, WIDTH),
            shape(TOK, WIDTH, dtype=F32),
            shape(TOK, WIDTH),
            shape(4, 4, 4, 128, 256),
            shape(32, 256, 128),
            shape(32, 256, 128),
        ],
        scratch_shapes=[
            big, big, big, big, rows, rows, rows,
            pltpu.VMEM((BOTH, CHUNK), BF16),
            pltpu.VMEM((BOTH, CHUNK), BF16),
            sums, sums, half, half, TWO, TWO, TWO, ONE,
        ],
        compiler_params=pltpu.CompilerParams(vmem_limit_bytes=ROOM),
        cost_estimate=work(40e9),
        name="ffn",
    )(places, up_bias.reshape(16, 1, UNIT), low_own, low_other, grad_own, grad_other, *weights)


BLOCK = 128
HALF = 512
PART = 3 * HALF


def row_tiles(places):
    core = places[24]
    for side in (0, 1):
        for slot in range(4):
            yield side, slot, place_of(places, side, "z", slot), core if side == 0 else 1 - core


def part_cols(part, cols):
    return slice(part * 2048 + cols.start, part * 2048 + cols.stop)


def fetch_part(places, part, pieces, buf, sem, cols):
    for side, slot, z, c in row_tiles(places):
        start(pieces[2 * side + slot // 2].at[slot % 2, :, :, part_cols(part, cols)], buf.at[z, :, c], sem)


def matrix(ref):
    return ref.reshape(WIDTH, ref.shape[-1])


def parts_buffer(cols):
    return pltpu.VMEM((4, 2, 2, 64, cols), BF16)


def lane_marks():
    low = lax.broadcasted_iota(jnp.int32, (1, 128), 1) < 64
    return low, jnp.where(low, 1.0, 0.0).astype(BF16), jnp.where(low, 0.0, 1.0).astype(BF16)


def front_kernel(places, ln1_ref, qkv_bias_ref, pair_ref, out_bias_ref, ln2_ref, tok, *refs):
    pieces, refs = refs[:4], refs[4:]
    low_out, qkv_out, prob_out, mixed_out, hidden_out, normed_out, qkv_buf0, qkv_buf1, out_buf0, out_buf1 = refs[:10]
    tok_ref, low_ref, qkv_ref, prob_ref, mixed_ref, hidden_ref, normed_ref, sem, out_sem = refs[10:]
    start(tok, tok_ref, sem.at[4])
    for part, buf in ((0, qkv_buf0), (1, qkv_buf1)):
        fetch_part(places, part, pieces, buf, sem.at[part], slice(0, PART))
    for part, buf in ((0, out_buf0), (1, out_buf1)):
        fetch_part(places, part, pieces, buf, sem.at[2 + part], slice(PART, 2048))
    wait(tok_ref, sem.at[4])

    @pl.loop(0, TOK // 128)
    def _(i):
        rows = pl.ds(i * 128, 128)
        unit, _ = normed(tok_ref[rows, :].astype(F32))
        low_ref[rows, :] = (unit * ln1_ref[0:1, :] + ln1_ref[1:2, :]).astype(BF16)

    start(low_ref, low_out, out_sem)
    for part, buf in ((0, qkv_buf0), (1, qkv_buf1)):
        wait(buf, sem.at[part])
        for n in range(3):
            cols = slice(n * HALF, (n + 1) * HALF)
            qkv_ref[part, :, cols] = (dot(low_ref[...], matrix(buf)[:, cols]) + qkv_bias_ref[part, :, cols]).astype(BF16)
        start(qkv_ref.at[part], qkv_out.at[part], out_sem)
    low, near, far = lane_marks()
    near, far = near * 0.125, far * 0.125

    @pl.loop(0, 8)
    def _(pair):
        part = lax.div(pair, 4)
        begin = pl.multiple_of(lax.rem(pair, 4) * 128, 128)
        lanes = pl.ds(pl.multiple_of(pair * 128, 128), 128)
        for block in range(TOK // BLOCK):
            rows = slice(block * BLOCK, (block + 1) * BLOCK)
            query = qkv_ref[part, rows, pl.ds(begin, 128)]
            key = qkv_ref[part, rows, pl.ds(begin + HALF, 128)]
            value = qkv_ref[part, rows, pl.ds(begin + 2 * HALF, 128)]
            bias = pair_ref[block]
            score = dot_t(jnp.concatenate([query * near, query * far], axis=0), key) + jnp.concatenate([bias, bias], axis=0)
            power = jnp.exp(score - jnp.max(score, axis=-1, keepdims=True))
            prob = (power * (1.0 / jnp.sum(power, axis=-1, keepdims=True))).astype(BF16)
            prob_ref[pair, block] = prob
            both = dot(prob, value)
            mixed_ref[rows, lanes] = jnp.where(low, both[:BLOCK], both[BLOCK:]).astype(BF16)

    start(prob_ref, prob_out, out_sem)
    start(mixed_ref, mixed_out, out_sem)
    for part, buf in ((0, out_buf0), (1, out_buf1)):
        cols = slice(part * HALF, (part + 1) * HALF)
        wait(buf, sem.at[2 + part])
        hidden_ref[:, cols] = tok_ref[:, cols].astype(F32) + dot(mixed_ref[...], matrix(buf)[...]) + out_bias_ref[:, cols]
    start(hidden_ref, hidden_out, out_sem)

    @pl.loop(0, TOK // 128)
    def _(i):
        rows = pl.ds(i * 128, 128)
        unit, _ = normed(hidden_ref[rows, :])
        normed_ref[rows, :] = (unit * ln2_ref[0:1, :] + ln2_ref[1:2, :]).astype(BF16)

    start(normed_ref, normed_out, out_sem)
    for ref in (low_ref, qkv_ref, prob_ref, mixed_ref, hidden_ref, normed_ref):
        wait(ref, out_sem)


def front(places, tokens, ln1, qkv_bias, allowed, out_bias, ln2, pieces):
    wide = ((TOK, WIDTH), BF16)
    outs = [wide, ((2, TOK, PART), BF16), ((8, 4, 2 * BLOCK, BLOCK), BF16), wide, ((TOK, WIDTH), F32), wide]
    return pl.pallas_call(
        front_kernel,
        in_specs=[SMEM] + [VMEM] * 5 + [HBM] * 5,
        out_specs=[HBM] * 6,
        out_shape=[jax.ShapeDtypeStruct(*out) for out in outs],
        scratch_shapes=[parts_buffer(PART)] * 2 + [parts_buffer(HALF)] * 2 + [pltpu.VMEM(*s) for s in [wide] + outs] + [FEW, ONE],
        compiler_params=pltpu.CompilerParams(vmem_limit_bytes=ROOM),
        cost_estimate=work(24e9),
        name="front",
    )(places, ln1, qkv_bias, allowed, out_bias.reshape(1, WIDTH), ln2, tokens, *pieces)


def turn(hidden_ref, gain_ref, gc_ref, got_ref, grad_ref, ghid_ref, glow_ref, vec_ref):
    @pl.loop(0, TOK // 128)
    def _(part):
        rows = pl.ds(part * 128, 128)
        unit, scale = normed(hidden_ref[rows, :])
        gc = gc_ref[rows, :] + got_ref[rows, :].astype(F32)
        gout = grad_ref[rows, :].astype(F32)
        ghid = gout + norm_back(gc * gain_ref[...], unit, scale)
        ghid_ref[rows, :] = ghid
        glow_ref[rows, :] = ghid.astype(BF16)
        vec_ref[4:5, :] += jnp.sum(ghid, axis=0, keepdims=True)
        vec_ref[5:6, :] += jnp.sum(gc * unit, axis=0, keepdims=True)
        vec_ref[6:7, :] += jnp.sum(gc, axis=0, keepdims=True)
        vec_ref[7:8, :] += jnp.sum(gout, axis=0, keepdims=True)


def back_kernel(places, ln1_ref, ln2_gain_ref, down_bias_ref, up_bias_grad_ref,
                hidden, gc, gc_got, cot, mixed, low_in, qkv, prob, tok, feed, feed_got, *refs):
    pieces, refs = refs[:4], refs[4:]
    gin_out, out_out, vec_ref, *outs = refs[:7]
    qkv_buf0, qkv_buf1, out_buf0, out_buf1, grad_buf0, grad_buf1 = refs[7:13]
    hidden_ref, gc_ref, gc_got_ref, cot_ref, mixed_ref, low_ref, qkv_ref, prob_ref, tok_ref, feed_ref, feed_got_ref = refs[13:24]
    ghid_ref, glow_ref, gmix_ref, gqkv_ref, flip, out_ref, sem, out_sem = refs[24:]
    for source, target in ((hidden, hidden_ref), (gc, gc_ref), (gc_got, gc_got_ref), (cot, cot_ref)):
        start(source, target, sem.at[0])
    start(mixed, mixed_ref, sem.at[1])
    for part, buf in ((0, out_buf0), (1, out_buf1)):
        fetch_part(places, part, pieces, buf, sem.at[2], slice(PART, 2048))
    start(qkv, qkv_ref, sem.at[3])
    start(prob, prob_ref, sem.at[3])
    start(low_in, low_ref, sem.at[4])
    for part, buf in ((0, qkv_buf0), (1, qkv_buf1)):
        fetch_part(places, part, pieces, buf, sem.at[5], slice(0, PART))
    for source, target in ((tok, tok_ref), (feed, feed_ref), (feed_got, feed_got_ref)):
        start(source, target, sem.at[6])
    vec_ref[...] = jnp.zeros_like(vec_ref)
    for block in range(16):
        row, col = 8 + block // 4, block % 4 * UNIT
        vec_ref[row : row + 1, col : col + UNIT] = up_bias_grad_ref[block]
    wait(mixed_ref, sem.at[1])
    flip[...] = mixed_ref[...].T
    for ref in (hidden_ref, gc_ref, gc_got_ref, cot_ref):
        wait(ref, sem.at[0])
    turn(hidden_ref, ln2_gain_ref, gc_ref, gc_got_ref, cot_ref, ghid_ref, glow_ref, vec_ref)
    grads = [matrix(grad_buf0), matrix(grad_buf1)]
    for part in (0, 1):
        heads = slice(part * HALF, (part + 1) * HALF)
        grads[part][:, PART:] = dot(flip[...], glow_ref[:, heads]).astype(BF16)
    for buf in (out_buf0, out_buf1):
        wait(buf, sem.at[2])
    gmix_ref[...] = (
        dot_t(glow_ref[:, :HALF], matrix(out_buf0)[...]) + dot_t(glow_ref[:, HALF:], matrix(out_buf1)[...])
    ).astype(BF16)
    wait(low_ref, sem.at[4])
    flip[...] = low_ref[...].T
    wait(qkv_ref, sem.at[3])
    wait(prob_ref, sem.at[3])
    low, near, far = lane_marks()

    for part, grad_buf in ((0, grad_buf0), (1, grad_buf1)):
        @pl.loop(0, 4)
        def _(pair, part=part):
            begin = pl.multiple_of(pair * 128, 128)
            for block in range(TOK // BLOCK):
                rows = slice(block * BLOCK, (block + 1) * BLOCK)
                query = qkv_ref[part, rows, pl.ds(begin, 128)]
                key = qkv_ref[part, rows, pl.ds(begin + HALF, 128)]
                value = qkv_ref[part, rows, pl.ds(begin + 2 * HALF, 128)]
                gmix = gmix_ref[rows, pl.ds(pl.multiple_of(begin + part * HALF, 128), 128)]
                gmix = jnp.concatenate([gmix * near, gmix * far], axis=0)
                query = jnp.concatenate([query * (near * 0.125), query * (far * 0.125)], axis=0)
                prob_low = prob_ref[pair + 4 * part, block]
                prob = prob_low.astype(F32)
                gprob = dot_t(gmix, value)
                gscore = (prob * (gprob - jnp.sum(prob * gprob, axis=-1, keepdims=True))).astype(BF16)
                both = dot(gscore, key) * 0.125
                gqkv_ref[part, rows, pl.ds(begin, 128)] = jnp.where(low, both[:BLOCK], both[BLOCK:]).astype(BF16)
                gqkv_ref[part, rows, pl.ds(begin + HALF, 128)] = dot(gscore.T, query).astype(BF16)
                gqkv_ref[part, rows, pl.ds(begin + 2 * HALF, 128)] = dot(prob_low.T, gmix).astype(BF16)

        for n in range(3):
            cols = slice(n * HALF, (n + 1) * HALF)
            grads[part][:, cols] = dot(flip[...], gqkv_ref[part, :, cols]).astype(BF16)
        for side, slot, z, c in row_tiles(places):
            start(grad_buf.at[z, :, c], outs[2 * side + slot // 2].at[slot % 2, :, :, part * 2048 : (part + 1) * 2048], out_sem)
        heads = slice(part * HALF, (part + 1) * HALF)
        for row, n in ((2, 0), (3, 2)):
            vec_ref[row : row + 1, heads] = jnp.sum(gqkv_ref[part, :, n * HALF : (n + 1) * HALF].astype(F32), axis=0, keepdims=True)

    for ref in (tok_ref, feed_ref, feed_got_ref):
        wait(ref, sem.at[6])
    out_ref[...] = (hidden_ref[...] + feed_ref[...] + feed_got_ref[...].astype(F32) + down_bias_ref[...]).astype(BF16)
    start(out_ref, out_out, out_sem)
    for buf in (qkv_buf0, qkv_buf1):
        wait(buf, sem.at[5])
    gc_ref[...] = dot_t(gqkv_ref[0], matrix(qkv_buf0)[...]) + dot_t(gqkv_ref[1], matrix(qkv_buf1)[...])

    @pl.loop(0, TOK // 128)
    def _(i):
        rows = pl.ds(i * 128, 128)
        unit, scale = normed(tok_ref[rows, :].astype(F32))
        grad = gc_ref[rows, :]
        ghid_ref[rows, :] += norm_back(grad * ln1_ref[0:1, :], unit, scale)
        vec_ref[0:1, :] += jnp.sum(grad * unit, axis=0, keepdims=True)
        vec_ref[1:2, :] += jnp.sum(grad, axis=0, keepdims=True)

    start(ghid_ref, gin_out, out_sem)
    for ref in (grad_buf0, grad_buf1, out_ref, ghid_ref):
        wait(ref, out_sem)


def back(places, ln1, ln2_gain, down_bias, up_bias_grad, streams, pieces):
    wide, high = ((TOK, WIDTH), BF16), ((TOK, WIDTH), F32)
    heads = ((2, TOK, PART), BF16)
    scratch = [high, high, wide, wide, wide, wide, heads, ((8, 4, 2 * BLOCK, BLOCK), BF16), wide, high, wide]
    scratch += [high, wide, wide, heads, ((WIDTH, TOK), BF16), wide]
    rows = shape(2, 2, 64, 4096)
    return pl.pallas_call(
        back_kernel,
        in_specs=[SMEM] + [VMEM] * 4 + [HBM] * 15,
        out_specs=[HBM] * 2 + [VMEM] + [HBM] * 4,
        out_shape=[shape(TOK, WIDTH, dtype=F32), shape(TOK, WIDTH), shape(16, WIDTH, dtype=F32), rows, rows, rows, rows],
        scratch_shapes=[parts_buffer(PART)] * 2 + [parts_buffer(HALF)] * 2 + [parts_buffer(2048)] * 2
        + [pltpu.VMEM(*s) for s in scratch]
        + [FEW, ONE],
        compiler_params=pltpu.CompilerParams(vmem_limit_bytes=ROOM),
        cost_estimate=work(40e9),
        name="back",
    )(places, ln1, ln2_gain.reshape(1, WIDTH), down_bias.reshape(1, WIDTH), up_bias_grad, *streams, *pieces)


AXES = ("z", "yh", "c", "x", "yl")
ALONG_Y, PLANE_XY = ("yh", "yl"), ("yh", "x", "yl")


def device_number(place):
    return (
        ((place["z"] * 2 + place["y"] // 2) * 2 + place["c"]) * 4 + place["x"]
    ) * 2 + place["y"] % 2


def exchange_pairs(axis, second, alike=False):
    pairs = []
    for z, y, c, x in itertools.product(range(4), range(4), range(2), range(4)):
        here = {"z": z, "y": y, "c": c, "x": x}
        mask = 1 if (c == 0 or alike) != second else 3
        there = dict(here)
        there[axis] = here[axis] ^ mask
        pairs.append((device_number(here), device_number(there)))
    return pairs


def swap_axis(values, axis, second, alike=False):
    return lax.ppermute(values, AXES, exchange_pairs(axis, second, alike))


def swap_core(values):
    return lax.ppermute(values, "c", [(0, 1), (1, 0)])


def position(axis):
    if axis == "y":
        return lax.axis_index("yh") * 2 + lax.axis_index("yl")
    return lax.axis_index(axis)


def distance_of(core, slot):
    return jnp.where(core == 0, slot ^ (slot >> 1), ((slot << 1) & 3) ^ ((slot ^ (slot >> 1)) & 1))


def place_table():
    core, slots = lax.axis_index("c"), jnp.arange(4, dtype=jnp.int32)
    rows = [
        distance_of(side, slots) ^ position(axis)
        for side in (core, 1 - core)
        for axis in ("x", "y", "z")
    ]
    return jnp.concatenate(rows + [jnp.full((8,), core, jnp.int32)])


def add(left, right, dtype=BF16):
    return (left.astype(F32) + right.astype(F32)).astype(dtype)


def halves(own, got):
    count = own.shape[0] // 2
    return add(own[count:], got[count:]), add(own[:count], got[:count])


def spread(values, axes):
    return lax.all_to_all(jnp.broadcast_to(values, (16,) + values.shape), axes, 0, 0)


def together(*values):
    return lax.optimization_barrier(values)


def pair_bias(clip_ids):
    clips = clip_ids.reshape(-1, BLOCK)
    row = lax.broadcasted_iota(jnp.int32, (BLOCK, BLOCK), 0)
    col = lax.broadcasted_iota(jnp.int32, (BLOCK, BLOCK), 1)
    allowed = (clips[:, :, None] == clips[:, None, :]) & (row >= col)[None]
    return jnp.where(allowed, 0.0, -1e30).astype(F32)


def on_device(
    tokens,
    qkv_weight,
    out_weight,
    up_weight,
    down_weight,
    ln1_gain,
    ln1_bias,
    q_bias,
    v_bias,
    out_bias,
    ln2_gain,
    ln2_bias,
    up_bias,
    down_bias,
    segment_ids,
    cotangent,
):
    places = place_table()
    ln1 = jnp.stack([ln1_gain, ln1_bias])
    nothing = jnp.zeros((HALF,), F32)
    qkv_bias = jnp.stack(
        [
            jnp.concatenate([q_bias[cols], nothing, v_bias[cols]])[None]
            for cols in (slice(0, HALF), slice(HALF, WIDTH))
        ]
    )
    ln2 = jnp.stack([ln2_gain, ln2_bias])
    allowed = pair_bias(segment_ids)

    heads = qkv_weight.reshape(8, 3, WIDTH)
    pieces = []
    for cols in (slice(0, HALF), slice(HALF, WIDTH)):
        pieces += [heads[:, :, cols].reshape(8, PART), out_weight[:, cols]]
    def join(pairs):
        return together(*[jnp.concatenate(pair) for pair in pairs])

    rows = spread(jnp.concatenate(pieces, axis=1), PLANE_XY)
    down, up = down_weight[None], up_weight[None]
    down, up = join(((down, swap_axis(down, "z", False)), (up, swap_axis(up, "z", False))))
    rows, down_got, up_got, places, ln1, ln2, qkv_bias, allowed = together(
        rows, swap_axis(down, "z", True), swap_axis(up, "z", True), places, ln1, ln2, qkv_bias, allowed
    )
    rows = rows.reshape(1, 2, 64, 4096)
    rows_got = swap_axis(rows, "z", False)
    down, up = join(((down, down_got), (up, up_got)))
    down, up = join(((down, swap_axis(down, "x", False)), (up, swap_axis(up, "y", False))))
    rows_got, down_got, up_got, grad_other = together(
        rows_got, swap_axis(down, "x", True), swap_axis(up, "y", True), swap_core(cotangent)
    )
    rows, down, up = join(((rows, rows_got), (down, down_got), (up, up_got)))
    up = lax.all_gather(up, "x", axis=0).reshape(64, 128, 256)
    (down,) = join(((down, swap_axis(down, "y", False)),))
    rows_got, down, other_rows = together(swap_axis(rows, "z", True), down, swap_core(rows))
    pieces = (rows, rows_got, other_rows, swap_core(rows_got))
    down_got = swap_axis(down, "y", True)

    low, qkv, prob, mixed, hidden, low2 = front(
        places, tokens, ln1, qkv_bias, allowed, out_bias, ln2, pieces
    )
    up_bias_grad, feed, feed_low, gc, gc_low, dup, keep_down, move_down = ffn(
        places, up_bias, low2, swap_core(low2), cotangent, grad_other, (up, down, down_got)
    )
    dup = lax.psum_scatter(dup, "x", scatter_dimension=0, tiled=True)[0]

    down_got = swap_axis(move_down, "y", True)
    grad_tokens, output, vector, own_keep, own_move, other_keep, other_move = back(
        places, ln1, ln2_gain, down_bias, up_bias_grad,
        (hidden, gc, swap_core(gc_low), cotangent, mixed, low, qkv, prob, tokens, feed, swap_core(feed_low)),
        pieces,
    )
    down_got, vector, own_keep, own_move, other_keep, other_move = together(
        down_got, vector, own_keep, own_move, other_keep, other_move
    )
    got_move, got_keep, vector_got = swap_core(other_move), swap_core(other_keep), swap_core(vector)
    move = add(own_move, got_move)
    move, down_got, vector, vector_got = together(move, down_got, vector, vector_got)
    got = swap_axis(move, "z", True)
    keep = add(own_keep, got_keep)
    move_down, keep_down = halves(keep_down, down_got)
    down_got = swap_axis(move_down, "y", False)
    move_down, keep_down = halves(keep_down, down_got)
    down_got = swap_axis(move_down, "x", True)
    vector = vector + vector_got
    vector = vector + swap_axis(vector, "x", False, True)
    vector_got = swap_axis(vector, "x", True, True)
    got, keep, down_got, vector_got, dup = together(got, keep, down_got, vector_got, dup)

    move, keep = halves(keep, got)
    move, down_got, vector_got = together(move, down_got, vector_got)
    got = swap_axis(move, "z", False)
    move_down, keep_down = halves(keep_down, down_got)
    down_got = swap_axis(move_down, "x", False)
    dup = lax.psum_scatter(dup, ALONG_Y, scatter_dimension=0, tiled=True)[0]
    vector = vector + vector_got
    vector = vector + swap_axis(vector, "y", False, True)
    vector_got = swap_axis(vector, "y", True, True)
    got, down_got, vector_got = together(got, down_got, vector_got)

    rows_sum = add(keep, got).reshape(16, 8, 4096)
    rows_sum, down_got, vector_got = together(rows_sum, down_got, vector_got)
    rows_parts = lax.all_to_all(rows_sum, PLANE_XY, 0, 0)
    vector = vector + vector_got
    for second in (False, True):
        vector = vector + swap_axis(vector, "z", second, True)
    for second in (True, False):
        move_down, keep_down = halves(keep_down, down_got)
        down_got = swap_axis(move_down, "z", second)
    up_got = swap_axis(dup[2:], "z", True)
    move_up, keep_up = halves(dup[:2], up_got)
    up_grad = add(keep_up, swap_axis(move_up, "z", False), F32)[0]
    down_grad = add(keep_down, down_got, F32)[0]
    row = jnp.sum(rows_parts.astype(F32), axis=0).reshape(8, 2, 2048)
    qkv_grad = row[:, :, :PART].reshape(8, 2, 3, HALF).transpose(0, 2, 1, 3).reshape(8, 3 * WIDTH)
    out_grad = row[:, :, PART:].reshape(8, WIDTH)
    summed = vector.reshape(-1)
    vectors = [summed[i * WIDTH : (i + 1) * WIDTH] for i in range(8)]
    return (
        output,
        grad_tokens,
        qkv_grad,
        out_grad,
        up_grad,
        down_grad,
        *vectors[:7],
        summed[8 * WIDTH : 12 * WIDTH],
        vectors[7],
    )


def solution(mesh):
    fine = Mesh(mesh.devices.reshape(4, 2, 2, 4, 2), AXES)
    every, hidden, model = AXES, ("z", "yh", "c"), ("x", "yl")
    weights = (P(every, None), P(every, None), P(model, hidden), P(hidden, model))
    return jax.shard_map(
        on_device,
        mesh=fine,
        in_specs=(P(every, None), *weights, *[P()] * 9, P(every), P(every, None)),
        out_specs=(P(every, None), P(every, None), *weights, *[P()] * 9),
        check_vma=False,
    )
```

```python
import functools
import itertools

import jax
import jax.numpy as jnp
from jax import lax
from jax.experimental import pallas as pl
from jax.experimental.pallas import tpu as pltpu
from jax.sharding import Mesh, PartitionSpec as P

F32, BF16 = jnp.float32, jnp.bfloat16
TOK, WIDTH, FF = 512, 1024, 4096
BOTH = 2 * TOK
CHUNK = 1024
UNIT = 256
ROOT = 0.7978845608028654
CUBE = 0.044715
VMEM, ANY, HBM, SMEM = (
    pl.BlockSpec(memory_space=kind) for kind in (pltpu.VMEM, pl.ANY, pltpu.HBM, pltpu.SMEM)
)
ROOM = 60 * 2**20
ONE = pltpu.SemaphoreType.DMA
TWO = pltpu.SemaphoreType.DMA((2,))
FEW = pltpu.SemaphoreType.DMA((8,))


def shape(*dims, dtype=BF16):
    return jax.ShapeDtypeStruct(dims, dtype)


def work(flops):
    return pl.CostEstimate(flops=int(flops * 0.4), bytes_accessed=1 << 20, transcendentals=0)


def dot(a, b):
    return lax.dot_general(a, b, (((1,), (0,)), ((), ())), preferred_element_type=F32)


def dot_t(a, b):
    return lax.dot_general(a, b, (((1,), (1,)), ((), ())), preferred_element_type=F32)


def normed(values):
    center = values - jnp.mean(values, axis=-1, keepdims=True)
    scale = lax.rsqrt(jnp.mean(center * center, axis=-1, keepdims=True) + 1e-05)
    return center * scale, scale


def norm_back(edge, unit, scale):
    return (edge - jnp.mean(edge, axis=-1, keepdims=True) - unit * jnp.mean(edge * unit, axis=-1, keepdims=True)) * scale


def start(source, target, sem):
    pltpu.make_async_copy(source, target, sem).start()


def wait(ref, sem):
    pltpu.make_async_copy(ref, ref, sem).wait()


def place_of(places, side, axis, slot):
    return places[side * 12 + "xyz".index(axis) * 4 + slot]


def ffn_kernel(places, bias_ref, low_own, low_other, grad_own, grad_other, up, down0, down1, down2, down3,
               bias_grad_ref, feed_ref, feed_low_ref, gc_ref, gc_low_ref, dup, ddown_keep, ddown_move,
               up_buf, down_buf, dup_buf, ddown_buf, low, grad, low_t, act_buf, gpre_buf, total, grad_total,
               feed_low, gc_low, in_sem, up_sem, down_sem, out_sem):
    core = places[24]

    def tiles(chunk, *parts):
        for part in parts or (0, 1):
            for sy in range(4):
                y = place_of(places, 0, "y", sy)
                yh, yl = lax.div(y, 2), lax.rem(y, 2)
                unit = pl.ds(pl.multiple_of((part * 2 + yh) * UNIT, UNIT), UNIT)
                for x in range(4):
                    yield sy, chunk * 2 + part, x, yl, unit

    def model(x, yl):
        return pl.ds(pl.multiple_of((x * 2 + yl) * 128, 128), 128)

    def fetch(chunk):
        for sy, sz, x, yl, unit in tiles(chunk):
            start(up.at[x * 16 + sy * 4 + sz], up_buf.at[chunk, model(x, yl), unit], up_sem.at[chunk])
        for sy, sz, sx, yl, unit in tiles(chunk):
            cols = model(place_of(places, 0, "x", sx), yl)
            start((down0, down1, down2, down3)[sy].at[sx * 4 + sz], down_buf.at[chunk, unit, cols], down_sem.at[chunk])

    def send(chunk, part):
        for y in range(4):
            for x in range(4):
                unit = slice((part * 2 + y // 2) * UNIT, (part * 2 + y // 2 + 1) * UNIT)
                start(dup_buf.at[chunk, model(x, y % 2), unit], dup.at[x, y, chunk * 2 + part], out_sem)
        for sy, sz, sx, yl, unit in tiles(chunk, part):
            source = ddown_buf.at[chunk, unit, model(place_of(places, 0, "x", sx), yl)]
            start(source, (ddown_keep, ddown_move)[sy // 2].at[sy % 2 * 16 + sx * 4 + sz], out_sem)

    start(low_own, low.at[pl.ds(0, TOK)], in_sem.at[0])
    start(low_other, low.at[pl.ds(TOK, TOK)], in_sem.at[0])
    fetch(0)
    start(grad_own, grad.at[pl.ds(0, TOK)], in_sem.at[1])
    start(grad_other, grad.at[pl.ds(TOK, TOK)], in_sem.at[1])
    bias_grad_ref[...] = jnp.zeros_like(bias_grad_ref)
    wait(low, in_sem.at[0])
    wait(grad, in_sem.at[1])

    for chunk in (0, 1):
        wait(up_buf.at[chunk], up_sem.at[chunk])
        wait(down_buf.at[chunk], down_sem.at[chunk])
        for n in range(CHUNK // UNIT):
            cols = slice(n * UNIT, (n + 1) * UNIT)
            block = (place_of(places, 0, "z", chunk * 2 + n // 2) * 2 + n % 2) * 2 + core
            pre = dot(low[...], up_buf[chunk, :, cols]) + bias_ref[block]
            gact = dot_t(grad[...], down_buf[chunk, cols, :])
            square = pre * pre
            bend = jnp.tanh(ROOT * (pre + CUBE * square * pre))
            half = 0.5 + 0.5 * bend
            act = (pre * half).astype(BF16)
            slope = half + 0.5 * pre * (1.0 - bend * bend) * (ROOT + 3.0 * ROOT * CUBE * square)
            gpre = (gact * slope).astype(BF16)
            if chunk == 0 and n == 0:
                fetch(1)
            act_buf[:, cols] = act
            gpre_buf[:, cols] = gpre
            bias_grad_ref[block] = jnp.sum(gpre.astype(F32), axis=0, keepdims=True)
            if chunk == 0 and n == 0:
                low_t[...] = low[...].T
            ddown_buf[chunk, cols, :] = dot(act.T, grad[...]).astype(BF16)
            dup_buf[chunk, :, cols] = dot(low_t[...], gpre).astype(BF16)
            if n % 2 == 1:
                send(chunk, n // 2)
        more = dot_t(gpre_buf[...], up_buf[chunk])
        feed = dot(act_buf[...], down_buf[chunk])
        if chunk == 0:
            grad_total[...] = more
            total[...] = feed
        else:
            grad_total[...] += more
            gc_low[...] = grad_total[TOK:, :].astype(BF16)
            start(gc_low, gc_low_ref, out_sem)
            start(grad_total.at[pl.ds(0, TOK)], gc_ref, out_sem)
            total[...] += feed
            feed_low[...] = total[TOK:, :].astype(BF16)
            start(feed_low, feed_low_ref, out_sem)
            start(total.at[pl.ds(0, TOK)], feed_ref, out_sem)
    for ref in (dup_buf, ddown_buf, gc_low, feed_low, grad_total.at[pl.ds(0, TOK)], total.at[pl.ds(0, TOK)]):
        wait(ref, out_sem)


def ffn(places, up_bias, low_own, low_other, grad_own, grad_other, weights):
    big = pltpu.VMEM((2, CHUNK, CHUNK), BF16)
    rows = pltpu.VMEM((BOTH, WIDTH), BF16)
    sums = pltpu.VMEM((BOTH, WIDTH), F32)
    half = pltpu.VMEM((TOK, WIDTH), BF16)
    return pl.pallas_call(
        ffn_kernel,
        in_specs=[SMEM, VMEM] + [HBM] * 9,
        out_specs=[VMEM] + [HBM] * 7,
        out_shape=[
            shape(16, 1, UNIT, dtype=F32),
            shape(TOK, WIDTH, dtype=F32),
            shape(TOK, WIDTH),
            shape(TOK, WIDTH, dtype=F32),
            shape(TOK, WIDTH),
            shape(4, 4, 4, 128, 256),
            shape(32, 256, 128),
            shape(32, 256, 128),
        ],
        scratch_shapes=[
            big, big, big, big, rows, rows, rows,
            pltpu.VMEM((BOTH, CHUNK), BF16),
            pltpu.VMEM((BOTH, CHUNK), BF16),
            sums, sums, half, half, TWO, TWO, TWO, ONE,
        ],
        compiler_params=pltpu.CompilerParams(vmem_limit_bytes=ROOM),
        cost_estimate=work(40e9),
        name="ffn",
    )(places, up_bias.reshape(16, 1, UNIT), low_own, low_other, grad_own, grad_other, *weights)


BLOCK = 128
HALF = 512
PART = 3 * HALF


def row_tiles(places):
    core = places[24]
    for side in (0, 1):
        for slot in range(4):
            yield side, slot, place_of(places, side, "z", slot), core if side == 0 else 1 - core


def part_cols(part, cols):
    return slice(part * 2048 + cols.start, part * 2048 + cols.stop)


def fetch_part(places, part, pieces, buf, sem, cols):
    for side, slot, z, c in row_tiles(places):
        start(pieces[2 * side + slot // 2].at[slot % 2, :, :, part_cols(part, cols)], buf.at[z, :, c], sem)


def matrix(ref):
    return ref.reshape(WIDTH, ref.shape[-1])


def parts_buffer(cols):
    return pltpu.VMEM((4, 2, 2, 64, cols), BF16)


def lane_marks():
    low = lax.broadcasted_iota(jnp.int32, (1, 128), 1) < 64
    return low, jnp.where(low, 1.0, 0.0).astype(BF16), jnp.where(low, 0.0, 1.0).astype(BF16)


def front_kernel(places, ln1_ref, qkv_bias_ref, pair_ref, out_bias_ref, ln2_ref, tok, *refs):
    pieces, refs = refs[:4], refs[4:]
    low_out, qkv_out, prob_out, mixed_out, hidden_out, normed_out, qkv_buf0, qkv_buf1, out_buf0, out_buf1 = refs[:10]
    tok_ref, low_ref, qkv_ref, prob_ref, mixed_ref, hidden_ref, normed_ref, sem, out_sem = refs[10:]
    start(tok, tok_ref, sem.at[4])
    for part, buf in ((0, qkv_buf0), (1, qkv_buf1)):
        fetch_part(places, part, pieces, buf, sem.at[part], slice(0, PART))
    for part, buf in ((0, out_buf0), (1, out_buf1)):
        fetch_part(places, part, pieces, buf, sem.at[2 + part], slice(PART, 2048))
    wait(tok_ref, sem.at[4])

    @pl.loop(0, TOK // 128)
    def _(i):
        rows = pl.ds(i * 128, 128)
        unit, _ = normed(tok_ref[rows, :].astype(F32))
        low_ref[rows, :] = (unit * ln1_ref[0:1, :] + ln1_ref[1:2, :]).astype(BF16)

    start(low_ref, low_out, out_sem)
    for part, buf in ((0, qkv_buf0), (1, qkv_buf1)):
        wait(buf, sem.at[part])
        for n in range(3):
            cols = slice(n * HALF, (n + 1) * HALF)
            qkv_ref[part, :, cols] = (dot(low_ref[...], matrix(buf)[:, cols]) + qkv_bias_ref[part, :, cols]).astype(BF16)
        start(qkv_ref.at[part], qkv_out.at[part], out_sem)
    low, near, far = lane_marks()
    near, far = near * 0.125, far * 0.125

    @pl.loop(0, 8)
    def _(pair):
        part = lax.div(pair, 4)
        begin = pl.multiple_of(lax.rem(pair, 4) * 128, 128)
        lanes = pl.ds(pl.multiple_of(pair * 128, 128), 128)
        for block in range(TOK // BLOCK):
            rows = slice(block * BLOCK, (block + 1) * BLOCK)
            query = qkv_ref[part, rows, pl.ds(begin, 128)]
            key = qkv_ref[part, rows, pl.ds(begin + HALF, 128)]
            value = qkv_ref[part, rows, pl.ds(begin + 2 * HALF, 128)]
            bias = pair_ref[block]
            score = dot_t(jnp.concatenate([query * near, query * far], axis=0), key) + jnp.concatenate([bias, bias], axis=0)
            power = jnp.exp(score - jnp.max(score, axis=-1, keepdims=True))
            prob = (power * (1.0 / jnp.sum(power, axis=-1, keepdims=True))).astype(BF16)
            prob_ref[pair, block] = prob
            both = dot(prob, value)
            mixed_ref[rows, lanes] = jnp.where(low, both[:BLOCK], both[BLOCK:]).astype(BF16)

    start(prob_ref, prob_out, out_sem)
    start(mixed_ref, mixed_out, out_sem)
    for part, buf in ((0, out_buf0), (1, out_buf1)):
        cols = slice(part * HALF, (part + 1) * HALF)
        wait(buf, sem.at[2 + part])
        hidden_ref[:, cols] = tok_ref[:, cols].astype(F32) + dot(mixed_ref[...], matrix(buf)[...]) + out_bias_ref[:, cols]
    start(hidden_ref, hidden_out, out_sem)

    @pl.loop(0, TOK // 128)
    def _(i):
        rows = pl.ds(i * 128, 128)
        unit, _ = normed(hidden_ref[rows, :])
        normed_ref[rows, :] = (unit * ln2_ref[0:1, :] + ln2_ref[1:2, :]).astype(BF16)

    start(normed_ref, normed_out, out_sem)
    for ref in (low_ref, qkv_ref, prob_ref, mixed_ref, hidden_ref, normed_ref):
        wait(ref, out_sem)


def front(places, tokens, ln1, qkv_bias, allowed, out_bias, ln2, pieces):
    wide = ((TOK, WIDTH), BF16)
    outs = [wide, ((2, TOK, PART), BF16), ((8, 4, 2 * BLOCK, BLOCK), BF16), wide, ((TOK, WIDTH), F32), wide]
    return pl.pallas_call(
        front_kernel,
        in_specs=[SMEM] + [VMEM] * 5 + [HBM] * 5,
        out_specs=[HBM] * 6,
        out_shape=[jax.ShapeDtypeStruct(*out) for out in outs],
        scratch_shapes=[parts_buffer(PART)] * 2 + [parts_buffer(HALF)] * 2 + [pltpu.VMEM(*s) for s in [wide] + outs] + [FEW, ONE],
        compiler_params=pltpu.CompilerParams(vmem_limit_bytes=ROOM),
        cost_estimate=work(24e9),
        name="front",
    )(places, ln1, qkv_bias, allowed, out_bias.reshape(1, WIDTH), ln2, tokens, *pieces)


def turn(hidden_ref, gain_ref, gc_ref, got_ref, grad_ref, ghid_ref, glow_ref, vec_ref):
    @pl.loop(0, TOK // 128)
    def _(part):
        rows = pl.ds(part * 128, 128)
        unit, scale = normed(hidden_ref[rows, :])
        gc = gc_ref[rows, :] + got_ref[rows, :].astype(F32)
        gout = grad_ref[rows, :].astype(F32)
        ghid = gout + norm_back(gc * gain_ref[...], unit, scale)
        ghid_ref[rows, :] = ghid
        glow_ref[rows, :] = ghid.astype(BF16)
        vec_ref[4:5, :] += jnp.sum(ghid, axis=0, keepdims=True)
        vec_ref[5:6, :] += jnp.sum(gc * unit, axis=0, keepdims=True)
        vec_ref[6:7, :] += jnp.sum(gc, axis=0, keepdims=True)
        vec_ref[7:8, :] += jnp.sum(gout, axis=0, keepdims=True)


def back_kernel(places, ln1_ref, ln2_gain_ref, down_bias_ref, up_bias_grad_ref,
                hidden, gc, gc_got, cot, mixed, low_in, qkv, prob, tok, feed, feed_got, *refs):
    pieces, refs = refs[:4], refs[4:]
    gin_out, out_out, vec_ref, *outs = refs[:7]
    qkv_buf0, qkv_buf1, out_buf0, out_buf1, grad_buf0, grad_buf1 = refs[7:13]
    hidden_ref, gc_ref, gc_got_ref, cot_ref, mixed_ref, low_ref, qkv_ref, prob_ref, tok_ref, feed_ref, feed_got_ref = refs[13:24]
    ghid_ref, glow_ref, gmix_ref, gqkv_ref, flip, out_ref, sem, out_sem = refs[24:]
    for source, target in ((hidden, hidden_ref), (gc, gc_ref), (gc_got, gc_got_ref), (cot, cot_ref)):
        start(source, target, sem.at[0])
    start(mixed, mixed_ref, sem.at[1])
    for part, buf in ((0, out_buf0), (1, out_buf1)):
        fetch_part(places, part, pieces, buf, sem.at[2], slice(PART, 2048))
    start(qkv, qkv_ref, sem.at[3])
    start(prob, prob_ref, sem.at[3])
    start(low_in, low_ref, sem.at[4])
    for part, buf in ((0, qkv_buf0), (1, qkv_buf1)):
        fetch_part(places, part, pieces, buf, sem.at[5], slice(0, PART))
    for source, target in ((tok, tok_ref), (feed, feed_ref), (feed_got, feed_got_ref)):
        start(source, target, sem.at[6])
    vec_ref[...] = jnp.zeros_like(vec_ref)
    for block in range(16):
        row, col = 8 + block // 4, block % 4 * UNIT
        vec_ref[row : row + 1, col : col + UNIT] = up_bias_grad_ref[block]
    wait(mixed_ref, sem.at[1])
    flip[...] = mixed_ref[...].T
    for ref in (hidden_ref, gc_ref, gc_got_ref, cot_ref):
        wait(ref, sem.at[0])
    turn(hidden_ref, ln2_gain_ref, gc_ref, gc_got_ref, cot_ref, ghid_ref, glow_ref, vec_ref)
    grads = [matrix(grad_buf0), matrix(grad_buf1)]
    for part in (0, 1):
        heads = slice(part * HALF, (part + 1) * HALF)
        grads[part][:, PART:] = dot(flip[...], glow_ref[:, heads]).astype(BF16)
    for buf in (out_buf0, out_buf1):
        wait(buf, sem.at[2])
    gmix_ref[...] = (
        dot_t(glow_ref[:, :HALF], matrix(out_buf0)[...]) + dot_t(glow_ref[:, HALF:], matrix(out_buf1)[...])
    ).astype(BF16)
    wait(low_ref, sem.at[4])
    flip[...] = low_ref[...].T
    wait(qkv_ref, sem.at[3])
    wait(prob_ref, sem.at[3])
    low, near, far = lane_marks()

    for part, grad_buf in ((0, grad_buf0), (1, grad_buf1)):
        @pl.loop(0, 4)
        def _(pair, part=part):
            begin = pl.multiple_of(pair * 128, 128)
            for block in range(TOK // BLOCK):
                rows = slice(block * BLOCK, (block + 1) * BLOCK)
                query = qkv_ref[part, rows, pl.ds(begin, 128)]
                key = qkv_ref[part, rows, pl.ds(begin + HALF, 128)]
                value = qkv_ref[part, rows, pl.ds(begin + 2 * HALF, 128)]
                gmix = gmix_ref[rows, pl.ds(pl.multiple_of(begin + part * HALF, 128), 128)]
                gmix = jnp.concatenate([gmix * near, gmix * far], axis=0)
                query = jnp.concatenate([query * (near * 0.125), query * (far * 0.125)], axis=0)
                prob_low = prob_ref[pair + 4 * part, block]
                prob = prob_low.astype(F32)
                gprob = dot_t(gmix, value)
                gscore = (prob * (gprob - jnp.sum(prob * gprob, axis=-1, keepdims=True))).astype(BF16)
                both = dot(gscore, key) * 0.125
                gqkv_ref[part, rows, pl.ds(begin, 128)] = jnp.where(low, both[:BLOCK], both[BLOCK:]).astype(BF16)
                gqkv_ref[part, rows, pl.ds(begin + HALF, 128)] = dot(gscore.T, query).astype(BF16)
                gqkv_ref[part, rows, pl.ds(begin + 2 * HALF, 128)] = dot(prob_low.T, gmix).astype(BF16)

        for n in range(3):
            cols = slice(n * HALF, (n + 1) * HALF)
            grads[part][:, cols] = dot(flip[...], gqkv_ref[part, :, cols]).astype(BF16)
        for side, slot, z, c in row_tiles(places):
            start(grad_buf.at[z, :, c], outs[2 * side + slot // 2].at[slot % 2, :, :, part * 2048 : (part + 1) * 2048], out_sem)
        heads = slice(part * HALF, (part + 1) * HALF)
        for row, n in ((2, 0), (3, 2)):
            vec_ref[row : row + 1, heads] = jnp.sum(gqkv_ref[part, :, n * HALF : (n + 1) * HALF].astype(F32), axis=0, keepdims=True)

    for ref in (tok_ref, feed_ref, feed_got_ref):
        wait(ref, sem.at[6])
    out_ref[...] = (hidden_ref[...] + feed_ref[...] + feed_got_ref[...].astype(F32) + down_bias_ref[...]).astype(BF16)
    start(out_ref, out_out, out_sem)
    for buf in (qkv_buf0, qkv_buf1):
        wait(buf, sem.at[5])
    gc_ref[...] = dot_t(gqkv_ref[0], matrix(qkv_buf0)[...]) + dot_t(gqkv_ref[1], matrix(qkv_buf1)[...])

    @pl.loop(0, TOK // 128)
    def _(i):
        rows = pl.ds(i * 128, 128)
        unit, scale = normed(tok_ref[rows, :].astype(F32))
        grad = gc_ref[rows, :]
        ghid_ref[rows, :] += norm_back(grad * ln1_ref[0:1, :], unit, scale)
        vec_ref[0:1, :] += jnp.sum(grad * unit, axis=0, keepdims=True)
        vec_ref[1:2, :] += jnp.sum(grad, axis=0, keepdims=True)

    start(ghid_ref, gin_out, out_sem)
    for ref in (grad_buf0, grad_buf1, out_ref, ghid_ref):
        wait(ref, out_sem)


def back(places, ln1, ln2_gain, down_bias, up_bias_grad, streams, pieces):
    wide, high = ((TOK, WIDTH), BF16), ((TOK, WIDTH), F32)
    heads = ((2, TOK, PART), BF16)
    scratch = [high, high, wide, wide, wide, wide, heads, ((8, 4, 2 * BLOCK, BLOCK), BF16), wide, high, wide]
    scratch += [high, wide, wide, heads, ((WIDTH, TOK), BF16), wide]
    rows = shape(2, 2, 64, 4096)
    return pl.pallas_call(
        back_kernel,
        in_specs=[SMEM] + [VMEM] * 4 + [HBM] * 15,
        out_specs=[HBM] * 2 + [VMEM] + [HBM] * 4,
        out_shape=[shape(TOK, WIDTH, dtype=F32), shape(TOK, WIDTH), shape(16, WIDTH, dtype=F32), rows, rows, rows, rows],
        scratch_shapes=[parts_buffer(PART)] * 2 + [parts_buffer(HALF)] * 2 + [parts_buffer(2048)] * 2
        + [pltpu.VMEM(*s) for s in scratch]
        + [FEW, ONE],
        compiler_params=pltpu.CompilerParams(vmem_limit_bytes=ROOM),
        cost_estimate=work(40e9),
        name="back",
    )(places, ln1, ln2_gain.reshape(1, WIDTH), down_bias.reshape(1, WIDTH), up_bias_grad, *streams, *pieces)


AXES = ("z", "yh", "c", "x", "yl")
ALONG_Y, PLANE_XY = ("yh", "yl"), ("yh", "x", "yl")


def device_number(place):
    return (
        ((place["z"] * 2 + place["y"] // 2) * 2 + place["c"]) * 4 + place["x"]
    ) * 2 + place["y"] % 2


def exchange_pairs(axis, second, alike=False):
    pairs = []
    for z, y, c, x in itertools.product(range(4), range(4), range(2), range(4)):
        here = {"z": z, "y": y, "c": c, "x": x}
        mask = 1 if (c == 0 or alike) != second else 3
        there = dict(here)
        there[axis] = here[axis] ^ mask
        pairs.append((device_number(here), device_number(there)))
    return pairs


def swap_axis(values, axis, second, alike=False):
    return lax.ppermute(values, AXES, exchange_pairs(axis, second, alike))


def swap_core(values):
    return lax.ppermute(values, "c", [(0, 1), (1, 0)])


def position(axis):
    if axis == "y":
        return lax.axis_index("yh") * 2 + lax.axis_index("yl")
    return lax.axis_index(axis)


def distance_of(core, slot):
    return jnp.where(core == 0, slot ^ (slot >> 1), ((slot << 1) & 3) ^ ((slot ^ (slot >> 1)) & 1))


def place_table():
    core, slots = lax.axis_index("c"), jnp.arange(4, dtype=jnp.int32)
    rows = [
        distance_of(side, slots) ^ position(axis)
        for side in (core, 1 - core)
        for axis in ("x", "y", "z")
    ]
    return jnp.concatenate(rows + [jnp.full((8,), core, jnp.int32)])


def add(left, right, dtype=BF16):
    return (left.astype(F32) + right.astype(F32)).astype(dtype)


def halves(own, got):
    count = own.shape[0] // 2
    return add(own[count:], got[count:]), add(own[:count], got[:count])


def spread(values, axes):
    return lax.all_to_all(jnp.broadcast_to(values, (16,) + values.shape), axes, 0, 0)


def together(*values):
    return lax.optimization_barrier(values)


def pair_bias(clip_ids):
    clips = clip_ids.reshape(-1, BLOCK)
    row = lax.broadcasted_iota(jnp.int32, (BLOCK, BLOCK), 0)
    col = lax.broadcasted_iota(jnp.int32, (BLOCK, BLOCK), 1)
    allowed = (clips[:, :, None] == clips[:, None, :]) & (row >= col)[None]
    return jnp.where(allowed, 0.0, -1e30).astype(F32)


def on_device(
    tokens,
    qkv_weight,
    out_weight,
    up_weight,
    down_weight,
    ln1_gain,
    ln1_bias,
    q_bias,
    v_bias,
    out_bias,
    ln2_gain,
    ln2_bias,
    up_bias,
    down_bias,
    segment_ids,
    cotangent,
):
    places = place_table()
    ln1 = jnp.stack([ln1_gain, ln1_bias])
    nothing = jnp.zeros((HALF,), F32)
    qkv_bias = jnp.stack(
        [
            jnp.concatenate([q_bias[cols], nothing, v_bias[cols]])[None]
            for cols in (slice(0, HALF), slice(HALF, WIDTH))
        ]
    )
    ln2 = jnp.stack([ln2_gain, ln2_bias])
    allowed = pair_bias(segment_ids)

    heads = qkv_weight.reshape(8, 3, WIDTH)
    pieces = []
    for cols in (slice(0, HALF), slice(HALF, WIDTH)):
        pieces += [heads[:, :, cols].reshape(8, PART), out_weight[:, cols]]
    def join(pairs):
        return together(*[jnp.concatenate(pair) for pair in pairs])

    rows = spread(jnp.concatenate(pieces, axis=1), PLANE_XY)
    down, up = down_weight[None], up_weight[None]
    down, up = join(((down, swap_axis(down, "z", False)), (up, swap_axis(up, "z", False))))
    rows, down_got, up_got, places, ln1, ln2, qkv_bias, allowed = together(
        rows, swap_axis(down, "z", True), swap_axis(up, "z", True), places, ln1, ln2, qkv_bias, allowed
    )
    rows = rows.reshape(1, 2, 64, 4096)
    rows_got = swap_axis(rows, "z", False)
    down, up = join(((down, down_got), (up, up_got)))
    down, up = join(((down, swap_axis(down, "x", False)), (up, swap_axis(up, "y", False))))
    rows_got, down_got, up_got, grad_other = together(
        rows_got, swap_axis(down, "x", True), swap_axis(up, "y", True), swap_core(cotangent)
    )
    rows, down, up = join(((rows, rows_got), (down, down_got), (up, up_got)))
    up = lax.all_gather(up, "x", axis=0).reshape(64, 128, 256)
    near, far = swap_axis(down, "y", False), swap_axis(down, "y", True)
    rows_got, near, far, other_rows = together(swap_axis(rows, "z", True), near, far, swap_core(rows))
    pieces = (rows, rows_got, other_rows, swap_core(rows_got))
    downs = (down, near, far, swap_axis(near, "y", True))

    low, qkv, prob, mixed, hidden, low2 = front(
        places, tokens, ln1, qkv_bias, allowed, out_bias, ln2, pieces
    )
    up_bias_grad, feed, feed_low, gc, gc_low, dup, keep_down, move_down = ffn(
        places, up_bias, low2, swap_core(low2), cotangent, grad_other, (up, *downs)
    )
    dup = lax.psum_scatter(dup, "x", scatter_dimension=0, tiled=True)[0]

    down_got = swap_axis(move_down, "y", True)
    grad_tokens, output, vector, own_keep, own_move, other_keep, other_move = back(
        places, ln1, ln2_gain, down_bias, up_bias_grad,
        (hidden, gc, swap_core(gc_low), cotangent, mixed, low, qkv, prob, tokens, feed, swap_core(feed_low)),
        pieces,
    )
    down_got, vector, own_keep, own_move, other_keep, other_move = together(
        down_got, vector, own_keep, own_move, other_keep, other_move
    )
    got_move, got_keep, vector_got = swap_core(other_move), swap_core(other_keep), swap_core(vector)
    move = add(own_move, got_move)
    move, down_got, vector, vector_got = together(move, down_got, vector, vector_got)
    got = swap_axis(move, "z", True)
    keep = add(own_keep, got_keep)
    move_down, keep_down = halves(keep_down, down_got)
    down_got = swap_axis(move_down, "y", False)
    move_down, keep_down = halves(keep_down, down_got)
    down_got = swap_axis(move_down, "x", True)
    vector = vector + vector_got
    vector_got, dup = together(swap_axis(vector, "x", False, True), dup)
    dup = lax.psum_scatter(dup, ALONG_Y, scatter_dimension=0, tiled=True)[0]
    vector = vector + vector_got
    vector_got = swap_axis(vector, "x", True, True)
    got, keep, down_got, vector_got = together(got, keep, down_got, vector_got)

    move, keep = halves(keep, got)
    move, down_got, vector_got = together(move, down_got, vector_got)
    got = swap_axis(move, "z", False)
    move_down, keep_down = halves(keep_down, down_got)
    down_got = swap_axis(move_down, "x", False)
    up_got = swap_axis(dup[2:], "z", True)
    vector = vector + vector_got
    vector = vector + swap_axis(vector, "y", False, True)
    vector_got = swap_axis(vector, "y", True, True)
    got, down_got, up_got, vector_got = together(got, down_got, up_got, vector_got)

    rows_sum = add(keep, got).reshape(16, 8, 4096)
    rows_sum, down_got, vector_got = together(rows_sum, down_got, vector_got)
    rows_parts = lax.all_to_all(rows_sum, PLANE_XY, 0, 0)
    vector = vector + vector_got
    for second in (False, True):
        vector = vector + swap_axis(vector, "z", second, True)
    for second in (True, False):
        move_down, keep_down = halves(keep_down, down_got)
        down_got = swap_axis(move_down, "z", second)
    move_up, keep_up = halves(dup[:2], up_got)
    up_grad = add(keep_up, swap_axis(move_up, "z", False), F32)[0]
    down_grad = add(keep_down, down_got, F32)[0]
    row = jnp.sum(rows_parts.astype(F32), axis=0).reshape(8, 2, 2048)
    qkv_grad = row[:, :, :PART].reshape(8, 2, 3, HALF).transpose(0, 2, 1, 3).reshape(8, 3 * WIDTH)
    out_grad = row[:, :, PART:].reshape(8, WIDTH)
    summed = vector.reshape(-1)
    vectors = [summed[i * WIDTH : (i + 1) * WIDTH] for i in range(8)]
    return (
        output,
        grad_tokens,
        qkv_grad,
        out_grad,
        up_grad,
        down_grad,
        *vectors[:7],
        summed[8 * WIDTH : 12 * WIDTH],
        vectors[7],
    )


def solution(mesh):
    fine = Mesh(mesh.devices.reshape(4, 2, 2, 4, 2), AXES)
    every, hidden, model = AXES, ("z", "yh", "c"), ("x", "yl")
    weights = (P(every, None), P(every, None), P(model, hidden), P(hidden, model))
    return jax.shard_map(
        on_device,
        mesh=fine,
        in_specs=(P(every, None), *weights, *[P()] * 9, P(every), P(every, None)),
        out_specs=(P(every, None), P(every, None), *weights, *[P()] * 9),
        check_vma=False,
    )
```

```python
import functools
import itertools

import jax
import jax.numpy as jnp
from jax import lax
from jax.experimental import pallas as pl
from jax.experimental.pallas import tpu as pltpu
from jax.sharding import Mesh, PartitionSpec as P

F32, BF16 = jnp.float32, jnp.bfloat16
TOK, WIDTH, FF = 512, 1024, 4096
BOTH = 2 * TOK
CHUNK = 1024
UNIT = 256
WIDE = 2 * UNIT
ROOT = 0.7978845608028654
CUBE = 0.044715
VMEM, ANY, HBM, SMEM = (
    pl.BlockSpec(memory_space=kind) for kind in (pltpu.VMEM, pl.ANY, pltpu.HBM, pltpu.SMEM)
)
ROOM = 60 * 2**20
ONE = pltpu.SemaphoreType.DMA
TWO = pltpu.SemaphoreType.DMA((2,))
FEW = pltpu.SemaphoreType.DMA((8,))


def shape(*dims, dtype=BF16):
    return jax.ShapeDtypeStruct(dims, dtype)


def work(flops):
    return pl.CostEstimate(flops=int(flops * 0.4), bytes_accessed=1 << 20, transcendentals=0)


def dot(a, b):
    return lax.dot_general(a, b, (((1,), (0,)), ((), ())), preferred_element_type=F32)


def dot_t(a, b):
    return lax.dot_general(a, b, (((1,), (1,)), ((), ())), preferred_element_type=F32)


def normed(values):
    center = values - jnp.mean(values, axis=-1, keepdims=True)
    scale = lax.rsqrt(jnp.mean(center * center, axis=-1, keepdims=True) + 1e-05)
    return center * scale, scale


def norm_back(edge, unit, scale):
    return (edge - jnp.mean(edge, axis=-1, keepdims=True) - unit * jnp.mean(edge * unit, axis=-1, keepdims=True)) * scale


def start(source, target, sem):
    pltpu.make_async_copy(source, target, sem).start()


def wait(ref, sem):
    pltpu.make_async_copy(ref, ref, sem).wait()


def place_of(places, side, axis, slot):
    return places[side * 12 + "xyz".index(axis) * 4 + slot]


def ffn_kernel(places, bias_ref, low_own, low_other, grad_own, grad_other, up, down0, down1, down2, down3,
               bias_grad_ref, feed_ref, feed_low_ref, gc_ref, gc_low_ref, dup, ddown_keep, ddown_move,
               up_buf, down_buf, dup_buf, ddown_buf, low, grad, low_t, act_buf, gpre_buf, total, grad_total,
               feed_low, gc_low, in_sem, up_sem, down_sem, out_sem):
    core = places[24]

    def tiles(chunk, *parts):
        for part in parts or (0, 1):
            for sy in range(4):
                y = place_of(places, 0, "y", sy)
                yh, yl = lax.div(y, 2), lax.rem(y, 2)
                unit = pl.ds(pl.multiple_of((part * 2 + yh) * UNIT, UNIT), UNIT)
                for x in range(4):
                    yield sy, chunk * 2 + part, x, yl, unit

    def model(x, yl):
        return pl.ds(pl.multiple_of((x * 2 + yl) * 128, 128), 128)

    def fetch(chunk):
        for sy, sz, x, yl, unit in tiles(chunk):
            start(up.at[x * 16 + sy * 4 + sz], up_buf.at[chunk, model(x, yl), unit], up_sem.at[chunk])
        for sy, sz, sx, yl, unit in tiles(chunk):
            cols = model(place_of(places, 0, "x", sx), yl)
            start((down0, down1, down2, down3)[sy].at[sx * 4 + sz], down_buf.at[chunk, unit, cols], down_sem.at[chunk])

    def send(chunk, part):
        for y in range(4):
            for x in range(4):
                unit = slice((part * 2 + y // 2) * UNIT, (part * 2 + y // 2 + 1) * UNIT)
                start(dup_buf.at[chunk, model(x, y % 2), unit], dup.at[x, y, chunk * 2 + part], out_sem)
        for sy, sz, sx, yl, unit in tiles(chunk, part):
            source = ddown_buf.at[chunk, unit, model(place_of(places, 0, "x", sx), yl)]
            start(source, (ddown_keep, ddown_move)[sy // 2].at[sy % 2 * 16 + sx * 4 + sz], out_sem)

    start(low_own, low.at[pl.ds(0, TOK)], in_sem.at[0])
    start(low_other, low.at[pl.ds(TOK, TOK)], in_sem.at[0])
    fetch(0)
    start(grad_own, grad.at[pl.ds(0, TOK)], in_sem.at[1])
    start(grad_other, grad.at[pl.ds(TOK, TOK)], in_sem.at[1])
    bias_grad_ref[...] = jnp.zeros_like(bias_grad_ref)
    wait(low, in_sem.at[0])
    wait(grad, in_sem.at[1])

    for chunk in (0, 1):
        wait(up_buf.at[chunk], up_sem.at[chunk])
        wait(down_buf.at[chunk], down_sem.at[chunk])
        for n in range(CHUNK // WIDE):
            cols = slice(n * WIDE, (n + 1) * WIDE)
            blocks = [(place_of(places, 0, "z", chunk * 2 + n) * 2 + yh) * 2 + core for yh in (0, 1)]
            bias = jnp.concatenate([bias_ref[block] for block in blocks], axis=1)
            pre = dot(low[...], up_buf[chunk, :, cols]) + bias
            gact = dot_t(grad[...], down_buf[chunk, cols, :])
            square = pre * pre
            bend = jnp.tanh(ROOT * (pre + CUBE * square * pre))
            half = 0.5 + 0.5 * bend
            act = (pre * half).astype(BF16)
            slope = half + 0.5 * pre * (1.0 - bend * bend) * (ROOT + 3.0 * ROOT * CUBE * square)
            gpre = (gact * slope).astype(BF16)
            if chunk == 0 and n == 0:
                fetch(1)
            act_buf[:, cols] = act
            gpre_buf[:, cols] = gpre
            bias_grad = jnp.sum(gpre.astype(F32), axis=0, keepdims=True)
            for yh, block in enumerate(blocks):
                bias_grad_ref[block] = bias_grad[:, yh * UNIT : (yh + 1) * UNIT]
            if chunk == 0 and n == 0:
                low_t[...] = low[...].T
            ddown_buf[chunk, cols, :] = dot(act.T, grad[...]).astype(BF16)
            dup_buf[chunk, :, cols] = dot(low_t[...], gpre).astype(BF16)
            send(chunk, n)
        more = dot_t(gpre_buf[...], up_buf[chunk])
        feed = dot(act_buf[...], down_buf[chunk])
        if chunk == 0:
            grad_total[...] = more
            total[...] = feed
        else:
            grad_total[...] += more
            gc_low[...] = grad_total[TOK:, :].astype(BF16)
            start(gc_low, gc_low_ref, out_sem)
            start(grad_total.at[pl.ds(0, TOK)], gc_ref, out_sem)
            total[...] += feed
            feed_low[...] = total[TOK:, :].astype(BF16)
            start(feed_low, feed_low_ref, out_sem)
            start(total.at[pl.ds(0, TOK)], feed_ref, out_sem)
    for ref in (dup_buf, ddown_buf, gc_low, feed_low, grad_total.at[pl.ds(0, TOK)], total.at[pl.ds(0, TOK)]):
        wait(ref, out_sem)


def ffn(places, up_bias, low_own, low_other, grad_own, grad_other, weights):
    big = pltpu.VMEM((2, CHUNK, CHUNK), BF16)
    rows = pltpu.VMEM((BOTH, WIDTH), BF16)
    sums = pltpu.VMEM((BOTH, WIDTH), F32)
    half = pltpu.VMEM((TOK, WIDTH), BF16)
    return pl.pallas_call(
        ffn_kernel,
        in_specs=[SMEM, VMEM] + [HBM] * 9,
        out_specs=[VMEM] + [HBM] * 7,
        out_shape=[
            shape(16, 1, UNIT, dtype=F32),
            shape(TOK, WIDTH, dtype=F32),
            shape(TOK, WIDTH),
            shape(TOK, WIDTH, dtype=F32),
            shape(TOK, WIDTH),
            shape(4, 4, 4, 128, 256),
            shape(32, 256, 128),
            shape(32, 256, 128),
        ],
        scratch_shapes=[
            big, big, big, big, rows, rows, rows,
            pltpu.VMEM((BOTH, CHUNK), BF16),
            pltpu.VMEM((BOTH, CHUNK), BF16),
            sums, sums, half, half, TWO, TWO, TWO, ONE,
        ],
        compiler_params=pltpu.CompilerParams(vmem_limit_bytes=ROOM),
        cost_estimate=work(40e9),
        name="ffn",
    )(places, up_bias.reshape(16, 1, UNIT), low_own, low_other, grad_own, grad_other, *weights)


BLOCK = 128
HALF = 512
PART = 3 * HALF


def row_tiles(places):
    core = places[24]
    for side in (0, 1):
        for slot in range(4):
            yield side, slot, place_of(places, side, "z", slot), core if side == 0 else 1 - core


def part_cols(part, cols):
    return slice(part * 2048 + cols.start, part * 2048 + cols.stop)


def fetch_part(places, part, pieces, buf, sem, cols):
    for side, slot, z, c in row_tiles(places):
        start(pieces[2 * side + slot // 2].at[slot % 2, :, :, part_cols(part, cols)], buf.at[z, :, c], sem)


def matrix(ref):
    return ref.reshape(WIDTH, ref.shape[-1])


def parts_buffer(cols):
    return pltpu.VMEM((4, 2, 2, 64, cols), BF16)


def lane_marks():
    low = lax.broadcasted_iota(jnp.int32, (1, 128), 1) < 64
    return low, jnp.where(low, 1.0, 0.0).astype(BF16), jnp.where(low, 0.0, 1.0).astype(BF16)


def front_kernel(places, ln1_ref, qkv_bias_ref, pair_ref, out_bias_ref, ln2_ref, tok, *refs):
    pieces, refs = refs[:4], refs[4:]
    low_out, qkv_out, prob_out, mixed_out, hidden_out, normed_out, qkv_buf0, qkv_buf1, out_buf0, out_buf1 = refs[:10]
    tok_ref, low_ref, qkv_ref, prob_ref, mixed_ref, hidden_ref, normed_ref, sem, out_sem = refs[10:]
    start(tok, tok_ref, sem.at[4])
    for part, buf in ((0, qkv_buf0), (1, qkv_buf1)):
        fetch_part(places, part, pieces, buf, sem.at[part], slice(0, PART))
    for part, buf in ((0, out_buf0), (1, out_buf1)):
        fetch_part(places, part, pieces, buf, sem.at[2 + part], slice(PART, 2048))
    wait(tok_ref, sem.at[4])

    @pl.loop(0, TOK // 128)
    def _(i):
        rows = pl.ds(i * 128, 128)
        unit, _ = normed(tok_ref[rows, :].astype(F32))
        low_ref[rows, :] = (unit * ln1_ref[0:1, :] + ln1_ref[1:2, :]).astype(BF16)

    start(low_ref, low_out, out_sem)
    for part, buf in ((0, qkv_buf0), (1, qkv_buf1)):
        wait(buf, sem.at[part])
        for n in range(3):
            cols = slice(n * HALF, (n + 1) * HALF)
            qkv_ref[part, :, cols] = (dot(low_ref[...], matrix(buf)[:, cols]) + qkv_bias_ref[part, :, cols]).astype(BF16)
        start(qkv_ref.at[part], qkv_out.at[part], out_sem)
    low, near, far = lane_marks()
    near, far = near * 0.125, far * 0.125

    @pl.loop(0, 8)
    def _(pair):
        part = lax.div(pair, 4)
        begin = pl.multiple_of(lax.rem(pair, 4) * 128, 128)
        lanes = pl.ds(pl.multiple_of(pair * 128, 128), 128)
        for block in range(TOK // BLOCK):
            rows = slice(block * BLOCK, (block + 1) * BLOCK)
            query = qkv_ref[part, rows, pl.ds(begin, 128)]
            key = qkv_ref[part, rows, pl.ds(begin + HALF, 128)]
            value = qkv_ref[part, rows, pl.ds(begin + 2 * HALF, 128)]
            bias = pair_ref[block]
            score = dot_t(jnp.concatenate([query * near, query * far], axis=0), key) + jnp.concatenate([bias, bias], axis=0)
            power = jnp.exp(score - jnp.max(score, axis=-1, keepdims=True))
            prob = (power * (1.0 / jnp.sum(power, axis=-1, keepdims=True))).astype(BF16)
            prob_ref[pair, block] = prob
            both = dot(prob, value)
            mixed_ref[rows, lanes] = jnp.where(low, both[:BLOCK], both[BLOCK:]).astype(BF16)

    start(prob_ref, prob_out, out_sem)
    start(mixed_ref, mixed_out, out_sem)
    for part, buf in ((0, out_buf0), (1, out_buf1)):
        cols = slice(part * HALF, (part + 1) * HALF)
        wait(buf, sem.at[2 + part])
        hidden_ref[:, cols] = tok_ref[:, cols].astype(F32) + dot(mixed_ref[...], matrix(buf)[...]) + out_bias_ref[:, cols]
    start(hidden_ref, hidden_out, out_sem)

    @pl.loop(0, TOK // 128)
    def _(i):
        rows = pl.ds(i * 128, 128)
        unit, _ = normed(hidden_ref[rows, :])
        normed_ref[rows, :] = (unit * ln2_ref[0:1, :] + ln2_ref[1:2, :]).astype(BF16)

    start(normed_ref, normed_out, out_sem)
    for ref in (low_ref, qkv_ref, prob_ref, mixed_ref, hidden_ref, normed_ref):
        wait(ref, out_sem)


def front(places, tokens, ln1, qkv_bias, allowed, out_bias, ln2, pieces):
    wide = ((TOK, WIDTH), BF16)
    outs = [wide, ((2, TOK, PART), BF16), ((8, 4, 2 * BLOCK, BLOCK), BF16), wide, ((TOK, WIDTH), F32), wide]
    return pl.pallas_call(
        front_kernel,
        in_specs=[SMEM] + [VMEM] * 5 + [HBM] * 5,
        out_specs=[HBM] * 6,
        out_shape=[jax.ShapeDtypeStruct(*out) for out in outs],
        scratch_shapes=[parts_buffer(PART)] * 2 + [parts_buffer(HALF)] * 2 + [pltpu.VMEM(*s) for s in [wide] + outs] + [FEW, ONE],
        compiler_params=pltpu.CompilerParams(vmem_limit_bytes=ROOM),
        cost_estimate=work(24e9),
        name="front",
    )(places, ln1, qkv_bias, allowed, out_bias.reshape(1, WIDTH), ln2, tokens, *pieces)


def turn(hidden_ref, gain_ref, gc_ref, got_ref, grad_ref, ghid_ref, glow_ref, vec_ref):
    @pl.loop(0, TOK // 128)
    def _(part):
        rows = pl.ds(part * 128, 128)
        unit, scale = normed(hidden_ref[rows, :])
        gc = gc_ref[rows, :] + got_ref[rows, :].astype(F32)
        gout = grad_ref[rows, :].astype(F32)
        ghid = gout + norm_back(gc * gain_ref[...], unit, scale)
        ghid_ref[rows, :] = ghid
        glow_ref[rows, :] = ghid.astype(BF16)
        vec_ref[4:5, :] += jnp.sum(ghid, axis=0, keepdims=True)
        vec_ref[5:6, :] += jnp.sum(gc * unit, axis=0, keepdims=True)
        vec_ref[6:7, :] += jnp.sum(gc, axis=0, keepdims=True)
        vec_ref[7:8, :] += jnp.sum(gout, axis=0, keepdims=True)


def back_kernel(places, ln1_ref, ln2_gain_ref, down_bias_ref, up_bias_grad_ref,
                hidden, gc, gc_got, cot, mixed, low_in, qkv, prob, tok, feed, feed_got, *refs):
    pieces, refs = refs[:4], refs[4:]
    gin_out, out_out, vec_ref, *outs = refs[:7]
    qkv_buf0, qkv_buf1, out_buf0, out_buf1, grad_buf0, grad_buf1 = refs[7:13]
    hidden_ref, gc_ref, gc_got_ref, cot_ref, mixed_ref, low_ref, qkv_ref, prob_ref, tok_ref, feed_ref, feed_got_ref = refs[13:24]
    ghid_ref, glow_ref, gmix_ref, gqkv_ref, flip, out_ref, sem, out_sem = refs[24:]
    for source, target in ((hidden, hidden_ref), (gc, gc_ref), (gc_got, gc_got_ref), (cot, cot_ref)):
        start(source, target, sem.at[0])
    start(mixed, mixed_ref, sem.at[1])
    for part, buf in ((0, out_buf0), (1, out_buf1)):
        fetch_part(places, part, pieces, buf, sem.at[2], slice(PART, 2048))
    start(qkv, qkv_ref, sem.at[3])
    start(prob, prob_ref, sem.at[3])
    start(low_in, low_ref, sem.at[4])
    for part, buf in ((0, qkv_buf0), (1, qkv_buf1)):
        fetch_part(places, part, pieces, buf, sem.at[5], slice(0, PART))
    for source, target in ((tok, tok_ref), (feed, feed_ref), (feed_got, feed_got_ref)):
        start(source, target, sem.at[6])
    vec_ref[...] = jnp.zeros_like(vec_ref)
    for block in range(16):
        row, col = 8 + block // 4, block % 4 * UNIT
        vec_ref[row : row + 1, col : col + UNIT] = up_bias_grad_ref[block]
    wait(mixed_ref, sem.at[1])
    flip[...] = mixed_ref[...].T
    for ref in (hidden_ref, gc_ref, gc_got_ref, cot_ref):
        wait(ref, sem.at[0])
    turn(hidden_ref, ln2_gain_ref, gc_ref, gc_got_ref, cot_ref, ghid_ref, glow_ref, vec_ref)
    grads = [matrix(grad_buf0), matrix(grad_buf1)]
    for part in (0, 1):
        heads = slice(part * HALF, (part + 1) * HALF)
        grads[part][:, PART:] = dot(flip[...], glow_ref[:, heads]).astype(BF16)
    for buf in (out_buf0, out_buf1):
        wait(buf, sem.at[2])
    gmix_ref[...] = (
        dot_t(glow_ref[:, :HALF], matrix(out_buf0)[...]) + dot_t(glow_ref[:, HALF:], matrix(out_buf1)[...])
    ).astype(BF16)
    wait(low_ref, sem.at[4])
    flip[...] = low_ref[...].T
    wait(qkv_ref, sem.at[3])
    wait(prob_ref, sem.at[3])
    low, near, far = lane_marks()

    for part, grad_buf in ((0, grad_buf0), (1, grad_buf1)):
        @pl.loop(0, 4)
        def _(pair, part=part):
            begin = pl.multiple_of(pair * 128, 128)
            for block in range(TOK // BLOCK):
                rows = slice(block * BLOCK, (block + 1) * BLOCK)
                query = qkv_ref[part, rows, pl.ds(begin, 128)]
                key = qkv_ref[part, rows, pl.ds(begin + HALF, 128)]
                value = qkv_ref[part, rows, pl.ds(begin + 2 * HALF, 128)]
                gmix = gmix_ref[rows, pl.ds(pl.multiple_of(begin + part * HALF, 128), 128)]
                gmix = jnp.concatenate([gmix * near, gmix * far], axis=0)
                query = jnp.concatenate([query * (near * 0.125), query * (far * 0.125)], axis=0)
                prob_low = prob_ref[pair + 4 * part, block]
                prob = prob_low.astype(F32)
                gprob = dot_t(gmix, value)
                gscore = (prob * (gprob - jnp.sum(prob * gprob, axis=-1, keepdims=True))).astype(BF16)
                both = dot(gscore, key) * 0.125
                gqkv_ref[part, rows, pl.ds(begin, 128)] = jnp.where(low, both[:BLOCK], both[BLOCK:]).astype(BF16)
                gqkv_ref[part, rows, pl.ds(begin + HALF, 128)] = dot(gscore.T, query).astype(BF16)
                gqkv_ref[part, rows, pl.ds(begin + 2 * HALF, 128)] = dot(prob_low.T, gmix).astype(BF16)

        for n in range(3):
            cols = slice(n * HALF, (n + 1) * HALF)
            grads[part][:, cols] = dot(flip[...], gqkv_ref[part, :, cols]).astype(BF16)
        for side, slot, z, c in row_tiles(places):
            start(grad_buf.at[z, :, c], outs[2 * side + slot // 2].at[slot % 2, :, :, part * 2048 : (part + 1) * 2048], out_sem)
        heads = slice(part * HALF, (part + 1) * HALF)
        for row, n in ((2, 0), (3, 2)):
            vec_ref[row : row + 1, heads] = jnp.sum(gqkv_ref[part, :, n * HALF : (n + 1) * HALF].astype(F32), axis=0, keepdims=True)

    for ref in (tok_ref, feed_ref, feed_got_ref):
        wait(ref, sem.at[6])
    out_ref[...] = (hidden_ref[...] + feed_ref[...] + feed_got_ref[...].astype(F32) + down_bias_ref[...]).astype(BF16)
    start(out_ref, out_out, out_sem)
    for buf in (qkv_buf0, qkv_buf1):
        wait(buf, sem.at[5])
    gc_ref[...] = dot_t(gqkv_ref[0], matrix(qkv_buf0)[...]) + dot_t(gqkv_ref[1], matrix(qkv_buf1)[...])

    @pl.loop(0, TOK // 128)
    def _(i):
        rows = pl.ds(i * 128, 128)
        unit, scale = normed(tok_ref[rows, :].astype(F32))
        grad = gc_ref[rows, :]
        ghid_ref[rows, :] += norm_back(grad * ln1_ref[0:1, :], unit, scale)
        vec_ref[0:1, :] += jnp.sum(grad * unit, axis=0, keepdims=True)
        vec_ref[1:2, :] += jnp.sum(grad, axis=0, keepdims=True)

    start(ghid_ref, gin_out, out_sem)
    for ref in (grad_buf0, grad_buf1, out_ref, ghid_ref):
        wait(ref, out_sem)


def back(places, ln1, ln2_gain, down_bias, up_bias_grad, streams, pieces):
    wide, high = ((TOK, WIDTH), BF16), ((TOK, WIDTH), F32)
    heads = ((2, TOK, PART), BF16)
    scratch = [high, high, wide, wide, wide, wide, heads, ((8, 4, 2 * BLOCK, BLOCK), BF16), wide, high, wide]
    scratch += [high, wide, wide, heads, ((WIDTH, TOK), BF16), wide]
    rows = shape(2, 2, 64, 4096)
    return pl.pallas_call(
        back_kernel,
        in_specs=[SMEM] + [VMEM] * 4 + [HBM] * 15,
        out_specs=[HBM] * 2 + [VMEM] + [HBM] * 4,
        out_shape=[shape(TOK, WIDTH, dtype=F32), shape(TOK, WIDTH), shape(16, WIDTH, dtype=F32), rows, rows, rows, rows],
        scratch_shapes=[parts_buffer(PART)] * 2 + [parts_buffer(HALF)] * 2 + [parts_buffer(2048)] * 2
        + [pltpu.VMEM(*s) for s in scratch]
        + [FEW, ONE],
        compiler_params=pltpu.CompilerParams(vmem_limit_bytes=ROOM),
        cost_estimate=work(40e9),
        name="back",
    )(places, ln1, ln2_gain.reshape(1, WIDTH), down_bias.reshape(1, WIDTH), up_bias_grad, *streams, *pieces)


AXES = ("z", "yh", "c", "x", "yl")
ALONG_Y, PLANE_XY = ("yh", "yl"), ("yh", "x", "yl")


def device_number(place):
    return (
        ((place["z"] * 2 + place["y"] // 2) * 2 + place["c"]) * 4 + place["x"]
    ) * 2 + place["y"] % 2


def exchange_pairs(axis, second, alike=False):
    pairs = []
    for z, y, c, x in itertools.product(range(4), range(4), range(2), range(4)):
        here = {"z": z, "y": y, "c": c, "x": x}
        mask = 1 if (c == 0 or alike) != second else 3
        there = dict(here)
        there[axis] = here[axis] ^ mask
        pairs.append((device_number(here), device_number(there)))
    return pairs


def swap_axis(values, axis, second, alike=False):
    return lax.ppermute(values, AXES, exchange_pairs(axis, second, alike))


def swap_core(values):
    return lax.ppermute(values, "c", [(0, 1), (1, 0)])


def position(axis):
    if axis == "y":
        return lax.axis_index("yh") * 2 + lax.axis_index("yl")
    return lax.axis_index(axis)


def distance_of(core, slot):
    return jnp.where(core == 0, slot ^ (slot >> 1), ((slot << 1) & 3) ^ ((slot ^ (slot >> 1)) & 1))


def place_table():
    core, slots = lax.axis_index("c"), jnp.arange(4, dtype=jnp.int32)
    rows = [
        distance_of(side, slots) ^ position(axis)
        for side in (core, 1 - core)
        for axis in ("x", "y", "z")
    ]
    return jnp.concatenate(rows + [jnp.full((8,), core, jnp.int32)])


def add(left, right, dtype=BF16):
    return (left.astype(F32) + right.astype(F32)).astype(dtype)


def halves(own, got):
    count = own.shape[0] // 2
    return add(own[count:], got[count:]), add(own[:count], got[:count])


def spread(values, axes):
    return lax.all_to_all(jnp.broadcast_to(values, (16,) + values.shape), axes, 0, 0)


def together(*values):
    return lax.optimization_barrier(values)


def pair_bias(clip_ids):
    clips = clip_ids.reshape(-1, BLOCK)
    row = lax.broadcasted_iota(jnp.int32, (BLOCK, BLOCK), 0)
    col = lax.broadcasted_iota(jnp.int32, (BLOCK, BLOCK), 1)
    allowed = (clips[:, :, None] == clips[:, None, :]) & (row >= col)[None]
    return jnp.where(allowed, 0.0, -1e30).astype(F32)


def on_device(
    tokens,
    qkv_weight,
    out_weight,
    up_weight,
    down_weight,
    ln1_gain,
    ln1_bias,
    q_bias,
    v_bias,
    out_bias,
    ln2_gain,
    ln2_bias,
    up_bias,
    down_bias,
    segment_ids,
    cotangent,
):
    places = place_table()
    ln1 = jnp.stack([ln1_gain, ln1_bias])
    nothing = jnp.zeros((HALF,), F32)
    qkv_bias = jnp.stack(
        [
            jnp.concatenate([q_bias[cols], nothing, v_bias[cols]])[None]
            for cols in (slice(0, HALF), slice(HALF, WIDTH))
        ]
    )
    ln2 = jnp.stack([ln2_gain, ln2_bias])
    allowed = pair_bias(segment_ids)

    heads = qkv_weight.reshape(8, 3, WIDTH)
    pieces = []
    for cols in (slice(0, HALF), slice(HALF, WIDTH)):
        pieces += [heads[:, :, cols].reshape(8, PART), out_weight[:, cols]]
    def join(pairs):
        return together(*[jnp.concatenate(pair) for pair in pairs])

    rows = spread(jnp.concatenate(pieces, axis=1), PLANE_XY)
    down, up = down_weight[None], up_weight[None]
    down, up = join(((down, swap_axis(down, "z", False)), (up, swap_axis(up, "z", False))))
    rows, down_got, up_got, places, ln1, ln2, qkv_bias, allowed = together(
        rows, swap_axis(down, "z", True), swap_axis(up, "z", True), places, ln1, ln2, qkv_bias, allowed
    )
    rows = rows.reshape(1, 2, 64, 4096)
    rows_got = swap_axis(rows, "z", False)
    down, up = join(((down, down_got), (up, up_got)))
    down, up = join(((down, swap_axis(down, "x", False)), (up, swap_axis(up, "y", False))))
    rows_got, down_got, up_got, grad_other = together(
        rows_got, swap_axis(down, "x", True), swap_axis(up, "y", True), swap_core(cotangent)
    )
    rows, down, up = join(((rows, rows_got), (down, down_got), (up, up_got)))
    up = lax.all_gather(up, "x", axis=0).reshape(64, 128, 256)
    near, far = swap_axis(down, "y", False), swap_axis(down, "y", True)
    rows_got, near, far, other_rows = together(swap_axis(rows, "z", True), near, far, swap_core(rows))
    pieces = (rows, rows_got, other_rows, swap_core(rows_got))
    downs = (down, near, far, swap_axis(near, "y", True))

    low, qkv, prob, mixed, hidden, low2 = front(
        places, tokens, ln1, qkv_bias, allowed, out_bias, ln2, pieces
    )
    up_bias_grad, feed, feed_low, gc, gc_low, dup, keep_down, move_down = ffn(
        places, up_bias, low2, swap_core(low2), cotangent, grad_other, (up, *downs)
    )
    dup = lax.psum_scatter(dup, "x", scatter_dimension=0, tiled=True)[0]

    down_got = swap_axis(move_down, "y", True)
    grad_tokens, output, vector, own_keep, own_move, other_keep, other_move = back(
        places, ln1, ln2_gain, down_bias, up_bias_grad,
        (hidden, gc, swap_core(gc_low), cotangent, mixed, low, qkv, prob, tokens, feed, swap_core(feed_low)),
        pieces,
    )
    down_got, vector, own_keep, own_move, other_keep, other_move = together(
        down_got, vector, own_keep, own_move, other_keep, other_move
    )
    got_move, got_keep, vector_got = swap_core(other_move), swap_core(other_keep), swap_core(vector)
    move = add(own_move, got_move)
    move, down_got, vector, vector_got = together(move, down_got, vector, vector_got)
    got = swap_axis(move, "z", True)
    keep = add(own_keep, got_keep)
    move_down, keep_down = halves(keep_down, down_got)
    down_got = swap_axis(move_down, "y", False)
    move_down, keep_down = halves(keep_down, down_got)
    down_got = swap_axis(move_down, "x", True)
    vector = vector + vector_got
    vector_got, dup = together(swap_axis(vector, "x", False, True), dup)
    dup = lax.psum_scatter(dup, ALONG_Y, scatter_dimension=0, tiled=True)[0]
    vector = vector + vector_got
    vector_got = swap_axis(vector, "x", True, True)
    got, keep, down_got, vector_got = together(got, keep, down_got, vector_got)

    move, keep = halves(keep, got)
    move, down_got, vector_got = together(move, down_got, vector_got)
    got = swap_axis(move, "z", False)
    move_down, keep_down = halves(keep_down, down_got)
    down_got = swap_axis(move_down, "x", False)
    vector = vector + vector_got
    vector = vector + swap_axis(vector, "y", False, True)
    vector_got = swap_axis(vector, "y", True, True)
    got, down_got, vector_got = together(got, down_got, vector_got)

    rows_sum = add(keep, got).reshape(16, 8, 4096)
    rows_sum, down_got, vector_got = together(rows_sum, down_got, vector_got)
    rows_parts = lax.all_to_all(rows_sum, PLANE_XY, 0, 0)
    vector = vector + vector_got
    move_down, keep_down = halves(keep_down, down_got)
    down_got, up_got, vector_got = together(
        swap_axis(move_down, "z", True), swap_axis(dup[2:], "z", True), swap_axis(vector, "z", False, True)
    )
    vector = vector + vector_got
    vector = vector + swap_axis(vector, "z", True, True)
    move_down, keep_down = halves(keep_down, down_got)
    down_grad = add(keep_down, swap_axis(move_down, "z", False), F32)[0]
    move_up, keep_up = halves(dup[:2], up_got)
    up_grad = add(keep_up, swap_axis(move_up, "z", False), F32)[0]
    row = jnp.sum(rows_parts.astype(F32), axis=0).reshape(8, 2, 2048)
    qkv_grad = row[:, :, :PART].reshape(8, 2, 3, HALF).transpose(0, 2, 1, 3).reshape(8, 3 * WIDTH)
    out_grad = row[:, :, PART:].reshape(8, WIDTH)
    summed = vector.reshape(-1)
    vectors = [summed[i * WIDTH : (i + 1) * WIDTH] for i in range(8)]
    return (
        output,
        grad_tokens,
        qkv_grad,
        out_grad,
        up_grad,
        down_grad,
        *vectors[:7],
        summed[8 * WIDTH : 12 * WIDTH],
        vectors[7],
    )


def solution(mesh):
    fine = Mesh(mesh.devices.reshape(4, 2, 2, 4, 2), AXES)
    every, hidden, model = AXES, ("z", "yh", "c"), ("x", "yl")
    weights = (P(every, None), P(every, None), P(model, hidden), P(hidden, model))
    return jax.shard_map(
        on_device,
        mesh=fine,
        in_specs=(P(every, None), *weights, *[P()] * 9, P(every), P(every, None)),
        out_specs=(P(every, None), P(every, None), *weights, *[P()] * 9),
        check_vma=False,
    )
```

```python
import functools
import itertools

import jax
import jax.numpy as jnp
from jax import lax
from jax.experimental import pallas as pl
from jax.experimental.pallas import tpu as pltpu
from jax.sharding import Mesh, PartitionSpec as P

F32, BF16 = jnp.float32, jnp.bfloat16
TOK, WIDTH, FF = 512, 1024, 4096
BOTH = 2 * TOK
CHUNK = 1024
UNIT = 256
WIDE = 2 * UNIT
ROOT = 0.7978845608028654
CUBE = 0.044715
VMEM, ANY, HBM, SMEM = (
    pl.BlockSpec(memory_space=kind) for kind in (pltpu.VMEM, pl.ANY, pltpu.HBM, pltpu.SMEM)
)
ROOM = 60 * 2**20
ONE = pltpu.SemaphoreType.DMA
TWO = pltpu.SemaphoreType.DMA((2,))
FEW = pltpu.SemaphoreType.DMA((8,))


def shape(*dims, dtype=BF16):
    return jax.ShapeDtypeStruct(dims, dtype)


def work(flops):
    return pl.CostEstimate(flops=int(flops * 0.4), bytes_accessed=1 << 20, transcendentals=0)


def dot(a, b):
    return lax.dot_general(a, b, (((1,), (0,)), ((), ())), preferred_element_type=F32)


def dot_t(a, b):
    return lax.dot_general(a, b, (((1,), (1,)), ((), ())), preferred_element_type=F32)


def normed(values):
    center = values - jnp.mean(values, axis=-1, keepdims=True)
    scale = lax.rsqrt(jnp.mean(center * center, axis=-1, keepdims=True) + 1e-05)
    return center * scale, scale


def norm_back(edge, unit, scale):
    return (edge - jnp.mean(edge, axis=-1, keepdims=True) - unit * jnp.mean(edge * unit, axis=-1, keepdims=True)) * scale


def start(source, target, sem):
    pltpu.make_async_copy(source, target, sem).start()


def wait(ref, sem):
    pltpu.make_async_copy(ref, ref, sem).wait()


def place_of(places, side, axis, slot):
    return places[side * 12 + "xyz".index(axis) * 4 + slot]


def ffn_kernel(places, bias_ref, low_own, low_other, grad_own, grad_other, up, down0, down1, down2, down3,
               bias_grad_ref, feed_ref, feed_low_ref, gc_ref, gc_low_ref, dup, ddown_keep, ddown_move,
               up_buf, down_buf, dup_buf, ddown_buf, low, grad, low_t, act_buf, gpre_buf, total, grad_total,
               feed_low, gc_low, in_sem, up_sem, down_sem, out_sem):
    core = places[24]

    def tiles(chunk, *parts):
        for part in parts or (0, 1):
            for sy in range(4):
                y = place_of(places, 0, "y", sy)
                yh, yl = lax.div(y, 2), lax.rem(y, 2)
                unit = pl.ds(pl.multiple_of((part * 2 + yh) * UNIT, UNIT), UNIT)
                for x in range(4):
                    yield sy, chunk * 2 + part, x, yl, unit

    def model(x, yl):
        return pl.ds(pl.multiple_of((x * 2 + yl) * 128, 128), 128)

    def fetch(chunk):
        for sy, sz, x, yl, unit in tiles(chunk):
            start(up.at[x * 16 + sy * 4 + sz], up_buf.at[chunk, model(x, yl), unit], up_sem.at[chunk])
        for sy, sz, sx, yl, unit in tiles(chunk):
            cols = model(place_of(places, 0, "x", sx), yl)
            start((down0, down1, down2, down3)[sy].at[sx * 4 + sz], down_buf.at[chunk, unit, cols], down_sem.at[chunk])

    def send(chunk, part):
        for y in range(4):
            for x in range(4):
                unit = slice((part * 2 + y // 2) * UNIT, (part * 2 + y // 2 + 1) * UNIT)
                start(dup_buf.at[chunk, model(x, y % 2), unit], dup.at[x, y, chunk * 2 + part], out_sem)
        for sy, sz, sx, yl, unit in tiles(chunk, part):
            source = ddown_buf.at[chunk, unit, model(place_of(places, 0, "x", sx), yl)]
            start(source, (ddown_keep, ddown_move)[sy // 2].at[sy % 2 * 16 + sx * 4 + sz], out_sem)

    start(low_own, low.at[pl.ds(0, TOK)], in_sem.at[0])
    start(low_other, low.at[pl.ds(TOK, TOK)], in_sem.at[0])
    fetch(0)
    start(grad_own, grad.at[pl.ds(0, TOK)], in_sem.at[1])
    start(grad_other, grad.at[pl.ds(TOK, TOK)], in_sem.at[1])
    bias_grad_ref[...] = jnp.zeros_like(bias_grad_ref)
    wait(low, in_sem.at[0])
    wait(grad, in_sem.at[1])

    for chunk in (0, 1):
        wait(up_buf.at[chunk], up_sem.at[chunk])
        wait(down_buf.at[chunk], down_sem.at[chunk])
        for n in range(CHUNK // WIDE):
            cols = slice(n * WIDE, (n + 1) * WIDE)
            blocks = [(place_of(places, 0, "z", chunk * 2 + n) * 2 + yh) * 2 + core for yh in (0, 1)]
            bias = jnp.concatenate([bias_ref[block] for block in blocks], axis=1)
            pre = dot(low[...], up_buf[chunk, :, cols]) + bias
            gact = dot_t(grad[...], down_buf[chunk, cols, :])
            square = pre * pre
            bend = jnp.tanh(ROOT * (pre + CUBE * square * pre))
            half = 0.5 + 0.5 * bend
            act = (pre * half).astype(BF16)
            slope = half + 0.5 * pre * (1.0 - bend * bend) * (ROOT + 3.0 * ROOT * CUBE * square)
            gpre = (gact * slope).astype(BF16)
            if chunk == 0 and n == 0:
                fetch(1)
            act_buf[:, cols] = act
            gpre_buf[:, cols] = gpre
            bias_grad = jnp.sum(gpre.astype(F32), axis=0, keepdims=True)
            for yh, block in enumerate(blocks):
                bias_grad_ref[block] = bias_grad[:, yh * UNIT : (yh + 1) * UNIT]
            if chunk == 0 and n == 0:
                low_t[...] = low[...].T
            ddown_buf[chunk, cols, :] = dot(act.T, grad[...]).astype(BF16)
            dup_buf[chunk, :, cols] = dot(low_t[...], gpre).astype(BF16)
            send(chunk, n)
        more = dot_t(gpre_buf[...], up_buf[chunk])
        feed = dot(act_buf[...], down_buf[chunk])
        if chunk == 0:
            grad_total[...] = more
            total[...] = feed
        else:
            grad_total[...] += more
            gc_low[...] = grad_total[TOK:, :].astype(BF16)
            start(gc_low, gc_low_ref, out_sem)
            start(grad_total.at[pl.ds(0, TOK)], gc_ref, out_sem)
            total[...] += feed
            feed_low[...] = total[TOK:, :].astype(BF16)
            start(feed_low, feed_low_ref, out_sem)
            start(total.at[pl.ds(0, TOK)], feed_ref, out_sem)
    for ref in (dup_buf, ddown_buf, gc_low, feed_low, grad_total.at[pl.ds(0, TOK)], total.at[pl.ds(0, TOK)]):
        wait(ref, out_sem)


def ffn(places, up_bias, low_own, low_other, grad_own, grad_other, weights):
    big = pltpu.VMEM((2, CHUNK, CHUNK), BF16)
    rows = pltpu.VMEM((BOTH, WIDTH), BF16)
    sums = pltpu.VMEM((BOTH, WIDTH), F32)
    half = pltpu.VMEM((TOK, WIDTH), BF16)
    return pl.pallas_call(
        ffn_kernel,
        in_specs=[SMEM, VMEM] + [HBM] * 9,
        out_specs=[VMEM] + [HBM] * 7,
        out_shape=[
            shape(16, 1, UNIT, dtype=F32),
            shape(TOK, WIDTH, dtype=F32),
            shape(TOK, WIDTH),
            shape(TOK, WIDTH, dtype=F32),
            shape(TOK, WIDTH),
            shape(4, 4, 4, 128, 256),
            shape(32, 256, 128),
            shape(32, 256, 128),
        ],
        scratch_shapes=[
            big, big, big, big, rows, rows, rows,
            pltpu.VMEM((BOTH, CHUNK), BF16),
            pltpu.VMEM((BOTH, CHUNK), BF16),
            sums, sums, half, half, TWO, TWO, TWO, ONE,
        ],
        compiler_params=pltpu.CompilerParams(vmem_limit_bytes=ROOM),
        cost_estimate=work(40e9),
        name="ffn",
    )(places, up_bias.reshape(16, 1, UNIT), low_own, low_other, grad_own, grad_other, *weights)


BLOCK = 128
HALF = 512
PART = 3 * HALF


def row_tiles(places):
    core = places[24]
    for side in (0, 1):
        for slot in range(4):
            yield side, slot, place_of(places, side, "z", slot), core if side == 0 else 1 - core


def part_cols(part, cols):
    return slice(part * 2048 + cols.start, part * 2048 + cols.stop)


def fetch_part(places, part, pieces, buf, sem, cols):
    for side, slot, z, c in row_tiles(places):
        start(pieces[2 * side + slot // 2].at[slot % 2, :, :, part_cols(part, cols)], buf.at[z, :, c], sem)


def matrix(ref):
    return ref.reshape(WIDTH, ref.shape[-1])


def parts_buffer(cols):
    return pltpu.VMEM((4, 2, 2, 64, cols), BF16)


def lane_marks():
    low = lax.broadcasted_iota(jnp.int32, (1, 128), 1) < 64
    return low, jnp.where(low, 1.0, 0.0).astype(BF16), jnp.where(low, 0.0, 1.0).astype(BF16)


def front_kernel(places, ln1_ref, qkv_bias_ref, pair_ref, out_bias_ref, ln2_ref, tok, *refs):
    pieces, refs = refs[:4], refs[4:]
    low_out, qkv_out, prob_out, mixed_out, hidden_out, normed_out, qkv_buf0, qkv_buf1, out_buf0, out_buf1 = refs[:10]
    tok_ref, low_ref, qkv_ref, prob_ref, mixed_ref, hidden_ref, normed_ref, sem, out_sem = refs[10:]
    start(tok, tok_ref, sem.at[4])
    for part, buf in ((0, qkv_buf0), (1, qkv_buf1)):
        fetch_part(places, part, pieces, buf, sem.at[part], slice(0, PART))
    for part, buf in ((0, out_buf0), (1, out_buf1)):
        fetch_part(places, part, pieces, buf, sem.at[2 + part], slice(PART, 2048))
    wait(tok_ref, sem.at[4])

    @pl.loop(0, TOK // 128)
    def _(i):
        rows = pl.ds(i * 128, 128)
        unit, _ = normed(tok_ref[rows, :].astype(F32))
        low_ref[rows, :] = (unit * ln1_ref[0:1, :] + ln1_ref[1:2, :]).astype(BF16)

    start(low_ref, low_out, out_sem)
    for part, buf in ((0, qkv_buf0), (1, qkv_buf1)):
        wait(buf, sem.at[part])
        for n in range(3):
            cols = slice(n * HALF, (n + 1) * HALF)
            qkv_ref[part, :, cols] = (dot(low_ref[...], matrix(buf)[:, cols]) + qkv_bias_ref[part, :, cols]).astype(BF16)
        start(qkv_ref.at[part], qkv_out.at[part], out_sem)
    low, near, far = lane_marks()
    near, far = near * 0.125, far * 0.125

    @pl.loop(0, 8)
    def _(pair):
        part = lax.div(pair, 4)
        begin = pl.multiple_of(lax.rem(pair, 4) * 128, 128)
        lanes = pl.ds(pl.multiple_of(pair * 128, 128), 128)
        for block in range(TOK // BLOCK):
            rows = slice(block * BLOCK, (block + 1) * BLOCK)
            query = qkv_ref[part, rows, pl.ds(begin, 128)]
            key = qkv_ref[part, rows, pl.ds(begin + HALF, 128)]
            value = qkv_ref[part, rows, pl.ds(begin + 2 * HALF, 128)]
            bias = pair_ref[block]
            score = dot_t(jnp.concatenate([query * near, query * far], axis=0), key) + jnp.concatenate([bias, bias], axis=0)
            power = jnp.exp(score - jnp.max(score, axis=-1, keepdims=True))
            prob = (power * (1.0 / jnp.sum(power, axis=-1, keepdims=True))).astype(BF16)
            prob_ref[pair, block] = prob
            both = dot(prob, value)
            mixed_ref[rows, lanes] = jnp.where(low, both[:BLOCK], both[BLOCK:]).astype(BF16)

    start(prob_ref, prob_out, out_sem)
    start(mixed_ref, mixed_out, out_sem)
    for part, buf in ((0, out_buf0), (1, out_buf1)):
        cols = slice(part * HALF, (part + 1) * HALF)
        wait(buf, sem.at[2 + part])
        hidden_ref[:, cols] = tok_ref[:, cols].astype(F32) + dot(mixed_ref[...], matrix(buf)[...]) + out_bias_ref[:, cols]
    start(hidden_ref, hidden_out, out_sem)

    @pl.loop(0, TOK // 128)
    def _(i):
        rows = pl.ds(i * 128, 128)
        unit, _ = normed(hidden_ref[rows, :])
        normed_ref[rows, :] = (unit * ln2_ref[0:1, :] + ln2_ref[1:2, :]).astype(BF16)

    start(normed_ref, normed_out, out_sem)
    for ref in (low_ref, qkv_ref, prob_ref, mixed_ref, hidden_ref, normed_ref):
        wait(ref, out_sem)


def front(places, tokens, ln1, qkv_bias, allowed, out_bias, ln2, pieces):
    wide = ((TOK, WIDTH), BF16)
    outs = [wide, ((2, TOK, PART), BF16), ((8, 4, 2 * BLOCK, BLOCK), BF16), wide, ((TOK, WIDTH), F32), wide]
    return pl.pallas_call(
        front_kernel,
        in_specs=[SMEM] + [VMEM] * 5 + [HBM] * 5,
        out_specs=[HBM] * 6,
        out_shape=[jax.ShapeDtypeStruct(*out) for out in outs],
        scratch_shapes=[parts_buffer(PART)] * 2 + [parts_buffer(HALF)] * 2 + [pltpu.VMEM(*s) for s in [wide] + outs] + [FEW, ONE],
        compiler_params=pltpu.CompilerParams(vmem_limit_bytes=ROOM),
        cost_estimate=work(24e9),
        name="front",
    )(places, ln1, qkv_bias, allowed, out_bias.reshape(1, WIDTH), ln2, tokens, *pieces)


def turn(hidden_ref, gain_ref, gc_ref, got_ref, grad_ref, ghid_ref, glow_ref, vec_ref):
    @pl.loop(0, TOK // 128)
    def _(part):
        rows = pl.ds(part * 128, 128)
        unit, scale = normed(hidden_ref[rows, :])
        gc = gc_ref[rows, :] + got_ref[rows, :].astype(F32)
        gout = grad_ref[rows, :].astype(F32)
        ghid = gout + norm_back(gc * gain_ref[...], unit, scale)
        ghid_ref[rows, :] = ghid
        glow_ref[rows, :] = ghid.astype(BF16)
        vec_ref[4:5, :] += jnp.sum(ghid, axis=0, keepdims=True)
        vec_ref[5:6, :] += jnp.sum(gc * unit, axis=0, keepdims=True)
        vec_ref[6:7, :] += jnp.sum(gc, axis=0, keepdims=True)
        vec_ref[7:8, :] += jnp.sum(gout, axis=0, keepdims=True)


def back_kernel(places, ln1_ref, ln2_gain_ref, down_bias_ref, up_bias_grad_ref,
                hidden, gc, gc_got, cot, mixed, low_in, qkv, prob, tok, feed, feed_got, *refs):
    pieces, refs = refs[:4], refs[4:]
    gin_out, out_out, vec_ref, *outs = refs[:7]
    qkv_buf0, qkv_buf1, out_buf0, out_buf1, grad_buf0, grad_buf1 = refs[7:13]
    hidden_ref, gc_ref, gc_got_ref, cot_ref, mixed_ref, low_ref, qkv_ref, prob_ref, tok_ref, feed_ref, feed_got_ref = refs[13:24]
    ghid_ref, glow_ref, gmix_ref, gqkv_ref, flip, out_ref, sem, out_sem = refs[24:]
    for source, target in ((hidden, hidden_ref), (gc, gc_ref), (gc_got, gc_got_ref), (cot, cot_ref)):
        start(source, target, sem.at[0])
    start(mixed, mixed_ref, sem.at[1])
    for part, buf in ((0, out_buf0), (1, out_buf1)):
        fetch_part(places, part, pieces, buf, sem.at[2], slice(PART, 2048))
    start(qkv, qkv_ref, sem.at[3])
    start(prob, prob_ref, sem.at[3])
    start(low_in, low_ref, sem.at[4])
    for part, buf in ((0, qkv_buf0), (1, qkv_buf1)):
        fetch_part(places, part, pieces, buf, sem.at[5], slice(0, PART))
    for source, target in ((tok, tok_ref), (feed, feed_ref), (feed_got, feed_got_ref)):
        start(source, target, sem.at[6])
    vec_ref[...] = jnp.zeros_like(vec_ref)
    for block in range(16):
        row, col = 8 + block // 4, block % 4 * UNIT
        vec_ref[row : row + 1, col : col + UNIT] = up_bias_grad_ref[block]
    wait(mixed_ref, sem.at[1])
    flip[...] = mixed_ref[...].T
    for ref in (hidden_ref, gc_ref, gc_got_ref, cot_ref):
        wait(ref, sem.at[0])
    turn(hidden_ref, ln2_gain_ref, gc_ref, gc_got_ref, cot_ref, ghid_ref, glow_ref, vec_ref)
    grads = [matrix(grad_buf0), matrix(grad_buf1)]
    for part in (0, 1):
        heads = slice(part * HALF, (part + 1) * HALF)
        grads[part][:, PART:] = dot(flip[...], glow_ref[:, heads]).astype(BF16)
    for buf in (out_buf0, out_buf1):
        wait(buf, sem.at[2])
    gmix_ref[...] = (
        dot_t(glow_ref[:, :HALF], matrix(out_buf0)[...]) + dot_t(glow_ref[:, HALF:], matrix(out_buf1)[...])
    ).astype(BF16)
    wait(low_ref, sem.at[4])
    flip[...] = low_ref[...].T
    wait(qkv_ref, sem.at[3])
    wait(prob_ref, sem.at[3])
    low, near, far = lane_marks()

    for part, grad_buf in ((0, grad_buf0), (1, grad_buf1)):
        @pl.loop(0, 4)
        def _(pair, part=part):
            begin = pl.multiple_of(pair * 128, 128)
            for block in range(TOK // BLOCK):
                rows = slice(block * BLOCK, (block + 1) * BLOCK)
                query = qkv_ref[part, rows, pl.ds(begin, 128)]
                key = qkv_ref[part, rows, pl.ds(begin + HALF, 128)]
                value = qkv_ref[part, rows, pl.ds(begin + 2 * HALF, 128)]
                gmix = gmix_ref[rows, pl.ds(pl.multiple_of(begin + part * HALF, 128), 128)]
                gmix = jnp.concatenate([gmix * near, gmix * far], axis=0)
                query = jnp.concatenate([query * (near * 0.125), query * (far * 0.125)], axis=0)
                prob_low = prob_ref[pair + 4 * part, block]
                prob = prob_low.astype(F32)
                gprob = dot_t(gmix, value)
                gscore = (prob * (gprob - jnp.sum(prob * gprob, axis=-1, keepdims=True))).astype(BF16)
                both = dot(gscore, key) * 0.125
                gqkv_ref[part, rows, pl.ds(begin, 128)] = jnp.where(low, both[:BLOCK], both[BLOCK:]).astype(BF16)
                gqkv_ref[part, rows, pl.ds(begin + HALF, 128)] = dot(gscore.T, query).astype(BF16)
                gqkv_ref[part, rows, pl.ds(begin + 2 * HALF, 128)] = dot(prob_low.T, gmix).astype(BF16)

        for n in range(3):
            cols = slice(n * HALF, (n + 1) * HALF)
            grads[part][:, cols] = dot(flip[...], gqkv_ref[part, :, cols]).astype(BF16)
        for side, slot, z, c in row_tiles(places):
            start(grad_buf.at[z, :, c], outs[2 * side + slot // 2].at[slot % 2, :, :, part * 2048 : (part + 1) * 2048], out_sem)
        heads = slice(part * HALF, (part + 1) * HALF)
        for row, n in ((2, 0), (3, 2)):
            vec_ref[row : row + 1, heads] = jnp.sum(gqkv_ref[part, :, n * HALF : (n + 1) * HALF].astype(F32), axis=0, keepdims=True)

    for ref in (tok_ref, feed_ref, feed_got_ref):
        wait(ref, sem.at[6])
    out_ref[...] = (hidden_ref[...] + feed_ref[...] + feed_got_ref[...].astype(F32) + down_bias_ref[...]).astype(BF16)
    start(out_ref, out_out, out_sem)
    for buf in (qkv_buf0, qkv_buf1):
        wait(buf, sem.at[5])
    gc_ref[...] = dot_t(gqkv_ref[0], matrix(qkv_buf0)[...]) + dot_t(gqkv_ref[1], matrix(qkv_buf1)[...])

    @pl.loop(0, TOK // 128)
    def _(i):
        rows = pl.ds(i * 128, 128)
        unit, scale = normed(tok_ref[rows, :].astype(F32))
        grad = gc_ref[rows, :]
        ghid_ref[rows, :] += norm_back(grad * ln1_ref[0:1, :], unit, scale)
        vec_ref[0:1, :] += jnp.sum(grad * unit, axis=0, keepdims=True)
        vec_ref[1:2, :] += jnp.sum(grad, axis=0, keepdims=True)

    start(ghid_ref, gin_out, out_sem)
    for ref in (grad_buf0, grad_buf1, out_ref, ghid_ref):
        wait(ref, out_sem)


def back(places, ln1, ln2_gain, down_bias, up_bias_grad, streams, pieces):
    wide, high = ((TOK, WIDTH), BF16), ((TOK, WIDTH), F32)
    heads = ((2, TOK, PART), BF16)
    scratch = [high, high, wide, wide, wide, wide, heads, ((8, 4, 2 * BLOCK, BLOCK), BF16), wide, high, wide]
    scratch += [high, wide, wide, heads, ((WIDTH, TOK), BF16), wide]
    rows = shape(2, 2, 64, 4096)
    return pl.pallas_call(
        back_kernel,
        in_specs=[SMEM] + [VMEM] * 4 + [HBM] * 15,
        out_specs=[HBM] * 2 + [VMEM] + [HBM] * 4,
        out_shape=[shape(TOK, WIDTH, dtype=F32), shape(TOK, WIDTH), shape(16, WIDTH, dtype=F32), rows, rows, rows, rows],
        scratch_shapes=[parts_buffer(PART)] * 2 + [parts_buffer(HALF)] * 2 + [parts_buffer(2048)] * 2
        + [pltpu.VMEM(*s) for s in scratch]
        + [FEW, ONE],
        compiler_params=pltpu.CompilerParams(vmem_limit_bytes=ROOM),
        cost_estimate=work(40e9),
        name="back",
    )(places, ln1, ln2_gain.reshape(1, WIDTH), down_bias.reshape(1, WIDTH), up_bias_grad, *streams, *pieces)


AXES = ("z", "yh", "c", "x", "yl")
ALONG_Y, PLANE_XY = ("yh", "yl"), ("yh", "x", "yl")


def device_number(place):
    return (
        ((place["z"] * 2 + place["y"] // 2) * 2 + place["c"]) * 4 + place["x"]
    ) * 2 + place["y"] % 2


def exchange_pairs(axis, second, alike=False):
    pairs = []
    for z, y, c, x in itertools.product(range(4), range(4), range(2), range(4)):
        here = {"z": z, "y": y, "c": c, "x": x}
        mask = 1 if (c == 0 or alike) != second else 3
        there = dict(here)
        there[axis] = here[axis] ^ mask
        pairs.append((device_number(here), device_number(there)))
    return pairs


def swap_axis(values, axis, second, alike=False):
    return lax.ppermute(values, AXES, exchange_pairs(axis, second, alike))


def swap_core(values):
    return lax.ppermute(values, "c", [(0, 1), (1, 0)])


def position(axis):
    if axis == "y":
        return lax.axis_index("yh") * 2 + lax.axis_index("yl")
    return lax.axis_index(axis)


def distance_of(core, slot):
    return jnp.where(core == 0, slot ^ (slot >> 1), ((slot << 1) & 3) ^ ((slot ^ (slot >> 1)) & 1))


def place_table():
    core, slots = lax.axis_index("c"), jnp.arange(4, dtype=jnp.int32)
    rows = [
        distance_of(side, slots) ^ position(axis)
        for side in (core, 1 - core)
        for axis in ("x", "y", "z")
    ]
    return jnp.concatenate(rows + [jnp.full((8,), core, jnp.int32)])


def add(left, right, dtype=BF16):
    return (left.astype(F32) + right.astype(F32)).astype(dtype)


def halves(own, got):
    count = own.shape[0] // 2
    return add(own[count:], got[count:]), add(own[:count], got[:count])


def spread(values, axes):
    return lax.all_to_all(jnp.broadcast_to(values, (16,) + values.shape), axes, 0, 0)


def together(*values):
    return lax.optimization_barrier(values)


def pair_bias(clip_ids):
    clips = clip_ids.reshape(-1, BLOCK)
    row = lax.broadcasted_iota(jnp.int32, (BLOCK, BLOCK), 0)
    col = lax.broadcasted_iota(jnp.int32, (BLOCK, BLOCK), 1)
    allowed = (clips[:, :, None] == clips[:, None, :]) & (row >= col)[None]
    return jnp.where(allowed, 0.0, -1e30).astype(F32)


def on_device(
    tokens,
    qkv_weight,
    out_weight,
    up_weight,
    down_weight,
    ln1_gain,
    ln1_bias,
    q_bias,
    v_bias,
    out_bias,
    ln2_gain,
    ln2_bias,
    up_bias,
    down_bias,
    segment_ids,
    cotangent,
):
    places = place_table()
    ln1 = jnp.stack([ln1_gain, ln1_bias])
    nothing = jnp.zeros((HALF,), F32)
    qkv_bias = jnp.stack(
        [
            jnp.concatenate([q_bias[cols], nothing, v_bias[cols]])[None]
            for cols in (slice(0, HALF), slice(HALF, WIDTH))
        ]
    )
    ln2 = jnp.stack([ln2_gain, ln2_bias])
    allowed = pair_bias(segment_ids)

    heads = qkv_weight.reshape(8, 3, WIDTH)
    pieces = []
    for cols in (slice(0, HALF), slice(HALF, WIDTH)):
        pieces += [heads[:, :, cols].reshape(8, PART), out_weight[:, cols]]
    def join(pairs):
        return together(*[jnp.concatenate(pair) for pair in pairs])

    rows = spread(jnp.concatenate(pieces, axis=1), PLANE_XY)
    down, up = down_weight[None], up_weight[None]
    down, up = join(((down, swap_axis(down, "z", False)), (up, swap_axis(up, "z", False))))
    rows, down_got, up_got, places, ln1, ln2, qkv_bias, allowed = together(
        rows, swap_axis(down, "z", True), swap_axis(up, "z", True), places, ln1, ln2, qkv_bias, allowed
    )
    rows = rows.reshape(1, 2, 64, 4096)
    rows_got = swap_axis(rows, "z", False)
    down, up = join(((down, down_got), (up, up_got)))
    down, up = join(((down, swap_axis(down, "x", False)), (up, swap_axis(up, "y", False))))
    rows_got, down_got, up_got, grad_other = together(
        rows_got, swap_axis(down, "x", True), swap_axis(up, "y", True), swap_core(cotangent)
    )
    rows, down, up = join(((rows, rows_got), (down, down_got), (up, up_got)))
    up = lax.all_gather(up, "x", axis=0).reshape(64, 128, 256)
    near, far = swap_axis(down, "y", False), swap_axis(down, "y", True)
    rows_got, near, far, other_rows = together(swap_axis(rows, "z", True), near, far, swap_core(rows))
    pieces = (rows, rows_got, other_rows, swap_core(rows_got))
    downs = (down, near, far, swap_axis(near, "y", True))

    low, qkv, prob, mixed, hidden, low2 = front(
        places, tokens, ln1, qkv_bias, allowed, out_bias, ln2, pieces
    )
    up_bias_grad, feed, feed_low, gc, gc_low, dup, keep_down, move_down = ffn(
        places, up_bias, low2, swap_core(low2), cotangent, grad_other, (up, *downs)
    )
    dup = lax.psum_scatter(dup, "x", scatter_dimension=0, tiled=True)[0]

    down_got = swap_axis(move_down, "y", True)
    grad_tokens, output, vector, own_keep, own_move, other_keep, other_move = back(
        places, ln1, ln2_gain, down_bias, up_bias_grad,
        (hidden, gc, swap_core(gc_low), cotangent, mixed, low, qkv, prob, tokens, feed, swap_core(feed_low)),
        pieces,
    )
    down_got, vector, own_keep, own_move, other_keep, other_move = together(
        down_got, vector, own_keep, own_move, other_keep, other_move
    )
    got_move, got_keep, vector_got = swap_core(other_move), swap_core(other_keep), swap_core(vector)
    move = add(own_move, got_move)
    move, down_got, vector, vector_got = together(move, down_got, vector, vector_got)
    got = swap_axis(move, "z", True)
    keep = add(own_keep, got_keep)
    move_down, keep_down = halves(keep_down, down_got)
    down_got = swap_axis(move_down, "y", False)
    move_down, keep_down = halves(keep_down, down_got)
    down_got = swap_axis(move_down, "x", True)
    vector = vector + vector_got
    vector_got, dup = together(swap_axis(vector, "x", False, True), dup)
    dup = lax.psum_scatter(dup, ALONG_Y, scatter_dimension=0, tiled=True)[0]
    vector = vector + vector_got
    vector_got = swap_axis(vector, "x", True, True)
    got, keep, down_got, vector_got, dup = together(got, keep, down_got, vector_got, dup)

    move, keep = halves(keep, got)
    move, down_got, vector_got = together(move, down_got, vector_got)
    got = swap_axis(move, "z", False)
    move_down, keep_down = halves(keep_down, down_got)
    down_got = swap_axis(move_down, "x", False)
    up_got = swap_axis(dup[2:], "z", True)
    vector = vector + vector_got
    vector = vector + swap_axis(vector, "y", False, True)
    vector_got = swap_axis(vector, "y", True, True)
    got, down_got, up_got, vector_got = together(got, down_got, up_got, vector_got)

    rows_sum = add(keep, got).reshape(16, 8, 4096)
    rows_sum, down_got, vector_got = together(rows_sum, down_got, vector_got)
    rows_parts = lax.all_to_all(rows_sum, PLANE_XY, 0, 0)
    vector = vector + vector_got
    for second in (False, True):
        vector = vector + swap_axis(vector, "z", second, True)
    for second in (True, False):
        move_down, keep_down = halves(keep_down, down_got)
        down_got = swap_axis(move_down, "z", second)
    move_up, keep_up = halves(dup[:2], up_got)
    up_grad = add(keep_up, swap_axis(move_up, "z", False), F32)[0]
    down_grad = add(keep_down, down_got, F32)[0]
    row = jnp.sum(rows_parts.astype(F32), axis=0).reshape(8, 2, 2048)
    qkv_grad = row[:, :, :PART].reshape(8, 2, 3, HALF).transpose(0, 2, 1, 3).reshape(8, 3 * WIDTH)
    out_grad = row[:, :, PART:].reshape(8, WIDTH)
    summed = vector.reshape(-1)
    vectors = [summed[i * WIDTH : (i + 1) * WIDTH] for i in range(8)]
    return (
        output,
        grad_tokens,
        qkv_grad,
        out_grad,
        up_grad,
        down_grad,
        *vectors[:7],
        summed[8 * WIDTH : 12 * WIDTH],
        vectors[7],
    )


def solution(mesh):
    fine = Mesh(mesh.devices.reshape(4, 2, 2, 4, 2), AXES)
    every, hidden, model = AXES, ("z", "yh", "c"), ("x", "yl")
    weights = (P(every, None), P(every, None), P(model, hidden), P(hidden, model))
    return jax.shard_map(
        on_device,
        mesh=fine,
        in_specs=(P(every, None), *weights, *[P()] * 9, P(every), P(every, None)),
        out_specs=(P(every, None), P(every, None), *weights, *[P()] * 9),
        check_vma=False,
    )
```

```python
import functools
import itertools

import jax
import jax.numpy as jnp
from jax import lax
from jax.experimental import pallas as pl
from jax.experimental.pallas import tpu as pltpu
from jax.sharding import Mesh, PartitionSpec as P

F32, BF16 = jnp.float32, jnp.bfloat16
TOK, WIDTH, FF = 512, 1024, 4096
BOTH = 2 * TOK
CHUNK = 1024
UNIT = 256
WIDE = 2 * UNIT
ROOT = 0.7978845608028654
CUBE = 0.044715
VMEM, ANY, HBM, SMEM = (
    pl.BlockSpec(memory_space=kind) for kind in (pltpu.VMEM, pl.ANY, pltpu.HBM, pltpu.SMEM)
)
ROOM = 60 * 2**20
ONE = pltpu.SemaphoreType.DMA
TWO = pltpu.SemaphoreType.DMA((2,))
FEW = pltpu.SemaphoreType.DMA((8,))


def shape(*dims, dtype=BF16):
    return jax.ShapeDtypeStruct(dims, dtype)


def work(flops):
    return pl.CostEstimate(flops=int(flops * 0.4), bytes_accessed=1 << 20, transcendentals=0)


def dot(a, b):
    return lax.dot_general(a, b, (((1,), (0,)), ((), ())), preferred_element_type=F32)


def dot_t(a, b):
    return lax.dot_general(a, b, (((1,), (1,)), ((), ())), preferred_element_type=F32)


def normed(values):
    center = values - jnp.mean(values, axis=-1, keepdims=True)
    scale = lax.rsqrt(jnp.mean(center * center, axis=-1, keepdims=True) + 1e-05)
    return center * scale, scale


def norm_back(edge, unit, scale):
    return (edge - jnp.mean(edge, axis=-1, keepdims=True) - unit * jnp.mean(edge * unit, axis=-1, keepdims=True)) * scale


def start(source, target, sem):
    pltpu.make_async_copy(source, target, sem).start()


def wait(ref, sem):
    pltpu.make_async_copy(ref, ref, sem).wait()


def place_of(places, side, axis, slot):
    return places[side * 12 + "xyz".index(axis) * 4 + slot]


def ffn_kernel(places, bias_ref, low_own, low_other, grad_own, grad_other, up, down0, down1, down2, down3,
               bias_grad_ref, feed_ref, feed_low_ref, gc_ref, gc_low_ref, dup, ddown_keep, ddown_move,
               up_buf, down_buf, dup_buf, ddown_buf, low, grad, low_t, act_buf, gpre_buf, total, grad_total,
               feed_low, gc_low, in_sem, up_sem, down_sem, out_sem):
    core = places[24]

    def tiles(chunk, *parts):
        for part in parts or (0, 1):
            for sy in range(4):
                y = place_of(places, 0, "y", sy)
                yh, yl = lax.div(y, 2), lax.rem(y, 2)
                unit = pl.ds(pl.multiple_of((part * 2 + yh) * UNIT, UNIT), UNIT)
                for x in range(4):
                    yield sy, chunk * 2 + part, x, yl, unit

    def model(x, yl):
        return pl.ds(pl.multiple_of((x * 2 + yl) * 128, 128), 128)

    def fetch(chunk):
        for sy, sz, x, yl, unit in tiles(chunk):
            start(up.at[x * 16 + sy * 4 + sz], up_buf.at[chunk, model(x, yl), unit], up_sem.at[chunk])
        for sy, sz, sx, yl, unit in tiles(chunk):
            cols = model(place_of(places, 0, "x", sx), yl)
            start((down0, down1, down2, down3)[sy].at[sx * 4 + sz], down_buf.at[chunk, unit, cols], down_sem.at[chunk])

    def send(chunk, part):
        for y in range(4):
            for x in range(4):
                unit = slice((part * 2 + y // 2) * UNIT, (part * 2 + y // 2 + 1) * UNIT)
                start(dup_buf.at[chunk, model(x, y % 2), unit], dup.at[x, y, chunk * 2 + part], out_sem)
        for sy, sz, sx, yl, unit in tiles(chunk, part):
            source = ddown_buf.at[chunk, unit, model(place_of(places, 0, "x", sx), yl)]
            start(source, (ddown_keep, ddown_move)[sy // 2].at[sy % 2 * 16 + sx * 4 + sz], out_sem)

    start(low_own, low.at[pl.ds(0, TOK)], in_sem.at[0])
    start(low_other, low.at[pl.ds(TOK, TOK)], in_sem.at[0])
    fetch(0)
    start(grad_own, grad.at[pl.ds(0, TOK)], in_sem.at[1])
    start(grad_other, grad.at[pl.ds(TOK, TOK)], in_sem.at[1])
    bias_grad_ref[...] = jnp.zeros_like(bias_grad_ref)
    wait(low, in_sem.at[0])
    wait(grad, in_sem.at[1])

    for chunk in (0, 1):
        wait(up_buf.at[chunk], up_sem.at[chunk])
        wait(down_buf.at[chunk], down_sem.at[chunk])
        for n in range(CHUNK // WIDE):
            cols = slice(n * WIDE, (n + 1) * WIDE)
            blocks = [(place_of(places, 0, "z", chunk * 2 + n) * 2 + yh) * 2 + core for yh in (0, 1)]
            bias = jnp.concatenate([bias_ref[block] for block in blocks], axis=1)
            pre = dot(low[...], up_buf[chunk, :, cols]) + bias
            gact = dot_t(grad[...], down_buf[chunk, cols, :])
            square = pre * pre
            bend = jnp.tanh(ROOT * (pre + CUBE * square * pre))
            half = 0.5 + 0.5 * bend
            act = (pre * half).astype(BF16)
            slope = half + 0.5 * pre * (1.0 - bend * bend) * (ROOT + 3.0 * ROOT * CUBE * square)
            gpre = (gact * slope).astype(BF16)
            if chunk == 0 and n == 0:
                fetch(1)
            act_buf[:, cols] = act
            gpre_buf[:, cols] = gpre
            bias_grad = jnp.sum(gpre.astype(F32), axis=0, keepdims=True)
            for yh, block in enumerate(blocks):
                bias_grad_ref[block] = bias_grad[:, yh * UNIT : (yh + 1) * UNIT]
            if chunk == 0 and n == 0:
                low_t[...] = low[...].T
            ddown_buf[chunk, cols, :] = dot(act.T, grad[...]).astype(BF16)
            dup_buf[chunk, :, cols] = dot(low_t[...], gpre).astype(BF16)
            send(chunk, n)
        more = dot_t(gpre_buf[...], up_buf[chunk])
        feed = dot(act_buf[...], down_buf[chunk])
        if chunk == 0:
            grad_total[...] = more
            total[...] = feed
        else:
            grad_total[...] += more
            gc_low[...] = grad_total[TOK:, :].astype(BF16)
            start(gc_low, gc_low_ref, out_sem)
            start(grad_total.at[pl.ds(0, TOK)], gc_ref, out_sem)
            total[...] += feed
            feed_low[...] = total[TOK:, :].astype(BF16)
            start(feed_low, feed_low_ref, out_sem)
            start(total.at[pl.ds(0, TOK)], feed_ref, out_sem)
    for ref in (dup_buf, ddown_buf, gc_low, feed_low, grad_total.at[pl.ds(0, TOK)], total.at[pl.ds(0, TOK)]):
        wait(ref, out_sem)


def ffn(places, up_bias, low_own, low_other, grad_own, grad_other, weights):
    big = pltpu.VMEM((2, CHUNK, CHUNK), BF16)
    rows = pltpu.VMEM((BOTH, WIDTH), BF16)
    sums = pltpu.VMEM((BOTH, WIDTH), F32)
    half = pltpu.VMEM((TOK, WIDTH), BF16)
    return pl.pallas_call(
        ffn_kernel,
        in_specs=[SMEM, VMEM] + [HBM] * 9,
        out_specs=[VMEM] + [HBM] * 7,
        out_shape=[
            shape(16, 1, UNIT, dtype=F32),
            shape(TOK, WIDTH, dtype=F32),
            shape(TOK, WIDTH),
            shape(TOK, WIDTH, dtype=F32),
            shape(TOK, WIDTH),
            shape(4, 4, 4, 128, 256),
            shape(32, 256, 128),
            shape(32, 256, 128),
        ],
        scratch_shapes=[
            big, big, big, big, rows, rows, rows,
            pltpu.VMEM((BOTH, CHUNK), BF16),
            pltpu.VMEM((BOTH, CHUNK), BF16),
            sums, sums, half, half, TWO, TWO, TWO, ONE,
        ],
        compiler_params=pltpu.CompilerParams(vmem_limit_bytes=ROOM),
        cost_estimate=work(40e9),
        name="ffn",
    )(places, up_bias.reshape(16, 1, UNIT), low_own, low_other, grad_own, grad_other, *weights)


BLOCK = 128
HALF = 512
PART = 3 * HALF


def row_tiles(places):
    core = places[24]
    for side in (0, 1):
        for slot in range(4):
            yield side, slot, place_of(places, side, "z", slot), core if side == 0 else 1 - core


def part_cols(part, cols):
    return slice(part * 2048 + cols.start, part * 2048 + cols.stop)


def fetch_part(places, part, pieces, buf, sem, cols):
    for side, slot, z, c in row_tiles(places):
        start(pieces[2 * side + slot // 2].at[slot % 2, :, :, part_cols(part, cols)], buf.at[z, :, c], sem)


def matrix(ref):
    return ref.reshape(WIDTH, ref.shape[-1])


def parts_buffer(cols):
    return pltpu.VMEM((4, 2, 2, 64, cols), BF16)


def lane_marks():
    low = lax.broadcasted_iota(jnp.int32, (1, 128), 1) < 64
    return low, jnp.where(low, 1.0, 0.0).astype(BF16), jnp.where(low, 0.0, 1.0).astype(BF16)


def front_kernel(places, ln1_ref, qkv_bias_ref, pair_ref, out_bias_ref, ln2_ref, tok, *refs):
    pieces, refs = refs[:4], refs[4:]
    low_out, qkv_out, prob_out, mixed_out, hidden_out, normed_out, qkv_buf0, qkv_buf1, out_buf0, out_buf1 = refs[:10]
    tok_ref, low_ref, qkv_ref, prob_ref, mixed_ref, hidden_ref, normed_ref, sem, out_sem = refs[10:]
    start(tok, tok_ref, sem.at[4])
    for part, buf in ((0, qkv_buf0), (1, qkv_buf1)):
        fetch_part(places, part, pieces, buf, sem.at[part], slice(0, PART))
    for part, buf in ((0, out_buf0), (1, out_buf1)):
        fetch_part(places, part, pieces, buf, sem.at[2 + part], slice(PART, 2048))
    wait(tok_ref, sem.at[4])

    @pl.loop(0, TOK // 128)
    def _(i):
        rows = pl.ds(i * 128, 128)
        unit, _ = normed(tok_ref[rows, :].astype(F32))
        low_ref[rows, :] = (unit * ln1_ref[0:1, :] + ln1_ref[1:2, :]).astype(BF16)

    start(low_ref, low_out, out_sem)
    for part, buf in ((0, qkv_buf0), (1, qkv_buf1)):
        wait(buf, sem.at[part])
        for n in range(3):
            cols = slice(n * HALF, (n + 1) * HALF)
            qkv_ref[part, :, cols] = (dot(low_ref[...], matrix(buf)[:, cols]) + qkv_bias_ref[part, :, cols]).astype(BF16)
        start(qkv_ref.at[part], qkv_out.at[part], out_sem)
    low, near, far = lane_marks()
    near, far = near * 0.125, far * 0.125

    @pl.loop(0, 8)
    def _(pair):
        part = lax.div(pair, 4)
        begin = pl.multiple_of(lax.rem(pair, 4) * 128, 128)
        lanes = pl.ds(pl.multiple_of(pair * 128, 128), 128)
        for block in range(TOK // BLOCK):
            rows = slice(block * BLOCK, (block + 1) * BLOCK)
            query = qkv_ref[part, rows, pl.ds(begin, 128)]
            key = qkv_ref[part, rows, pl.ds(begin + HALF, 128)]
            value = qkv_ref[part, rows, pl.ds(begin + 2 * HALF, 128)]
            bias = pair_ref[block]
            score = dot_t(jnp.concatenate([query * near, query * far], axis=0), key) + jnp.concatenate([bias, bias], axis=0)
            power = jnp.exp(score - jnp.max(score, axis=-1, keepdims=True))
            prob = (power * (1.0 / jnp.sum(power, axis=-1, keepdims=True))).astype(BF16)
            prob_ref[pair, block] = prob
            both = dot(prob, value)
            mixed_ref[rows, lanes] = jnp.where(low, both[:BLOCK], both[BLOCK:]).astype(BF16)

    start(prob_ref, prob_out, out_sem)
    start(mixed_ref, mixed_out, out_sem)
    for part, buf in ((0, out_buf0), (1, out_buf1)):
        cols = slice(part * HALF, (part + 1) * HALF)
        wait(buf, sem.at[2 + part])
        hidden_ref[:, cols] = tok_ref[:, cols].astype(F32) + dot(mixed_ref[...], matrix(buf)[...]) + out_bias_ref[:, cols]
    start(hidden_ref, hidden_out, out_sem)

    @pl.loop(0, TOK // 128)
    def _(i):
        rows = pl.ds(i * 128, 128)
        unit, _ = normed(hidden_ref[rows, :])
        normed_ref[rows, :] = (unit * ln2_ref[0:1, :] + ln2_ref[1:2, :]).astype(BF16)

    start(normed_ref, normed_out, out_sem)
    for ref in (low_ref, qkv_ref, prob_ref, mixed_ref, hidden_ref, normed_ref):
        wait(ref, out_sem)


def front(places, tokens, ln1, qkv_bias, allowed, out_bias, ln2, pieces):
    wide = ((TOK, WIDTH), BF16)
    outs = [wide, ((2, TOK, PART), BF16), ((8, 4, 2 * BLOCK, BLOCK), BF16), wide, ((TOK, WIDTH), F32), wide]
    return pl.pallas_call(
        front_kernel,
        in_specs=[SMEM] + [VMEM] * 5 + [HBM] * 5,
        out_specs=[HBM] * 6,
        out_shape=[jax.ShapeDtypeStruct(*out) for out in outs],
        scratch_shapes=[parts_buffer(PART)] * 2 + [parts_buffer(HALF)] * 2 + [pltpu.VMEM(*s) for s in [wide] + outs] + [FEW, ONE],
        compiler_params=pltpu.CompilerParams(vmem_limit_bytes=ROOM),
        cost_estimate=work(24e9),
        name="front",
    )(places, ln1, qkv_bias, allowed, out_bias.reshape(1, WIDTH), ln2, tokens, *pieces)


def turn(hidden_ref, gain_ref, gc_ref, got_ref, grad_ref, ghid_ref, glow_ref, vec_ref):
    @pl.loop(0, TOK // 128)
    def _(part):
        rows = pl.ds(part * 128, 128)
        unit, scale = normed(hidden_ref[rows, :])
        gc = gc_ref[rows, :] + got_ref[rows, :].astype(F32)
        gout = grad_ref[rows, :].astype(F32)
        ghid = gout + norm_back(gc * gain_ref[...], unit, scale)
        ghid_ref[rows, :] = ghid
        glow_ref[rows, :] = ghid.astype(BF16)
        vec_ref[4:5, :] += jnp.sum(ghid, axis=0, keepdims=True)
        vec_ref[5:6, :] += jnp.sum(gc * unit, axis=0, keepdims=True)
        vec_ref[6:7, :] += jnp.sum(gc, axis=0, keepdims=True)
        vec_ref[7:8, :] += jnp.sum(gout, axis=0, keepdims=True)


def back_kernel(places, ln1_ref, ln2_gain_ref, down_bias_ref, up_bias_grad_ref,
                hidden, gc, gc_got, cot, mixed, low_in, qkv, prob, tok, feed, feed_got, *refs):
    pieces, refs = refs[:4], refs[4:]
    gin_out, out_out, vec_ref, *outs = refs[:7]
    qkv_buf0, qkv_buf1, out_buf0, out_buf1, grad_buf0, grad_buf1 = refs[7:13]
    hidden_ref, gc_ref, gc_got_ref, cot_ref, mixed_ref, low_ref, qkv_ref, prob_ref, tok_ref, feed_ref, feed_got_ref = refs[13:24]
    ghid_ref, glow_ref, gmix_ref, gqkv_ref, flip, out_ref, sem, out_sem = refs[24:]
    start(mixed, mixed_ref, sem.at[1])
    for source, target in ((hidden, hidden_ref), (gc, gc_ref), (gc_got, gc_got_ref), (cot, cot_ref)):
        start(source, target, sem.at[0])
    for part, buf in ((0, out_buf0), (1, out_buf1)):
        fetch_part(places, part, pieces, buf, sem.at[2], slice(PART, 2048))
    start(qkv, qkv_ref, sem.at[3])
    start(prob, prob_ref, sem.at[3])
    start(low_in, low_ref, sem.at[4])
    for part, buf in ((0, qkv_buf0), (1, qkv_buf1)):
        fetch_part(places, part, pieces, buf, sem.at[5], slice(0, PART))
    for source, target in ((tok, tok_ref), (feed, feed_ref), (feed_got, feed_got_ref)):
        start(source, target, sem.at[6])
    vec_ref[...] = jnp.zeros_like(vec_ref)
    for block in range(16):
        row, col = 8 + block // 4, block % 4 * UNIT
        vec_ref[row : row + 1, col : col + UNIT] = up_bias_grad_ref[block]
    wait(mixed_ref, sem.at[1])
    flip[...] = mixed_ref[...].T
    for ref in (hidden_ref, gc_ref, gc_got_ref, cot_ref):
        wait(ref, sem.at[0])
    turn(hidden_ref, ln2_gain_ref, gc_ref, gc_got_ref, cot_ref, ghid_ref, glow_ref, vec_ref)
    grads = [matrix(grad_buf0), matrix(grad_buf1)]
    for part in (0, 1):
        heads = slice(part * HALF, (part + 1) * HALF)
        grads[part][:, PART:] = dot(flip[...], glow_ref[:, heads]).astype(BF16)
    for buf in (out_buf0, out_buf1):
        wait(buf, sem.at[2])
    gmix_ref[...] = (
        dot_t(glow_ref[:, :HALF], matrix(out_buf0)[...]) + dot_t(glow_ref[:, HALF:], matrix(out_buf1)[...])
    ).astype(BF16)
    wait(low_ref, sem.at[4])
    flip[...] = low_ref[...].T
    wait(qkv_ref, sem.at[3])
    wait(prob_ref, sem.at[3])
    low, near, far = lane_marks()

    for part, grad_buf in ((0, grad_buf0), (1, grad_buf1)):
        @pl.loop(0, 4)
        def _(pair, part=part):
            begin = pl.multiple_of(pair * 128, 128)
            for block in range(TOK // BLOCK):
                rows = slice(block * BLOCK, (block + 1) * BLOCK)
                query = qkv_ref[part, rows, pl.ds(begin, 128)]
                key = qkv_ref[part, rows, pl.ds(begin + HALF, 128)]
                value = qkv_ref[part, rows, pl.ds(begin + 2 * HALF, 128)]
                gmix = gmix_ref[rows, pl.ds(pl.multiple_of(begin + part * HALF, 128), 128)]
                gmix = jnp.concatenate([gmix * near, gmix * far], axis=0)
                query = jnp.concatenate([query * (near * 0.125), query * (far * 0.125)], axis=0)
                prob_low = prob_ref[pair + 4 * part, block]
                prob = prob_low.astype(F32)
                gprob = dot_t(gmix, value)
                gscore = (prob * (gprob - jnp.sum(prob * gprob, axis=-1, keepdims=True))).astype(BF16)
                both = dot(gscore, key) * 0.125
                gqkv_ref[part, rows, pl.ds(begin, 128)] = jnp.where(low, both[:BLOCK], both[BLOCK:]).astype(BF16)
                gqkv_ref[part, rows, pl.ds(begin + HALF, 128)] = dot(gscore.T, query).astype(BF16)
                gqkv_ref[part, rows, pl.ds(begin + 2 * HALF, 128)] = dot(prob_low.T, gmix).astype(BF16)

        for n in range(3):
            cols = slice(n * HALF, (n + 1) * HALF)
            grads[part][:, cols] = dot(flip[...], gqkv_ref[part, :, cols]).astype(BF16)
        for side, slot, z, c in row_tiles(places):
            start(grad_buf.at[z, :, c], outs[2 * side + slot // 2].at[slot % 2, :, :, part * 2048 : (part + 1) * 2048], out_sem)
        heads = slice(part * HALF, (part + 1) * HALF)
        for row, n in ((2, 0), (3, 2)):
            vec_ref[row : row + 1, heads] = jnp.sum(gqkv_ref[part, :, n * HALF : (n + 1) * HALF].astype(F32), axis=0, keepdims=True)

    for ref in (tok_ref, feed_ref, feed_got_ref):
        wait(ref, sem.at[6])
    out_ref[...] = (hidden_ref[...] + feed_ref[...] + feed_got_ref[...].astype(F32) + down_bias_ref[...]).astype(BF16)
    start(out_ref, out_out, out_sem)
    for buf in (qkv_buf0, qkv_buf1):
        wait(buf, sem.at[5])
    gc_ref[...] = dot_t(gqkv_ref[0], matrix(qkv_buf0)[...]) + dot_t(gqkv_ref[1], matrix(qkv_buf1)[...])

    @pl.loop(0, TOK // 128)
    def _(i):
        rows = pl.ds(i * 128, 128)
        unit, scale = normed(tok_ref[rows, :].astype(F32))
        grad = gc_ref[rows, :]
        ghid_ref[rows, :] += norm_back(grad * ln1_ref[0:1, :], unit, scale)
        vec_ref[0:1, :] += jnp.sum(grad * unit, axis=0, keepdims=True)
        vec_ref[1:2, :] += jnp.sum(grad, axis=0, keepdims=True)

    start(ghid_ref, gin_out, out_sem)
    for ref in (grad_buf0, grad_buf1, out_ref, ghid_ref):
        wait(ref, out_sem)


def back(places, ln1, ln2_gain, down_bias, up_bias_grad, streams, pieces):
    wide, high = ((TOK, WIDTH), BF16), ((TOK, WIDTH), F32)
    heads = ((2, TOK, PART), BF16)
    scratch = [high, high, wide, wide, wide, wide, heads, ((8, 4, 2 * BLOCK, BLOCK), BF16), wide, high, wide]
    scratch += [high, wide, wide, heads, ((WIDTH, TOK), BF16), wide]
    rows = shape(2, 2, 64, 4096)
    return pl.pallas_call(
        back_kernel,
        in_specs=[SMEM] + [VMEM] * 4 + [HBM] * 15,
        out_specs=[HBM] * 2 + [VMEM] + [HBM] * 4,
        out_shape=[shape(TOK, WIDTH, dtype=F32), shape(TOK, WIDTH), shape(16, WIDTH, dtype=F32), rows, rows, rows, rows],
        scratch_shapes=[parts_buffer(PART)] * 2 + [parts_buffer(HALF)] * 2 + [parts_buffer(2048)] * 2
        + [pltpu.VMEM(*s) for s in scratch]
        + [FEW, ONE],
        compiler_params=pltpu.CompilerParams(vmem_limit_bytes=ROOM),
        cost_estimate=work(40e9),
        name="back",
    )(places, ln1, ln2_gain.reshape(1, WIDTH), down_bias.reshape(1, WIDTH), up_bias_grad, *streams, *pieces)


AXES = ("z", "yh", "c", "x", "yl")
ALONG_Y, PLANE_XY = ("yh", "yl"), ("yh", "x", "yl")


def device_number(place):
    return (
        ((place["z"] * 2 + place["y"] // 2) * 2 + place["c"]) * 4 + place["x"]
    ) * 2 + place["y"] % 2


def exchange_pairs(axis, second, alike=False):
    pairs = []
    for z, y, c, x in itertools.product(range(4), range(4), range(2), range(4)):
        here = {"z": z, "y": y, "c": c, "x": x}
        mask = 1 if (c == 0 or alike) != second else 3
        there = dict(here)
        there[axis] = here[axis] ^ mask
        pairs.append((device_number(here), device_number(there)))
    return pairs


def swap_axis(values, axis, second, alike=False):
    return lax.ppermute(values, AXES, exchange_pairs(axis, second, alike))


def swap_core(values):
    return lax.ppermute(values, "c", [(0, 1), (1, 0)])


def position(axis):
    if axis == "y":
        return lax.axis_index("yh") * 2 + lax.axis_index("yl")
    return lax.axis_index(axis)


def distance_of(core, slot):
    return jnp.where(core == 0, slot ^ (slot >> 1), ((slot << 1) & 3) ^ ((slot ^ (slot >> 1)) & 1))


def place_table():
    core, slots = lax.axis_index("c"), jnp.arange(4, dtype=jnp.int32)
    rows = [
        distance_of(side, slots) ^ position(axis)
        for side in (core, 1 - core)
        for axis in ("x", "y", "z")
    ]
    return jnp.concatenate(rows + [jnp.full((8,), core, jnp.int32)])


def add(left, right, dtype=BF16):
    return (left.astype(F32) + right.astype(F32)).astype(dtype)


def halves(own, got):
    count = own.shape[0] // 2
    return add(own[count:], got[count:]), add(own[:count], got[:count])


def spread(values, axes):
    return lax.all_to_all(jnp.broadcast_to(values, (16,) + values.shape), axes, 0, 0)


def together(*values):
    return lax.optimization_barrier(values)


def pair_bias(clip_ids):
    clips = clip_ids.reshape(-1, BLOCK)
    row = lax.broadcasted_iota(jnp.int32, (BLOCK, BLOCK), 0)
    col = lax.broadcasted_iota(jnp.int32, (BLOCK, BLOCK), 1)
    allowed = (clips[:, :, None] == clips[:, None, :]) & (row >= col)[None]
    return jnp.where(allowed, 0.0, -1e30).astype(F32)


def on_device(
    tokens,
    qkv_weight,
    out_weight,
    up_weight,
    down_weight,
    ln1_gain,
    ln1_bias,
    q_bias,
    v_bias,
    out_bias,
    ln2_gain,
    ln2_bias,
    up_bias,
    down_bias,
    segment_ids,
    cotangent,
):
    places = place_table()
    ln1 = jnp.stack([ln1_gain, ln1_bias])
    nothing = jnp.zeros((HALF,), F32)
    qkv_bias = jnp.stack(
        [
            jnp.concatenate([q_bias[cols], nothing, v_bias[cols]])[None]
            for cols in (slice(0, HALF), slice(HALF, WIDTH))
        ]
    )
    ln2 = jnp.stack([ln2_gain, ln2_bias])
    allowed = pair_bias(segment_ids)

    heads = qkv_weight.reshape(8, 3, WIDTH)
    pieces = []
    for cols in (slice(0, HALF), slice(HALF, WIDTH)):
        pieces += [heads[:, :, cols].reshape(8, PART), out_weight[:, cols]]
    def join(pairs):
        return together(*[jnp.concatenate(pair) for pair in pairs])

    rows = spread(jnp.concatenate(pieces, axis=1), PLANE_XY)
    down, up = down_weight[None], up_weight[None]
    down, up = join(((down, swap_axis(down, "z", False)), (up, swap_axis(up, "z", False))))
    rows, down_got, up_got, places, ln1, ln2, qkv_bias, allowed = together(
        rows, swap_axis(down, "z", True), swap_axis(up, "z", True), places, ln1, ln2, qkv_bias, allowed
    )
    rows = rows.reshape(1, 2, 64, 4096)
    rows_got = swap_axis(rows, "z", False)
    down, up = join(((down, down_got), (up, up_got)))
    down, up = join(((down, swap_axis(down, "x", False)), (up, swap_axis(up, "y", False))))
    rows_got, down_got, up_got, grad_other = together(
        rows_got, swap_axis(down, "x", True), swap_axis(up, "y", True), swap_core(cotangent)
    )
    rows, down, up = join(((rows, rows_got), (down, down_got), (up, up_got)))
    up = lax.all_gather(up, "x", axis=0).reshape(64, 128, 256)
    near, far = swap_axis(down, "y", False), swap_axis(down, "y", True)
    rows_got, near, far, other_rows = together(swap_axis(rows, "z", True), near, far, swap_core(rows))
    pieces = (rows, rows_got, other_rows, swap_core(rows_got))
    downs = (down, near, far, swap_axis(near, "y", True))

    low, qkv, prob, mixed, hidden, low2 = front(
        places, tokens, ln1, qkv_bias, allowed, out_bias, ln2, pieces
    )
    up_bias_grad, feed, feed_low, gc, gc_low, dup, keep_down, move_down = ffn(
        places, up_bias, low2, swap_core(low2), cotangent, grad_other, (up, *downs)
    )
    dup = lax.psum_scatter(dup, "x", scatter_dimension=0, tiled=True)[0]

    down_got = swap_axis(move_down, "y", True)
    grad_tokens, output, vector, own_keep, own_move, other_keep, other_move = back(
        places, ln1, ln2_gain, down_bias, up_bias_grad,
        (hidden, gc, swap_core(gc_low), cotangent, mixed, low, qkv, prob, tokens, feed, swap_core(feed_low)),
        pieces,
    )
    down_got, vector, own_keep, own_move, other_keep, other_move = together(
        down_got, vector, own_keep, own_move, other_keep, other_move
    )
    got_move, got_keep, vector_got = swap_core(other_move), swap_core(other_keep), swap_core(vector)
    move = add(own_move, got_move)
    move, down_got, vector, vector_got = together(move, down_got, vector, vector_got)
    got = swap_axis(move, "z", True)
    keep = add(own_keep, got_keep)
    move_down, keep_down = halves(keep_down, down_got)
    down_got = swap_axis(move_down, "y", False)
    move_down, keep_down = halves(keep_down, down_got)
    down_got = swap_axis(move_down, "x", True)
    vector = vector + vector_got
    vector_got, dup = together(swap_axis(vector, "x", False, True), dup)
    dup = lax.psum_scatter(dup, ALONG_Y, scatter_dimension=0, tiled=True)[0]
    vector = vector + vector_got
    vector_got = swap_axis(vector, "x", True, True)
    got, keep, down_got, vector_got, dup = together(got, keep, down_got, vector_got, dup)

    move, keep = halves(keep, got)
    move, down_got, vector_got = together(move, down_got, vector_got)
    got = swap_axis(move, "z", False)
    move_down, keep_down = halves(keep_down, down_got)
    down_got = swap_axis(move_down, "x", False)
    move_down, keep_down = halves(keep_down, down_got)
    down_got = swap_axis(move_down, "z", True)
    up_got = swap_axis(dup[2:], "z", True)
    vector = vector + vector_got
    vector = vector + swap_axis(vector, "y", False, True)
    vector_got = swap_axis(vector, "y", True, True)
    got, down_got, up_got, vector_got = together(got, down_got, up_got, vector_got)

    rows_sum = add(keep, got).reshape(16, 8, 4096)
    rows_sum, down_got, vector_got = together(rows_sum, down_got, vector_got)
    rows_parts = lax.all_to_all(rows_sum, PLANE_XY, 0, 0)
    vector = vector + vector_got
    for second in (False, True):
        vector = vector + swap_axis(vector, "z", second, True)
    move_down, keep_down = halves(keep_down, down_got)
    down_got = swap_axis(move_down, "z", False)
    move_up, keep_up = halves(dup[:2], up_got)
    up_grad = add(keep_up, swap_axis(move_up, "z", False), F32)[0]
    down_grad = add(keep_down, down_got, F32)[0]
    row = jnp.sum(rows_parts.astype(F32), axis=0).reshape(8, 2, 2048)
    qkv_grad = row[:, :, :PART].reshape(8, 2, 3, HALF).transpose(0, 2, 1, 3).reshape(8, 3 * WIDTH)
    out_grad = row[:, :, PART:].reshape(8, WIDTH)
    summed = vector.reshape(-1)
    vectors = [summed[i * WIDTH : (i + 1) * WIDTH] for i in range(8)]
    return (
        output,
        grad_tokens,
        qkv_grad,
        out_grad,
        up_grad,
        down_grad,
        *vectors[:7],
        summed[8 * WIDTH : 12 * WIDTH],
        vectors[7],
    )


def solution(mesh):
    fine = Mesh(mesh.devices.reshape(4, 2, 2, 4, 2), AXES)
    every, hidden, model = AXES, ("z", "yh", "c"), ("x", "yl")
    weights = (P(every, None), P(every, None), P(model, hidden), P(hidden, model))
    return jax.shard_map(
        on_device,
        mesh=fine,
        in_specs=(P(every, None), *weights, *[P()] * 9, P(every), P(every, None)),
        out_specs=(P(every, None), P(every, None), *weights, *[P()] * 9),
        check_vma=False,
    )
```
